32 devices in a mesh: slab: 4 (over x, core), coil: 8 (over z, y).
Axes of the slice: x: 2, y: 2, z: 4, core: 2. Of those that a mesh axis runs over, the one named last changes fastest.
Arguments:
- prior_image: float32 [256, 128, 128], P(('slab', 'coil')), may hold values from -12 to 12
- coil_maps: bfloat16 [8, 256, 128, 128], P('coil', 'slab'), may hold values from -3 to 3
- kspace: bfloat16 [8, 128, 256, 128], P('coil', 'slab'), may hold values from -6 to 6
- sampling: int32 [128, 256], P('slab'), may hold values 0 or 1
- weight_first: bfloat16 [3, 3, 3, 32, 2], replicated, may hold values from -0.875 to 0.875
- bias_first: float32 [32], replicated, may hold values from -3 to 3
- weight_middle: bfloat16 [3, 3, 3, 32, 32], replicated, may hold values from -0.21875 to 0.21875
- bias_middle: float32 [32], replicated, may hold values from -3 to 3
- weight_last: bfloat16 [3, 3, 3, 2, 32], replicated, may hold values from -0.21875 to 0.21875
- bias_last: float32 [2], replicated, may hold values from -3 to 3
Outputs:
- solution: float32 [256, 128, 128], P(('slab', 'coil'))
- residual: float32 [256, 128, 128], P(('slab', 'coil'))
The draws below stay inside these ranges and needn't reach their ends.
All inputs are finite; a program needn't handle non-finite values. No bound on the sum of `sampling` on one device may be relied on, other than what follows from the above.
Results may differ from the reference program's by a relative error of at most 0.0018.
Values may be sent and summed in bfloat16 or wider, within the bound.
No kernel may reach another device: no remote copies, remote signals or barrier semaphores. Data moves between devices by JAX's collectives and lax.ppermute only.
A program may use at most 192 MiB of HBM per device.

```python
import jax
import jax.numpy as jnp
from jax import lax

Y = 256
Z = 128
X = 64
CHANNELS = 32
CG_ITERS = 2
COILS = 8


def envelope_draw(key, shape_rows, shape_planes, last_size, spread):
    row_index = jnp.arange(shape_rows, dtype=jnp.float32)
    envelope = jnp.sqrt(1.0 + 5.0 * row_index / shape_rows)[:, None, None]
    values = jax.random.normal(key, (shape_rows, shape_planes, last_size))
    return values * envelope * spread


def draw_prior_image(key, part):
    values = envelope_draw(jax.random.fold_in(key, 11), Y, Z, 2 * X, 1.0)
    return jnp.clip(values, -12.0, 12.0).astype(jnp.float32)


def draw_coil_maps(key, part):
    keys = jax.random.split(jax.random.fold_in(key, 23), COILS)
    spread = 1.0 / jnp.sqrt(2.0 * COILS)
    values = jax.vmap(lambda coil_key: envelope_draw(coil_key, Y, Z, 2 * X, spread))(keys)
    return jnp.clip(values, -3.0, 3.0).astype(jnp.bfloat16)


def plant(values, own_key, least, largest):
    dims = values.shape
    place = [jax.random.randint(jax.random.fold_in(own_key, axis), (), 0, dims[axis]) for axis in range(len(dims))]
    values = values.at[tuple(place)].set(least)
    longest = dims.index(max(dims))
    place[longest] = (place[longest] + 1) % dims[longest]
    return values.at[tuple(place)].set(largest)


def steps_of(key, dims, cuts, least, high):
    level = 1.0
    for dim, blocks in cuts:
        heights = jax.random.uniform(jax.random.fold_in(jax.random.fold_in(key, 6), dim), (blocks,), jnp.float32, least / len(cuts), high / len(cuts))
        level = level * jnp.repeat(jnp.exp(heights), dims[dim] // blocks).reshape((-1,) + (1,) * (len(dims) - 1 - dim))
    return level


def scatter_about(rng, dims, scale, bound, cuts=(), kind=jnp.bfloat16):
    gain = steps_of(rng, dims, cuts, -0.22, 0.18) if cuts else 1.0
    entries = jax.random.normal(rng, dims, jnp.float32) * scale * gain
    return jnp.minimum(jnp.maximum(entries, -bound), bound).astype(kind)


def setup_inputs(seed: int = 0) -> dict:
    seeds = jax.random.split(jax.random.key(seed), 11)
    return {
        "prior_image": draw_prior_image(jax.random.fold_in(seeds[10], 71), 0),
        "coil_maps": draw_coil_maps(jax.random.fold_in(seeds[10], 71), 0),
        "kspace": scatter_about(seeds[2], (COILS, Z, Y, 2 * X), 1.0, 6.0, ((0, 8), (1, 4))),
        "sampling": plant((jax.random.randint(seeds[3], (Z, Y), 0, 3) < 1).astype(jnp.int32), jax.random.fold_in(seeds[3], 1), 0, 1),
        "weight_first": scatter_about(seeds[4], (3, 3, 3, CHANNELS, 2), 54 ** -0.5, 0.875),
        "bias_first": scatter_about(seeds[5], (CHANNELS,), 0.5, 3.0, (), jnp.float32),
        "weight_middle": scatter_about(seeds[6], (3, 3, 3, CHANNELS, CHANNELS), (27 * CHANNELS) ** -0.5, 0.21875),
        "bias_middle": scatter_about(seeds[7], (CHANNELS,), 0.5, 3.0, (), jnp.float32),
        "weight_last": scatter_about(seeds[8], (3, 3, 3, 2, CHANNELS), (27 * CHANNELS) ** -0.5, 0.21875),
        "bias_last": scatter_about(seeds[9], (2,), 0.5, 3.0, (), jnp.float32),
    }


penalty = 0.5


def convolve(features, weights, offsets):
    kernel = jnp.transpose(weights.astype(jnp.float32), (3, 4, 0, 1, 2))
    result = lax.conv_general_dilated(features.astype(jnp.float32)[None], kernel, (1, 1, 1), ((1, 1), (1, 1), (1, 1)), dimension_numbers=("NCDHW", "OIDHW", "NCDHW"), precision=lax.Precision.HIGHEST)
    return result[0] + offsets.astype(jnp.float32)[:, None, None, None]


def as_complex(volume):
    half_width = volume.shape[-1] // 2
    return lax.complex(volume[..., :half_width], volume[..., half_width:])


def as_real(volume):
    return jnp.concatenate([jnp.real(volume), jnp.imag(volume)], axis=-1)


def reference(prior_image, coil_maps, kspace, sampling, weight_first, bias_first, weight_middle, bias_middle, weight_last, bias_last):
    half_width = prior_image.shape[-1] // 2
    features = jnp.stack([prior_image[..., :half_width], prior_image[..., half_width:]]).astype(jnp.bfloat16)
    hidden = jax.nn.relu(convolve(features, weight_first, bias_first)).astype(jnp.bfloat16)
    hidden = jax.nn.relu(convolve(hidden, weight_middle, bias_middle)).astype(jnp.bfloat16)
    output = convolve(hidden, weight_last, bias_last)
    denoised = prior_image + jnp.concatenate([output[0], output[1]], axis=-1)
    sampled = jnp.transpose(sampling).astype(jnp.float32)[:, :, None]

    def adjoint_step(running, pair):
        coil_map, measured = pair
        sensitivity = as_complex(coil_map.astype(jnp.float32))
        spectrum = as_complex(jnp.transpose(measured.astype(jnp.float32), (1, 0, 2))) * sampled
        image_side = jnp.fft.ifft2(spectrum, axes=(0, 1), norm="ortho")
        return running + jnp.conj(sensitivity) * image_side, None

    adjoint = lax.scan(adjoint_step, as_complex(jnp.zeros_like(prior_image)), (coil_maps, kspace))[0]
    right_side = as_real(adjoint) + penalty * denoised

    def operator(direction):
        field_value = as_complex(direction)

        def coil_step(running, coil_map):
            sensitivity = as_complex(coil_map.astype(jnp.float32))
            spectrum = jnp.fft.fft2(sensitivity * field_value, axes=(0, 1), norm="ortho") * sampled
            image_side = jnp.fft.ifft2(spectrum, axes=(0, 1), norm="ortho")
            return running + jnp.conj(sensitivity) * image_side, None

        running = lax.scan(coil_step, as_complex(jnp.zeros_like(direction)), coil_maps)[0]
        return as_real(running) + penalty * direction

    solution = jnp.zeros_like(right_side)
    residual = right_side
    direction = right_side
    norm_now = jnp.sum(residual * residual)
    for iteration in range(CG_ITERS):
        image_dir = operator(direction)
        step_size = norm_now / jnp.sum(direction * image_dir)
        solution = solution + step_size * direction
        residual = residual - step_size * image_dir
        if iteration + 1 < CG_ITERS:
            norm_next = jnp.sum(residual * residual)
            direction = residual + (norm_next / norm_now) * direction
            norm_now = norm_next
    return solution, residual
```

```python
import functools
import math

import jax
import jax.numpy as jnp
import numpy as np
from jax import lax
from jax.experimental import pallas as pl
from jax.experimental.pallas import tpu as pltpu
from jax.sharding import PartitionSpec as P

CG_ITERS = 2


penalty = 0.5
axes = ("slab", "coil")


def padded_2(cells, sides, width):
    for axis, dim in sides:
        count = lax.axis_size(axis)
        ends = count - 1
        head = lax.slice_in_dim(cells, 0, width, axis=dim)
        tail = lax.slice_in_dim(cells, cells.shape[dim] - width, cells.shape[dim], axis=dim)
        cells = jnp.concatenate(
            [
                lax.ppermute(tail, axis, [(i, (i + 1) % count) for i in range(ends)]),
                cells,
                lax.ppermute(head, axis, [((i + 1) % count, i) for i in range(ends)]),
            ],
            axis=dim,
        )
    return cells


def convolve_layer(features, weights, offsets, readout):
    row_total = features.shape[0]
    in_channels = features.shape[1]
    span_cells = features.shape[2]
    out_channels = weights.shape[3]
    extended = padded_2(features, ((("slab", "coil"), 0),), 1)
    padded = jnp.pad(extended, ((0, 0), (0, 0), (readout + 1, readout + 1)))
    column = (jnp.arange(padded.shape[2], dtype=jnp.int32) - 1) % readout
    zero_value = jnp.zeros((), padded.dtype)
    sources = (
        jnp.where(column != readout - 1, padded, zero_value),
        padded,
        jnp.where(column != 0, padded, zero_value),
    )
    running = jnp.zeros((row_total, out_channels, span_cells), jnp.float32)
    for row_shift in range(3):
        for plane_shift in range(3):
            pieces = []
            for column_shift in range(3):
                first_cell = plane_shift * readout + column_shift
                pieces.append(
                    lax.slice(
                        sources[column_shift],
                        (row_shift, 0, first_cell),
                        (row_shift + row_total, in_channels, first_cell + span_cells),
                    )
                )
            stacked = jnp.concatenate(pieces, axis=1)
            kernel = jnp.transpose(weights[row_shift, plane_shift], (1, 0, 2)).reshape(
                out_channels, 3 * in_channels
            )
            running = running + jnp.einsum(
                "oc,ycn->yon", kernel, stacked, preferred_element_type=jnp.float32
            )
    return running + offsets[None, :, None]


def denoise(
    prior_image, weight_first, bias_first, weight_middle, bias_middle, weight_last, bias_last
):
    readout = prior_image.shape[2] // 2
    own_rows = prior_image.shape[0]
    planes = prior_image.shape[1]
    features = (
        jnp.stack([prior_image[..., :readout], prior_image[..., readout:]], axis=1)
        .reshape(own_rows, 2, planes * readout)
        .astype(jnp.bfloat16)
    )
    hidden = jax.nn.relu(convolve_layer(features, weight_first, bias_first, readout)).astype(
        jnp.bfloat16
    )
    hidden = jax.nn.relu(convolve_layer(hidden, weight_middle, bias_middle, readout)).astype(
        jnp.bfloat16
    )
    output = convolve_layer(hidden, weight_last, bias_last, readout).reshape(
        own_rows, 2, planes, readout
    )
    return prior_image + jnp.concatenate([output[:, 0], output[:, 1]], axis=-1)


def table_parts(table):
    high = table.astype(jnp.bfloat16)
    low = (table - high.astype(np.float64)).astype(jnp.bfloat16)
    return high, low


def dft_parts(length):
    positions = np.arange(length, dtype=np.int64)
    angles = (positions[:, None] * positions[None, :] % length) * (2.0 * math.pi / length)
    scale = 1.0 / math.sqrt(length)
    return np.cos(angles) * scale, np.sin(angles) * scale


def row_table(length):
    cos_part, sin_part = dft_parts(length)
    high, low = table_parts(np.concatenate([cos_part, sin_part], axis=0))
    return np.concatenate([high, low, high], axis=1)


def plane_table(length, inverse):
    cos_part, sin_part = dft_parts(length)
    if inverse:
        sin_part = -sin_part
    table = np.concatenate(
        [
            np.concatenate([cos_part, -sin_part], axis=1),
            np.concatenate([sin_part, cos_part], axis=1),
        ],
        axis=0,
    )
    high, low = table_parts(table)
    return np.concatenate([high, low, high], axis=0)


def value_parts(value):
    high = value.astype(jnp.bfloat16)
    low = (value - high.astype(jnp.float32)).astype(jnp.bfloat16)
    return high, low


def along_planes(value, table):
    high, low = value_parts(value)
    return jnp.dot(
        jnp.concatenate([high, high, low], axis=1), table, preferred_element_type=jnp.float32
    )


def along_rows(table, value):
    high, low = value_parts(value)
    return jnp.dot(
        table, jnp.concatenate([high, high, low], axis=0), preferred_element_type=jnp.float32
    )


def rows_combined(stacked, inverse):
    rows = stacked.shape[0] // 2
    half = stacked.shape[1] // 2
    cos_real, cos_imag = stacked[:rows, :half], stacked[:rows, half:]
    sin_real, sin_imag = stacked[rows:, :half], stacked[rows:, half:]
    if inverse:
        return cos_real - sin_imag, cos_imag + sin_real
    return cos_real + sin_imag, cos_imag - sin_real


def plane_of(ref, part):
    value = ref[:, part, 0]
    return value.reshape(value.shape[0] * value.shape[1], value.shape[2])


def map_of(ref, part):
    value = ref[:, 0, part, 0]
    return value.reshape(value.shape[0] * value.shape[1], value.shape[2]).astype(jnp.float32)


def normal_product(map_real, map_imag, real, imag, mask, rows, planes, inverse_planes):
    half = real.shape[1]
    coil_real = map_real * real - map_imag * imag
    coil_imag = map_real * imag + map_imag * real
    field = along_planes(jnp.concatenate([coil_real, coil_imag], axis=1), planes)
    real, imag = rows_combined(along_rows(rows, field), False)
    spectrum = jnp.concatenate([real * mask, imag * mask], axis=1)
    real, imag = rows_combined(along_rows(rows, spectrum), True)
    field = along_planes(jnp.concatenate([real, imag], axis=1), inverse_planes)
    real, imag = field[:, :half], field[:, half:]
    return map_real * real + map_imag * imag, map_real * imag - map_imag * real


def adjoint_kernel(kspace_ref, maps_ref, mask_ref, rows_ref, inverse_ref, out_ref):
    mask = mask_ref[...]
    parts = []
    for part in range(2):
        parts.append((jnp.transpose(map_of(kspace_ref, part)) * mask).astype(jnp.bfloat16))
    spectrum = jnp.concatenate(parts, axis=1)
    length = spectrum.shape[0]
    stacked = jnp.dot(
        rows_ref[:, : 2 * length],
        jnp.concatenate([spectrum, spectrum], axis=0),
        preferred_element_type=jnp.float32,
    )
    real, imag = rows_combined(stacked, True)
    half = real.shape[1]
    field = along_planes(jnp.concatenate([real, imag], axis=1), inverse_ref[...])
    real, imag = field[:, :half], field[:, half:]
    map_real, map_imag = map_of(maps_ref, 0), map_of(maps_ref, 1)
    shape = out_ref.shape[0], out_ref.shape[3], out_ref.shape[4]
    sums = (map_real * real + map_imag * imag, map_real * imag - map_imag * real)

    @pl.when(pl.program_id(1) == 0)
    def _():
        for part in range(2):
            out_ref[:, part, 0] = sums[part].reshape(shape)

    @pl.when(pl.program_id(1) > 0)
    def _():
        for part in range(2):
            out_ref[:, part, 0] += sums[part].reshape(shape)


def first_kernel(
    maps_ref, adjoint_ref, denoised_ref, mask_ref, rows_ref, planes_ref, inverse_ref, right_ref, out_ref
):
    @pl.when(pl.program_id(1) == 0)
    def _():
        right = adjoint_ref[...] + penalty * denoised_ref[...]
        right_ref[...] = right
        out_ref[...] = jnp.zeros_like(out_ref)

    sums = normal_product(
        map_of(maps_ref, 0),
        map_of(maps_ref, 1),
        plane_of(right_ref, 0),
        plane_of(right_ref, 1),
        mask_ref[...],
        rows_ref[...],
        planes_ref[...],
        inverse_ref[...],
    )
    shape = out_ref.shape[0], out_ref.shape[3], out_ref.shape[4]
    for part in range(2):
        out_ref[:, part, 0] += sums[part].reshape(shape)


def second_kernel(
    maps_ref, right_ref, field_ref, mask_ref, rows_ref, planes_ref, inverse_ref, out_ref, total_ref
):
    x_index = pl.program_id(0)
    x_count = pl.num_programs(0)
    blocks, block_rows, planes = out_ref.shape[0], out_ref.shape[2], out_ref.shape[3]
    shape = blocks, block_rows, planes

    @pl.when(pl.program_id(1) == 0)
    def _():
        for part in range(2):
            out_ref[:, part * x_count + x_index] = jnp.zeros(shape, jnp.float32)

    sums = normal_product(
        map_of(maps_ref, 0),
        map_of(maps_ref, 1),
        plane_of(field_ref, 0),
        plane_of(field_ref, 1),
        mask_ref[...],
        rows_ref[...],
        planes_ref[...],
        inverse_ref[...],
    )
    for part in range(2):
        out_ref[:, part * x_count + x_index] += sums[part].reshape(shape)

    @pl.when(pl.program_id(1) == pl.num_programs(1) - 1)
    def _():
        rights = [right_ref[:, part, 0] for part in range(2)]
        fields = [field_ref[:, part, 0] for part in range(2)]
        images = [out_ref[:, part * x_count + x_index] for part in range(2)]

        def lane_sums(left, other):
            product = left[0] * other[0] + left[1] * other[1]
            return jnp.sum(jnp.sum(product, axis=0), axis=0, keepdims=True)

        totals = jnp.concatenate(
            [
                lane_sums(rights, rights),
                lane_sums(rights, fields),
                lane_sums(fields, fields),
                lane_sums(fields, images),
                jnp.zeros((4, planes), jnp.float32),
            ],
            axis=0,
        )

        @pl.when(x_index == 0)
        def _():
            total_ref[...] = totals

        @pl.when(x_index > 0)
        def _():
            total_ref[...] += totals


def plan_specs(maps, blocks, block_rows, mask):
    slabs, coils, _, x_count, slab_rows, planes = maps.shape
    row_count = slabs * slab_rows
    maps_spec = pl.BlockSpec(
        (slabs, 1, 2, 1, slab_rows, planes), lambda x, c: (0, c, 0, x, 0, 0)
    )
    field_spec = pl.BlockSpec((blocks, 2, 1, block_rows, planes), lambda x, c: (0, 0, x, 0, 0))

    def whole(shape):
        return pl.BlockSpec(shape, lambda x, c: (0,) * len(shape))

    rows = row_table(row_count)
    forward = plane_table(planes, False)
    inverse = plane_table(planes, True)
    return maps_spec, field_spec, whole, rows, forward, inverse


def compute_params():
    return pltpu.CompilerParams(
        dimension_semantics=("arbitrary", "arbitrary"), vmem_limit_bytes=48 * 1024 * 1024
    )


def product_cost(maps, passes):
    slabs, coils, _, x_count, slab_rows, planes = maps.shape
    rows = slabs * slab_rows
    per_plane = 2 * 2 * rows * planes * (2 * rows + 2 * planes)
    return pl.CostEstimate(
        flops=int(coils * x_count * per_plane * passes), bytes_accessed=int(2 * maps.size), transcendentals=0
    )


def adjoint_call(spectra, maps, mask, blocks):
    slabs, coils, _, x_count, slab_planes, row_count = spectra.shape
    planes = slabs * slab_planes
    block_rows = row_count // blocks
    maps_spec, field_spec, whole, rows, _, inverse = plan_specs(maps, blocks, block_rows, mask)
    spectra_spec = pl.BlockSpec(
        (slabs, 1, 2, 1, slab_planes, row_count), lambda x, c: (0, c, 0, x, 0, 0)
    )
    return pl.pallas_call(
        adjoint_kernel,
        grid=(x_count, coils),
        in_specs=[spectra_spec, maps_spec, whole(mask.shape), whole(rows.shape), whole(inverse.shape)],
        out_specs=field_spec,
        out_shape=jax.ShapeDtypeStruct((blocks, 2, x_count, block_rows, planes), jnp.float32),
        compiler_params=compute_params(),
        cost_estimate=product_cost(maps, 3),
        name="adjoint",
    )(spectra, maps, mask, rows, inverse)


def first_call(maps, adjoint, denoised, mask):
    blocks, _, x_count, block_rows, planes = adjoint.shape
    maps_spec, field_spec, whole, rows, forward, inverse = plan_specs(
        maps, blocks, block_rows, mask
    )
    return pl.pallas_call(
        first_kernel,
        grid=(x_count, maps.shape[1]),
        in_specs=[
            maps_spec,
            field_spec,
            field_spec,
            whole(mask.shape),
            whole(rows.shape),
            whole(forward.shape),
            whole(inverse.shape),
        ],
        out_specs=[field_spec, field_spec],
        out_shape=[jax.ShapeDtypeStruct(adjoint.shape, jnp.float32)] * 2,
        compiler_params=compute_params(),
        cost_estimate=product_cost(maps, 6),
        name="first_product",
    )(maps, adjoint, denoised, mask, rows, forward, inverse)


def second_call(maps, right, field, mask):
    blocks, _, x_count, block_rows, planes = field.shape
    maps_spec, field_spec, whole, rows, forward, inverse = plan_specs(
        maps, blocks, block_rows, mask
    )
    out_shape = (blocks, 2 * x_count, block_rows, planes)
    return pl.pallas_call(
        second_kernel,
        grid=(x_count, maps.shape[1]),
        in_specs=[
            maps_spec,
            field_spec,
            field_spec,
            whole(mask.shape),
            whole(rows.shape),
            whole(forward.shape),
            whole(inverse.shape),
        ],
        out_specs=[whole(out_shape), whole((8, planes))],
        out_shape=[
            jax.ShapeDtypeStruct(out_shape, jnp.float32),
            jax.ShapeDtypeStruct((8, planes), jnp.float32),
        ],
        compiler_params=compute_params(),
        cost_estimate=product_cost(maps, 6),
        name="second_product",
    )(maps, right, field, mask, rows, forward, inverse)


def exchange(blocks, axis):
    return lax.all_to_all(blocks, axis, split_axis=0, concat_axis=0, tiled=True)


def x_first(cells, parts):
    rows, planes, width = cells.shape
    split = cells.reshape(rows, planes, 2, parts, width // (2 * parts))
    return jnp.transpose(split, (3, 2, 4, 0, 1))


def x_last(blocks):
    parts, _, x_count, rows, planes = blocks.shape
    return jnp.transpose(blocks, (3, 4, 1, 0, 2)).reshape(rows, planes, 2 * parts * x_count)


def combined(right, field, image, squares):
    right_right, right_field, field_field, field_image = (squares[i] for i in range(4))
    ratio = right_field / right_right
    alpha = right_right / (right_field + penalty * right_right)
    fresh = alpha * alpha * (field_field - ratio * right_field)
    weight = alpha * ratio + fresh / right_right
    mixed = weight * alpha
    curvature = (
        weight * weight * right_field - 2.0 * mixed * field_field + alpha * alpha * field_image
    ) + penalty * (
        weight * weight * right_right - 2.0 * mixed * right_field + alpha * alpha * field_field
    )
    second = fresh / curvature
    solution = (alpha + second * weight) * right - (second * alpha) * field
    residual = (
        (alpha * ratio - penalty * second * weight) * right
        - (alpha + second * weight - penalty * second * alpha) * field
        + (second * alpha) * image
    )
    return solution, residual


def body(
    prior_image,
    coil_maps,
    kspace,
    sampling,
    weight_first,
    bias_first,
    weight_middle,
    bias_middle,
    weight_last,
    bias_last,
):
    readout = prior_image.shape[2] // 2
    own_rows = prior_image.shape[0]
    planes = prior_image.shape[1]
    slabs = lax.axis_size("slab")
    coils = lax.axis_size("coil")
    devices = slabs * coils
    mask = jnp.transpose(
        lax.all_gather(sampling.astype(jnp.bfloat16), "slab", axis=0, tiled=True)
    ).astype(jnp.float32)
    spread = readout % devices == 0
    parts = devices if spread else coils

    def coils_to_x(values):
        blocks = x_first(values, parts)
        tail = blocks.shape[1:]
        if spread:
            return exchange(blocks, axes).reshape((slabs, coils) + tail)
        blocks = exchange(blocks, "coil").reshape((slabs, coils // slabs) + tail)
        return exchange(blocks, "slab")

    spectra = coils_to_x(kspace[0])
    maps = coils_to_x(coil_maps[0])
    denoised = denoise(
        prior_image, weight_first, bias_first, weight_middle, bias_middle, weight_last, bias_last
    )
    blocks = x_first(denoised, parts)
    if spread:
        denoised = exchange(blocks, axes)
        adjoint = adjoint_call(spectra, maps, mask, devices)
        right, field = first_call(maps, adjoint, denoised, mask)
        right_rows = x_last(exchange(right, axes))
        field_rows = x_last(exchange(field, axes))
        image, totals = second_call(maps, right, field, mask)
        payload = jnp.concatenate(
            [image, jnp.broadcast_to(totals[None, None], (devices, 1) + totals.shape)], axis=1
        )
        payload = exchange(payload, axes)
        squares = jnp.sum(payload[:, -1], axis=(0, 2))
        image_rows = x_last(payload[:, :-1].reshape(blocks.shape))
        return combined(right_rows, field_rows, image_rows, squares)

    tail = blocks.shape[1:3]

    def whole_rows(parts_in):
        moved = lax.all_gather(exchange(parts_in, "coil"), "slab", axis=0, tiled=True)
        return jnp.transpose(moved, (1, 2, 0, 3, 4)).reshape((1,) + tail + (-1, planes))

    def own_part(whole):
        rows = whole.shape[3] // slabs
        mine = lax.dynamic_slice_in_dim(whole, lax.axis_index("slab") * rows, rows, axis=3)
        split = jnp.transpose(mine.reshape(tail + (coils, own_rows, planes)), (2, 0, 1, 3, 4))
        return x_last(exchange(split, "coil"))

    adjoint = lax.psum(adjoint_call(spectra, maps, mask, 1), "slab")
    right = adjoint + penalty * whole_rows(blocks)
    _, field = first_call(maps, right, jnp.zeros_like(right), mask)
    field = lax.psum(field, "slab")
    image, _ = second_call(maps, right, field, mask)
    image = lax.psum(image.reshape(field.shape), "slab")
    squares = lax.psum(
        jnp.stack(
            [
                jnp.sum(right * right),
                jnp.sum(right * field),
                jnp.sum(field * field),
                jnp.sum(field * image),
            ]
        ),
        "coil",
    )
    return combined(own_part(right), own_part(field), own_part(image), squares)


def solution(mesh):
    placed = (
        P(("slab", "coil"), None, None),
        P("coil", "slab", None, None),
        P("coil", "slab", None, None),
        P("slab", None),
        P(),
        P(),
        P(),
        P(),
        P(),
        P(),
    )
    return jax.shard_map(
        body,
        mesh=mesh,
        in_specs=placed,
        out_specs=(P(("slab", "coil"), None, None), P(("slab", "coil"), None, None)),
        check_vma=False,
    )
```

```python
import functools
import math

import jax
import jax.numpy as jnp
import numpy as np
from jax import lax
from jax.experimental import pallas as pl
from jax.experimental.pallas import tpu as pltpu
from jax.sharding import PartitionSpec as P

CG_ITERS = 2


penalty = 0.5
axes = ("slab", "coil")


def with_halo(cells, width):
    rows = cells.shape[0]
    count = lax.axis_size("slab") * lax.axis_size("coil")
    above, below = [], []
    for hop in range(1, -(-width // rows) + 1):
        taken = min(width - (hop - 1) * rows, rows)
        ends = count - hop
        tail = lax.slice_in_dim(cells, rows - taken, rows, axis=0)
        head = lax.slice_in_dim(cells, 0, taken, axis=0)
        above.insert(0, lax.ppermute(tail, axes, [(i, i + hop) for i in range(ends)]))
        below.append(lax.ppermute(head, axes, [(i + hop, i) for i in range(ends)]))
    return jnp.concatenate(above + [cells] + below, axis=0)


def chunk_rows(rows):
    return max(size for size in range(1, 7) if rows % size == 0)


def chained(lhs_pieces):
    rows = lhs_pieces[0].shape[0] * lhs_pieces[0].shape[1]
    lhs = jnp.concatenate(lhs_pieces, axis=2)
    return lhs.reshape(rows, lhs.shape[2])


def denoise_kernel(
    group,
    first_ref,
    features_ref,
    prior_ref,
    weight_first_ref,
    bias_first_ref,
    weight_middle_ref,
    bias_middle_ref,
    weight_last_ref,
    bias_last_ref,
    out_ref,
    one_ref,
    two_ref,
    taps_ref,
):
    planes = out_ref.shape[1]
    width = out_ref.shape[2]
    edge = (one_ref.shape[2] - two_ref.shape[2]) // 2
    groups = two_ref.shape[2] // group
    first = first_ref[0]
    total = first_ref[1]
    one_ref[:, :, :edge] = jnp.zeros(one_ref.shape[:2] + (edge,), one_ref.dtype)
    one_ref[:, :, edge + two_ref.shape[2] :] = jnp.zeros(
        one_ref.shape[:2] + (edge,), one_ref.dtype
    )

    def store(ref, start, count, lanes, value, reach):
        value = jnp.maximum(value, 0.0).reshape(count, planes, group)
        for row in range(count):
            place = first + (start + row - reach)
            kept = jnp.where((place >= 0) & (place < total), value[row], 0.0)
            ref[start + row, :, lanes] = kept.astype(ref.dtype)

    def first_layer(index, carry):
        lanes = pl.ds(pl.multiple_of(index * group, group), group)
        placed = pl.ds(pl.multiple_of(edge + index * group, 128), group)
        count = chunk_rows(one_ref.shape[0])
        for start in range(0, one_ref.shape[0], count):
            lhs = chained([features_ref[start + tap : start + tap + count] for tap in range(3)])
            value = jnp.dot(lhs, weight_first_ref[:, lanes], preferred_element_type=jnp.float32)
            store(one_ref, start, count, placed, value + bias_first_ref[:, lanes], 2)
        return carry

    lax.fori_loop(0, groups, first_layer, 0)

    def shifted(value, plane, step):
        rows = value.shape[0]
        if step > 0:
            return jnp.where(plane == 0, 0.0, pltpu.roll(value, 1, 0))
        return jnp.where(plane == planes - 1, 0.0, pltpu.roll(value, rows - 1, 0))

    def plane_index(count, lanes):
        return lax.broadcasted_iota(jnp.int32, (count, planes, lanes), 1).reshape(
            count * planes, lanes
        )

    def middle_layer(index, carry):
        lanes = pl.ds(pl.multiple_of(index * group, group), group)
        window = pl.ds(pl.multiple_of(index * group, group), group + 2 * edge)
        count = chunk_rows(two_ref.shape[0])
        plane = plane_index(count, group)
        for start in range(0, two_ref.shape[0], count):
            lhs = chained([one_ref[start + tap : start + tap + count, :, window] for tap in range(3)])
            value = jnp.dot(lhs, weight_middle_ref[...], preferred_element_type=jnp.float32)
            value = (
                value[:, group : 2 * group]
                + shifted(value[:, :group], plane, 1)
                + shifted(value[:, 2 * group :], plane, -1)
            )
            store(two_ref, start, count, lanes, value + bias_middle_ref[:, lanes], 1)
        return carry

    lax.fori_loop(0, groups, middle_layer, 0)

    count = chunk_rows(two_ref.shape[0])

    def last_layer(index, carry):
        start = index * count
        lhs = two_ref[pl.ds(start, count)].reshape(count * planes, two_ref.shape[2])
        value = jnp.dot(lhs, weight_last_ref[...], preferred_element_type=jnp.float32)
        taps_ref[pl.ds(start, count)] = value.reshape(count, planes, value.shape[1])
        return carry

    lax.fori_loop(0, two_ref.shape[0] // count, last_layer, 0)
    plane = plane_index(1, width)

    def last_sum(row, carry):
        sums = []
        for plane_tap in range(3):
            running = None
            for row_tap in range(3):
                lanes = pl.ds((row_tap * 3 + plane_tap) * width, width)
                value = taps_ref[row + row_tap, :, lanes]
                running = value if running is None else running + value
            sums.append(running)
        value = sums[1] + shifted(sums[0], plane, 1) + shifted(sums[2], plane, -1)
        out_ref[row] = prior_ref[row] + (value + bias_last_ref[...])
        return carry

    lax.fori_loop(0, out_ref.shape[0], last_sum, 0)


def banded(tiles, inner, outer, offset):
    shape = jnp.broadcast_shapes(tiles[0].shape, inner.shape, outer.shape)
    result = jnp.zeros(shape, jnp.bfloat16)
    for tap in range(3):
        result = jnp.where(inner - outer + offset == tap, tiles[tap], result)
    return result


def denoise(
    prior_image, weight_first, bias_first, weight_middle, bias_middle, weight_last, bias_last
):
    own_rows, planes, width = prior_image.shape
    readout = width // 2
    channels = weight_first.shape[3]
    span = readout * channels
    group = min(256, span)
    held = group // channels
    edge = 128
    reach = edge // channels
    window = group + 2 * edge

    def lane_place(count, inside):
        return jnp.arange(count * inside, dtype=jnp.int32) // inside

    tiles = jnp.transpose(weight_first, (2, 0, 1, 4, 3)).reshape(3, 18, 1, 1, channels)
    tiles = jnp.broadcast_to(tiles, (3, 18, 1, readout, channels)).reshape(3, 18, 1, span)
    first_table = banded(
        tiles,
        jnp.arange(readout, dtype=jnp.int32)[None, :, None],
        lane_place(readout, channels)[None, None, :],
        1,
    ).reshape(18 * readout, span)
    tiles = jnp.transpose(weight_middle, (2, 0, 4, 1, 3)).reshape(3, 3, 1, channels, 3, 1, channels)
    tiles = jnp.broadcast_to(tiles, (3, 3, 1, channels, 3, held, channels))
    tiles = tiles.reshape(3, 3, 1, channels, 3 * group)
    middle_table = banded(
        tiles,
        jnp.arange(window // channels, dtype=jnp.int32)[None, :, None, None] - reach,
        jnp.tile(lane_place(held, channels), 3)[None, None, None, :],
        1,
    ).reshape(3 * window, 3 * group)
    tiles = jnp.transpose(weight_last, (2, 4, 0, 1, 3)).reshape(3, 1, channels, 18, 1)
    tiles = jnp.broadcast_to(tiles, (3, 1, channels, 18, readout)).reshape(
        3, 1, channels, 18 * readout
    )
    last_table = banded(
        tiles,
        jnp.arange(readout, dtype=jnp.int32)[:, None, None],
        jnp.tile(jnp.arange(readout, dtype=jnp.int32), 18)[None, None, :],
        1,
    ).reshape(span, 18 * readout)

    features = with_halo(prior_image.astype(jnp.bfloat16), 3)
    rim = jnp.zeros_like(features[:, :1])
    features = jnp.concatenate(
        [
            jnp.concatenate([rim, features[:, :-1]], axis=1),
            features,
            jnp.concatenate([features[:, 1:], rim], axis=1),
        ],
        axis=2,
    )
    total = own_rows * lax.axis_size("slab") * lax.axis_size("coil")
    first = lax.axis_index(axes) * own_rows
    places = jnp.stack([first, jnp.asarray(total)]).astype(jnp.int32)
    vmem = pl.BlockSpec(memory_space=pltpu.VMEM)
    flops = 2 * own_rows * planes * (
        features.shape[2] * 3 * span * 3 // 2 + 9 * span * 512 * 5 // 4 + span * 18 * readout * 5 // 4
    )
    return pl.pallas_call(
        functools.partial(denoise_kernel, group),
        in_specs=[pl.BlockSpec(memory_space=pltpu.SMEM)] + [vmem] * 8,
        out_specs=vmem,
        out_shape=jax.ShapeDtypeStruct(prior_image.shape, jnp.float32),
        scratch_shapes=[
            pltpu.VMEM((own_rows + 4, planes, span + 2 * edge), jnp.bfloat16),
            pltpu.VMEM((own_rows + 2, planes, span), jnp.bfloat16),
            pltpu.VMEM((own_rows + 2, planes, 18 * readout), jnp.float32),
        ],
        compiler_params=pltpu.CompilerParams(vmem_limit_bytes=56 * 1024 * 1024),
        cost_estimate=pl.CostEstimate(
            flops=int(flops), bytes_accessed=16 * 1024 * 1024, transcendentals=0
        ),
        name="denoise",
    )(
        places,
        features,
        prior_image,
        first_table,
        jnp.tile(bias_first, readout)[None, :],
        middle_table,
        jnp.tile(bias_middle, readout)[None, :],
        last_table,
        jnp.repeat(bias_last, readout)[None, :],
    )


def table_parts(table):
    high = table.astype(jnp.bfloat16)
    low = (table - high.astype(np.float64)).astype(jnp.bfloat16)
    return high, low


def dft_parts(length):
    positions = np.arange(length, dtype=np.int64)
    angles = (positions[:, None] * positions[None, :] % length) * (2.0 * math.pi / length)
    scale = 1.0 / math.sqrt(length)
    return np.cos(angles) * scale, np.sin(angles) * scale


def row_table(length):
    cos_part, sin_part = dft_parts(length)
    high, low = table_parts(np.concatenate([cos_part, sin_part], axis=0))
    return np.concatenate([high, low, high], axis=1)


def plane_table(length, inverse):
    cos_part, sin_part = dft_parts(length)
    if inverse:
        sin_part = -sin_part
    table = np.concatenate(
        [
            np.concatenate([cos_part, -sin_part], axis=1),
            np.concatenate([sin_part, cos_part], axis=1),
        ],
        axis=0,
    )
    high, low = table_parts(table)
    return np.concatenate([high, low, high], axis=0)


def value_parts(value):
    high = value.astype(jnp.bfloat16)
    low = (value - high.astype(jnp.float32)).astype(jnp.bfloat16)
    return high, low


def along_planes(value, table):
    high, low = value_parts(value)
    return jnp.dot(
        jnp.concatenate([high, high, low], axis=1), table, preferred_element_type=jnp.float32
    )


def along_rows(table, value):
    high, low = value_parts(value)
    return jnp.dot(
        table, jnp.concatenate([high, high, low], axis=0), preferred_element_type=jnp.float32
    )


def rows_combined(stacked, inverse):
    rows = stacked.shape[0] // 2
    half = stacked.shape[1] // 2
    cos_real, cos_imag = stacked[:rows, :half], stacked[:rows, half:]
    sin_real, sin_imag = stacked[rows:, :half], stacked[rows:, half:]
    if inverse:
        return cos_real - sin_imag, cos_imag + sin_real
    return cos_real + sin_imag, cos_imag - sin_real


def plane_of(ref, part):
    value = ref[:, part, 0]
    return value.reshape(value.shape[0] * value.shape[1], value.shape[2])


def map_of(ref, part):
    value = ref[:, 0, part, 0]
    return value.reshape(value.shape[0] * value.shape[1], value.shape[2]).astype(jnp.float32)


def normal_product(map_real, map_imag, real, imag, mask, rows, planes, inverse_planes):
    half = real.shape[1]
    coil_real = map_real * real - map_imag * imag
    coil_imag = map_real * imag + map_imag * real
    field = along_planes(jnp.concatenate([coil_real, coil_imag], axis=1), planes)
    real, imag = rows_combined(along_rows(rows, field), False)
    spectrum = jnp.concatenate([real * mask, imag * mask], axis=1)
    real, imag = rows_combined(along_rows(rows, spectrum), True)
    field = along_planes(jnp.concatenate([real, imag], axis=1), inverse_planes)
    real, imag = field[:, :half], field[:, half:]
    return map_real * real + map_imag * imag, map_real * imag - map_imag * real


def adjoint_kernel(kspace_ref, maps_ref, mask_ref, rows_ref, inverse_ref, out_ref):
    mask = mask_ref[...]
    parts = []
    for part in range(2):
        parts.append((jnp.transpose(map_of(kspace_ref, part)) * mask).astype(jnp.bfloat16))
    spectrum = jnp.concatenate(parts, axis=1)
    length = spectrum.shape[0]
    stacked = jnp.dot(
        rows_ref[:, : 2 * length],
        jnp.concatenate([spectrum, spectrum], axis=0),
        preferred_element_type=jnp.float32,
    )
    real, imag = rows_combined(stacked, True)
    half = real.shape[1]
    field = along_planes(jnp.concatenate([real, imag], axis=1), inverse_ref[...])
    real, imag = field[:, :half], field[:, half:]
    map_real, map_imag = map_of(maps_ref, 0), map_of(maps_ref, 1)
    shape = out_ref.shape[0], out_ref.shape[3], out_ref.shape[4]
    sums = (map_real * real + map_imag * imag, map_real * imag - map_imag * real)

    @pl.when(pl.program_id(1) == 0)
    def _():
        for part in range(2):
            out_ref[:, part, 0] = sums[part].reshape(shape)

    @pl.when(pl.program_id(1) > 0)
    def _():
        for part in range(2):
            out_ref[:, part, 0] += sums[part].reshape(shape)


def first_kernel(
    maps_ref, adjoint_ref, denoised_ref, mask_ref, rows_ref, planes_ref, inverse_ref, right_ref, out_ref
):
    @pl.when(pl.program_id(1) == 0)
    def _():
        right = adjoint_ref[...] + penalty * denoised_ref[...]
        right_ref[...] = right
        out_ref[...] = jnp.zeros_like(out_ref)

    sums = normal_product(
        map_of(maps_ref, 0),
        map_of(maps_ref, 1),
        plane_of(right_ref, 0),
        plane_of(right_ref, 1),
        mask_ref[...],
        rows_ref[...],
        planes_ref[...],
        inverse_ref[...],
    )
    shape = out_ref.shape[0], out_ref.shape[3], out_ref.shape[4]
    for part in range(2):
        out_ref[:, part, 0] += sums[part].reshape(shape)


def second_kernel(
    maps_ref, right_ref, field_ref, mask_ref, rows_ref, planes_ref, inverse_ref, out_ref, total_ref
):
    x_index = pl.program_id(0)
    x_count = pl.num_programs(0)
    blocks, block_rows, planes = out_ref.shape[0], out_ref.shape[2], out_ref.shape[3]
    shape = blocks, block_rows, planes

    @pl.when(pl.program_id(1) == 0)
    def _():
        for part in range(2):
            out_ref[:, part * x_count + x_index] = jnp.zeros(shape, jnp.float32)

    sums = normal_product(
        map_of(maps_ref, 0),
        map_of(maps_ref, 1),
        plane_of(field_ref, 0),
        plane_of(field_ref, 1),
        mask_ref[...],
        rows_ref[...],
        planes_ref[...],
        inverse_ref[...],
    )
    for part in range(2):
        out_ref[:, part * x_count + x_index] += sums[part].reshape(shape)

    @pl.when(pl.program_id(1) == pl.num_programs(1) - 1)
    def _():
        rights = [right_ref[:, part, 0] for part in range(2)]
        fields = [field_ref[:, part, 0] for part in range(2)]
        images = [out_ref[:, part * x_count + x_index] for part in range(2)]

        def lane_sums(left, other):
            product = left[0] * other[0] + left[1] * other[1]
            return jnp.sum(jnp.sum(product, axis=0), axis=0, keepdims=True)

        totals = jnp.concatenate(
            [
                lane_sums(rights, rights),
                lane_sums(rights, fields),
                lane_sums(fields, fields),
                lane_sums(fields, images),
                jnp.zeros((4, planes), jnp.float32),
            ],
            axis=0,
        )

        @pl.when(x_index == 0)
        def _():
            total_ref[...] = totals

        @pl.when(x_index > 0)
        def _():
            total_ref[...] += totals


def plan_specs(maps, blocks, block_rows, mask):
    slabs, coils, _, x_count, slab_rows, planes = maps.shape
    row_count = slabs * slab_rows
    maps_spec = pl.BlockSpec(
        (slabs, 1, 2, 1, slab_rows, planes), lambda x, c: (0, c, 0, x, 0, 0)
    )
    field_spec = pl.BlockSpec((blocks, 2, 1, block_rows, planes), lambda x, c: (0, 0, x, 0, 0))

    def whole(shape):
        return pl.BlockSpec(shape, lambda x, c: (0,) * len(shape))

    rows = row_table(row_count)
    forward = plane_table(planes, False)
    inverse = plane_table(planes, True)
    return maps_spec, field_spec, whole, rows, forward, inverse


def compute_params():
    return pltpu.CompilerParams(
        dimension_semantics=("arbitrary", "arbitrary"), vmem_limit_bytes=48 * 1024 * 1024
    )


def product_cost(maps, passes):
    slabs, coils, _, x_count, slab_rows, planes = maps.shape
    rows = slabs * slab_rows
    per_plane = 2 * 2 * rows * planes * (2 * rows + 2 * planes)
    return pl.CostEstimate(
        flops=int(coils * x_count * per_plane * passes), bytes_accessed=int(2 * maps.size), transcendentals=0
    )


def adjoint_call(spectra, maps, mask, blocks):
    slabs, coils, _, x_count, slab_planes, row_count = spectra.shape
    planes = slabs * slab_planes
    block_rows = row_count // blocks
    maps_spec, field_spec, whole, rows, _, inverse = plan_specs(maps, blocks, block_rows, mask)
    spectra_spec = pl.BlockSpec(
        (slabs, 1, 2, 1, slab_planes, row_count), lambda x, c: (0, c, 0, x, 0, 0)
    )
    return pl.pallas_call(
        adjoint_kernel,
        grid=(x_count, coils),
        in_specs=[spectra_spec, maps_spec, whole(mask.shape), whole(rows.shape), whole(inverse.shape)],
        out_specs=field_spec,
        out_shape=jax.ShapeDtypeStruct((blocks, 2, x_count, block_rows, planes), jnp.float32),
        compiler_params=compute_params(),
        cost_estimate=product_cost(maps, 3),
        name="adjoint",
    )(spectra, maps, mask, rows, inverse)


def first_call(maps, adjoint, denoised, mask):
    blocks, _, x_count, block_rows, planes = adjoint.shape
    maps_spec, field_spec, whole, rows, forward, inverse = plan_specs(
        maps, blocks, block_rows, mask
    )
    return pl.pallas_call(
        first_kernel,
        grid=(x_count, maps.shape[1]),
        in_specs=[
            maps_spec,
            field_spec,
            field_spec,
            whole(mask.shape),
            whole(rows.shape),
            whole(forward.shape),
            whole(inverse.shape),
        ],
        out_specs=[field_spec, field_spec],
        out_shape=[jax.ShapeDtypeStruct(adjoint.shape, jnp.float32)] * 2,
        compiler_params=compute_params(),
        cost_estimate=product_cost(maps, 6),
        name="first_product",
    )(maps, adjoint, denoised, mask, rows, forward, inverse)


def second_call(maps, right, field, mask):
    blocks, _, x_count, block_rows, planes = field.shape
    maps_spec, field_spec, whole, rows, forward, inverse = plan_specs(
        maps, blocks, block_rows, mask
    )
    out_shape = (blocks, 2 * x_count, block_rows, planes)
    return pl.pallas_call(
        second_kernel,
        grid=(x_count, maps.shape[1]),
        in_specs=[
            maps_spec,
            field_spec,
            field_spec,
            whole(mask.shape),
            whole(rows.shape),
            whole(forward.shape),
            whole(inverse.shape),
        ],
        out_specs=[whole(out_shape), whole((8, planes))],
        out_shape=[
            jax.ShapeDtypeStruct(out_shape, jnp.float32),
            jax.ShapeDtypeStruct((8, planes), jnp.float32),
        ],
        compiler_params=compute_params(),
        cost_estimate=product_cost(maps, 6),
        name="second_product",
    )(maps, right, field, mask, rows, forward, inverse)


def exchange(blocks, axis):
    return lax.all_to_all(blocks, axis, split_axis=0, concat_axis=0, tiled=True)


def x_first(cells, parts):
    rows, planes, width = cells.shape
    split = cells.reshape(rows, planes, 2, parts, width // (2 * parts))
    return jnp.transpose(split, (3, 2, 4, 0, 1))


def x_last(blocks):
    parts, _, x_count, rows, planes = blocks.shape
    return jnp.transpose(blocks, (3, 4, 1, 0, 2)).reshape(rows, planes, 2 * parts * x_count)


def combined(right, field, image, squares):
    right_right, right_field, field_field, field_image = (squares[i] for i in range(4))
    ratio = right_field / right_right
    alpha = right_right / (right_field + penalty * right_right)
    fresh = alpha * alpha * (field_field - ratio * right_field)
    weight = alpha * ratio + fresh / right_right
    mixed = weight * alpha
    curvature = (
        weight * weight * right_field - 2.0 * mixed * field_field + alpha * alpha * field_image
    ) + penalty * (
        weight * weight * right_right - 2.0 * mixed * right_field + alpha * alpha * field_field
    )
    second = fresh / curvature
    solution = (alpha + second * weight) * right - (second * alpha) * field
    residual = (
        (alpha * ratio - penalty * second * weight) * right
        - (alpha + second * weight - penalty * second * alpha) * field
        + (second * alpha) * image
    )
    return solution, residual


def body(
    prior_image,
    coil_maps,
    kspace,
    sampling,
    weight_first,
    bias_first,
    weight_middle,
    bias_middle,
    weight_last,
    bias_last,
):
    readout = prior_image.shape[2] // 2
    own_rows = prior_image.shape[0]
    planes = prior_image.shape[1]
    slabs = lax.axis_size("slab")
    coils = lax.axis_size("coil")
    devices = slabs * coils
    mask = jnp.transpose(
        lax.all_gather(sampling.astype(jnp.bfloat16), "slab", axis=0, tiled=True)
    ).astype(jnp.float32)
    spread = readout % devices == 0
    parts = devices if spread else coils

    def coils_to_x(values):
        blocks = x_first(values, parts)
        tail = blocks.shape[1:]
        if spread:
            return exchange(blocks, axes).reshape((slabs, coils) + tail)
        blocks = exchange(blocks, "coil").reshape((slabs, coils // slabs) + tail)
        return exchange(blocks, "slab")

    spectra = coils_to_x(kspace[0])
    maps = coils_to_x(coil_maps[0])
    denoised = denoise(
        prior_image, weight_first, bias_first, weight_middle, bias_middle, weight_last, bias_last
    )
    blocks = x_first(denoised, parts)
    if spread:
        denoised = exchange(blocks, axes)
        adjoint = adjoint_call(spectra, maps, mask, devices)
        right, field = first_call(maps, adjoint, denoised, mask)
        right_rows = x_last(exchange(right, axes))
        field_rows = x_last(exchange(field, axes))
        image, totals = second_call(maps, right, field, mask)
        payload = jnp.concatenate(
            [image, jnp.broadcast_to(totals[None, None], (devices, 1) + totals.shape)], axis=1
        )
        payload = exchange(payload, axes)
        squares = jnp.sum(payload[:, -1], axis=(0, 2))
        image_rows = x_last(payload[:, :-1].reshape(blocks.shape))
        return combined(right_rows, field_rows, image_rows, squares)

    tail = blocks.shape[1:3]

    def whole_rows(parts_in):
        moved = lax.all_gather(exchange(parts_in, "coil"), "slab", axis=0, tiled=True)
        return jnp.transpose(moved, (1, 2, 0, 3, 4)).reshape((1,) + tail + (-1, planes))

    def own_part(whole):
        rows = whole.shape[3] // slabs
        mine = lax.dynamic_slice_in_dim(whole, lax.axis_index("slab") * rows, rows, axis=3)
        split = jnp.transpose(mine.reshape(tail + (coils, own_rows, planes)), (2, 0, 1, 3, 4))
        return x_last(exchange(split, "coil"))

    adjoint = lax.psum(adjoint_call(spectra, maps, mask, 1), "slab")
    right = adjoint + penalty * whole_rows(blocks)
    _, field = first_call(maps, right, jnp.zeros_like(right), mask)
    field = lax.psum(field, "slab")
    image, _ = second_call(maps, right, field, mask)
    image = lax.psum(image.reshape(field.shape), "slab")
    squares = lax.psum(
        jnp.stack(
            [
                jnp.sum(right * right),
                jnp.sum(right * field),
                jnp.sum(field * field),
                jnp.sum(field * image),
            ]
        ),
        "coil",
    )
    return combined(own_part(right), own_part(field), own_part(image), squares)


def solution(mesh):
    placed = (
        P(("slab", "coil"), None, None),
        P("coil", "slab", None, None),
        P("coil", "slab", None, None),
        P("slab", None),
        P(),
        P(),
        P(),
        P(),
        P(),
        P(),
    )
    return jax.shard_map(
        body,
        mesh=mesh,
        in_specs=placed,
        out_specs=(P(("slab", "coil"), None, None), P(("slab", "coil"), None, None)),
        check_vma=False,
    )
```

```python
import functools
import math

import jax
import jax.numpy as jnp
import numpy as np
from jax import lax
from jax.experimental import pallas as pl
from jax.experimental.pallas import tpu as pltpu
from jax.sharding import PartitionSpec as P

CG_ITERS = 2


penalty = 0.5
axes = ("slab", "coil")


def with_halo(cells, width):
    rows = cells.shape[0]
    count = lax.axis_size("slab") * lax.axis_size("coil")
    above, below = [], []
    for hop in range(1, -(-width // rows) + 1):
        taken = min(width - (hop - 1) * rows, rows)
        ends = count - hop
        tail = lax.slice_in_dim(cells, rows - taken, rows, axis=0)
        head = lax.slice_in_dim(cells, 0, taken, axis=0)
        above.insert(0, lax.ppermute(tail, axes, [(i, i + hop) for i in range(ends)]))
        below.append(lax.ppermute(head, axes, [(i + hop, i) for i in range(ends)]))
    return jnp.concatenate(above + [cells] + below, axis=0)


def chunk_rows(rows):
    return max(size for size in range(1, 7) if rows % size == 0)


def chained(lhs_pieces):
    rows = lhs_pieces[0].shape[0] * lhs_pieces[0].shape[1]
    lhs = jnp.concatenate(lhs_pieces, axis=2)
    return lhs.reshape(rows, lhs.shape[2])


def denoise_kernel(
    group,
    first_ref,
    features_ref,
    prior_ref,
    weight_first_ref,
    bias_first_ref,
    weight_middle_ref,
    bias_middle_ref,
    weight_last_ref,
    bias_last_ref,
    out_ref,
    one_ref,
    two_ref,
    taps_ref,
):
    planes = out_ref.shape[1]
    width = out_ref.shape[2]
    edge = (one_ref.shape[2] - two_ref.shape[2]) // 2
    groups = two_ref.shape[2] // group
    first = first_ref[0]
    total = first_ref[1]
    one_ref[:, :, :edge] = jnp.zeros(one_ref.shape[:2] + (edge,), one_ref.dtype)
    one_ref[:, :, edge + two_ref.shape[2] :] = jnp.zeros(
        one_ref.shape[:2] + (edge,), one_ref.dtype
    )

    def store(ref, start, count, lanes, value, reach):
        value = jnp.maximum(value, 0.0).reshape(count, planes, group)
        for row in range(count):
            place = first + (start + row - reach)
            kept = jnp.where((place >= 0) & (place < total), value[row], 0.0)
            ref[start + row, :, lanes] = kept.astype(ref.dtype)

    def first_layer(index, carry):
        lanes = pl.ds(pl.multiple_of(index * group, group), group)
        placed = pl.ds(pl.multiple_of(edge + index * group, 128), group)
        count = chunk_rows(one_ref.shape[0])
        for start in range(0, one_ref.shape[0], count):
            lhs = chained([features_ref[start + tap : start + tap + count] for tap in range(3)])
            value = jnp.dot(lhs, weight_first_ref[:, lanes], preferred_element_type=jnp.float32)
            store(one_ref, start, count, placed, value + bias_first_ref[:, lanes], 2)
        return carry

    lax.fori_loop(0, groups, first_layer, 0)

    def shifted(value, plane, step):
        rows = value.shape[0]
        if step > 0:
            return jnp.where(plane == 0, 0.0, pltpu.roll(value, 1, 0))
        return jnp.where(plane == planes - 1, 0.0, pltpu.roll(value, rows - 1, 0))

    def plane_index(count, lanes):
        return lax.broadcasted_iota(jnp.int32, (count, planes, lanes), 1).reshape(
            count * planes, lanes
        )

    def middle_layer(index, carry):
        lanes = pl.ds(pl.multiple_of(index * group, group), group)
        window = pl.ds(pl.multiple_of(index * group, group), group + 2 * edge)
        count = chunk_rows(two_ref.shape[0])
        plane = plane_index(count, group)
        for start in range(0, two_ref.shape[0], count):
            lhs = chained([one_ref[start + tap : start + tap + count, :, window] for tap in range(3)])
            value = jnp.dot(lhs, weight_middle_ref[...], preferred_element_type=jnp.float32)
            value = (
                value[:, group : 2 * group]
                + shifted(value[:, :group], plane, 1)
                + shifted(value[:, 2 * group :], plane, -1)
            )
            store(two_ref, start, count, lanes, value + bias_middle_ref[:, lanes], 1)
        return carry

    lax.fori_loop(0, groups, middle_layer, 0)

    count = chunk_rows(two_ref.shape[0])

    def last_layer(index, carry):
        start = index * count
        lhs = two_ref[pl.ds(start, count)].reshape(count * planes, two_ref.shape[2])
        value = jnp.dot(lhs, weight_last_ref[...], preferred_element_type=jnp.float32)
        taps_ref[pl.ds(start, count)] = value.reshape(count, planes, value.shape[1])
        return carry

    lax.fori_loop(0, two_ref.shape[0] // count, last_layer, 0)
    plane = plane_index(1, width)

    def last_sum(row, carry):
        sums = []
        for plane_tap in range(3):
            running = None
            for row_tap in range(3):
                lanes = pl.ds((row_tap * 3 + plane_tap) * width, width)
                value = taps_ref[row + row_tap, :, lanes]
                running = value if running is None else running + value
            sums.append(running)
        value = sums[1] + shifted(sums[0], plane, 1) + shifted(sums[2], plane, -1)
        out_ref[row] = prior_ref[row] + (value + bias_last_ref[...])
        return carry

    lax.fori_loop(0, out_ref.shape[0], last_sum, 0)


def banded(tiles, inner, outer, offset):
    shape = jnp.broadcast_shapes(tiles[0].shape, inner.shape, outer.shape)
    result = jnp.zeros(shape, jnp.bfloat16)
    for tap in range(3):
        result = jnp.where(inner - outer + offset == tap, tiles[tap], result)
    return result


def denoise(
    prior_image, weight_first, bias_first, weight_middle, bias_middle, weight_last, bias_last
):
    own_rows, planes, width = prior_image.shape
    readout = width // 2
    channels = weight_first.shape[3]
    span = readout * channels
    group = min(256, span)
    held = group // channels
    edge = 128
    reach = edge // channels
    window = group + 2 * edge

    def lane_place(count, inside):
        return jnp.arange(count * inside, dtype=jnp.int32) // inside

    tiles = jnp.transpose(weight_first, (2, 0, 1, 4, 3)).reshape(3, 18, 1, 1, channels)
    tiles = jnp.broadcast_to(tiles, (3, 18, 1, readout, channels)).reshape(3, 18, 1, span)
    first_table = banded(
        tiles,
        jnp.arange(readout, dtype=jnp.int32)[None, :, None],
        lane_place(readout, channels)[None, None, :],
        1,
    ).reshape(18 * readout, span)
    tiles = jnp.transpose(weight_middle, (2, 0, 4, 1, 3)).reshape(3, 3, 1, channels, 3, 1, channels)
    tiles = jnp.broadcast_to(tiles, (3, 3, 1, channels, 3, held, channels))
    tiles = tiles.reshape(3, 3, 1, channels, 3 * group)
    middle_table = banded(
        tiles,
        jnp.arange(window // channels, dtype=jnp.int32)[None, :, None, None] - reach,
        jnp.tile(lane_place(held, channels), 3)[None, None, None, :],
        1,
    ).reshape(3 * window, 3 * group)
    tiles = jnp.transpose(weight_last, (2, 4, 0, 1, 3)).reshape(3, 1, channels, 18, 1)
    tiles = jnp.broadcast_to(tiles, (3, 1, channels, 18, readout)).reshape(
        3, 1, channels, 18 * readout
    )
    last_table = banded(
        tiles,
        jnp.arange(readout, dtype=jnp.int32)[:, None, None],
        jnp.tile(jnp.arange(readout, dtype=jnp.int32), 18)[None, None, :],
        1,
    ).reshape(span, 18 * readout)

    features = with_halo(prior_image.astype(jnp.bfloat16), 3)
    rim = jnp.zeros_like(features[:, :1])
    features = jnp.concatenate(
        [
            jnp.concatenate([rim, features[:, :-1]], axis=1),
            features,
            jnp.concatenate([features[:, 1:], rim], axis=1),
        ],
        axis=2,
    )
    total = own_rows * lax.axis_size("slab") * lax.axis_size("coil")
    first = lax.axis_index(axes) * own_rows
    places = jnp.stack([first, jnp.asarray(total)]).astype(jnp.int32)
    vmem = pl.BlockSpec(memory_space=pltpu.VMEM)
    flops = 2 * own_rows * planes * (
        features.shape[2] * 3 * span * 3 // 2 + 9 * span * 512 * 5 // 4 + span * 18 * readout * 5 // 4
    )
    return pl.pallas_call(
        functools.partial(denoise_kernel, group),
        in_specs=[pl.BlockSpec(memory_space=pltpu.SMEM)] + [vmem] * 8,
        out_specs=vmem,
        out_shape=jax.ShapeDtypeStruct(prior_image.shape, jnp.float32),
        scratch_shapes=[
            pltpu.VMEM((own_rows + 4, planes, span + 2 * edge), jnp.bfloat16),
            pltpu.VMEM((own_rows + 2, planes, span), jnp.bfloat16),
            pltpu.VMEM((own_rows + 2, planes, 18 * readout), jnp.float32),
        ],
        compiler_params=pltpu.CompilerParams(vmem_limit_bytes=56 * 1024 * 1024),
        cost_estimate=pl.CostEstimate(
            flops=int(flops), bytes_accessed=16 * 1024 * 1024, transcendentals=0
        ),
        name="denoise",
    )(
        places,
        features,
        prior_image,
        first_table,
        jnp.tile(bias_first, readout)[None, :],
        middle_table,
        jnp.tile(bias_middle, readout)[None, :],
        last_table,
        jnp.repeat(bias_last, readout)[None, :],
    )


def table_parts(table):
    high = table.astype(jnp.bfloat16)
    low = (table - high.astype(np.float64)).astype(jnp.bfloat16)
    return high, low


def dft_parts(length):
    positions = np.arange(length, dtype=np.int64)
    angles = (positions[:, None] * positions[None, :] % length) * (2.0 * math.pi / length)
    scale = 1.0 / math.sqrt(length)
    return np.cos(angles) * scale, np.sin(angles) * scale


def turn_block(length):
    cos_part, sin_part = dft_parts(length)
    return np.concatenate(
        [
            np.concatenate([cos_part, sin_part], axis=1),
            np.concatenate([-sin_part, cos_part], axis=1),
        ],
        axis=0,
    )


def dft_table(rows, planes):
    rows_high, rows_low = table_parts(turn_block(rows))
    planes_parts = np.concatenate(table_parts(turn_block(planes).T), axis=0)
    short = max(2 * rows - planes_parts.shape[0], 0)
    planes_parts = np.pad(planes_parts, ((0, short), (0, 0)))
    return np.concatenate([rows_high, rows_low, planes_parts], axis=1)


def value_parts(value):
    high = value.astype(jnp.bfloat16)
    low = (value - high.astype(jnp.float32)).astype(jnp.bfloat16)
    return high, low


def tables_of(ref, rows, planes):
    high, low = ref[:, : 2 * rows], ref[:, 2 * rows : 4 * rows]
    row_table = jnp.concatenate([high, low, high], axis=1)
    high, low = ref[: 2 * planes, 4 * rows :], ref[2 * planes : 4 * planes, 4 * rows :]
    return row_table, jnp.concatenate([high, low, high], axis=0)


def along_planes(fields, table):
    rows, planes = fields[0][0].shape
    stacked = jnp.concatenate([jnp.concatenate(field, axis=1) for field in fields], axis=0)
    high, low = value_parts(stacked)
    moved = jnp.dot(
        jnp.concatenate([high, high, low], axis=1), table, preferred_element_type=jnp.float32
    )
    return [
        (
            moved[index * rows : (index + 1) * rows, :planes],
            moved[index * rows : (index + 1) * rows, planes:],
        )
        for index in range(len(fields))
    ]


def side_by_side(fields):
    return jnp.concatenate(
        [jnp.concatenate([field[part] for field in fields], axis=1) for part in range(2)], axis=0
    )


def along_rows(table, fields):
    rows, planes = fields[0][0].shape
    high, low = value_parts(side_by_side(fields))
    moved = jnp.dot(
        table, jnp.concatenate([high, high, low], axis=0), preferred_element_type=jnp.float32
    )
    return apart(moved, len(fields))


def apart(moved, count):
    rows = moved.shape[0] // 2
    planes = moved.shape[1] // count
    return [
        (
            moved[:rows, index * planes : (index + 1) * planes],
            moved[rows:, index * planes : (index + 1) * planes],
        )
        for index in range(count)
    ]


def plane_of(ref, part):
    value = ref[:, part, 0]
    return value.reshape(value.shape[0] * value.shape[1], value.shape[2])


def coil_plane(ref, coil, part):
    value = ref[:, coil, part, 0]
    return value.reshape(value.shape[0] * value.shape[1], value.shape[2])


def map_of(ref, coil):
    return [coil_plane(ref, coil, part).astype(jnp.float32) for part in range(2)]


def image_sums(maps, fields):
    sums = None
    for (map_real, map_imag), (real, imag) in zip(maps, fields):
        terms = (map_real * real - map_imag * imag, -(map_real * imag + map_imag * real))
        sums = terms if sums is None else (sums[0] + terms[0], sums[1] + terms[1])
    return sums


def units_of(ref):
    count = ref.shape[1]
    held = 2 if count % 2 == 0 else 1
    return [tuple(range(first, first + held)) for first in range(0, count, held)]


def normal_sums(maps_ref, real, imag, mask, tables):
    row_table, plane_table = tables
    total = None
    for unit in units_of(maps_ref):
        maps = [map_of(maps_ref, coil) for coil in unit]
        fields = [
            (map_real * real - map_imag * imag, map_real * imag + map_imag * real)
            for map_real, map_imag in maps
        ]
        fields = along_rows(row_table, along_planes(fields, plane_table))
        fields = [(real_part * mask, imag_part * -mask) for real_part, imag_part in fields]
        fields = along_planes(along_rows(row_table, fields), plane_table)
        sums = image_sums(maps, fields)
        total = sums if total is None else (total[0] + sums[0], total[1] + sums[1])
    return total


def adjoint_kernel(kspace_ref, maps_ref, mask_ref, table_ref, out_ref):
    mask = mask_ref[...]
    rows, planes = mask.shape
    row_table, plane_table = tables_of(table_ref, rows, planes)
    total = None
    for unit in units_of(maps_ref):
        spectra = []
        for coil in unit:
            real, imag = (
                jnp.transpose(coil_plane(kspace_ref, coil, part).astype(jnp.float32))
                for part in range(2)
            )
            spectra.append((real * mask, imag * -mask))
        spectrum = side_by_side(spectra).astype(jnp.bfloat16)
        moved = jnp.dot(
            row_table[:, : 4 * rows],
            jnp.concatenate([spectrum, spectrum], axis=0),
            preferred_element_type=jnp.float32,
        )
        fields = along_planes(apart(moved, len(unit)), plane_table)
        sums = image_sums([map_of(maps_ref, coil) for coil in unit], fields)
        total = sums if total is None else (total[0] + sums[0], total[1] + sums[1])
    shape = out_ref.shape[0], out_ref.shape[3], out_ref.shape[4]

    @pl.when(pl.program_id(1) == 0)
    def _():
        for part in range(2):
            out_ref[:, part, 0] = total[part].reshape(shape)

    @pl.when(pl.program_id(1) > 0)
    def _():
        for part in range(2):
            out_ref[:, part, 0] += total[part].reshape(shape)


def first_kernel(maps_ref, field_ref, mask_ref, table_ref, out_ref):
    mask = mask_ref[...]
    sums = normal_sums(
        maps_ref,
        plane_of(field_ref, 0),
        plane_of(field_ref, 1),
        mask,
        tables_of(table_ref, *mask.shape),
    )
    shape = out_ref.shape[0], out_ref.shape[3], out_ref.shape[4]

    @pl.when(pl.program_id(1) == 0)
    def _():
        for part in range(2):
            out_ref[:, part, 0] = sums[part].reshape(shape)

    @pl.when(pl.program_id(1) > 0)
    def _():
        for part in range(2):
            out_ref[:, part, 0] += sums[part].reshape(shape)


def second_kernel(maps_ref, right_ref, field_ref, mask_ref, table_ref, out_ref, total_ref):
    x_index = pl.program_id(0)
    x_count = pl.num_programs(0)
    blocks, block_rows, planes = out_ref.shape[0], out_ref.shape[2], out_ref.shape[3]
    shape = blocks, block_rows, planes
    mask = mask_ref[...]
    sums = normal_sums(
        maps_ref,
        plane_of(field_ref, 0),
        plane_of(field_ref, 1),
        mask,
        tables_of(table_ref, *mask.shape),
    )

    @pl.when(pl.program_id(1) == 0)
    def _():
        for part in range(2):
            out_ref[:, part * x_count + x_index] = sums[part].reshape(shape)

    @pl.when(pl.program_id(1) > 0)
    def _():
        for part in range(2):
            out_ref[:, part * x_count + x_index] += sums[part].reshape(shape)

    @pl.when(pl.program_id(1) == pl.num_programs(1) - 1)
    def _():
        rights = [right_ref[:, part, 0] for part in range(2)]
        fields = [field_ref[:, part, 0] for part in range(2)]
        images = [out_ref[:, part * x_count + x_index] for part in range(2)]

        def lane_sums(left, other):
            product = left[0] * other[0] + left[1] * other[1]
            return jnp.sum(jnp.sum(product, axis=0), axis=0, keepdims=True)

        totals = jnp.concatenate(
            [
                lane_sums(rights, rights),
                lane_sums(rights, fields),
                lane_sums(fields, fields),
                lane_sums(fields, images),
                jnp.zeros((4, planes), jnp.float32),
            ],
            axis=0,
        )

        @pl.when(x_index == 0)
        def _():
            total_ref[...] = totals

        @pl.when(x_index > 0)
        def _():
            total_ref[...] += totals


def held_coils(count):
    return max(size for size in (1, 2, 4) if count % size == 0)


def whole(shape):
    return pl.BlockSpec(shape, lambda x, c: (0,) * len(shape))


def maps_spec(maps):
    slabs, coils, _, _, slab_rows, planes = maps.shape
    return pl.BlockSpec(
        (slabs, held_coils(coils), 2, 1, slab_rows, planes), lambda x, c: (0, c, 0, x, 0, 0)
    )


def field_spec(shape):
    return pl.BlockSpec((shape[0], 2, 1) + shape[3:], lambda x, c: (0, 0, x, 0, 0))


def grid_of(maps):
    return maps.shape[3], maps.shape[1] // held_coils(maps.shape[1])


def compute_params():
    return pltpu.CompilerParams(
        dimension_semantics=("arbitrary", "arbitrary"), vmem_limit_bytes=48 * 1024 * 1024
    )


def product_cost(maps, passes):
    slabs, coils, _, x_count, slab_rows, planes = maps.shape
    rows = slabs * slab_rows
    per_plane = 2 * 2 * rows * planes * (2 * rows + 2 * planes)
    return pl.CostEstimate(
        flops=int(coils * x_count * per_plane * passes),
        bytes_accessed=int(2 * maps.size),
        transcendentals=0,
    )


def adjoint_call(spectra, maps, mask, table, blocks):
    rows, planes = mask.shape
    shape = (blocks, 2, maps.shape[3], rows // blocks, planes)
    return pl.pallas_call(
        adjoint_kernel,
        grid=grid_of(maps),
        in_specs=[maps_spec(spectra), maps_spec(maps), whole(mask.shape), whole(table.shape)],
        out_specs=field_spec(shape),
        out_shape=jax.ShapeDtypeStruct(shape, jnp.float32),
        compiler_params=compute_params(),
        cost_estimate=product_cost(maps, 3),
        name="adjoint",
    )(spectra, maps, mask, table)


def first_call(maps, field, mask, table):
    return pl.pallas_call(
        first_kernel,
        grid=grid_of(maps),
        in_specs=[maps_spec(maps), field_spec(field.shape), whole(mask.shape), whole(table.shape)],
        out_specs=field_spec(field.shape),
        out_shape=jax.ShapeDtypeStruct(field.shape, jnp.float32),
        compiler_params=compute_params(),
        cost_estimate=product_cost(maps, 6),
        name="first_product",
    )(maps, field, mask, table)


def second_call(maps, right, field, mask, table):
    blocks, _, x_count, block_rows, planes = field.shape
    out_shape = (blocks, 2 * x_count, block_rows, planes)
    return pl.pallas_call(
        second_kernel,
        grid=grid_of(maps),
        in_specs=[
            maps_spec(maps),
            field_spec(field.shape),
            field_spec(field.shape),
            whole(mask.shape),
            whole(table.shape),
        ],
        out_specs=[whole(out_shape), whole((8, planes))],
        out_shape=[
            jax.ShapeDtypeStruct(out_shape, jnp.float32),
            jax.ShapeDtypeStruct((8, planes), jnp.float32),
        ],
        compiler_params=compute_params(),
        cost_estimate=product_cost(maps, 6),
        name="second_product",
    )(maps, right, field, mask, table)


def exchange(blocks, axis):
    return lax.all_to_all(blocks, axis, split_axis=0, concat_axis=0, tiled=True)


def x_first(cells, parts):
    rows, planes, width = cells.shape
    split = cells.reshape(rows, planes, 2, parts, width // (2 * parts))
    return jnp.transpose(split, (3, 2, 4, 0, 1))


def x_last(blocks):
    parts, _, x_count, rows, planes = blocks.shape
    return jnp.transpose(blocks, (3, 4, 1, 0, 2)).reshape(rows, planes, 2 * parts * x_count)


def combined(right, field, image, squares):
    right_right, right_field, field_field, field_image = (squares[i] for i in range(4))
    ratio = right_field / right_right
    alpha = right_right / (right_field + penalty * right_right)
    fresh = alpha * alpha * (field_field - ratio * right_field)
    weight = alpha * ratio + fresh / right_right
    mixed = weight * alpha
    curvature = (
        weight * weight * right_field - 2.0 * mixed * field_field + alpha * alpha * field_image
    ) + penalty * (
        weight * weight * right_right - 2.0 * mixed * right_field + alpha * alpha * field_field
    )
    second = fresh / curvature
    solution = (alpha + second * weight) * right - (second * alpha) * field
    residual = (
        (alpha * ratio - penalty * second * weight) * right
        - (alpha + second * weight - penalty * second * alpha) * field
        + (second * alpha) * image
    )
    return solution, residual


def body(
    prior_image,
    coil_maps,
    kspace,
    sampling,
    weight_first,
    bias_first,
    weight_middle,
    bias_middle,
    weight_last,
    bias_last,
):
    readout = prior_image.shape[2] // 2
    own_rows = prior_image.shape[0]
    planes = prior_image.shape[1]
    slabs = lax.axis_size("slab")
    coils = lax.axis_size("coil")
    devices = slabs * coils
    mask = jnp.transpose(
        lax.all_gather(sampling.astype(jnp.bfloat16), "slab", axis=0, tiled=True)
    ).astype(jnp.float32)
    spread = readout % devices == 0
    parts = devices if spread else coils

    def coils_to_x(values):
        blocks = x_first(values, parts)
        tail = blocks.shape[1:]
        if spread:
            return exchange(blocks, axes).reshape((slabs, coils) + tail)
        blocks = exchange(blocks, "coil").reshape((slabs, coils // slabs) + tail)
        return exchange(blocks, "slab")

    maps = coils_to_x(coil_maps[0])
    measured, mask = lax.optimization_barrier((kspace[0], mask))
    spectra = coils_to_x(measured)
    table = jnp.asarray(dft_table(sampling.shape[1], planes))
    denoised = denoise(
        prior_image, weight_first, bias_first, weight_middle, bias_middle, weight_last, bias_last
    )
    blocks = x_first(denoised, parts)
    if spread:
        denoised = exchange(blocks, axes)
        right = adjoint_call(spectra, maps, mask, table, devices) + penalty * denoised
        right_rows = x_last(exchange(right, axes))
        field = first_call(maps, right, mask, table)
        field_rows = x_last(exchange(field, axes))
        image, totals = second_call(maps, right, field, mask, table)
        payload = jnp.concatenate(
            [image, jnp.broadcast_to(totals[None, None], (devices, 1) + totals.shape)], axis=1
        )
        payload = exchange(payload, axes)
        squares = jnp.sum(payload[:, -1], axis=(0, 2))
        image_rows = x_last(payload[:, :-1].reshape(blocks.shape))
        return combined(right_rows, field_rows, image_rows, squares)

    tail = blocks.shape[1:3]

    def whole_rows(parts_in):
        moved = lax.all_gather(exchange(parts_in, "coil"), "slab", axis=0, tiled=True)
        return jnp.transpose(moved, (1, 2, 0, 3, 4)).reshape((1,) + tail + (-1, planes))

    def own_part(whole):
        rows = whole.shape[3] // slabs
        mine = lax.dynamic_slice_in_dim(whole, lax.axis_index("slab") * rows, rows, axis=3)
        split = jnp.transpose(mine.reshape(tail + (coils, own_rows, planes)), (2, 0, 1, 3, 4))
        return x_last(exchange(split, "coil"))

    adjoint = lax.psum(adjoint_call(spectra, maps, mask, table, 1), "slab")
    right = adjoint + penalty * whole_rows(blocks)
    field = lax.psum(first_call(maps, right, mask, table), "slab")
    image, _ = second_call(maps, right, field, mask, table)
    image = lax.psum(image.reshape(field.shape), "slab")
    squares = lax.psum(
        jnp.stack(
            [
                jnp.sum(right * right),
                jnp.sum(right * field),
                jnp.sum(field * field),
                jnp.sum(field * image),
            ]
        ),
        "coil",
    )
    return combined(own_part(right), own_part(field), own_part(image), squares)


def solution(mesh):
    placed = (
        P(("slab", "coil"), None, None),
        P("coil", "slab", None, None),
        P("coil", "slab", None, None),
        P("slab", None),
        P(),
        P(),
        P(),
        P(),
        P(),
        P(),
    )
    return jax.shard_map(
        body,
        mesh=mesh,
        in_specs=placed,
        out_specs=(P(("slab", "coil"), None, None), P(("slab", "coil"), None, None)),
        check_vma=False,
    )
```

```python
import functools
import math

import jax
import jax.numpy as jnp
import numpy as np
from jax import lax
from jax.experimental import pallas as pl
from jax.experimental.pallas import tpu as pltpu
from jax.sharding import PartitionSpec as P

CG_ITERS = 2


penalty = 0.5
axes = ("slab", "coil")


def with_halo(cells, width):
    rows = cells.shape[0]
    count = lax.axis_size("slab") * lax.axis_size("coil")
    above, below = [], []
    for hop in range(1, -(-width // rows) + 1):
        taken = min(width - (hop - 1) * rows, rows)
        ends = count - hop
        tail = lax.slice_in_dim(cells, rows - taken, rows, axis=0)
        head = lax.slice_in_dim(cells, 0, taken, axis=0)
        above.insert(0, lax.ppermute(tail, axes, [(i, i + hop) for i in range(ends)]))
        below.append(lax.ppermute(head, axes, [(i + hop, i) for i in range(ends)]))
    return jnp.concatenate(above + [cells] + below, axis=0)


def chunk_rows(rows):
    return max(size for size in range(1, 7) if rows % size == 0)


def chained(lhs_pieces):
    rows = lhs_pieces[0].shape[0] * lhs_pieces[0].shape[1]
    lhs = jnp.concatenate(lhs_pieces, axis=2)
    return lhs.reshape(rows, lhs.shape[2])


def denoise_kernel(
    group,
    first_ref,
    features_ref,
    prior_ref,
    weight_first_ref,
    bias_first_ref,
    weight_middle_ref,
    bias_middle_ref,
    weight_last_ref,
    bias_last_ref,
    out_ref,
    one_ref,
    two_ref,
    taps_ref,
):
    planes = out_ref.shape[1]
    width = out_ref.shape[2]
    edge = (one_ref.shape[2] - two_ref.shape[2]) // 2
    groups = two_ref.shape[2] // group
    first = first_ref[0]
    total = first_ref[1]
    one_ref[:, :, :edge] = jnp.zeros(one_ref.shape[:2] + (edge,), one_ref.dtype)
    one_ref[:, :, edge + two_ref.shape[2] :] = jnp.zeros(
        one_ref.shape[:2] + (edge,), one_ref.dtype
    )

    def store(ref, start, count, lanes, value, reach):
        value = jnp.maximum(value, 0.0).reshape(count, planes, group)
        for row in range(count):
            place = first + (start + row - reach)
            kept = jnp.where((place >= 0) & (place < total), value[row], 0.0)
            ref[start + row, :, lanes] = kept.astype(ref.dtype)

    def first_layer(index, carry):
        lanes = pl.ds(pl.multiple_of(index * group, group), group)
        placed = pl.ds(pl.multiple_of(edge + index * group, 128), group)
        count = chunk_rows(one_ref.shape[0])
        for start in range(0, one_ref.shape[0], count):
            lhs = chained([features_ref[start + tap : start + tap + count] for tap in range(3)])
            value = jnp.dot(lhs, weight_first_ref[:, lanes], preferred_element_type=jnp.float32)
            store(one_ref, start, count, placed, value + bias_first_ref[:, lanes], 2)
        return carry

    lax.fori_loop(0, groups, first_layer, 0)

    def shifted(value, plane, step):
        rows = value.shape[0]
        if step > 0:
            return jnp.where(plane == 0, 0.0, pltpu.roll(value, 1, 0))
        return jnp.where(plane == planes - 1, 0.0, pltpu.roll(value, rows - 1, 0))

    def plane_index(count, lanes):
        return lax.broadcasted_iota(jnp.int32, (count, planes, lanes), 1).reshape(
            count * planes, lanes
        )

    def middle_layer(index, carry):
        lanes = pl.ds(pl.multiple_of(index * group, group), group)
        window = pl.ds(pl.multiple_of(index * group, group), group + 2 * edge)
        count = chunk_rows(two_ref.shape[0])
        plane = plane_index(count, group)
        for start in range(0, two_ref.shape[0], count):
            lhs = chained([one_ref[start + tap : start + tap + count, :, window] for tap in range(3)])
            value = jnp.dot(lhs, weight_middle_ref[...], preferred_element_type=jnp.float32)
            value = (
                value[:, group : 2 * group]
                + shifted(value[:, :group], plane, 1)
                + shifted(value[:, 2 * group :], plane, -1)
            )
            store(two_ref, start, count, lanes, value + bias_middle_ref[:, lanes], 1)
        return carry

    lax.fori_loop(0, groups, middle_layer, 0)

    count = chunk_rows(two_ref.shape[0])

    def last_layer(index, carry):
        start = index * count
        lhs = two_ref[pl.ds(start, count)].reshape(count * planes, two_ref.shape[2])
        value = jnp.dot(lhs, weight_last_ref[...], preferred_element_type=jnp.float32)
        taps_ref[pl.ds(start, count)] = value.reshape(count, planes, value.shape[1])
        return carry

    lax.fori_loop(0, two_ref.shape[0] // count, last_layer, 0)
    plane = plane_index(1, width)

    def last_sum(row, carry):
        sums = []
        for plane_tap in range(3):
            running = None
            for row_tap in range(3):
                lanes = pl.ds((row_tap * 3 + plane_tap) * width, width)
                value = taps_ref[row + row_tap, :, lanes]
                running = value if running is None else running + value
            sums.append(running)
        value = sums[1] + shifted(sums[0], plane, 1) + shifted(sums[2], plane, -1)
        out_ref[row] = prior_ref[row] + (value + bias_last_ref[...])
        return carry

    lax.fori_loop(0, out_ref.shape[0], last_sum, 0)


def banded(tiles, inner, outer, offset):
    shape = jnp.broadcast_shapes(tiles[0].shape, inner.shape, outer.shape)
    result = jnp.zeros(shape, jnp.bfloat16)
    for tap in range(3):
        result = jnp.where(inner - outer + offset == tap, tiles[tap], result)
    return result


def denoise(
    features, prior_image, weight_first, bias_first, weight_middle, bias_middle, weight_last, bias_last
):
    own_rows, planes, width = prior_image.shape
    readout = width // 2
    channels = weight_first.shape[3]
    span = readout * channels
    group = min(256, span)
    held = group // channels
    edge = 128
    reach = edge // channels
    window = group + 2 * edge

    def lane_place(count, inside):
        return jnp.arange(count * inside, dtype=jnp.int32) // inside

    tiles = jnp.transpose(weight_first, (2, 0, 1, 4, 3)).reshape(3, 18, 1, 1, channels)
    tiles = jnp.broadcast_to(tiles, (3, 18, 1, readout, channels)).reshape(3, 18, 1, span)
    first_table = banded(
        tiles,
        jnp.arange(readout, dtype=jnp.int32)[None, :, None],
        lane_place(readout, channels)[None, None, :],
        1,
    ).reshape(18 * readout, span)
    tiles = jnp.transpose(weight_middle, (2, 0, 4, 1, 3)).reshape(3, 3, 1, channels, 3, 1, channels)
    tiles = jnp.broadcast_to(tiles, (3, 3, 1, channels, 3, held, channels))
    tiles = tiles.reshape(3, 3, 1, channels, 3 * group)
    middle_table = banded(
        tiles,
        jnp.arange(window // channels, dtype=jnp.int32)[None, :, None, None] - reach,
        jnp.tile(lane_place(held, channels), 3)[None, None, None, :],
        1,
    ).reshape(3 * window, 3 * group)
    tiles = jnp.transpose(weight_last, (2, 4, 0, 1, 3)).reshape(3, 1, channels, 18, 1)
    tiles = jnp.broadcast_to(tiles, (3, 1, channels, 18, readout)).reshape(
        3, 1, channels, 18 * readout
    )
    last_table = banded(
        tiles,
        jnp.arange(readout, dtype=jnp.int32)[:, None, None],
        jnp.tile(jnp.arange(readout, dtype=jnp.int32), 18)[None, None, :],
        1,
    ).reshape(span, 18 * readout)

    features = with_halo(features, 3)
    rim = jnp.zeros_like(features[:, :1])
    features = jnp.concatenate(
        [
            jnp.concatenate([rim, features[:, :-1]], axis=1),
            features,
            jnp.concatenate([features[:, 1:], rim], axis=1),
        ],
        axis=2,
    )
    total = own_rows * lax.axis_size("slab") * lax.axis_size("coil")
    first = lax.axis_index(axes) * own_rows
    places = jnp.stack([first, jnp.asarray(total)]).astype(jnp.int32)
    vmem = pl.BlockSpec(memory_space=pltpu.VMEM)
    flops = 2 * own_rows * planes * (
        features.shape[2] * 3 * span * 3 // 2 + 9 * span * 512 * 5 // 4 + span * 18 * readout * 5 // 4
    )
    return pl.pallas_call(
        functools.partial(denoise_kernel, group),
        in_specs=[pl.BlockSpec(memory_space=pltpu.SMEM)] + [vmem] * 8,
        out_specs=vmem,
        out_shape=jax.ShapeDtypeStruct(prior_image.shape, jnp.float32),
        scratch_shapes=[
            pltpu.VMEM((own_rows + 4, planes, span + 2 * edge), jnp.bfloat16),
            pltpu.VMEM((own_rows + 2, planes, span), jnp.bfloat16),
            pltpu.VMEM((own_rows + 2, planes, 18 * readout), jnp.float32),
        ],
        compiler_params=pltpu.CompilerParams(vmem_limit_bytes=56 * 1024 * 1024),
        cost_estimate=pl.CostEstimate(
            flops=int(flops), bytes_accessed=16 * 1024 * 1024, transcendentals=0
        ),
        name="denoise",
    )(
        places,
        features,
        prior_image,
        first_table,
        jnp.tile(bias_first, readout)[None, :],
        middle_table,
        jnp.tile(bias_middle, readout)[None, :],
        last_table,
        jnp.repeat(bias_last, readout)[None, :],
    )


def table_parts(table):
    high = table.astype(jnp.bfloat16)
    low = (table - high.astype(np.float64)).astype(jnp.bfloat16)
    return high, low


def dft_parts(length):
    positions = np.arange(length, dtype=np.int64)
    angles = (positions[:, None] * positions[None, :] % length) * (2.0 * math.pi / length)
    scale = 1.0 / math.sqrt(length)
    return np.cos(angles) * scale, np.sin(angles) * scale


def turn_block(length):
    cos_part, sin_part = dft_parts(length)
    return np.concatenate(
        [
            np.concatenate([cos_part, sin_part], axis=1),
            np.concatenate([-sin_part, cos_part], axis=1),
        ],
        axis=0,
    )


def dft_table(rows, planes):
    rows_high, rows_low = table_parts(turn_block(rows))
    planes_parts = np.concatenate(table_parts(turn_block(planes).T), axis=0)
    short = max(2 * rows - planes_parts.shape[0], 0)
    planes_parts = np.pad(planes_parts, ((0, short), (0, 0)))
    return np.concatenate([rows_high, rows_low, planes_parts], axis=1)


def value_parts(value):
    high = value.astype(jnp.bfloat16)
    low = (value - high.astype(jnp.float32)).astype(jnp.bfloat16)
    return high, low


def tables_of(ref, rows, planes):
    high, low = ref[:, : 2 * rows], ref[:, 2 * rows : 4 * rows]
    row_table = jnp.concatenate([high, low, high], axis=1)
    high, low = ref[: 2 * planes, 4 * rows :], ref[2 * planes : 4 * planes, 4 * rows :]
    return row_table, jnp.concatenate([high, low, high], axis=0)


def along_planes(fields, table):
    rows, planes = fields[0][0].shape
    stacked = jnp.concatenate([jnp.concatenate(field, axis=1) for field in fields], axis=0)
    high, low = value_parts(stacked)
    moved = jnp.dot(
        jnp.concatenate([high, high, low], axis=1), table, preferred_element_type=jnp.float32
    )
    return [
        (
            moved[index * rows : (index + 1) * rows, :planes],
            moved[index * rows : (index + 1) * rows, planes:],
        )
        for index in range(len(fields))
    ]


def side_by_side(fields):
    return jnp.concatenate(
        [jnp.concatenate([field[part] for field in fields], axis=1) for part in range(2)], axis=0
    )


def along_rows(table, fields):
    rows, planes = fields[0][0].shape
    high, low = value_parts(side_by_side(fields))
    moved = jnp.dot(
        table, jnp.concatenate([high, high, low], axis=0), preferred_element_type=jnp.float32
    )
    return apart(moved, len(fields))


def apart(moved, count):
    rows = moved.shape[0] // 2
    planes = moved.shape[1] // count
    return [
        (
            moved[:rows, index * planes : (index + 1) * planes],
            moved[rows:, index * planes : (index + 1) * planes],
        )
        for index in range(count)
    ]


def plane_of(ref, part):
    value = ref[:, part, 0]
    return value.reshape(value.shape[0] * value.shape[1], value.shape[2])


def coil_plane(ref, coil, part):
    value = ref[:, coil, part, 0]
    return value.reshape(value.shape[0] * value.shape[1], value.shape[2])


def map_of(ref, coil):
    return [coil_plane(ref, coil, part).astype(jnp.float32) for part in range(2)]


def image_sums(maps, fields):
    sums = None
    for (map_real, map_imag), (real, imag) in zip(maps, fields):
        terms = (map_real * real - map_imag * imag, -(map_real * imag + map_imag * real))
        sums = terms if sums is None else (sums[0] + terms[0], sums[1] + terms[1])
    return sums


def units_of(ref):
    count = ref.shape[1]
    held = 2 if count % 2 == 0 else 1
    return [tuple(range(first, first + held)) for first in range(0, count, held)]


def normal_sums(maps_ref, real, imag, mask, tables):
    row_table, plane_table = tables
    units = units_of(maps_ref)
    fields = []
    for unit in units:
        products = []
        for coil in unit:
            map_real, map_imag = map_of(maps_ref, coil)
            products.append(
                (map_real * real - map_imag * imag, map_real * imag + map_imag * real)
            )
        fields.append(along_planes(products, plane_table))
    fields = [along_rows(row_table, field) for field in fields]
    spectra = [
        [(real_part * mask, imag_part * -mask) for real_part, imag_part in field]
        for field in fields
    ]
    fields = [along_rows(row_table, spectrum) for spectrum in spectra]
    fields = [along_planes(field, plane_table) for field in fields]
    total = None
    for unit, field in zip(units, fields):
        sums = image_sums([map_of(maps_ref, coil) for coil in unit], field)
        total = sums if total is None else (total[0] + sums[0], total[1] + sums[1])
    return total


def adjoint_kernel(kspace_ref, maps_ref, mask_ref, table_ref, out_ref):
    mask = mask_ref[...]
    rows, planes = mask.shape
    row_table, plane_table = tables_of(table_ref, rows, planes)
    units = units_of(maps_ref)
    images = []
    for unit in units:
        spectra = []
        for coil in unit:
            real, imag = (
                jnp.transpose(coil_plane(kspace_ref, coil, part).astype(jnp.float32))
                for part in range(2)
            )
            spectra.append((real * mask, imag * -mask))
        spectrum = side_by_side(spectra).astype(jnp.bfloat16)
        moved = jnp.dot(
            row_table[:, : 4 * rows],
            jnp.concatenate([spectrum, spectrum], axis=0),
            preferred_element_type=jnp.float32,
        )
        images.append(apart(moved, len(unit)))
    images = [along_planes(image, plane_table) for image in images]
    total = None
    for unit, image in zip(units, images):
        sums = image_sums([map_of(maps_ref, coil) for coil in unit], image)
        total = sums if total is None else (total[0] + sums[0], total[1] + sums[1])
    shape = out_ref.shape[0], out_ref.shape[3], out_ref.shape[4]

    @pl.when(pl.program_id(1) == 0)
    def _():
        for part in range(2):
            out_ref[:, part, 0] = total[part].reshape(shape)

    @pl.when(pl.program_id(1) > 0)
    def _():
        for part in range(2):
            out_ref[:, part, 0] += total[part].reshape(shape)


def first_kernel(maps_ref, field_ref, mask_ref, table_ref, out_ref):
    mask = mask_ref[...]
    sums = normal_sums(
        maps_ref,
        plane_of(field_ref, 0),
        plane_of(field_ref, 1),
        mask,
        tables_of(table_ref, *mask.shape),
    )
    shape = out_ref.shape[0], out_ref.shape[3], out_ref.shape[4]

    @pl.when(pl.program_id(1) == 0)
    def _():
        for part in range(2):
            out_ref[:, part, 0] = sums[part].reshape(shape)

    @pl.when(pl.program_id(1) > 0)
    def _():
        for part in range(2):
            out_ref[:, part, 0] += sums[part].reshape(shape)


def second_kernel(maps_ref, right_ref, field_ref, mask_ref, table_ref, out_ref, total_ref):
    x_index = pl.program_id(0)
    x_count = pl.num_programs(0)
    blocks, block_rows, planes = out_ref.shape[0], out_ref.shape[2], out_ref.shape[3]
    shape = blocks, block_rows, planes
    mask = mask_ref[...]
    sums = normal_sums(
        maps_ref,
        plane_of(field_ref, 0),
        plane_of(field_ref, 1),
        mask,
        tables_of(table_ref, *mask.shape),
    )

    @pl.when(pl.program_id(1) == 0)
    def _():
        for part in range(2):
            out_ref[:, part * x_count + x_index] = sums[part].reshape(shape)

    @pl.when(pl.program_id(1) > 0)
    def _():
        for part in range(2):
            out_ref[:, part * x_count + x_index] += sums[part].reshape(shape)

    @pl.when(pl.program_id(1) == pl.num_programs(1) - 1)
    def _():
        rights = [right_ref[:, part, 0] for part in range(2)]
        fields = [field_ref[:, part, 0] for part in range(2)]
        images = [out_ref[:, part * x_count + x_index] for part in range(2)]

        def lane_sums(left, other):
            product = left[0] * other[0] + left[1] * other[1]
            return jnp.sum(jnp.sum(product, axis=0), axis=0, keepdims=True)

        totals = jnp.concatenate(
            [
                lane_sums(rights, rights),
                lane_sums(rights, fields),
                lane_sums(fields, fields),
                lane_sums(fields, images),
                jnp.zeros((4, planes), jnp.float32),
            ],
            axis=0,
        )

        @pl.when(x_index == 0)
        def _():
            total_ref[...] = totals

        @pl.when(x_index > 0)
        def _():
            total_ref[...] += totals


def held_coils(count):
    return max(size for size in (1, 2, 4, 8) if count % size == 0)


def whole(shape):
    return pl.BlockSpec(shape, lambda x, c: (0,) * len(shape))


def maps_spec(maps):
    slabs, coils, _, _, slab_rows, planes = maps.shape
    return pl.BlockSpec(
        (slabs, held_coils(coils), 2, 1, slab_rows, planes), lambda x, c: (0, c, 0, x, 0, 0)
    )


def field_spec(shape):
    return pl.BlockSpec((shape[0], 2, 1) + shape[3:], lambda x, c: (0, 0, x, 0, 0))


def grid_of(maps):
    return maps.shape[3], maps.shape[1] // held_coils(maps.shape[1])


def compute_params():
    return pltpu.CompilerParams(
        dimension_semantics=("arbitrary", "arbitrary"), vmem_limit_bytes=48 * 1024 * 1024
    )


def product_cost(maps, passes):
    slabs, coils, _, x_count, slab_rows, planes = maps.shape
    rows = slabs * slab_rows
    per_plane = 2 * 2 * rows * planes * (2 * rows + 2 * planes)
    return pl.CostEstimate(
        flops=int(coils * x_count * per_plane * passes),
        bytes_accessed=int(2 * maps.size),
        transcendentals=0,
    )


def adjoint_call(spectra, maps, mask, table, blocks):
    rows, planes = mask.shape
    shape = (blocks, 2, maps.shape[3], rows // blocks, planes)
    return pl.pallas_call(
        adjoint_kernel,
        grid=grid_of(maps),
        in_specs=[maps_spec(spectra), maps_spec(maps), whole(mask.shape), whole(table.shape)],
        out_specs=field_spec(shape),
        out_shape=jax.ShapeDtypeStruct(shape, jnp.float32),
        compiler_params=compute_params(),
        cost_estimate=product_cost(maps, 3),
        name="adjoint",
    )(spectra, maps, mask, table)


def first_call(maps, field, mask, table):
    return pl.pallas_call(
        first_kernel,
        grid=grid_of(maps),
        in_specs=[maps_spec(maps), field_spec(field.shape), whole(mask.shape), whole(table.shape)],
        out_specs=field_spec(field.shape),
        out_shape=jax.ShapeDtypeStruct(field.shape, jnp.float32),
        compiler_params=compute_params(),
        cost_estimate=product_cost(maps, 6),
        name="first_product",
    )(maps, field, mask, table)


def second_call(maps, right, field, mask, table):
    blocks, _, x_count, block_rows, planes = field.shape
    out_shape = (blocks, 2 * x_count, block_rows, planes)
    return pl.pallas_call(
        second_kernel,
        grid=grid_of(maps),
        in_specs=[
            maps_spec(maps),
            field_spec(field.shape),
            field_spec(field.shape),
            whole(mask.shape),
            whole(table.shape),
        ],
        out_specs=[whole(out_shape), whole((8, planes))],
        out_shape=[
            jax.ShapeDtypeStruct(out_shape, jnp.float32),
            jax.ShapeDtypeStruct((8, planes), jnp.float32),
        ],
        compiler_params=compute_params(),
        cost_estimate=product_cost(maps, 6),
        name="second_product",
    )(maps, right, field, mask, table)


def exchange(blocks, axis):
    return lax.all_to_all(blocks, axis, split_axis=0, concat_axis=0, tiled=True)


def x_first(cells, parts):
    rows, planes, width = cells.shape
    split = cells.reshape(rows, planes, 2, parts, width // (2 * parts))
    return jnp.transpose(split, (3, 2, 4, 0, 1))


def x_last(blocks):
    parts, _, x_count, rows, planes = blocks.shape
    return jnp.transpose(blocks, (3, 4, 1, 0, 2)).reshape(rows, planes, 2 * parts * x_count)


def combined(right, field, image, squares):
    right_right, right_field, field_field, field_image = (squares[i] for i in range(4))
    ratio = right_field / right_right
    alpha = right_right / (right_field + penalty * right_right)
    fresh = alpha * alpha * (field_field - ratio * right_field)
    weight = alpha * ratio + fresh / right_right
    mixed = weight * alpha
    curvature = (
        weight * weight * right_field - 2.0 * mixed * field_field + alpha * alpha * field_image
    ) + penalty * (
        weight * weight * right_right - 2.0 * mixed * right_field + alpha * alpha * field_field
    )
    second = fresh / curvature
    solution = (alpha + second * weight) * right - (second * alpha) * field
    residual = (
        (alpha * ratio - penalty * second * weight) * right
        - (alpha + second * weight - penalty * second * alpha) * field
        + (second * alpha) * image
    )
    return solution, residual


def body(
    prior_image,
    coil_maps,
    kspace,
    sampling,
    weight_first,
    bias_first,
    weight_middle,
    bias_middle,
    weight_last,
    bias_last,
):
    readout = prior_image.shape[2] // 2
    own_rows = prior_image.shape[0]
    planes = prior_image.shape[1]
    slabs = lax.axis_size("slab")
    coils = lax.axis_size("coil")
    devices = slabs * coils
    mask = jnp.transpose(
        lax.all_gather(sampling.astype(jnp.bfloat16), "slab", axis=0, tiled=True)
    ).astype(jnp.float32)
    spread = readout % devices == 0
    parts = devices if spread else coils

    def coils_to_x(blocks):
        tail = blocks.shape[1:]
        if spread:
            return exchange(blocks, axes).reshape((slabs, coils) + tail)
        blocks = exchange(blocks, "coil").reshape((slabs, coils // slabs) + tail)
        return exchange(blocks, "slab")

    map_blocks, measured = lax.optimization_barrier(
        (x_first(coil_maps[0], parts), kspace[0])
    )
    maps = coils_to_x(map_blocks)
    blocks, features, mask = lax.optimization_barrier(
        (x_first(measured, parts), prior_image.astype(jnp.bfloat16), mask)
    )
    spectra = coils_to_x(blocks)
    table = jnp.asarray(dft_table(sampling.shape[1], planes))
    denoised = denoise(
        features, prior_image, weight_first, bias_first, weight_middle, bias_middle, weight_last, bias_last
    )
    blocks = x_first(denoised, parts)
    if spread:
        denoised = exchange(blocks, axes)
        right = adjoint_call(spectra, maps, mask, table, devices) + penalty * denoised
        field, right_back = lax.optimization_barrier(
            (first_call(maps, right, mask, table), exchange(right, axes))
        )
        right_rows = x_last(right_back)
        field_rows = x_last(exchange(field, axes))
        image, totals = second_call(maps, right, field, mask, table)
        payload = jnp.concatenate(
            [image, jnp.broadcast_to(totals[None, None], (devices, 1) + totals.shape)], axis=1
        )
        payload = exchange(payload, axes)
        squares = jnp.sum(payload[:, -1], axis=(0, 2))
        image_rows = x_last(payload[:, :-1].reshape(blocks.shape))
        return combined(right_rows, field_rows, image_rows, squares)

    tail = blocks.shape[1:3]

    def whole_rows(parts_in):
        moved = lax.all_gather(exchange(parts_in, "coil"), "slab", axis=0, tiled=True)
        return jnp.transpose(moved, (1, 2, 0, 3, 4)).reshape((1,) + tail + (-1, planes))

    def own_part(whole):
        rows = whole.shape[3] // slabs
        mine = lax.dynamic_slice_in_dim(whole, lax.axis_index("slab") * rows, rows, axis=3)
        split = jnp.transpose(mine.reshape(tail + (coils, own_rows, planes)), (2, 0, 1, 3, 4))
        return x_last(exchange(split, "coil"))

    adjoint = lax.psum(adjoint_call(spectra, maps, mask, table, 1), "slab")
    right = adjoint + penalty * whole_rows(blocks)
    field = lax.psum(first_call(maps, right, mask, table), "slab")
    image, _ = second_call(maps, right, field, mask, table)
    image = lax.psum(image.reshape(field.shape), "slab")
    squares = lax.psum(
        jnp.stack(
            [
                jnp.sum(right * right),
                jnp.sum(right * field),
                jnp.sum(field * field),
                jnp.sum(field * image),
            ]
        ),
        "coil",
    )
    return combined(own_part(right), own_part(field), own_part(image), squares)


def solution(mesh):
    placed = (
        P(("slab", "coil"), None, None),
        P("coil", "slab", None, None),
        P("coil", "slab", None, None),
        P("slab", None),
        P(),
        P(),
        P(),
        P(),
        P(),
        P(),
    )
    return jax.shard_map(
        body,
        mesh=mesh,
        in_specs=placed,
        out_specs=(P(("slab", "coil"), None, None), P(("slab", "coil"), None, None)),
        check_vma=False,
    )
```

```python
import functools
import math

import jax
import jax.numpy as jnp
import numpy as np
from jax import lax
from jax.experimental import pallas as pl
from jax.experimental.pallas import tpu as pltpu
from jax.sharding import PartitionSpec as P

CG_ITERS = 2


penalty = 0.5
axes = ("slab", "coil")


def with_halo(cells, width):
    rows = cells.shape[0]
    count = lax.axis_size("slab") * lax.axis_size("coil")
    above, below = [], []
    for hop in range(1, -(-width // rows) + 1):
        taken = min(width - (hop - 1) * rows, rows)
        ends = count - hop
        tail = lax.slice_in_dim(cells, rows - taken, rows, axis=0)
        head = lax.slice_in_dim(cells, 0, taken, axis=0)
        above.insert(0, lax.ppermute(tail, axes, [(i, i + hop) for i in range(ends)]))
        below.append(lax.ppermute(head, axes, [(i + hop, i) for i in range(ends)]))
    return jnp.concatenate(above + [cells] + below, axis=0)


def chunk_rows(rows):
    return max(size for size in range(1, 7) if rows % size == 0)


def chained(lhs_pieces):
    rows = lhs_pieces[0].shape[0] * lhs_pieces[0].shape[1]
    lhs = jnp.concatenate(lhs_pieces, axis=2)
    return lhs.reshape(rows, lhs.shape[2])


def denoise_kernel(
    group,
    first_ref,
    features_ref,
    prior_ref,
    weight_first_ref,
    bias_first_ref,
    weight_middle_ref,
    bias_middle_ref,
    weight_last_ref,
    bias_last_ref,
    out_ref,
    one_ref,
    two_ref,
    taps_ref,
):
    planes = out_ref.shape[1]
    width = out_ref.shape[2]
    edge = (one_ref.shape[2] - two_ref.shape[2]) // 2
    groups = two_ref.shape[2] // group
    first = first_ref[0]
    total = first_ref[1]
    one_ref[:, :, :edge] = jnp.zeros(one_ref.shape[:2] + (edge,), one_ref.dtype)
    one_ref[:, :, edge + two_ref.shape[2] :] = jnp.zeros(
        one_ref.shape[:2] + (edge,), one_ref.dtype
    )

    def store(ref, start, count, lanes, value, reach):
        value = jnp.maximum(value, 0.0).reshape(count, planes, group)
        for row in range(count):
            place = first + (start + row - reach)
            kept = jnp.where((place >= 0) & (place < total), value[row], 0.0)
            ref[start + row, :, lanes] = kept.astype(ref.dtype)

    def first_layer(index, carry):
        lanes = pl.ds(pl.multiple_of(index * group, group), group)
        placed = pl.ds(pl.multiple_of(edge + index * group, 128), group)
        count = chunk_rows(one_ref.shape[0])
        for start in range(0, one_ref.shape[0], count):
            lhs = chained([features_ref[start + tap : start + tap + count] for tap in range(3)])
            value = jnp.dot(lhs, weight_first_ref[:, lanes], preferred_element_type=jnp.float32)
            store(one_ref, start, count, placed, value + bias_first_ref[:, lanes], 2)
        return carry

    lax.fori_loop(0, groups, first_layer, 0)

    def shifted(value, plane, step):
        rows = value.shape[0]
        if step > 0:
            return jnp.where(plane == 0, 0.0, pltpu.roll(value, 1, 0))
        return jnp.where(plane == planes - 1, 0.0, pltpu.roll(value, rows - 1, 0))

    def plane_index(count, lanes):
        return lax.broadcasted_iota(jnp.int32, (count, planes, lanes), 1).reshape(
            count * planes, lanes
        )

    def middle_layer(index, carry):
        lanes = pl.ds(pl.multiple_of(index * group, group), group)
        window = pl.ds(pl.multiple_of(index * group, group), group + 2 * edge)
        count = chunk_rows(two_ref.shape[0])
        plane = plane_index(count, group)
        for start in range(0, two_ref.shape[0], count):
            lhs = chained([one_ref[start + tap : start + tap + count, :, window] for tap in range(3)])
            value = jnp.dot(lhs, weight_middle_ref[...], preferred_element_type=jnp.float32)
            value = (
                value[:, group : 2 * group]
                + shifted(value[:, :group], plane, 1)
                + shifted(value[:, 2 * group :], plane, -1)
            )
            store(two_ref, start, count, lanes, value + bias_middle_ref[:, lanes], 1)
        return carry

    lax.fori_loop(0, groups, middle_layer, 0)

    count = chunk_rows(two_ref.shape[0])

    def last_layer(index, carry):
        start = index * count
        lhs = two_ref[pl.ds(start, count)].reshape(count * planes, two_ref.shape[2])
        value = jnp.dot(lhs, weight_last_ref[...], preferred_element_type=jnp.float32)
        taps_ref[pl.ds(start, count)] = value.reshape(count, planes, value.shape[1])
        return carry

    lax.fori_loop(0, two_ref.shape[0] // count, last_layer, 0)
    plane = plane_index(1, width)

    def last_sum(row, carry):
        sums = []
        for plane_tap in range(3):
            running = None
            for row_tap in range(3):
                lanes = pl.ds((row_tap * 3 + plane_tap) * width, width)
                value = taps_ref[row + row_tap, :, lanes]
                running = value if running is None else running + value
            sums.append(running)
        value = sums[1] + shifted(sums[0], plane, 1) + shifted(sums[2], plane, -1)
        out_ref[row] = prior_ref[row] + (value + bias_last_ref[...])
        return carry

    lax.fori_loop(0, out_ref.shape[0], last_sum, 0)


def banded(tiles, inner, outer, offset):
    shape = jnp.broadcast_shapes(tiles[0].shape, inner.shape, outer.shape)
    result = jnp.zeros(shape, jnp.bfloat16)
    for tap in range(3):
        result = jnp.where(inner - outer + offset == tap, tiles[tap], result)
    return result


def denoise(
    prior_image, weight_first, bias_first, weight_middle, bias_middle, weight_last, bias_last
):
    own_rows, planes, width = prior_image.shape
    readout = width // 2
    channels = weight_first.shape[3]
    span = readout * channels
    group = min(256, span)
    held = group // channels
    edge = 128
    reach = edge // channels
    window = group + 2 * edge

    def lane_place(count, inside):
        return jnp.arange(count * inside, dtype=jnp.int32) // inside

    tiles = jnp.transpose(weight_first, (2, 0, 1, 4, 3)).reshape(3, 18, 1, 1, channels)
    tiles = jnp.broadcast_to(tiles, (3, 18, 1, readout, channels)).reshape(3, 18, 1, span)
    first_table = banded(
        tiles,
        jnp.arange(readout, dtype=jnp.int32)[None, :, None],
        lane_place(readout, channels)[None, None, :],
        1,
    ).reshape(18 * readout, span)
    tiles = jnp.transpose(weight_middle, (2, 0, 4, 1, 3)).reshape(3, 3, 1, channels, 3, 1, channels)
    tiles = jnp.broadcast_to(tiles, (3, 3, 1, channels, 3, held, channels))
    tiles = tiles.reshape(3, 3, 1, channels, 3 * group)
    middle_table = banded(
        tiles,
        jnp.arange(window // channels, dtype=jnp.int32)[None, :, None, None] - reach,
        jnp.tile(lane_place(held, channels), 3)[None, None, None, :],
        1,
    ).reshape(3 * window, 3 * group)
    tiles = jnp.transpose(weight_last, (2, 4, 0, 1, 3)).reshape(3, 1, channels, 18, 1)
    tiles = jnp.broadcast_to(tiles, (3, 1, channels, 18, readout)).reshape(
        3, 1, channels, 18 * readout
    )
    last_table = banded(
        tiles,
        jnp.arange(readout, dtype=jnp.int32)[:, None, None],
        jnp.tile(jnp.arange(readout, dtype=jnp.int32), 18)[None, None, :],
        1,
    ).reshape(span, 18 * readout)

    features = with_halo(prior_image.astype(jnp.bfloat16), 3)
    rim = jnp.zeros_like(features[:, :1])
    features = jnp.concatenate(
        [
            jnp.concatenate([rim, features[:, :-1]], axis=1),
            features,
            jnp.concatenate([features[:, 1:], rim], axis=1),
        ],
        axis=2,
    )
    total = own_rows * lax.axis_size("slab") * lax.axis_size("coil")
    first = lax.axis_index(axes) * own_rows
    places = jnp.stack([first, jnp.asarray(total)]).astype(jnp.int32)
    vmem = pl.BlockSpec(memory_space=pltpu.VMEM)
    flops = 2 * own_rows * planes * (
        features.shape[2] * 3 * span * 3 // 2 + 9 * span * 512 * 5 // 4 + span * 18 * readout * 5 // 4
    )
    return pl.pallas_call(
        functools.partial(denoise_kernel, group),
        in_specs=[pl.BlockSpec(memory_space=pltpu.SMEM)] + [vmem] * 8,
        out_specs=vmem,
        out_shape=jax.ShapeDtypeStruct(prior_image.shape, jnp.float32),
        scratch_shapes=[
            pltpu.VMEM((own_rows + 4, planes, span + 2 * edge), jnp.bfloat16),
            pltpu.VMEM((own_rows + 2, planes, span), jnp.bfloat16),
            pltpu.VMEM((own_rows + 2, planes, 18 * readout), jnp.float32),
        ],
        compiler_params=pltpu.CompilerParams(vmem_limit_bytes=56 * 1024 * 1024),
        cost_estimate=pl.CostEstimate(
            flops=int(flops), bytes_accessed=16 * 1024 * 1024, transcendentals=0
        ),
        name="denoise",
    )(
        places,
        features,
        prior_image,
        first_table,
        jnp.tile(bias_first, readout)[None, :],
        middle_table,
        jnp.tile(bias_middle, readout)[None, :],
        last_table,
        jnp.repeat(bias_last, readout)[None, :],
    )


def table_parts(table):
    high = table.astype(jnp.bfloat16)
    low = (table - high.astype(np.float64)).astype(jnp.bfloat16)
    return high, low


def dft_parts(length):
    positions = np.arange(length, dtype=np.int64)
    angles = (positions[:, None] * positions[None, :] % length) * (2.0 * math.pi / length)
    scale = 1.0 / math.sqrt(length)
    return np.cos(angles) * scale, np.sin(angles) * scale


def turn_block(length):
    cos_part, sin_part = dft_parts(length)
    return np.concatenate(
        [
            np.concatenate([cos_part, sin_part], axis=1),
            np.concatenate([-sin_part, cos_part], axis=1),
        ],
        axis=0,
    )


def dft_table(rows, planes):
    rows_high, rows_low = table_parts(turn_block(rows))
    planes_parts = np.concatenate(table_parts(turn_block(planes).T), axis=0)
    short = max(2 * rows - planes_parts.shape[0], 0)
    planes_parts = np.pad(planes_parts, ((0, short), (0, 0)))
    return np.concatenate([rows_high, rows_low, planes_parts], axis=1)


def value_parts(value):
    high = value.astype(jnp.bfloat16)
    low = (value - high.astype(jnp.float32)).astype(jnp.bfloat16)
    return high, low


def tables_of(ref, rows, planes):
    high, low = ref[:, : 2 * rows], ref[:, 2 * rows : 4 * rows]
    row_table = jnp.concatenate([high, low, high], axis=1)
    high, low = ref[: 2 * planes, 4 * rows :], ref[2 * planes : 4 * planes, 4 * rows :]
    return row_table, jnp.concatenate([high, low, high], axis=0)


def along_planes(fields, table):
    rows, planes = fields[0][0].shape
    stacked = jnp.concatenate([jnp.concatenate(field, axis=1) for field in fields], axis=0)
    high, low = value_parts(stacked)
    moved = jnp.dot(
        jnp.concatenate([high, high, low], axis=1), table, preferred_element_type=jnp.float32
    )
    return [
        (
            moved[index * rows : (index + 1) * rows, :planes],
            moved[index * rows : (index + 1) * rows, planes:],
        )
        for index in range(len(fields))
    ]


def side_by_side(fields):
    return jnp.concatenate(
        [jnp.concatenate([field[part] for field in fields], axis=1) for part in range(2)], axis=0
    )


def along_rows(table, fields):
    rows, planes = fields[0][0].shape
    high, low = value_parts(side_by_side(fields))
    moved = jnp.dot(
        table, jnp.concatenate([high, high, low], axis=0), preferred_element_type=jnp.float32
    )
    return apart(moved, len(fields))


def apart(moved, count):
    rows = moved.shape[0] // 2
    planes = moved.shape[1] // count
    return [
        (
            moved[:rows, index * planes : (index + 1) * planes],
            moved[rows:, index * planes : (index + 1) * planes],
        )
        for index in range(count)
    ]


def plane_of(ref, part):
    value = ref[:, part, 0]
    return value.reshape(value.shape[0] * value.shape[1], value.shape[2])


def coil_plane(ref, coil, part):
    value = ref[:, coil, part, 0]
    return value.reshape(value.shape[0] * value.shape[1], value.shape[2])


def map_of(ref, coil):
    return [coil_plane(ref, coil, part).astype(jnp.float32) for part in range(2)]


def image_sums(maps, fields):
    sums = None
    for (map_real, map_imag), (real, imag) in zip(maps, fields):
        terms = (map_real * real - map_imag * imag, -(map_real * imag + map_imag * real))
        sums = terms if sums is None else (sums[0] + terms[0], sums[1] + terms[1])
    return sums


def units_of(ref):
    count = ref.shape[1]
    held = 2 if count % 2 == 0 else 1
    return [tuple(range(first, first + held)) for first in range(0, count, held)]


def normal_sums(maps_ref, real, imag, mask, tables):
    row_table, plane_table = tables
    units = units_of(maps_ref)
    fields = []
    for unit in units:
        products = []
        for coil in unit:
            map_real, map_imag = map_of(maps_ref, coil)
            products.append(
                (map_real * real - map_imag * imag, map_real * imag + map_imag * real)
            )
        fields.append(along_planes(products, plane_table))
    fields = [along_rows(row_table, field) for field in fields]
    spectra = [
        [(real_part * mask, imag_part * -mask) for real_part, imag_part in field]
        for field in fields
    ]
    fields = [along_rows(row_table, spectrum) for spectrum in spectra]
    fields = [along_planes(field, plane_table) for field in fields]
    total = None
    for unit, field in zip(units, fields):
        sums = image_sums([map_of(maps_ref, coil) for coil in unit], field)
        total = sums if total is None else (total[0] + sums[0], total[1] + sums[1])
    return total


def adjoint_kernel(kspace_ref, maps_ref, mask_ref, table_ref, out_ref):
    mask = mask_ref[...]
    rows, planes = mask.shape
    row_table, plane_table = tables_of(table_ref, rows, planes)
    units = units_of(maps_ref)
    images = []
    for unit in units:
        spectra = []
        for coil in unit:
            real, imag = (
                jnp.transpose(coil_plane(kspace_ref, coil, part).astype(jnp.float32))
                for part in range(2)
            )
            spectra.append((real * mask, imag * -mask))
        spectrum = side_by_side(spectra).astype(jnp.bfloat16)
        moved = jnp.dot(
            row_table[:, : 4 * rows],
            jnp.concatenate([spectrum, spectrum], axis=0),
            preferred_element_type=jnp.float32,
        )
        images.append(apart(moved, len(unit)))
    images = [along_planes(image, plane_table) for image in images]
    total = None
    for unit, image in zip(units, images):
        sums = image_sums([map_of(maps_ref, coil) for coil in unit], image)
        total = sums if total is None else (total[0] + sums[0], total[1] + sums[1])
    shape = out_ref.shape[0], out_ref.shape[3], out_ref.shape[4]

    @pl.when(pl.program_id(1) == 0)
    def _():
        for part in range(2):
            out_ref[:, part, 0] = total[part].reshape(shape)

    @pl.when(pl.program_id(1) > 0)
    def _():
        for part in range(2):
            out_ref[:, part, 0] += total[part].reshape(shape)


def first_kernel(maps_ref, field_ref, mask_ref, table_ref, out_ref):
    mask = mask_ref[...]
    sums = normal_sums(
        maps_ref,
        plane_of(field_ref, 0),
        plane_of(field_ref, 1),
        mask,
        tables_of(table_ref, *mask.shape),
    )
    shape = out_ref.shape[0], out_ref.shape[3], out_ref.shape[4]

    @pl.when(pl.program_id(1) == 0)
    def _():
        for part in range(2):
            out_ref[:, part, 0] = sums[part].reshape(shape)

    @pl.when(pl.program_id(1) > 0)
    def _():
        for part in range(2):
            out_ref[:, part, 0] += sums[part].reshape(shape)


def second_kernel(maps_ref, right_ref, field_ref, mask_ref, table_ref, out_ref):
    x_index = pl.program_id(0)
    x_count = pl.num_programs(0)
    blocks, block_rows, planes = out_ref.shape[0], out_ref.shape[2], out_ref.shape[3]
    shape = blocks, block_rows, planes
    mask = mask_ref[...]
    sums = normal_sums(
        maps_ref,
        plane_of(field_ref, 0),
        plane_of(field_ref, 1),
        mask,
        tables_of(table_ref, *mask.shape),
    )

    @pl.when(pl.program_id(1) == 0)
    def _():
        for part in range(2):
            out_ref[:, part * x_count + x_index] = sums[part].reshape(shape)

    @pl.when(pl.program_id(1) > 0)
    def _():
        for part in range(2):
            out_ref[:, part * x_count + x_index] += sums[part].reshape(shape)

    @pl.when(pl.program_id(1) == pl.num_programs(1) - 1)
    def _():
        rights = [right_ref[:, part, 0] for part in range(2)]
        fields = [field_ref[:, part, 0] for part in range(2)]
        images = [out_ref[:, part * x_count + x_index] for part in range(2)]
        for part in range(2):
            out_ref[:, (2 + part) * x_count + x_index] = fields[part]

        def lane_sums(left, other):
            product = left[0] * other[0] + left[1] * other[1]
            return jnp.sum(jnp.sum(product, axis=0), axis=0, keepdims=True)

        totals = jnp.concatenate(
            [
                lane_sums(rights, rights),
                lane_sums(rights, fields),
                lane_sums(fields, fields),
                lane_sums(fields, images),
                jnp.zeros((block_rows - 4, planes), jnp.float32),
            ],
            axis=0,
        )
        totals = jnp.broadcast_to(totals[None], shape)

        @pl.when(x_index == 0)
        def _():
            out_ref[:, 4 * x_count] = totals

        @pl.when(x_index > 0)
        def _():
            out_ref[:, 4 * x_count] += totals


def held_coils(count):
    return max(size for size in (1, 2, 4, 8) if count % size == 0)


def whole(shape):
    return pl.BlockSpec(shape, lambda x, c: (0,) * len(shape))


def maps_spec(maps):
    slabs, coils, _, _, slab_rows, planes = maps.shape
    return pl.BlockSpec(
        (slabs, held_coils(coils), 2, 1, slab_rows, planes), lambda x, c: (0, c, 0, x, 0, 0)
    )


def field_spec(shape):
    return pl.BlockSpec((shape[0], 2, 1) + shape[3:], lambda x, c: (0, 0, x, 0, 0))


def grid_of(maps):
    return maps.shape[3], maps.shape[1] // held_coils(maps.shape[1])


def compute_params():
    return pltpu.CompilerParams(
        dimension_semantics=("arbitrary", "arbitrary"), vmem_limit_bytes=48 * 1024 * 1024
    )


def product_cost(maps, passes):
    slabs, coils, _, x_count, slab_rows, planes = maps.shape
    rows = slabs * slab_rows
    per_plane = 2 * 2 * rows * planes * (2 * rows + 2 * planes)
    return pl.CostEstimate(
        flops=int(coils * x_count * per_plane * passes),
        bytes_accessed=int(2 * maps.size),
        transcendentals=0,
    )


def adjoint_call(spectra, maps, mask, table, blocks):
    rows, planes = mask.shape
    shape = (blocks, 2, maps.shape[3], rows // blocks, planes)
    return pl.pallas_call(
        adjoint_kernel,
        grid=grid_of(maps),
        in_specs=[maps_spec(spectra), maps_spec(maps), whole(mask.shape), whole(table.shape)],
        out_specs=field_spec(shape),
        out_shape=jax.ShapeDtypeStruct(shape, jnp.float32),
        compiler_params=compute_params(),
        cost_estimate=product_cost(maps, 3),
        name="adjoint",
    )(spectra, maps, mask, table)


def first_call(maps, field, mask, table):
    return pl.pallas_call(
        first_kernel,
        grid=grid_of(maps),
        in_specs=[maps_spec(maps), field_spec(field.shape), whole(mask.shape), whole(table.shape)],
        out_specs=field_spec(field.shape),
        out_shape=jax.ShapeDtypeStruct(field.shape, jnp.float32),
        compiler_params=compute_params(),
        cost_estimate=product_cost(maps, 6),
        name="first_product",
    )(maps, field, mask, table)


def second_call(maps, right, field, mask, table):
    blocks, _, x_count, block_rows, planes = field.shape
    out_shape = (blocks, 4 * x_count + 1, block_rows, planes)
    return pl.pallas_call(
        second_kernel,
        grid=grid_of(maps),
        in_specs=[
            maps_spec(maps),
            field_spec(field.shape),
            field_spec(field.shape),
            whole(mask.shape),
            whole(table.shape),
        ],
        out_specs=whole(out_shape),
        out_shape=jax.ShapeDtypeStruct(out_shape, jnp.float32),
        compiler_params=compute_params(),
        cost_estimate=product_cost(maps, 6),
        name="second_product",
    )(maps, right, field, mask, table)


def exchange(blocks, axis):
    return lax.all_to_all(blocks, axis, split_axis=0, concat_axis=0, tiled=True)


def x_first(cells, parts):
    rows, planes, width = cells.shape
    split = cells.reshape(rows, planes, 2, parts, width // (2 * parts))
    return jnp.transpose(split, (3, 2, 4, 0, 1))


def x_last(blocks):
    parts, _, x_count, rows, planes = blocks.shape
    return jnp.transpose(blocks, (3, 4, 1, 0, 2)).reshape(rows, planes, 2 * parts * x_count)


def combined(right, field, image, squares):
    right_right, right_field, field_field, field_image = (squares[i] for i in range(4))
    ratio = right_field / right_right
    alpha = right_right / (right_field + penalty * right_right)
    fresh = alpha * alpha * (field_field - ratio * right_field)
    weight = alpha * ratio + fresh / right_right
    mixed = weight * alpha
    curvature = (
        weight * weight * right_field - 2.0 * mixed * field_field + alpha * alpha * field_image
    ) + penalty * (
        weight * weight * right_right - 2.0 * mixed * right_field + alpha * alpha * field_field
    )
    second = fresh / curvature
    solution = (alpha + second * weight) * right - (second * alpha) * field
    residual = (
        (alpha * ratio - penalty * second * weight) * right
        - (alpha + second * weight - penalty * second * alpha) * field
        + (second * alpha) * image
    )
    return solution, residual


def body(
    prior_image,
    coil_maps,
    kspace,
    sampling,
    weight_first,
    bias_first,
    weight_middle,
    bias_middle,
    weight_last,
    bias_last,
):
    readout = prior_image.shape[2] // 2
    own_rows = prior_image.shape[0]
    planes = prior_image.shape[1]
    slabs = lax.axis_size("slab")
    coils = lax.axis_size("coil")
    devices = slabs * coils
    mask = jnp.transpose(
        lax.all_gather(sampling.astype(jnp.bfloat16), "slab", axis=0, tiled=True)
    ).astype(jnp.float32)
    spread = readout % devices == 0
    parts = devices if spread else coils

    def coils_to_x(blocks):
        tail = blocks.shape[1:]
        if spread:
            return exchange(blocks, axes).reshape((slabs, coils) + tail)
        blocks = exchange(blocks, "coil").reshape((slabs, coils // slabs) + tail)
        return exchange(blocks, "slab")

    maps = coils_to_x(x_first(coil_maps[0], parts))
    spectra = coils_to_x(x_first(kspace[0], parts))
    table = jnp.asarray(dft_table(sampling.shape[1], planes))
    denoised = denoise(
        prior_image, weight_first, bias_first, weight_middle, bias_middle, weight_last, bias_last
    )
    blocks = x_first(denoised, parts)
    if spread:
        x_count = blocks.shape[2]
        denoised = exchange(blocks, axes)
        right = adjoint_call(spectra, maps, mask, table, devices) + penalty * denoised
        field, right_back = lax.optimization_barrier(
            (first_call(maps, right, mask, table), exchange(right, axes))
        )
        right_rows = x_last(right_back)
        payload = exchange(second_call(maps, right, field, mask, table), axes)
        squares = jnp.sum(payload[:, -1], axis=(0, 2))
        image_rows, field_rows = (
            x_last(payload[:, first : first + 2 * x_count].reshape(blocks.shape))
            for first in (0, 2 * x_count)
        )
        return combined(right_rows, field_rows, image_rows, squares)

    tail = blocks.shape[1:3]

    def whole_rows(parts_in):
        moved = lax.all_gather(exchange(parts_in, "coil"), "slab", axis=0, tiled=True)
        return jnp.transpose(moved, (1, 2, 0, 3, 4)).reshape((1,) + tail + (-1, planes))

    def own_part(whole):
        rows = whole.shape[3] // slabs
        mine = lax.dynamic_slice_in_dim(whole, lax.axis_index("slab") * rows, rows, axis=3)
        split = jnp.transpose(mine.reshape(tail + (coils, own_rows, planes)), (2, 0, 1, 3, 4))
        return x_last(exchange(split, "coil"))

    adjoint = lax.psum(adjoint_call(spectra, maps, mask, table, 1), "slab")
    right = adjoint + penalty * whole_rows(blocks)
    field = lax.psum(first_call(maps, right, mask, table), "slab")
    image = lax.psum(first_call(maps, field, mask, table), "slab")
    squares = lax.psum(
        jnp.stack(
            [
                jnp.sum(right * right),
                jnp.sum(right * field),
                jnp.sum(field * field),
                jnp.sum(field * image),
            ]
        ),
        "coil",
    )
    return combined(own_part(right), own_part(field), own_part(image), squares)


def solution(mesh):
    placed = (
        P(("slab", "coil"), None, None),
        P("coil", "slab", None, None),
        P("coil", "slab", None, None),
        P("slab", None),
        P(),
        P(),
        P(),
        P(),
        P(),
        P(),
    )
    return jax.shard_map(
        body,
        mesh=mesh,
        in_specs=placed,
        out_specs=(P(("slab", "coil"), None, None), P(("slab", "coil"), None, None)),
        check_vma=False,
    )
```

```python
import functools
import math

import jax
import jax.numpy as jnp
import numpy as np
from jax import lax
from jax.experimental import pallas as pl
from jax.experimental.pallas import tpu as pltpu
from jax.sharding import PartitionSpec as P

CG_ITERS = 2


penalty = 0.5
axes = ("slab", "coil")


def with_halo(cells, width):
    rows = cells.shape[0]
    count = lax.axis_size("slab") * lax.axis_size("coil")
    above, below = [], []
    for hop in range(1, -(-width // rows) + 1):
        taken = min(width - (hop - 1) * rows, rows)
        ends = count - hop
        tail = lax.slice_in_dim(cells, rows - taken, rows, axis=0)
        head = lax.slice_in_dim(cells, 0, taken, axis=0)
        above.insert(0, lax.ppermute(tail, axes, [(i, i + hop) for i in range(ends)]))
        below.append(lax.ppermute(head, axes, [(i + hop, i) for i in range(ends)]))
    return jnp.concatenate(above + [cells] + below, axis=0)


def chunk_rows(rows):
    return max(size for size in range(1, 7) if rows % size == 0)


def chained(lhs_pieces):
    rows = lhs_pieces[0].shape[0] * lhs_pieces[0].shape[1]
    lhs = jnp.concatenate(lhs_pieces, axis=2)
    return lhs.reshape(rows, lhs.shape[2])


def denoise_kernel(
    group,
    first_ref,
    features_ref,
    prior_ref,
    weight_first_ref,
    bias_first_ref,
    weight_middle_ref,
    bias_middle_ref,
    weight_last_ref,
    bias_last_ref,
    out_ref,
    one_ref,
    two_ref,
    taps_ref,
    *turned_refs,
):
    own_rows, planes, width = prior_ref.shape
    edge = (one_ref.shape[2] - two_ref.shape[2]) // 2
    groups = two_ref.shape[2] // group
    first = first_ref[0]
    total = first_ref[1]
    one_ref[:, :, :edge] = jnp.zeros(one_ref.shape[:2] + (edge,), one_ref.dtype)
    one_ref[:, :, edge + two_ref.shape[2] :] = jnp.zeros(
        one_ref.shape[:2] + (edge,), one_ref.dtype
    )

    def store(ref, start, count, lanes, value, reach):
        value = jnp.maximum(value, 0.0).reshape(count, planes, group)
        for row in range(count):
            place = first + (start + row - reach)
            kept = jnp.where((place >= 0) & (place < total), value[row], 0.0)
            ref[start + row, :, lanes] = kept.astype(ref.dtype)

    def first_layer(index, carry):
        lanes = pl.ds(pl.multiple_of(index * group, group), group)
        placed = pl.ds(pl.multiple_of(edge + index * group, 128), group)
        count = chunk_rows(one_ref.shape[0])
        for start in range(0, one_ref.shape[0], count):
            lhs = chained([features_ref[start + tap : start + tap + count] for tap in range(3)])
            value = jnp.dot(lhs, weight_first_ref[:, lanes], preferred_element_type=jnp.float32)
            store(one_ref, start, count, placed, value + bias_first_ref[:, lanes], 2)
        return carry

    lax.fori_loop(0, groups, first_layer, 0)

    def shifted(value, plane, step):
        rows = value.shape[0]
        if step > 0:
            return jnp.where(plane == 0, 0.0, pltpu.roll(value, 1, 0))
        return jnp.where(plane == planes - 1, 0.0, pltpu.roll(value, rows - 1, 0))

    def plane_index(count, lanes):
        return lax.broadcasted_iota(jnp.int32, (count, planes, lanes), 1).reshape(
            count * planes, lanes
        )

    def middle_layer(index, carry):
        lanes = pl.ds(pl.multiple_of(index * group, group), group)
        window = pl.ds(pl.multiple_of(index * group, group), group + 2 * edge)
        count = chunk_rows(two_ref.shape[0])
        plane = plane_index(count, group)
        for start in range(0, two_ref.shape[0], count):
            lhs = chained([one_ref[start + tap : start + tap + count, :, window] for tap in range(3)])
            value = jnp.dot(lhs, weight_middle_ref[...], preferred_element_type=jnp.float32)
            value = (
                value[:, group : 2 * group]
                + shifted(value[:, :group], plane, 1)
                + shifted(value[:, 2 * group :], plane, -1)
            )
            store(two_ref, start, count, lanes, value + bias_middle_ref[:, lanes], 1)
        return carry

    lax.fori_loop(0, groups, middle_layer, 0)

    count = chunk_rows(two_ref.shape[0])

    def last_layer(index, carry):
        start = index * count
        lhs = two_ref[pl.ds(start, count)].reshape(count * planes, two_ref.shape[2])
        value = jnp.dot(lhs, weight_last_ref[...], preferred_element_type=jnp.float32)
        taps_ref[pl.ds(start, count)] = value.reshape(count, planes, value.shape[1])
        return carry

    lax.fori_loop(0, two_ref.shape[0] // count, last_layer, 0)
    plane = plane_index(1, width)

    def last_sum(row):
        sums = []
        for plane_tap in range(3):
            running = None
            for row_tap in range(3):
                lanes = pl.ds((row_tap * 3 + plane_tap) * width, width)
                value = taps_ref[row + row_tap, :, lanes]
                running = value if running is None else running + value
            sums.append(running)
        value = sums[1] + shifted(sums[0], plane, 1) + shifted(sums[2], plane, -1)
        return prior_ref[row] + (value + bias_last_ref[...])

    if not turned_refs:
        for row in range(own_rows):
            out_ref[row] = last_sum(row)
        return

    turned_ref = turned_refs[0]
    for row in range(own_rows):
        turned_ref[pl.ds(row, width, stride=own_rows), :] = jnp.transpose(last_sum(row))
    blocks, _, x_count = out_ref.shape[:3]
    for block in range(blocks):
        for part in range(2):
            for inner in range(x_count):
                place = part * (width // 2) + block * x_count + inner
                out_ref[block, part, inner] = turned_ref[place * own_rows : (place + 1) * own_rows]


def banded(tiles, inner, outer, offset):
    shape = jnp.broadcast_shapes(tiles[0].shape, inner.shape, outer.shape)
    result = jnp.zeros(shape, jnp.bfloat16)
    for tap in range(3):
        result = jnp.where(inner - outer + offset == tap, tiles[tap], result)
    return result


def denoise(
    parts, prior_image, weight_first, bias_first, weight_middle, bias_middle, weight_last, bias_last
):
    own_rows, planes, width = prior_image.shape
    turned = own_rows % 8 == 0
    out_shape = (parts, 2, width // (2 * parts), own_rows, planes) if turned else prior_image.shape
    readout = width // 2
    channels = weight_first.shape[3]
    span = readout * channels
    group = min(256, span)
    held = group // channels
    edge = 128
    reach = edge // channels
    window = group + 2 * edge

    def lane_place(count, inside):
        return jnp.arange(count * inside, dtype=jnp.int32) // inside

    tiles = jnp.transpose(weight_first, (2, 0, 1, 4, 3)).reshape(3, 18, 1, 1, channels)
    tiles = jnp.broadcast_to(tiles, (3, 18, 1, readout, channels)).reshape(3, 18, 1, span)
    first_table = banded(
        tiles,
        jnp.arange(readout, dtype=jnp.int32)[None, :, None],
        lane_place(readout, channels)[None, None, :],
        1,
    ).reshape(18 * readout, span)
    tiles = jnp.transpose(weight_middle, (2, 0, 4, 1, 3)).reshape(3, 3, 1, channels, 3, 1, channels)
    tiles = jnp.broadcast_to(tiles, (3, 3, 1, channels, 3, held, channels))
    tiles = tiles.reshape(3, 3, 1, channels, 3 * group)
    middle_table = banded(
        tiles,
        jnp.arange(window // channels, dtype=jnp.int32)[None, :, None, None] - reach,
        jnp.tile(lane_place(held, channels), 3)[None, None, None, :],
        1,
    ).reshape(3 * window, 3 * group)
    tiles = jnp.transpose(weight_last, (2, 4, 0, 1, 3)).reshape(3, 1, channels, 18, 1)
    tiles = jnp.broadcast_to(tiles, (3, 1, channels, 18, readout)).reshape(
        3, 1, channels, 18 * readout
    )
    last_table = banded(
        tiles,
        jnp.arange(readout, dtype=jnp.int32)[:, None, None],
        jnp.tile(jnp.arange(readout, dtype=jnp.int32), 18)[None, None, :],
        1,
    ).reshape(span, 18 * readout)

    features = with_halo(prior_image.astype(jnp.bfloat16), 3)
    rim = jnp.zeros_like(features[:, :1])
    features = jnp.concatenate(
        [
            jnp.concatenate([rim, features[:, :-1]], axis=1),
            features,
            jnp.concatenate([features[:, 1:], rim], axis=1),
        ],
        axis=2,
    )
    total = own_rows * lax.axis_size("slab") * lax.axis_size("coil")
    first = lax.axis_index(axes) * own_rows
    places = jnp.stack([first, jnp.asarray(total)]).astype(jnp.int32)
    vmem = pl.BlockSpec(memory_space=pltpu.VMEM)
    flops = 2 * own_rows * planes * (
        features.shape[2] * 3 * span * 3 // 2 + 9 * span * 512 * 5 // 4 + span * 18 * readout * 5 // 4
    )
    return pl.pallas_call(
        functools.partial(denoise_kernel, group),
        in_specs=[pl.BlockSpec(memory_space=pltpu.SMEM)] + [vmem] * 8,
        out_specs=vmem,
        out_shape=jax.ShapeDtypeStruct(out_shape, jnp.float32),
        scratch_shapes=[
            pltpu.VMEM((own_rows + 4, planes, span + 2 * edge), jnp.bfloat16),
            pltpu.VMEM((own_rows + 2, planes, span), jnp.bfloat16),
            pltpu.VMEM((own_rows + 2, planes, 18 * readout), jnp.float32),
        ]
        + [pltpu.VMEM((width * own_rows, planes), jnp.float32)] * turned,
        compiler_params=pltpu.CompilerParams(vmem_limit_bytes=56 * 1024 * 1024),
        cost_estimate=pl.CostEstimate(
            flops=int(flops), bytes_accessed=16 * 1024 * 1024, transcendentals=0
        ),
        name="denoise",
    )(
        places,
        features,
        prior_image,
        first_table,
        jnp.tile(bias_first, readout)[None, :],
        middle_table,
        jnp.tile(bias_middle, readout)[None, :],
        last_table,
        jnp.repeat(bias_last, readout)[None, :],
    )


def table_parts(table):
    high = table.astype(jnp.bfloat16)
    low = (table - high.astype(np.float64)).astype(jnp.bfloat16)
    return high, low


def dft_parts(length):
    positions = np.arange(length, dtype=np.int64)
    angles = (positions[:, None] * positions[None, :] % length) * (2.0 * math.pi / length)
    scale = 1.0 / math.sqrt(length)
    return np.cos(angles) * scale, np.sin(angles) * scale


def turn_block(length):
    cos_part, sin_part = dft_parts(length)
    return np.concatenate(
        [
            np.concatenate([cos_part, sin_part], axis=1),
            np.concatenate([-sin_part, cos_part], axis=1),
        ],
        axis=0,
    )


def dft_table(rows, planes):
    rows_high, rows_low = table_parts(turn_block(rows))
    planes_parts = np.concatenate(table_parts(turn_block(planes).T), axis=0)
    short = max(2 * rows - planes_parts.shape[0], 0)
    planes_parts = np.pad(planes_parts, ((0, short), (0, 0)))
    return np.concatenate([rows_high, rows_low, planes_parts], axis=1)


def value_parts(value):
    high = value.astype(jnp.bfloat16)
    low = (value - high.astype(jnp.float32)).astype(jnp.bfloat16)
    return high, low


def tables_of(ref, rows, planes):
    high, low = ref[:, : 2 * rows], ref[:, 2 * rows : 4 * rows]
    row_table = jnp.concatenate([high, low, high], axis=1)
    high, low = ref[: 2 * planes, 4 * rows :], ref[2 * planes : 4 * planes, 4 * rows :]
    return row_table, jnp.concatenate([high, low, high], axis=0)


def along_planes(fields, table):
    rows, planes = fields[0][0].shape
    stacked = jnp.concatenate([jnp.concatenate(field, axis=1) for field in fields], axis=0)
    high, low = value_parts(stacked)
    moved = jnp.dot(
        jnp.concatenate([high, high, low], axis=1), table, preferred_element_type=jnp.float32
    )
    return [
        (
            moved[index * rows : (index + 1) * rows, :planes],
            moved[index * rows : (index + 1) * rows, planes:],
        )
        for index in range(len(fields))
    ]


def side_by_side(fields):
    return jnp.concatenate(
        [jnp.concatenate([field[part] for field in fields], axis=1) for part in range(2)], axis=0
    )


def along_rows(table, fields):
    rows, planes = fields[0][0].shape
    high, low = value_parts(side_by_side(fields))
    moved = jnp.dot(
        table, jnp.concatenate([high, high, low], axis=0), preferred_element_type=jnp.float32
    )
    return apart(moved, len(fields))


def apart(moved, count):
    rows = moved.shape[0] // 2
    planes = moved.shape[1] // count
    return [
        (
            moved[:rows, index * planes : (index + 1) * planes],
            moved[rows:, index * planes : (index + 1) * planes],
        )
        for index in range(count)
    ]


def plane_of(ref, part):
    value = ref[:, part, 0]
    return value.reshape(value.shape[0] * value.shape[1], value.shape[2])


def coil_plane(ref, coil, part):
    value = ref[:, coil, part, 0]
    return value.reshape(value.shape[0] * value.shape[1], value.shape[2])


def map_of(ref, coil):
    return [coil_plane(ref, coil, part).astype(jnp.float32) for part in range(2)]


def image_sums(maps, fields):
    sums = None
    for (map_real, map_imag), (real, imag) in zip(maps, fields):
        terms = (map_real * real - map_imag * imag, -(map_real * imag + map_imag * real))
        sums = terms if sums is None else (sums[0] + terms[0], sums[1] + terms[1])
    return sums


def units_of(ref):
    count = ref.shape[1]
    held = 2 if count % 2 == 0 else 1
    return [tuple(range(first, first + held)) for first in range(0, count, held)]


def normal_sums(maps_ref, real, imag, mask, tables):
    row_table, plane_table = tables
    units = units_of(maps_ref)
    fields = []
    for unit in units:
        products = []
        for coil in unit:
            map_real, map_imag = map_of(maps_ref, coil)
            products.append(
                (map_real * real - map_imag * imag, map_real * imag + map_imag * real)
            )
        fields.append(along_planes(products, plane_table))
    fields = [along_rows(row_table, field) for field in fields]
    spectra = [
        [(real_part * mask, imag_part * -mask) for real_part, imag_part in field]
        for field in fields
    ]
    fields = [along_rows(row_table, spectrum) for spectrum in spectra]
    fields = [along_planes(field, plane_table) for field in fields]
    total = None
    for unit, field in zip(units, fields):
        sums = image_sums([map_of(maps_ref, coil) for coil in unit], field)
        total = sums if total is None else (total[0] + sums[0], total[1] + sums[1])
    return total


def adjoint_kernel(kspace_ref, maps_ref, mask_ref, table_ref, out_ref):
    mask = mask_ref[...]
    rows, planes = mask.shape
    row_table, plane_table = tables_of(table_ref, rows, planes)
    units = units_of(maps_ref)
    images = []
    for unit in units:
        spectra = []
        for coil in unit:
            real, imag = (
                jnp.transpose(coil_plane(kspace_ref, coil, part).astype(jnp.float32))
                for part in range(2)
            )
            spectra.append((real * mask, imag * -mask))
        spectrum = side_by_side(spectra).astype(jnp.bfloat16)
        moved = jnp.dot(
            row_table[:, : 4 * rows],
            jnp.concatenate([spectrum, spectrum], axis=0),
            preferred_element_type=jnp.float32,
        )
        images.append(apart(moved, len(unit)))
    images = [along_planes(image, plane_table) for image in images]
    total = None
    for unit, image in zip(units, images):
        sums = image_sums([map_of(maps_ref, coil) for coil in unit], image)
        total = sums if total is None else (total[0] + sums[0], total[1] + sums[1])
    shape = out_ref.shape[0], out_ref.shape[3], out_ref.shape[4]

    @pl.when(pl.program_id(1) == 0)
    def _():
        for part in range(2):
            out_ref[:, part, 0] = total[part].reshape(shape)

    @pl.when(pl.program_id(1) > 0)
    def _():
        for part in range(2):
            out_ref[:, part, 0] += total[part].reshape(shape)


def first_kernel(maps_ref, field_ref, mask_ref, table_ref, out_ref):
    mask = mask_ref[...]
    sums = normal_sums(
        maps_ref,
        plane_of(field_ref, 0),
        plane_of(field_ref, 1),
        mask,
        tables_of(table_ref, *mask.shape),
    )
    shape = out_ref.shape[0], out_ref.shape[3], out_ref.shape[4]

    @pl.when(pl.program_id(1) == 0)
    def _():
        for part in range(2):
            out_ref[:, part, 0] = sums[part].reshape(shape)

    @pl.when(pl.program_id(1) > 0)
    def _():
        for part in range(2):
            out_ref[:, part, 0] += sums[part].reshape(shape)


def second_kernel(maps_ref, right_ref, field_ref, mask_ref, table_ref, out_ref):
    x_index = pl.program_id(0)
    x_count = pl.num_programs(0)
    blocks, block_rows, planes = out_ref.shape[0], out_ref.shape[2], out_ref.shape[3]
    shape = blocks, block_rows, planes
    mask = mask_ref[...]
    sums = normal_sums(
        maps_ref,
        plane_of(field_ref, 0),
        plane_of(field_ref, 1),
        mask,
        tables_of(table_ref, *mask.shape),
    )

    @pl.when(pl.program_id(1) == 0)
    def _():
        for part in range(2):
            out_ref[:, part * x_count + x_index] = sums[part].reshape(shape)

    @pl.when(pl.program_id(1) > 0)
    def _():
        for part in range(2):
            out_ref[:, part * x_count + x_index] += sums[part].reshape(shape)

    @pl.when(pl.program_id(1) == pl.num_programs(1) - 1)
    def _():
        rights = [right_ref[:, part, 0] for part in range(2)]
        fields = [field_ref[:, part, 0] for part in range(2)]
        images = [out_ref[:, part * x_count + x_index] for part in range(2)]

        def lane_sums(left, other):
            product = left[0] * other[0] + left[1] * other[1]
            return jnp.sum(jnp.sum(product, axis=0), axis=0, keepdims=True)

        totals = jnp.concatenate(
            [
                lane_sums(rights, rights),
                lane_sums(rights, fields),
                lane_sums(fields, fields),
                lane_sums(fields, images),
                jnp.zeros((block_rows - 4, planes), jnp.float32),
            ],
            axis=0,
        )
        totals = jnp.broadcast_to(totals[None], shape)

        @pl.when(x_index == 0)
        def _():
            out_ref[:, 2 * x_count] = totals

        @pl.when(x_index > 0)
        def _():
            out_ref[:, 2 * x_count] += totals


def held_coils(count):
    return max(size for size in (1, 2, 4, 8) if count % size == 0)


def whole(shape):
    return pl.BlockSpec(shape, lambda x, c: (0,) * len(shape))


def maps_spec(maps):
    slabs, coils, _, _, slab_rows, planes = maps.shape
    return pl.BlockSpec(
        (slabs, held_coils(coils), 2, 1, slab_rows, planes), lambda x, c: (0, c, 0, x, 0, 0)
    )


def field_spec(shape):
    return pl.BlockSpec((shape[0], 2, 1) + shape[3:], lambda x, c: (0, 0, x, 0, 0))


def grid_of(maps):
    return maps.shape[3], maps.shape[1] // held_coils(maps.shape[1])


def compute_params():
    return pltpu.CompilerParams(
        dimension_semantics=("arbitrary", "arbitrary"), vmem_limit_bytes=48 * 1024 * 1024
    )


def product_cost(maps, passes):
    slabs, coils, _, x_count, slab_rows, planes = maps.shape
    rows = slabs * slab_rows
    per_plane = 2 * 2 * rows * planes * (2 * rows + 2 * planes)
    return pl.CostEstimate(
        flops=int(coils * x_count * per_plane * passes),
        bytes_accessed=int(2 * maps.size),
        transcendentals=0,
    )


def adjoint_call(spectra, maps, mask, table, blocks):
    rows, planes = mask.shape
    shape = (blocks, 2, maps.shape[3], rows // blocks, planes)
    return pl.pallas_call(
        adjoint_kernel,
        grid=grid_of(maps),
        in_specs=[maps_spec(spectra), maps_spec(maps), whole(mask.shape), whole(table.shape)],
        out_specs=field_spec(shape),
        out_shape=jax.ShapeDtypeStruct(shape, jnp.float32),
        compiler_params=compute_params(),
        cost_estimate=product_cost(maps, 3),
        name="adjoint",
    )(spectra, maps, mask, table)


def first_call(maps, field, mask, table):
    return pl.pallas_call(
        first_kernel,
        grid=grid_of(maps),
        in_specs=[maps_spec(maps), field_spec(field.shape), whole(mask.shape), whole(table.shape)],
        out_specs=field_spec(field.shape),
        out_shape=jax.ShapeDtypeStruct(field.shape, jnp.float32),
        compiler_params=compute_params(),
        cost_estimate=product_cost(maps, 6),
        name="first_product",
    )(maps, field, mask, table)


def second_call(maps, right, field, mask, table):
    blocks, _, x_count, block_rows, planes = field.shape
    out_shape = (blocks, 2 * x_count + 1, block_rows, planes)
    return pl.pallas_call(
        second_kernel,
        grid=grid_of(maps),
        in_specs=[
            maps_spec(maps),
            field_spec(field.shape),
            field_spec(field.shape),
            whole(mask.shape),
            whole(table.shape),
        ],
        out_specs=whole(out_shape),
        out_shape=jax.ShapeDtypeStruct(out_shape, jnp.float32),
        compiler_params=compute_params(),
        cost_estimate=product_cost(maps, 6),
        name="second_product",
    )(maps, right, field, mask, table)


def exchange(blocks, axis):
    return lax.all_to_all(blocks, axis, split_axis=0, concat_axis=0, tiled=True)


def x_first(cells, parts):
    rows, planes, width = cells.shape
    split = cells.reshape(rows, planes, 2, parts, width // (2 * parts))
    return jnp.transpose(split, (3, 2, 4, 0, 1))


def x_last(blocks):
    parts, _, x_count, rows, planes = blocks.shape
    return jnp.transpose(blocks, (3, 4, 1, 0, 2)).reshape(rows, planes, 2 * parts * x_count)


def factors(right_right, right_field, field_field, field_image):
    ratio = right_field / right_right
    alpha = right_right / (right_field + penalty * right_right)
    fresh = alpha * alpha * (field_field - ratio * right_field)
    weight = alpha * ratio + fresh / right_right
    mixed = weight * alpha
    curvature = (
        weight * weight * right_field - 2.0 * mixed * field_field + alpha * alpha * field_image
    ) + penalty * (
        weight * weight * right_right - 2.0 * mixed * right_field + alpha * alpha * field_field
    )
    second = fresh / curvature
    moved = alpha + second * weight
    bent = second * alpha
    return (moved, -bent), (alpha * ratio - penalty * second * weight, penalty * bent - moved, bent)


def finish_kernel(right_ref, field_ref, image_ref, solution_ref, residual_ref, rows_ref):
    blocks, _, x_count, rows, planes = right_ref.shape
    readout = blocks * x_count
    totals = jnp.sum(jnp.sum(image_ref[:, 2 * x_count], axis=0), axis=1, keepdims=True)
    found = factors(*(totals[index : index + 1] for index in range(4)))
    for out_ref, scales in zip((solution_ref, residual_ref), found):
        scales = [jnp.broadcast_to(scale, (rows, planes))[None] for scale in scales]
        for part in range(2):
            for inner in range(x_count):
                value = scales[0] * right_ref[:, part, inner] + scales[1] * field_ref[:, part, inner]
                if len(scales) > 2:
                    value = value + scales[2] * image_ref[:, part * x_count + inner]
                for block in range(blocks):
                    place = part * readout + block * x_count + inner
                    rows_ref[place * rows : (place + 1) * rows] = value[block]
        for row in range(rows):
            out_ref[row] = jnp.transpose(rows_ref[pl.ds(row, 2 * readout, stride=rows), :])


def finish_call(right, field, image):
    blocks, _, x_count, rows, planes = right.shape
    shape = (rows, planes, 2 * blocks * x_count)
    vmem = pl.BlockSpec(memory_space=pltpu.VMEM)
    return pl.pallas_call(
        finish_kernel,
        in_specs=[vmem] * 3,
        out_specs=[vmem] * 2,
        out_shape=[jax.ShapeDtypeStruct(shape, jnp.float32)] * 2,
        scratch_shapes=[pltpu.VMEM((2 * blocks * x_count * rows, planes), jnp.float32)],
        compiler_params=pltpu.CompilerParams(vmem_limit_bytes=32 * 1024 * 1024),
        cost_estimate=pl.CostEstimate(
            flops=8 * right.size, bytes_accessed=20 * right.size, transcendentals=0
        ),
        name="finish",
    )(right, field, image)


def body(
    prior_image,
    coil_maps,
    kspace,
    sampling,
    weight_first,
    bias_first,
    weight_middle,
    bias_middle,
    weight_last,
    bias_last,
):
    readout = prior_image.shape[2] // 2
    own_rows = prior_image.shape[0]
    planes = prior_image.shape[1]
    slabs = lax.axis_size("slab")
    coils = lax.axis_size("coil")
    devices = slabs * coils
    mask = jnp.transpose(
        lax.all_gather(sampling.astype(jnp.bfloat16), "slab", axis=0, tiled=True)
    ).astype(jnp.float32)
    spread = readout % devices == 0 and own_rows % 8 == 0
    parts = devices if spread else coils

    def coils_to_x(blocks):
        tail = blocks.shape[1:]
        if spread:
            return exchange(blocks, axes).reshape((slabs, coils) + tail)
        blocks = exchange(blocks, "coil").reshape((slabs, coils // slabs) + tail)
        return exchange(blocks, "slab")

    maps = coils_to_x(x_first(coil_maps[0], parts))
    spectra = coils_to_x(x_first(kspace[0], parts))
    table = jnp.asarray(dft_table(sampling.shape[1], planes))
    blocks = denoise(
        parts,
        prior_image,
        weight_first,
        bias_first,
        weight_middle,
        bias_middle,
        weight_last,
        bias_last,
    )
    if blocks.ndim == 3:
        blocks = x_first(blocks, parts)
    if spread:
        denoised = exchange(blocks, axes)
        right = adjoint_call(spectra, maps, mask, table, devices) + penalty * denoised
        field, right_back = lax.optimization_barrier(
            (first_call(maps, right, mask, table), exchange(right, axes))
        )
        payload, field_back = lax.optimization_barrier(
            (second_call(maps, right, field, mask, table), exchange(field, axes))
        )
        return tuple(finish_call(right_back, field_back, exchange(payload, axes)))

    tail = blocks.shape[1:3]

    def whole_rows(parts_in):
        moved = lax.all_gather(exchange(parts_in, "coil"), "slab", axis=0, tiled=True)
        return jnp.transpose(moved, (1, 2, 0, 3, 4)).reshape((1,) + tail + (-1, planes))

    def own_part(whole):
        rows = whole.shape[3] // slabs
        mine = lax.dynamic_slice_in_dim(whole, lax.axis_index("slab") * rows, rows, axis=3)
        split = jnp.transpose(mine.reshape(tail + (coils, own_rows, planes)), (2, 0, 1, 3, 4))
        return x_last(exchange(split, "coil"))

    adjoint = lax.psum(adjoint_call(spectra, maps, mask, table, 1), "slab")
    right = adjoint + penalty * whole_rows(blocks)
    field = lax.psum(first_call(maps, right, mask, table), "slab")
    image = lax.psum(first_call(maps, field, mask, table), "slab")
    squares = lax.psum(
        jnp.stack(
            [
                jnp.sum(right * right),
                jnp.sum(right * field),
                jnp.sum(field * field),
                jnp.sum(field * image),
            ]
        ),
        "coil",
    )
    scales, others = factors(*(squares[index] for index in range(4)))
    right, field, image = own_part(right), own_part(field), own_part(image)
    return (
        scales[0] * right + scales[1] * field,
        others[0] * right + others[1] * field + others[2] * image,
    )


def solution(mesh):
    placed = (
        P(("slab", "coil"), None, None),
        P("coil", "slab", None, None),
        P("coil", "slab", None, None),
        P("slab", None),
        P(),
        P(),
        P(),
        P(),
        P(),
        P(),
    )
    return jax.shard_map(
        body,
        mesh=mesh,
        in_specs=placed,
        out_specs=(P(("slab", "coil"), None, None), P(("slab", "coil"), None, None)),
        check_vma=False,
    )
```

```python
import functools
import math

import jax
import jax.numpy as jnp
import numpy as np
from jax import lax
from jax.experimental import pallas as pl
from jax.experimental.pallas import tpu as pltpu
from jax.sharding import PartitionSpec as P

CG_ITERS = 2


penalty = 0.5
axes = ("slab", "coil")


def with_halo(cells, width):
    rows = cells.shape[0]
    count = lax.axis_size("slab") * lax.axis_size("coil")
    above, below = [], []
    for hop in range(1, -(-width // rows) + 1):
        taken = min(width - (hop - 1) * rows, rows)
        ends = count - hop
        tail = lax.slice_in_dim(cells, rows - taken, rows, axis=0)
        head = lax.slice_in_dim(cells, 0, taken, axis=0)
        above.insert(0, lax.ppermute(tail, axes, [(i, i + hop) for i in range(ends)]))
        below.append(lax.ppermute(head, axes, [(i + hop, i) for i in range(ends)]))
    return jnp.concatenate(above + [cells] + below, axis=0)


def chunk_rows(rows):
    return max(size for size in range(1, 7) if rows % size == 0)


def chained(lhs_pieces):
    rows = lhs_pieces[0].shape[0] * lhs_pieces[0].shape[1]
    lhs = jnp.concatenate(lhs_pieces, axis=2)
    return lhs.reshape(rows, lhs.shape[2])


def denoise_kernel(
    group,
    first_ref,
    features_ref,
    prior_ref,
    weight_first_ref,
    bias_first_ref,
    weight_middle_ref,
    bias_middle_ref,
    weight_last_ref,
    bias_last_ref,
    out_ref,
    one_ref,
    two_ref,
    taps_ref,
    *turned_refs,
):
    own_rows, planes, width = prior_ref.shape
    edge = (one_ref.shape[2] - two_ref.shape[2]) // 2
    groups = two_ref.shape[2] // group
    first = first_ref[0]
    total = first_ref[1]
    one_ref[:, :, :edge] = jnp.zeros(one_ref.shape[:2] + (edge,), one_ref.dtype)
    one_ref[:, :, edge + two_ref.shape[2] :] = jnp.zeros(
        one_ref.shape[:2] + (edge,), one_ref.dtype
    )

    def store(ref, start, count, lanes, value, reach):
        value = jnp.maximum(value, 0.0).reshape(count, planes, group)
        for row in range(count):
            place = first + (start + row - reach)
            kept = jnp.where((place >= 0) & (place < total), value[row], 0.0)
            ref[start + row, :, lanes] = kept.astype(ref.dtype)

    def first_layer(index, carry):
        lanes = pl.ds(pl.multiple_of(index * group, group), group)
        placed = pl.ds(pl.multiple_of(edge + index * group, 128), group)
        count = chunk_rows(one_ref.shape[0])
        for start in range(0, one_ref.shape[0], count):
            lhs = chained([features_ref[start + tap : start + tap + count] for tap in range(3)])
            value = jnp.dot(lhs, weight_first_ref[:, lanes], preferred_element_type=jnp.float32)
            store(one_ref, start, count, placed, value + bias_first_ref[:, lanes], 2)
        return carry

    lax.fori_loop(0, groups, first_layer, 0)

    def shifted(value, plane, step):
        rows = value.shape[0]
        if step > 0:
            return jnp.where(plane == 0, 0.0, pltpu.roll(value, 1, 0))
        return jnp.where(plane == planes - 1, 0.0, pltpu.roll(value, rows - 1, 0))

    def plane_index(count, lanes):
        return lax.broadcasted_iota(jnp.int32, (count, planes, lanes), 1).reshape(
            count * planes, lanes
        )

    def middle_layer(index, carry):
        lanes = pl.ds(pl.multiple_of(index * group, group), group)
        window = pl.ds(pl.multiple_of(index * group, group), group + 2 * edge)
        count = chunk_rows(two_ref.shape[0])
        plane = plane_index(count, group)
        for start in range(0, two_ref.shape[0], count):
            lhs = chained([one_ref[start + tap : start + tap + count, :, window] for tap in range(3)])
            value = jnp.dot(lhs, weight_middle_ref[...], preferred_element_type=jnp.float32)
            value = (
                value[:, group : 2 * group]
                + shifted(value[:, :group], plane, 1)
                + shifted(value[:, 2 * group :], plane, -1)
            )
            store(two_ref, start, count, lanes, value + bias_middle_ref[:, lanes], 1)
        return carry

    lax.fori_loop(0, groups, middle_layer, 0)

    count = chunk_rows(two_ref.shape[0])

    def last_layer(index, carry):
        start = index * count
        lhs = two_ref[pl.ds(start, count)].reshape(count * planes, two_ref.shape[2])
        value = jnp.dot(lhs, weight_last_ref[...], preferred_element_type=jnp.float32)
        taps_ref[pl.ds(start, count)] = value.reshape(count, planes, value.shape[1])
        return carry

    lax.fori_loop(0, two_ref.shape[0] // count, last_layer, 0)
    plane = plane_index(1, width)

    def last_sum(row):
        sums = []
        for plane_tap in range(3):
            running = None
            for row_tap in range(3):
                lanes = pl.ds((row_tap * 3 + plane_tap) * width, width)
                value = taps_ref[row + row_tap, :, lanes]
                running = value if running is None else running + value
            sums.append(running)
        value = sums[1] + shifted(sums[0], plane, 1) + shifted(sums[2], plane, -1)
        return prior_ref[row] + (value + bias_last_ref[...])

    if not turned_refs:
        for row in range(own_rows):
            out_ref[row] = last_sum(row)
        return

    turned_ref = turned_refs[0]
    for row in range(own_rows):
        turned_ref[pl.ds(row, width, stride=own_rows), :] = jnp.transpose(last_sum(row))
    blocks, _, x_count = out_ref.shape[:3]
    for block in range(blocks):
        for part in range(2):
            for inner in range(x_count):
                place = part * (width // 2) + block * x_count + inner
                out_ref[block, part, inner] = turned_ref[place * own_rows : (place + 1) * own_rows]


def banded(tiles, inner, outer, offset):
    shape = jnp.broadcast_shapes(tiles[0].shape, inner.shape, outer.shape)
    result = jnp.zeros(shape, jnp.bfloat16)
    for tap in range(3):
        result = jnp.where(inner - outer + offset == tap, tiles[tap], result)
    return result


def denoise(
    parts,
    features,
    prior_image,
    weight_first,
    bias_first,
    weight_middle,
    bias_middle,
    weight_last,
    bias_last,
):
    own_rows, planes, width = prior_image.shape
    turned = own_rows % 8 == 0
    out_shape = (parts, 2, width // (2 * parts), own_rows, planes) if turned else prior_image.shape
    readout = width // 2
    channels = weight_first.shape[3]
    span = readout * channels
    group = min(256, span)
    held = group // channels
    edge = 128
    reach = edge // channels
    window = group + 2 * edge

    def lane_place(count, inside):
        return jnp.arange(count * inside, dtype=jnp.int32) // inside

    tiles = jnp.transpose(weight_first, (2, 0, 1, 4, 3)).reshape(3, 18, 1, 1, channels)
    tiles = jnp.broadcast_to(tiles, (3, 18, 1, readout, channels)).reshape(3, 18, 1, span)
    first_table = banded(
        tiles,
        jnp.arange(readout, dtype=jnp.int32)[None, :, None],
        lane_place(readout, channels)[None, None, :],
        1,
    ).reshape(18 * readout, span)
    tiles = jnp.transpose(weight_middle, (2, 0, 4, 1, 3)).reshape(3, 3, 1, channels, 3, 1, channels)
    tiles = jnp.broadcast_to(tiles, (3, 3, 1, channels, 3, held, channels))
    tiles = tiles.reshape(3, 3, 1, channels, 3 * group)
    middle_table = banded(
        tiles,
        jnp.arange(window // channels, dtype=jnp.int32)[None, :, None, None] - reach,
        jnp.tile(lane_place(held, channels), 3)[None, None, None, :],
        1,
    ).reshape(3 * window, 3 * group)
    tiles = jnp.transpose(weight_last, (2, 4, 0, 1, 3)).reshape(3, 1, channels, 18, 1)
    tiles = jnp.broadcast_to(tiles, (3, 1, channels, 18, readout)).reshape(
        3, 1, channels, 18 * readout
    )
    last_table = banded(
        tiles,
        jnp.arange(readout, dtype=jnp.int32)[:, None, None],
        jnp.tile(jnp.arange(readout, dtype=jnp.int32), 18)[None, None, :],
        1,
    ).reshape(span, 18 * readout)

    rim = jnp.zeros_like(features[:, :1])
    features = jnp.concatenate(
        [
            jnp.concatenate([rim, features[:, :-1]], axis=1),
            features,
            jnp.concatenate([features[:, 1:], rim], axis=1),
        ],
        axis=2,
    )
    total = own_rows * lax.axis_size("slab") * lax.axis_size("coil")
    first = lax.axis_index(axes) * own_rows
    places = jnp.stack([first, jnp.asarray(total)]).astype(jnp.int32)
    vmem = pl.BlockSpec(memory_space=pltpu.VMEM)
    flops = 2 * own_rows * planes * (
        features.shape[2] * 3 * span * 3 // 2 + 9 * span * 512 * 5 // 4 + span * 18 * readout * 5 // 4
    )
    return pl.pallas_call(
        functools.partial(denoise_kernel, group),
        in_specs=[pl.BlockSpec(memory_space=pltpu.SMEM)] + [vmem] * 8,
        out_specs=vmem,
        out_shape=jax.ShapeDtypeStruct(out_shape, jnp.float32),
        scratch_shapes=[
            pltpu.VMEM((own_rows + 4, planes, span + 2 * edge), jnp.bfloat16),
            pltpu.VMEM((own_rows + 2, planes, span), jnp.bfloat16),
            pltpu.VMEM((own_rows + 2, planes, 18 * readout), jnp.float32),
        ]
        + [pltpu.VMEM((width * own_rows, planes), jnp.float32)] * turned,
        compiler_params=pltpu.CompilerParams(vmem_limit_bytes=56 * 1024 * 1024),
        cost_estimate=pl.CostEstimate(
            flops=int(flops), bytes_accessed=16 * 1024 * 1024, transcendentals=0
        ),
        name="denoise",
    )(
        places,
        features,
        prior_image,
        first_table,
        jnp.tile(bias_first, readout)[None, :],
        middle_table,
        jnp.tile(bias_middle, readout)[None, :],
        last_table,
        jnp.repeat(bias_last, readout)[None, :],
    )


def table_parts(table):
    high = table.astype(jnp.bfloat16)
    low = (table - high.astype(np.float64)).astype(jnp.bfloat16)
    return high, low


def dft_parts(length):
    positions = np.arange(length, dtype=np.int64)
    angles = (positions[:, None] * positions[None, :] % length) * (2.0 * math.pi / length)
    scale = 1.0 / math.sqrt(length)
    return np.cos(angles) * scale, np.sin(angles) * scale


def turn_block(length):
    cos_part, sin_part = dft_parts(length)
    return np.concatenate(
        [
            np.concatenate([cos_part, sin_part], axis=1),
            np.concatenate([-sin_part, cos_part], axis=1),
        ],
        axis=0,
    )


def dft_table(rows, planes):
    rows_high, rows_low = table_parts(turn_block(rows))
    planes_parts = np.concatenate(table_parts(turn_block(planes).T), axis=0)
    short = max(2 * rows - planes_parts.shape[0], 0)
    planes_parts = np.pad(planes_parts, ((0, short), (0, 0)))
    return np.concatenate([rows_high, rows_low, planes_parts], axis=1)


def value_parts(value):
    high = value.astype(jnp.bfloat16)
    low = (value - high.astype(jnp.float32)).astype(jnp.bfloat16)
    return high, low


def tables_of(ref, rows, planes):
    high, low = ref[:, : 2 * rows], ref[:, 2 * rows : 4 * rows]
    row_table = jnp.concatenate([high, low, high], axis=1)
    high, low = ref[: 2 * planes, 4 * rows :], ref[2 * planes : 4 * planes, 4 * rows :]
    return row_table, jnp.concatenate([high, low, high], axis=0)


def along_planes(fields, table):
    rows, planes = fields[0][0].shape
    stacked = jnp.concatenate([jnp.concatenate(field, axis=1) for field in fields], axis=0)
    high, low = value_parts(stacked)
    moved = jnp.dot(
        jnp.concatenate([high, high, low], axis=1), table, preferred_element_type=jnp.float32
    )
    return [
        (
            moved[index * rows : (index + 1) * rows, :planes],
            moved[index * rows : (index + 1) * rows, planes:],
        )
        for index in range(len(fields))
    ]


def side_by_side(fields):
    return jnp.concatenate(
        [jnp.concatenate([field[part] for field in fields], axis=1) for part in range(2)], axis=0
    )


def along_rows(table, fields):
    rows, planes = fields[0][0].shape
    high, low = value_parts(side_by_side(fields))
    moved = jnp.dot(
        table, jnp.concatenate([high, high, low], axis=0), preferred_element_type=jnp.float32
    )
    return apart(moved, len(fields))


def apart(moved, count):
    rows = moved.shape[0] // 2
    planes = moved.shape[1] // count
    return [
        (
            moved[:rows, index * planes : (index + 1) * planes],
            moved[rows:, index * planes : (index + 1) * planes],
        )
        for index in range(count)
    ]


def plane_of(ref, part):
    value = ref[:, part, 0]
    return value.reshape(value.shape[0] * value.shape[1], value.shape[2])


def coil_plane(ref, coil):
    value = ref[:, coil, 0]
    return value.reshape(value.shape[0] * value.shape[1], value.shape[2])


def map_of(refs, coil):
    return [coil_plane(ref, coil).astype(jnp.float32) for ref in refs]


def spectrum_plane(ref, coil, rows):
    value = ref[:, coil, 0]
    slabs, held, lanes = value.shape
    planes = held * lanes // rows
    pieces = [
        value[:, first : first + planes].reshape(slabs * planes, lanes)
        for first in range(0, held, planes)
    ]
    return jnp.concatenate(pieces, axis=1)


def image_sums(maps, fields):
    sums = None
    for (map_real, map_imag), (real, imag) in zip(maps, fields):
        terms = (map_real * real - map_imag * imag, -(map_real * imag + map_imag * real))
        sums = terms if sums is None else (sums[0] + terms[0], sums[1] + terms[1])
    return sums


def units_of(refs):
    count = refs[0].shape[1]
    held = 2 if count % 2 == 0 else 1
    return [tuple(range(first, first + held)) for first in range(0, count, held)]


def normal_sums(maps_refs, real, imag, mask, tables):
    row_table, plane_table = tables
    units = units_of(maps_refs)
    fields = []
    for unit in units:
        products = []
        for coil in unit:
            map_real, map_imag = map_of(maps_refs, coil)
            products.append(
                (map_real * real - map_imag * imag, map_real * imag + map_imag * real)
            )
        fields.append(along_planes(products, plane_table))
    fields = [along_rows(row_table, field) for field in fields]
    spectra = [
        [(real_part * mask, imag_part * -mask) for real_part, imag_part in field]
        for field in fields
    ]
    fields = [along_rows(row_table, spectrum) for spectrum in spectra]
    fields = [along_planes(field, plane_table) for field in fields]
    total = None
    for unit, field in zip(units, fields):
        sums = image_sums([map_of(maps_refs, coil) for coil in unit], field)
        total = sums if total is None else (total[0] + sums[0], total[1] + sums[1])
    return total


def accumulate(out_ref, values, places):
    shape = out_ref.shape[0], out_ref.shape[-2], out_ref.shape[-1]

    @pl.when(pl.program_id(1) == 0)
    def _():
        for value, place in zip(values, places):
            out_ref[(slice(None),) + place] = value.reshape(shape)

    @pl.when(pl.program_id(1) > 0)
    def _():
        for value, place in zip(values, places):
            out_ref[(slice(None),) + place] += value.reshape(shape)


def adjoint_kernel(
    spectra_real_ref, spectra_imag_ref, maps_real_ref, maps_imag_ref, mask_ref, table_ref, out_ref
):
    maps_refs = maps_real_ref, maps_imag_ref
    mask = mask_ref[...]
    rows, planes = mask.shape
    row_table, plane_table = tables_of(table_ref, rows, planes)
    units = units_of(maps_refs)
    images = []
    for unit in units:
        spectra = []
        for coil in unit:
            real, imag = (
                jnp.transpose(spectrum_plane(ref, coil, rows).astype(jnp.float32))
                for ref in (spectra_real_ref, spectra_imag_ref)
            )
            spectra.append((real * mask, imag * -mask))
        spectrum = side_by_side(spectra).astype(jnp.bfloat16)
        moved = jnp.dot(
            row_table[:, : 4 * rows],
            jnp.concatenate([spectrum, spectrum], axis=0),
            preferred_element_type=jnp.float32,
        )
        images.append(apart(moved, len(unit)))
    images = [along_planes(image, plane_table) for image in images]
    total = None
    for unit, image in zip(units, images):
        sums = image_sums([map_of(maps_refs, coil) for coil in unit], image)
        total = sums if total is None else (total[0] + sums[0], total[1] + sums[1])
    accumulate(out_ref, total, ((0, 0), (1, 0)))


def lane_sums(left, other):
    product = left[0] * other[0] + left[1] * other[1]
    return jnp.sum(jnp.sum(product, axis=0), axis=0, keepdims=True)


def first_kernel(
    maps_real_ref, maps_imag_ref, adjoint_ref, denoised_ref, mask_ref, table_ref, out_ref, total_ref
):
    mask = mask_ref[...]
    rights = [
        plane_of(adjoint_ref, part) + penalty * plane_of(denoised_ref, part) for part in range(2)
    ]
    sums = normal_sums(
        (maps_real_ref, maps_imag_ref), *rights, mask, tables_of(table_ref, *mask.shape)
    )
    accumulate(out_ref, sums, ((0, 0), (1, 0)))

    @pl.when(pl.program_id(1) == pl.num_programs(1) - 1)
    def _():
        shape = out_ref.shape[0], out_ref.shape[3], out_ref.shape[4]
        sides = [right.reshape(shape) for right in rights]
        fields = [out_ref[:, part, 0] for part in range(2)]
        totals = jnp.concatenate(
            [
                lane_sums(sides, sides),
                lane_sums(sides, fields),
                lane_sums(fields, fields),
                jnp.zeros((total_ref.shape[0] - 3, total_ref.shape[1]), jnp.float32),
            ],
            axis=0,
        )

        @pl.when(pl.program_id(0) == 0)
        def _():
            total_ref[...] = totals

        @pl.when(pl.program_id(0) > 0)
        def _():
            total_ref[...] += totals


def second_kernel(
    maps_real_ref, maps_imag_ref, field_ref, total_ref, mask_ref, table_ref, out_ref
):
    x_index = pl.program_id(0)
    x_count = pl.num_programs(0)
    blocks, block_rows, planes = out_ref.shape[0], out_ref.shape[2], out_ref.shape[3]
    mask = mask_ref[...]
    sums = normal_sums(
        (maps_real_ref, maps_imag_ref),
        plane_of(field_ref, 0),
        plane_of(field_ref, 1),
        mask,
        tables_of(table_ref, *mask.shape),
    )
    places = [(part * x_count + x_index,) for part in range(2)]
    accumulate(out_ref, sums, places)

    @pl.when(pl.program_id(1) == pl.num_programs(1) - 1)
    def _():
        fields = [field_ref[:, part, 0] for part in range(2)]
        images = [out_ref[(slice(None),) + place] for place in places]
        totals = jnp.concatenate(
            [
                jnp.zeros((3, planes), jnp.float32),
                lane_sums(fields, images),
                jnp.zeros((block_rows - 4, planes), jnp.float32),
            ],
            axis=0,
        )

        @pl.when(x_index == 0)
        def _():
            out_ref[:, 2 * x_count] = jnp.broadcast_to(
                (total_ref[...] + totals)[None], (blocks, block_rows, planes)
            )

        @pl.when(x_index > 0)
        def _():
            out_ref[:, 2 * x_count] += totals[None]


def held_coils(count):
    return max(size for size in (1, 2, 4, 8) if count % size == 0)


def whole(shape):
    return pl.BlockSpec(shape, lambda x, c: (0,) * len(shape))


def coils_spec(planes):
    values, first = planes
    slabs, coils, _, rows, lanes = values.shape
    return pl.BlockSpec(
        (slabs, held_coils(coils), 1, rows, lanes), lambda x, c: (0, c, first + x, 0, 0)
    )


def field_spec(shape):
    return pl.BlockSpec((shape[0], 2, 1) + shape[3:], lambda x, c: (0, 0, x, 0, 0))


def compute_params():
    return pltpu.CompilerParams(
        dimension_semantics=("arbitrary", "arbitrary"), vmem_limit_bytes=48 * 1024 * 1024
    )


def product_call(kernel, name, x_count, coil_planes, fields, extras, constants, outs, passes):
    coils = coil_planes[0][0].shape[1]
    mask = constants[0]
    rows, planes = mask.shape
    flops = 2 * 2 * rows * planes * (2 * rows + 2 * planes) * coils * x_count * passes
    values = [planes_of[0] for planes_of in coil_planes] + fields + extras + constants
    return pl.pallas_call(
        kernel,
        grid=(x_count, coils // held_coils(coils)),
        in_specs=[coils_spec(planes_of) for planes_of in coil_planes]
        + [field_spec(field.shape) for field in fields]
        + [whole(value.shape) for value in extras + constants],
        out_specs=[spec for spec, _ in outs],
        out_shape=[jax.ShapeDtypeStruct(shape, jnp.float32) for _, shape in outs],
        compiler_params=compute_params(),
        cost_estimate=pl.CostEstimate(
            flops=int(flops), bytes_accessed=8 * 1024 * 1024, transcendentals=0
        ),
        name=name,
    )(*values)


def adjoint_call(spectra, maps, constants, x_count, blocks):
    rows, planes = constants[0].shape
    shape = (blocks, 2, x_count, rows // blocks, planes)
    outs = [(field_spec(shape), shape)]
    return product_call(
        adjoint_kernel, "adjoint", x_count, spectra + maps, [], [], constants, outs, 3
    )[0]


def first_call(maps, adjoint, denoised, constants):
    shape = adjoint.shape
    totals = (8, shape[4])
    outs = [(field_spec(shape), shape), (whole(totals), totals)]
    return product_call(
        first_kernel, "first_product", shape[2], maps, [adjoint, denoised], [], constants, outs, 6
    )


def second_call(maps, field, totals, constants):
    blocks, _, x_count, block_rows, planes = field.shape
    shape = (blocks, 2 * x_count + 1, block_rows, planes)
    outs = [(whole(shape), shape)]
    return product_call(
        second_kernel, "second_product", x_count, maps, [field], [totals], constants, outs, 6
    )[0]


def exchange(blocks, axis):
    return lax.all_to_all(blocks, axis, split_axis=0, concat_axis=0, tiled=True)


def x_first(cells, parts, count=2):
    rows, planes, width = cells.shape
    split = cells.reshape(rows, planes, count, parts, width // (count * parts))
    return jnp.transpose(split, (3, 2, 4, 0, 1))


def x_last(blocks):
    parts, _, x_count, rows, planes = blocks.shape
    return jnp.transpose(blocks, (3, 4, 1, 0, 2)).reshape(rows, planes, 2 * parts * x_count)


def factors(right_right, right_field, field_field, field_image):
    ratio = right_field / right_right
    alpha = right_right / (right_field + penalty * right_right)
    fresh = alpha * alpha * (field_field - ratio * right_field)
    weight = alpha * ratio + fresh / right_right
    mixed = weight * alpha
    curvature = (
        weight * weight * right_field - 2.0 * mixed * field_field + alpha * alpha * field_image
    ) + penalty * (
        weight * weight * right_right - 2.0 * mixed * right_field + alpha * alpha * field_field
    )
    second = fresh / curvature
    moved = alpha + second * weight
    bent = second * alpha
    return (moved, -bent), (alpha * ratio - penalty * second * weight, penalty * bent - moved, bent)


def finish_kernel(
    adjoint_ref, denoised_ref, field_ref, image_ref, solution_ref, residual_ref, rows_ref
):
    blocks, _, x_count, rows, planes = adjoint_ref.shape
    readout = blocks * x_count
    totals = jnp.sum(jnp.sum(image_ref[:, 2 * x_count], axis=0), axis=1, keepdims=True)
    found = factors(*(totals[index : index + 1] for index in range(4)))
    for out_ref, scales in zip((solution_ref, residual_ref), found):
        scales = [jnp.broadcast_to(scale, (rows, planes))[None] for scale in scales]
        for part in range(2):
            for inner in range(x_count):
                right = adjoint_ref[:, part, inner] + penalty * denoised_ref[:, part, inner]
                value = scales[0] * right + scales[1] * field_ref[:, part, inner]
                if len(scales) > 2:
                    value = value + scales[2] * image_ref[:, part * x_count + inner]
                for block in range(blocks):
                    place = part * readout + block * x_count + inner
                    rows_ref[place * rows : (place + 1) * rows] = value[block]
        for row in range(rows):
            out_ref[row] = jnp.transpose(rows_ref[pl.ds(row, 2 * readout, stride=rows), :])


def finish_call(adjoint, denoised, field, image):
    blocks, _, x_count, rows, planes = adjoint.shape
    shape = (rows, planes, 2 * blocks * x_count)
    vmem = pl.BlockSpec(memory_space=pltpu.VMEM)
    return pl.pallas_call(
        finish_kernel,
        in_specs=[vmem] * 4,
        out_specs=[vmem] * 2,
        out_shape=[jax.ShapeDtypeStruct(shape, jnp.float32)] * 2,
        scratch_shapes=[pltpu.VMEM((2 * blocks * x_count * rows, planes), jnp.float32)],
        compiler_params=pltpu.CompilerParams(vmem_limit_bytes=32 * 1024 * 1024),
        cost_estimate=pl.CostEstimate(
            flops=8 * adjoint.size, bytes_accessed=24 * adjoint.size, transcendentals=0
        ),
        name="finish",
    )(adjoint, denoised, field, image)


def body(
    prior_image,
    coil_maps,
    kspace,
    sampling,
    weight_first,
    bias_first,
    weight_middle,
    bias_middle,
    weight_last,
    bias_last,
):
    readout = prior_image.shape[2] // 2
    own_rows = prior_image.shape[0]
    planes = prior_image.shape[1]
    slabs = lax.axis_size("slab")
    coils = lax.axis_size("coil")
    devices = slabs * coils
    spread = readout % devices == 0 and own_rows % 8 == 0 and coil_maps.shape[1] % 16 == 0
    parts = devices if spread else coils
    x_count = readout // parts
    mask = lax.all_gather(sampling.astype(jnp.bfloat16), "slab", axis=0, tiled=True)
    features, mask = lax.optimization_barrier(
        (with_halo(prior_image.astype(jnp.bfloat16), 3), mask)
    )
    constants = [
        jnp.transpose(mask).astype(jnp.float32),
        jnp.asarray(dft_table(sampling.shape[1], planes)),
    ]

    if spread:
        own_maps, measured = coil_maps[0], kspace[0]
        real = x_first(own_maps[..., :readout], parts, 1)
        imag = x_first(own_maps[..., readout:], parts, 1)
        slab_rows = own_maps.shape[0]
        slab_planes, row_count = measured.shape[:2]
        measured = measured.reshape(
            slab_planes, row_count // planes, planes, 2, parts, x_count
        )
        measured = jnp.transpose(measured, (4, 3, 5, 1, 0, 2)).reshape(
            parts, 2 * x_count, slab_rows, planes
        )
        real = exchange(real.reshape(parts, x_count, slab_rows, planes), axes)
        rest = exchange(
            jnp.concatenate([imag.reshape(parts, x_count, slab_rows, planes), measured], axis=1),
            axes,
        )
        real = real.reshape((slabs, coils) + real.shape[1:])
        rest = rest.reshape((slabs, coils) + rest.shape[1:])
        maps = [(real, 0), (rest, 0)]
        spectra = [(rest, x_count), (rest, 2 * x_count)]
    else:

        def coils_to_x(values):
            blocks = x_first(values, parts)
            tail = blocks.shape[1:]
            blocks = exchange(blocks, "coil").reshape((slabs, coils // slabs) + tail)
            blocks = exchange(blocks, "slab")
            return [(blocks[:, :, part], 0) for part in range(2)]

        maps = coils_to_x(coil_maps[0])
        spectra = coils_to_x(kspace[0])

    blocks = denoise(
        parts,
        features,
        prior_image,
        weight_first,
        bias_first,
        weight_middle,
        bias_middle,
        weight_last,
        bias_last,
    )
    if blocks.ndim == 3:
        blocks = x_first(blocks, parts)
    if spread:
        adjoint = adjoint_call(spectra, maps, constants, x_count, devices)
        field, totals = first_call(maps, adjoint, exchange(blocks, axes), constants)
        field, adjoint_back = lax.optimization_barrier((field, exchange(adjoint, axes)))
        payload, field_back = lax.optimization_barrier(
            (second_call(maps, field, totals, constants), exchange(field, axes))
        )
        return tuple(finish_call(adjoint_back, blocks, field_back, exchange(payload, axes)))

    tail = blocks.shape[1:3]

    def whole_rows(parts_in):
        moved = lax.all_gather(exchange(parts_in, "coil"), "slab", axis=0, tiled=True)
        return jnp.transpose(moved, (1, 2, 0, 3, 4)).reshape((1,) + tail + (-1, planes))

    def own_part(whole):
        rows = whole.shape[3] // slabs
        mine = lax.dynamic_slice_in_dim(whole, lax.axis_index("slab") * rows, rows, axis=3)
        split = jnp.transpose(mine.reshape(tail + (coils, own_rows, planes)), (2, 0, 1, 3, 4))
        return x_last(exchange(split, "coil"))

    adjoint = lax.psum(adjoint_call(spectra, maps, constants, x_count, 1), "slab")
    denoised = whole_rows(blocks)
    right = adjoint + penalty * denoised
    field = lax.psum(first_call(maps, adjoint, denoised, constants)[0], "slab")
    image = lax.psum(first_call(maps, field, jnp.zeros_like(field), constants)[0], "slab")
    squares = lax.psum(
        jnp.stack(
            [
                jnp.sum(right * right),
                jnp.sum(right * field),
                jnp.sum(field * field),
                jnp.sum(field * image),
            ]
        ),
        "coil",
    )
    scales, others = factors(*(squares[index] for index in range(4)))
    right, field, image = own_part(right), own_part(field), own_part(image)
    return (
        scales[0] * right + scales[1] * field,
        others[0] * right + others[1] * field + others[2] * image,
    )


def solution(mesh):
    placed = (
        P(("slab", "coil"), None, None),
        P("coil", "slab", None, None),
        P("coil", "slab", None, None),
        P("slab", None),
        P(),
        P(),
        P(),
        P(),
        P(),
        P(),
    )
    return jax.shard_map(
        body,
        mesh=mesh,
        in_specs=placed,
        out_specs=(P(("slab", "coil"), None, None), P(("slab", "coil"), None, None)),
        check_vma=False,
    )
```

```python
import functools
import math

import jax
import jax.numpy as jnp
import numpy as np
from jax import lax
from jax.experimental import pallas as pl
from jax.experimental.pallas import tpu as pltpu
from jax.sharding import PartitionSpec as P

CG_ITERS = 2


penalty = 0.5
axes = ("slab", "coil")


def with_halo(cells, width):
    rows = cells.shape[0]
    count = lax.axis_size("slab") * lax.axis_size("coil")
    above, below = [], []
    for hop in range(1, -(-width // rows) + 1):
        taken = min(width - (hop - 1) * rows, rows)
        ends = count - hop
        tail = lax.slice_in_dim(cells, rows - taken, rows, axis=0)
        head = lax.slice_in_dim(cells, 0, taken, axis=0)
        above.insert(0, lax.ppermute(tail, axes, [(i, i + hop) for i in range(ends)]))
        below.append(lax.ppermute(head, axes, [(i + hop, i) for i in range(ends)]))
    return jnp.concatenate(above + [cells] + below, axis=0)


def chunk_rows(rows):
    return max(size for size in range(1, 7) if rows % size == 0)


def chained(lhs_pieces):
    rows = lhs_pieces[0].shape[0] * lhs_pieces[0].shape[1]
    lhs = jnp.concatenate(lhs_pieces, axis=2)
    return lhs.reshape(rows, lhs.shape[2])


def denoise_kernel(
    group,
    first_ref,
    features_ref,
    prior_ref,
    weight_first_ref,
    bias_first_ref,
    weight_middle_ref,
    bias_middle_ref,
    weight_last_ref,
    bias_last_ref,
    out_ref,
    one_ref,
    two_ref,
    taps_ref,
    *turned_refs,
):
    own_rows, planes, width = prior_ref.shape
    edge = (one_ref.shape[2] - two_ref.shape[2]) // 2
    groups = two_ref.shape[2] // group
    first = first_ref[0]
    total = first_ref[1]
    one_ref[:, :, :edge] = jnp.zeros(one_ref.shape[:2] + (edge,), one_ref.dtype)
    one_ref[:, :, edge + two_ref.shape[2] :] = jnp.zeros(
        one_ref.shape[:2] + (edge,), one_ref.dtype
    )

    def store(ref, start, count, lanes, value, reach):
        value = jnp.maximum(value, 0.0).reshape(count, planes, group)
        for row in range(count):
            place = first + (start + row - reach)
            kept = jnp.where((place >= 0) & (place < total), value[row], 0.0)
            ref[start + row, :, lanes] = kept.astype(ref.dtype)

    def first_layer(index, carry):
        lanes = pl.ds(pl.multiple_of(index * group, group), group)
        placed = pl.ds(pl.multiple_of(edge + index * group, 128), group)
        count = chunk_rows(one_ref.shape[0])
        for start in range(0, one_ref.shape[0], count):
            lhs = chained([features_ref[start + tap : start + tap + count] for tap in range(3)])
            value = jnp.dot(lhs, weight_first_ref[:, lanes], preferred_element_type=jnp.float32)
            store(one_ref, start, count, placed, value + bias_first_ref[:, lanes], 2)
        return carry

    lax.fori_loop(0, groups, first_layer, 0)

    def shifted(value, plane, step):
        rows = value.shape[0]
        if step > 0:
            return jnp.where(plane == 0, 0.0, pltpu.roll(value, 1, 0))
        return jnp.where(plane == planes - 1, 0.0, pltpu.roll(value, rows - 1, 0))

    def plane_index(count, lanes):
        return lax.broadcasted_iota(jnp.int32, (count, planes, lanes), 1).reshape(
            count * planes, lanes
        )

    def middle_layer(index, carry):
        lanes = pl.ds(pl.multiple_of(index * group, group), group)
        window = pl.ds(pl.multiple_of(index * group, group), group + 2 * edge)
        count = chunk_rows(two_ref.shape[0])
        plane = plane_index(count, group)
        for start in range(0, two_ref.shape[0], count):
            lhs = chained([one_ref[start + tap : start + tap + count, :, window] for tap in range(3)])
            value = jnp.dot(lhs, weight_middle_ref[...], preferred_element_type=jnp.float32)
            value = (
                value[:, group : 2 * group]
                + shifted(value[:, :group], plane, 1)
                + shifted(value[:, 2 * group :], plane, -1)
            )
            store(two_ref, start, count, lanes, value + bias_middle_ref[:, lanes], 1)
        return carry

    lax.fori_loop(0, groups, middle_layer, 0)

    count = chunk_rows(two_ref.shape[0])

    def last_layer(index, carry):
        start = index * count
        lhs = two_ref[pl.ds(start, count)].reshape(count * planes, two_ref.shape[2])
        value = jnp.dot(lhs, weight_last_ref[...], preferred_element_type=jnp.float32)
        taps_ref[pl.ds(start, count)] = value.reshape(count, planes, value.shape[1])
        return carry

    lax.fori_loop(0, two_ref.shape[0] // count, last_layer, 0)
    plane = plane_index(1, width)

    def last_sum(row):
        sums = []
        for plane_tap in range(3):
            running = None
            for row_tap in range(3):
                lanes = pl.ds((row_tap * 3 + plane_tap) * width, width)
                value = taps_ref[row + row_tap, :, lanes]
                running = value if running is None else running + value
            sums.append(running)
        value = sums[1] + shifted(sums[0], plane, 1) + shifted(sums[2], plane, -1)
        return prior_ref[row] + (value + bias_last_ref[...])

    if not turned_refs:
        for row in range(own_rows):
            out_ref[row] = last_sum(row)
        return

    turned_ref = turned_refs[0]
    for row in range(own_rows):
        turned_ref[pl.ds(row, width, stride=own_rows), :] = jnp.transpose(last_sum(row))
    blocks, _, x_count = out_ref.shape[:3]
    for block in range(blocks):
        for part in range(2):
            for inner in range(x_count):
                place = part * (width // 2) + block * x_count + inner
                out_ref[block, part, inner] = turned_ref[place * own_rows : (place + 1) * own_rows]


def banded(tiles, inner, outer, offset):
    shape = jnp.broadcast_shapes(tiles[0].shape, inner.shape, outer.shape)
    result = jnp.zeros(shape, jnp.bfloat16)
    for tap in range(3):
        result = jnp.where(inner - outer + offset == tap, tiles[tap], result)
    return result


def denoise(
    parts,
    features,
    prior_image,
    weight_first,
    bias_first,
    weight_middle,
    bias_middle,
    weight_last,
    bias_last,
):
    own_rows, planes, width = prior_image.shape
    turned = own_rows % 8 == 0
    out_shape = (parts, 2, width // (2 * parts), own_rows, planes) if turned else prior_image.shape
    readout = width // 2
    channels = weight_first.shape[3]
    span = readout * channels
    group = min(256, span)
    held = group // channels
    edge = 128
    reach = edge // channels
    window = group + 2 * edge

    def lane_place(count, inside):
        return jnp.arange(count * inside, dtype=jnp.int32) // inside

    tiles = jnp.transpose(weight_first, (2, 0, 1, 4, 3)).reshape(3, 18, 1, 1, channels)
    tiles = jnp.broadcast_to(tiles, (3, 18, 1, readout, channels)).reshape(3, 18, 1, span)
    first_table = banded(
        tiles,
        jnp.arange(readout, dtype=jnp.int32)[None, :, None],
        lane_place(readout, channels)[None, None, :],
        1,
    ).reshape(18 * readout, span)
    tiles = jnp.transpose(weight_middle, (2, 0, 4, 1, 3)).reshape(3, 3, 1, channels, 3, 1, channels)
    tiles = jnp.broadcast_to(tiles, (3, 3, 1, channels, 3, held, channels))
    tiles = tiles.reshape(3, 3, 1, channels, 3 * group)
    middle_table = banded(
        tiles,
        jnp.arange(window // channels, dtype=jnp.int32)[None, :, None, None] - reach,
        jnp.tile(lane_place(held, channels), 3)[None, None, None, :],
        1,
    ).reshape(3 * window, 3 * group)
    tiles = jnp.transpose(weight_last, (2, 4, 0, 1, 3)).reshape(3, 1, channels, 18, 1)
    tiles = jnp.broadcast_to(tiles, (3, 1, channels, 18, readout)).reshape(
        3, 1, channels, 18 * readout
    )
    last_table = banded(
        tiles,
        jnp.arange(readout, dtype=jnp.int32)[:, None, None],
        jnp.tile(jnp.arange(readout, dtype=jnp.int32), 18)[None, None, :],
        1,
    ).reshape(span, 18 * readout)

    rim = jnp.zeros_like(features[:, :1])
    features = jnp.concatenate(
        [
            jnp.concatenate([rim, features[:, :-1]], axis=1),
            features,
            jnp.concatenate([features[:, 1:], rim], axis=1),
        ],
        axis=2,
    )
    total = own_rows * lax.axis_size("slab") * lax.axis_size("coil")
    first = lax.axis_index(axes) * own_rows
    places = jnp.stack([first, jnp.asarray(total)]).astype(jnp.int32)
    vmem = pl.BlockSpec(memory_space=pltpu.VMEM)
    flops = 2 * own_rows * planes * (
        features.shape[2] * 3 * span * 3 // 2 + 9 * span * 512 * 5 // 4 + span * 18 * readout * 5 // 4
    )
    return pl.pallas_call(
        functools.partial(denoise_kernel, group),
        in_specs=[pl.BlockSpec(memory_space=pltpu.SMEM)] + [vmem] * 8,
        out_specs=vmem,
        out_shape=jax.ShapeDtypeStruct(out_shape, jnp.float32),
        scratch_shapes=[
            pltpu.VMEM((own_rows + 4, planes, span + 2 * edge), jnp.bfloat16),
            pltpu.VMEM((own_rows + 2, planes, span), jnp.bfloat16),
            pltpu.VMEM((own_rows + 2, planes, 18 * readout), jnp.float32),
        ]
        + [pltpu.VMEM((width * own_rows, planes), jnp.float32)] * turned,
        compiler_params=pltpu.CompilerParams(vmem_limit_bytes=56 * 1024 * 1024),
        cost_estimate=pl.CostEstimate(
            flops=int(flops), bytes_accessed=16 * 1024 * 1024, transcendentals=0
        ),
        name="denoise",
    )(
        places,
        features,
        prior_image,
        first_table,
        jnp.tile(bias_first, readout)[None, :],
        middle_table,
        jnp.tile(bias_middle, readout)[None, :],
        last_table,
        jnp.repeat(bias_last, readout)[None, :],
    )


def table_parts(table):
    high = table.astype(jnp.bfloat16)
    low = (table - high.astype(np.float64)).astype(jnp.bfloat16)
    return high, low


def dft_parts(length):
    positions = np.arange(length, dtype=np.int64)
    angles = (positions[:, None] * positions[None, :] % length) * (2.0 * math.pi / length)
    scale = 1.0 / math.sqrt(length)
    return np.cos(angles) * scale, np.sin(angles) * scale


def turn_block(length):
    cos_part, sin_part = dft_parts(length)
    return np.concatenate(
        [
            np.concatenate([cos_part, sin_part], axis=1),
            np.concatenate([-sin_part, cos_part], axis=1),
        ],
        axis=0,
    )


def dft_table(rows, planes):
    rows_high, rows_low = table_parts(turn_block(rows))
    planes_parts = np.concatenate(table_parts(turn_block(planes).T), axis=0)
    short = max(2 * rows - planes_parts.shape[0], 0)
    planes_parts = np.pad(planes_parts, ((0, short), (0, 0)))
    return np.concatenate([rows_high, rows_low, planes_parts], axis=1)


def half_tables(rows, planes):
    rows_parts = np.concatenate(table_parts(turn_block(rows // 2) * math.sqrt(0.5)), axis=1)
    planes_parts = np.concatenate(table_parts(turn_block(planes).T), axis=0)
    angles = np.arange(rows // 2) * (2.0 * math.pi / rows)
    turns = np.stack([np.cos(angles), np.sin(angles)])[:, :, None]
    turns = np.broadcast_to(turns, (2, rows // 2, planes)).astype(np.float32)
    return [rows_parts, planes_parts, turns]


def value_parts(value):
    high = value.astype(jnp.bfloat16)
    low = (value - high.astype(jnp.float32)).astype(jnp.bfloat16)
    return high, low


def tables_of(ref, rows, planes):
    high, low = ref[:, : 2 * rows], ref[:, 2 * rows : 4 * rows]
    row_table = jnp.concatenate([high, low, high], axis=1)
    high, low = ref[: 2 * planes, 4 * rows :], ref[2 * planes : 4 * planes, 4 * rows :]
    return row_table, jnp.concatenate([high, low, high], axis=0)


def along_planes(fields, table):
    rows, planes = fields[0][0].shape
    stacked = jnp.concatenate([jnp.concatenate(field, axis=1) for field in fields], axis=0)
    high, low = value_parts(stacked)
    moved = jnp.dot(
        jnp.concatenate([high, high, low], axis=1), table, preferred_element_type=jnp.float32
    )
    return [
        (
            moved[index * rows : (index + 1) * rows, :planes],
            moved[index * rows : (index + 1) * rows, planes:],
        )
        for index in range(len(fields))
    ]


def side_by_side(fields):
    return jnp.concatenate(
        [jnp.concatenate([field[part] for field in fields], axis=1) for part in range(2)], axis=0
    )


def along_rows(table, fields):
    rows, planes = fields[0][0].shape
    high, low = value_parts(side_by_side(fields))
    moved = jnp.dot(
        table, jnp.concatenate([high, high, low], axis=0), preferred_element_type=jnp.float32
    )
    return apart(moved, len(fields))


def apart(moved, count):
    rows = moved.shape[0] // 2
    planes = moved.shape[1] // count
    return [
        (
            moved[:rows, index * planes : (index + 1) * planes],
            moved[rows:, index * planes : (index + 1) * planes],
        )
        for index in range(count)
    ]


def plane_of(ref, part):
    value = ref[:, part, 0]
    return value.reshape(value.shape[0] * value.shape[1], value.shape[2])


def coil_plane(ref, coil):
    value = ref[:, coil, 0]
    return value.reshape(value.shape[0] * value.shape[1], value.shape[2])


def map_of(refs, coil):
    return [coil_plane(ref, coil).astype(jnp.float32) for ref in refs]


def image_sums(maps, fields):
    sums = None
    for (map_real, map_imag), (real, imag) in zip(maps, fields):
        terms = (map_real * real - map_imag * imag, -(map_real * imag + map_imag * real))
        sums = terms if sums is None else (sums[0] + terms[0], sums[1] + terms[1])
    return sums


def units_of(refs):
    count = refs[0].shape[1]
    held = 2 if count % 2 == 0 else 1
    return [tuple(range(first, first + held)) for first in range(0, count, held)]


def halved(fields, turns):
    evens, odds = [], []
    rows = fields[0][0].shape[0] // 2
    for real, imag in fields:
        evens.append((real[:rows] + real[rows:], imag[:rows] + imag[rows:]))
        real, imag = real[:rows] - real[rows:], imag[:rows] - imag[rows:]
        odds.append((real * turns[0] + imag * turns[1], imag * turns[0] - real * turns[1]))
    return evens, odds


def rejoined(evens, odds, turns):
    fields = []
    for (even_real, even_imag), (real, imag) in zip(evens, odds):
        real, imag = real * turns[0] + imag * turns[1], imag * turns[0] - real * turns[1]
        fields.append(
            (
                jnp.concatenate([even_real + real, even_real - real], axis=0),
                jnp.concatenate([even_imag + imag, even_imag - imag], axis=0),
            )
        )
    return fields


def masked(fields, mask):
    return [(real * mask, imag * -mask) for real, imag in fields]


def in_groups(values, size):
    return [values[first : first + size] for first in range(0, len(values), size)]


def normal_sums(maps_refs, real, imag, mask_ref, rows_ref, planes_ref, turns_ref):
    half = rows_ref.shape[1] // 2
    row_table = jnp.concatenate([rows_ref[:, :half], rows_ref[:, half:], rows_ref[:, :half]], axis=1)
    half = planes_ref.shape[0] // 2
    plane_table = jnp.concatenate([planes_ref[:half], planes_ref[half:], planes_ref[:half]], axis=0)
    turns = turns_ref[0], turns_ref[1]
    half = turns[0].shape[0]
    masks = mask_ref[:half], mask_ref[half:]
    coils = list(range(maps_refs[0].shape[1]))
    fields = []
    for group in in_groups(coils, 4):
        products = []
        for coil in group:
            map_real, map_imag = map_of(maps_refs, coil)
            products.append(
                (map_real * real - map_imag * imag, map_real * imag + map_imag * real)
            )
        fields += along_planes(products, plane_table)
    units = [halved(unit, turns) for unit in in_groups(fields, 2)]
    units = [[along_rows(row_table, part) for part in unit] for unit in units]
    units = [[masked(part, mask) for part, mask in zip(unit, masks)] for unit in units]
    units = [[along_rows(row_table, part) for part in unit] for unit in units]
    fields = sum((rejoined(*unit, turns) for unit in units), [])
    images = []
    for group in in_groups(fields, 4):
        images += along_planes(group, plane_table)
    total = None
    for group in in_groups(coils, 2):
        sums = image_sums(
            [map_of(maps_refs, coil) for coil in group], [images[coil] for coil in group]
        )
        total = sums if total is None else (total[0] + sums[0], total[1] + sums[1])
    return total


def accumulate(out_ref, values, places):
    shape = out_ref.shape[0], out_ref.shape[-2], out_ref.shape[-1]

    @pl.when(pl.program_id(1) == 0)
    def _():
        for value, place in zip(values, places):
            out_ref[(slice(None),) + place] = value.reshape(shape)

    @pl.when(pl.program_id(1) > 0)
    def _():
        for value, place in zip(values, places):
            out_ref[(slice(None),) + place] += value.reshape(shape)


def adjoint_kernel(
    spectra_real_ref, spectra_imag_ref, maps_real_ref, maps_imag_ref, mask_ref, table_ref, out_ref
):
    maps_refs = maps_real_ref, maps_imag_ref
    mask = mask_ref[...]
    rows, planes = mask.shape
    row_table, plane_table = tables_of(table_ref, rows, planes)
    units = units_of(maps_refs)
    images = []
    for unit in units:
        spectra = []
        for coil in unit:
            real, imag = (
                jnp.transpose(coil_plane(ref, coil).astype(jnp.float32))
                for ref in (spectra_real_ref, spectra_imag_ref)
            )
            spectra.append((real * mask, imag * -mask))
        spectrum = side_by_side(spectra).astype(jnp.bfloat16)
        moved = jnp.dot(
            row_table[:, : 4 * rows],
            jnp.concatenate([spectrum, spectrum], axis=0),
            preferred_element_type=jnp.float32,
        )
        images.append(apart(moved, len(unit)))
    images = [along_planes(image, plane_table) for image in images]
    total = None
    for unit, image in zip(units, images):
        sums = image_sums([map_of(maps_refs, coil) for coil in unit], image)
        total = sums if total is None else (total[0] + sums[0], total[1] + sums[1])
    accumulate(out_ref, total, ((0, 0), (1, 0)))


def lane_sums(left, other):
    product = left[0] * other[0] + left[1] * other[1]
    return jnp.sum(jnp.sum(product, axis=0), axis=0, keepdims=True)


def first_kernel(
    maps_real_ref, maps_imag_ref, adjoint_ref, denoised_ref, *refs
):
    constants, (out_ref, total_ref) = refs[:-2], refs[-2:]
    rights = [
        plane_of(adjoint_ref, part) + penalty * plane_of(denoised_ref, part) for part in range(2)
    ]
    sums = normal_sums((maps_real_ref, maps_imag_ref), *rights, *constants)
    accumulate(out_ref, sums, ((0, 0), (1, 0)))

    @pl.when(pl.program_id(1) == pl.num_programs(1) - 1)
    def _():
        shape = out_ref.shape[0], out_ref.shape[3], out_ref.shape[4]
        sides = [right.reshape(shape) for right in rights]
        fields = [out_ref[:, part, 0] for part in range(2)]
        totals = jnp.concatenate(
            [
                lane_sums(sides, sides),
                lane_sums(sides, fields),
                lane_sums(fields, fields),
                jnp.zeros((total_ref.shape[0] - 3, total_ref.shape[1]), jnp.float32),
            ],
            axis=0,
        )

        @pl.when(pl.program_id(0) == 0)
        def _():
            total_ref[...] = totals

        @pl.when(pl.program_id(0) > 0)
        def _():
            total_ref[...] += totals


def second_kernel(maps_real_ref, maps_imag_ref, field_ref, total_ref, *refs):
    constants, out_ref = refs[:-1], refs[-1]
    x_index = pl.program_id(0)
    x_count = pl.num_programs(0)
    blocks, block_rows, planes = out_ref.shape[0], out_ref.shape[2], out_ref.shape[3]
    sums = normal_sums(
        (maps_real_ref, maps_imag_ref), plane_of(field_ref, 0), plane_of(field_ref, 1), *constants
    )
    places = [(part * x_count + x_index,) for part in range(2)]
    accumulate(out_ref, sums, places)

    @pl.when(pl.program_id(1) == pl.num_programs(1) - 1)
    def _():
        fields = [field_ref[:, part, 0] for part in range(2)]
        images = [out_ref[(slice(None),) + place] for place in places]
        for part in range(2):
            out_ref[:, (2 + part) * x_count + x_index] = fields[part]
        totals = jnp.concatenate(
            [
                jnp.zeros((3, planes), jnp.float32),
                lane_sums(fields, images),
                jnp.zeros((block_rows - 4, planes), jnp.float32),
            ],
            axis=0,
        )

        @pl.when(x_index == 0)
        def _():
            out_ref[:, 4 * x_count] = jnp.broadcast_to(
                (total_ref[...] + totals)[None], (blocks, block_rows, planes)
            )

        @pl.when(x_index > 0)
        def _():
            out_ref[:, 4 * x_count] += totals[None]


def held_coils(count):
    return max(size for size in (1, 2, 4, 8) if count % size == 0)


def whole(shape):
    return pl.BlockSpec(shape, lambda x, c: (0,) * len(shape))


def coils_spec(planes):
    values, first = planes
    slabs, coils, _, rows, lanes = values.shape
    return pl.BlockSpec(
        (slabs, held_coils(coils), 1, rows, lanes), lambda x, c: (0, c, first + x, 0, 0)
    )


def field_spec(shape):
    return pl.BlockSpec((shape[0], 2, 1) + shape[3:], lambda x, c: (0, 0, x, 0, 0))


def compute_params():
    return pltpu.CompilerParams(
        dimension_semantics=("arbitrary", "arbitrary"), vmem_limit_bytes=48 * 1024 * 1024
    )


def product_call(kernel, name, x_count, coil_planes, fields, extras, constants, outs, passes):
    coils = coil_planes[0][0].shape[1]
    mask = constants[0]
    rows, planes = mask.shape
    flops = 2 * 2 * rows * planes * (2 * rows + 2 * planes) * coils * x_count * passes
    values = [planes_of[0] for planes_of in coil_planes] + fields + extras + constants
    return pl.pallas_call(
        kernel,
        grid=(x_count, coils // held_coils(coils)),
        in_specs=[coils_spec(planes_of) for planes_of in coil_planes]
        + [field_spec(field.shape) for field in fields]
        + [whole(value.shape) for value in extras + constants],
        out_specs=[spec for spec, _ in outs],
        out_shape=[jax.ShapeDtypeStruct(shape, jnp.float32) for _, shape in outs],
        compiler_params=compute_params(),
        cost_estimate=pl.CostEstimate(
            flops=int(flops), bytes_accessed=8 * 1024 * 1024, transcendentals=0
        ),
        name=name,
    )(*values)


def adjoint_call(spectra, maps, constants, x_count, blocks):
    rows, planes = constants[0].shape
    shape = (blocks, 2, x_count, rows // blocks, planes)
    outs = [(field_spec(shape), shape)]
    return product_call(
        adjoint_kernel, "adjoint", x_count, spectra + maps, [], [], constants, outs, 3
    )[0]


def first_call(maps, adjoint, denoised, constants):
    shape = adjoint.shape
    totals = (8, shape[4])
    outs = [(field_spec(shape), shape), (whole(totals), totals)]
    return product_call(
        first_kernel, "first_product", shape[2], maps, [adjoint, denoised], [], constants, outs, 6
    )


def second_call(maps, field, totals, constants):
    blocks, _, x_count, block_rows, planes = field.shape
    shape = (blocks, 4 * x_count + 1, block_rows, planes)
    outs = [(whole(shape), shape)]
    return product_call(
        second_kernel, "second_product", x_count, maps, [field], [totals], constants, outs, 6
    )[0]


def exchange(blocks, axis):
    return lax.all_to_all(blocks, axis, split_axis=0, concat_axis=0, tiled=True)


def x_first(cells, parts):
    rows, planes, width = cells.shape
    split = cells.reshape(rows, planes, 2, parts, width // (2 * parts))
    return jnp.transpose(split, (3, 2, 4, 0, 1))


def x_last(blocks):
    parts, _, x_count, rows, planes = blocks.shape
    return jnp.transpose(blocks, (3, 4, 1, 0, 2)).reshape(rows, planes, 2 * parts * x_count)


def factors(right_right, right_field, field_field, field_image):
    ratio = right_field / right_right
    alpha = right_right / (right_field + penalty * right_right)
    fresh = alpha * alpha * (field_field - ratio * right_field)
    weight = alpha * ratio + fresh / right_right
    mixed = weight * alpha
    curvature = (
        weight * weight * right_field - 2.0 * mixed * field_field + alpha * alpha * field_image
    ) + penalty * (
        weight * weight * right_right - 2.0 * mixed * right_field + alpha * alpha * field_field
    )
    second = fresh / curvature
    moved = alpha + second * weight
    bent = second * alpha
    return (moved, -bent), (alpha * ratio - penalty * second * weight, penalty * bent - moved, bent)


def finish_kernel(
    adjoint_ref, denoised_ref, moved_ref, solution_ref, residual_ref, rows_ref
):
    blocks, _, x_count, rows, planes = adjoint_ref.shape
    readout = blocks * x_count
    totals = jnp.sum(jnp.sum(moved_ref[:, 4 * x_count], axis=0), axis=1, keepdims=True)
    found = factors(*(totals[index : index + 1] for index in range(4)))
    for out_ref, scales in zip((solution_ref, residual_ref), found):
        scales = [jnp.broadcast_to(scale, (rows, planes))[None] for scale in scales]
        for part in range(2):
            for inner in range(x_count):
                right = adjoint_ref[:, part, inner] + penalty * denoised_ref[:, part, inner]
                value = (
                    scales[0] * right
                    + scales[1] * moved_ref[:, (2 + part) * x_count + inner]
                )
                if len(scales) > 2:
                    value = value + scales[2] * moved_ref[:, part * x_count + inner]
                for block in range(blocks):
                    place = part * readout + block * x_count + inner
                    rows_ref[place * rows : (place + 1) * rows] = value[block]
        for row in range(rows):
            out_ref[row] = jnp.transpose(rows_ref[pl.ds(row, 2 * readout, stride=rows), :])


def finish_call(adjoint, denoised, moved):
    blocks, _, x_count, rows, planes = adjoint.shape
    shape = (rows, planes, 2 * blocks * x_count)
    vmem = pl.BlockSpec(memory_space=pltpu.VMEM)
    return pl.pallas_call(
        finish_kernel,
        in_specs=[vmem] * 3,
        out_specs=[vmem] * 2,
        out_shape=[jax.ShapeDtypeStruct(shape, jnp.float32)] * 2,
        scratch_shapes=[pltpu.VMEM((2 * blocks * x_count * rows, planes), jnp.float32)],
        compiler_params=pltpu.CompilerParams(vmem_limit_bytes=32 * 1024 * 1024),
        cost_estimate=pl.CostEstimate(
            flops=8 * adjoint.size, bytes_accessed=24 * adjoint.size, transcendentals=0
        ),
        name="finish",
    )(adjoint, denoised, moved)


def body(
    prior_image,
    coil_maps,
    kspace,
    sampling,
    weight_first,
    bias_first,
    weight_middle,
    bias_middle,
    weight_last,
    bias_last,
):
    readout = prior_image.shape[2] // 2
    own_rows = prior_image.shape[0]
    planes = prior_image.shape[1]
    slabs = lax.axis_size("slab")
    coils = lax.axis_size("coil")
    devices = slabs * coils
    spread = readout % devices == 0 and own_rows % 8 == 0
    parts = devices if spread else coils
    x_count = readout // parts
    mask = lax.all_gather(sampling.astype(jnp.bfloat16), "slab", axis=0, tiled=True)
    features, mask = lax.optimization_barrier(
        (with_halo(prior_image.astype(jnp.bfloat16), 3), mask)
    )
    mask = jnp.transpose(mask).astype(jnp.float32)
    row_count = mask.shape[0]
    half_mask = jnp.concatenate([mask[::2], mask[1::2]], axis=0)
    constants = [half_mask] + half_tables(row_count, planes)
    constants = [jnp.asarray(value) for value in constants]
    adjoint_constants = [mask, jnp.asarray(dft_table(row_count, planes))]

    def coils_to_x(values):
        blocks = x_first(values, parts)
        tail = (2 * x_count,) + blocks.shape[3:]
        if spread:
            blocks = exchange(blocks, axes).reshape((slabs, coils) + tail)
        else:
            blocks = exchange(blocks, "coil").reshape((slabs, coils // slabs) + tail)
            blocks = exchange(blocks, "slab")
        return [(blocks, 0), (blocks, x_count)]

    maps = coils_to_x(coil_maps[0])
    spectra = coils_to_x(kspace[0])
    blocks = denoise(
        parts,
        features,
        prior_image,
        weight_first,
        bias_first,
        weight_middle,
        bias_middle,
        weight_last,
        bias_last,
    )
    if blocks.ndim == 3:
        blocks = x_first(blocks, parts)
    if spread:
        adjoint = adjoint_call(spectra, maps, adjoint_constants, x_count, devices)
        field, totals = first_call(maps, adjoint, exchange(blocks, axes), constants)
        field, adjoint_back = lax.optimization_barrier((field, exchange(adjoint, axes)))
        payload = exchange(second_call(maps, field, totals, constants), axes)
        return tuple(finish_call(adjoint_back, blocks, payload))

    tail = blocks.shape[1:3]

    def whole_rows(parts_in):
        moved = lax.all_gather(exchange(parts_in, "coil"), "slab", axis=0, tiled=True)
        return jnp.transpose(moved, (1, 2, 0, 3, 4)).reshape((1,) + tail + (-1, planes))

    def own_part(whole):
        rows = whole.shape[3] // slabs
        mine = lax.dynamic_slice_in_dim(whole, lax.axis_index("slab") * rows, rows, axis=3)
        split = jnp.transpose(mine.reshape(tail + (coils, own_rows, planes)), (2, 0, 1, 3, 4))
        return x_last(exchange(split, "coil"))

    adjoint = lax.psum(adjoint_call(spectra, maps, adjoint_constants, x_count, 1), "slab")
    denoised = whole_rows(blocks)
    right = adjoint + penalty * denoised
    field = lax.psum(first_call(maps, adjoint, denoised, constants)[0], "slab")
    image = lax.psum(first_call(maps, field, jnp.zeros_like(field), constants)[0], "slab")
    squares = lax.psum(
        jnp.stack(
            [
                jnp.sum(right * right),
                jnp.sum(right * field),
                jnp.sum(field * field),
                jnp.sum(field * image),
            ]
        ),
        "coil",
    )
    scales, others = factors(*(squares[index] for index in range(4)))
    right, field, image = own_part(right), own_part(field), own_part(image)
    return (
        scales[0] * right + scales[1] * field,
        others[0] * right + others[1] * field + others[2] * image,
    )


def solution(mesh):
    placed = (
        P(("slab", "coil"), None, None),
        P("coil", "slab", None, None),
        P("coil", "slab", None, None),
        P("slab", None),
        P(),
        P(),
        P(),
        P(),
        P(),
        P(),
    )
    return jax.shard_map(
        body,
        mesh=mesh,
        in_specs=placed,
        out_specs=(P(("slab", "coil"), None, None), P(("slab", "coil"), None, None)),
        check_vma=False,
    )
```

```python
import functools
import math

import jax
import jax.numpy as jnp
import numpy as np
from jax import lax
from jax.experimental import pallas as pl
from jax.experimental.pallas import tpu as pltpu
from jax.sharding import PartitionSpec as P

CG_ITERS = 2


penalty = 0.5
axes = ("slab", "coil")


def with_halo(cells, width):
    rows = cells.shape[0]
    count = lax.axis_size("slab") * lax.axis_size("coil")
    above, below = [], []
    for hop in range(1, -(-width // rows) + 1):
        taken = min(width - (hop - 1) * rows, rows)
        ends = count - hop
        tail = lax.slice_in_dim(cells, rows - taken, rows, axis=0)
        head = lax.slice_in_dim(cells, 0, taken, axis=0)
        above.insert(0, lax.ppermute(tail, axes, [(i, i + hop) for i in range(ends)]))
        below.append(lax.ppermute(head, axes, [(i + hop, i) for i in range(ends)]))
    return jnp.concatenate(above + [cells] + below, axis=0)


def chunk_rows(rows):
    return max(size for size in range(1, 13) if rows % size == 0)


def chained(lhs_pieces):
    rows = lhs_pieces[0].shape[0] * lhs_pieces[0].shape[1]
    lhs = jnp.concatenate(lhs_pieces, axis=2)
    return lhs.reshape(rows, lhs.shape[2])


def denoise_kernel(
    group,
    first_ref,
    features_ref,
    prior_ref,
    weight_first_ref,
    bias_first_ref,
    weight_middle_ref,
    bias_middle_ref,
    weight_last_ref,
    bias_last_ref,
    out_ref,
    one_ref,
    two_ref,
    taps_ref,
    *turned_refs,
):
    own_rows, planes, width = prior_ref.shape
    edge = (one_ref.shape[2] - two_ref.shape[2]) // 2
    groups = two_ref.shape[2] // group
    first = first_ref[0]
    total = first_ref[1]
    one_ref[:, :, :edge] = jnp.zeros(one_ref.shape[:2] + (edge,), one_ref.dtype)
    one_ref[:, :, edge + two_ref.shape[2] :] = jnp.zeros(
        one_ref.shape[:2] + (edge,), one_ref.dtype
    )

    def store(ref, start, count, lanes, value, reach):
        value = jnp.maximum(value, 0.0).reshape(count, planes, group)
        for row in range(count):
            place = first + (start + row - reach)
            kept = jnp.where((place >= 0) & (place < total), value[row], 0.0)
            ref[start + row, :, lanes] = kept.astype(ref.dtype)

    def first_layer(index, carry):
        lanes = pl.ds(pl.multiple_of(index * group, group), group)
        placed = pl.ds(pl.multiple_of(edge + index * group, 128), group)
        count = chunk_rows(one_ref.shape[0])
        for start in range(0, one_ref.shape[0], count):
            lhs = chained([features_ref[start + tap : start + tap + count] for tap in range(3)])
            value = jnp.dot(lhs, weight_first_ref[:, lanes], preferred_element_type=jnp.float32)
            store(one_ref, start, count, placed, value + bias_first_ref[:, lanes], 2)
        return carry

    lax.fori_loop(0, groups, first_layer, 0)

    def shifted(value, plane, step):
        rows = value.shape[0]
        if step > 0:
            return jnp.where(plane == 0, 0.0, pltpu.roll(value, 1, 0))
        return jnp.where(plane == planes - 1, 0.0, pltpu.roll(value, rows - 1, 0))

    def plane_index(count, lanes):
        return lax.broadcasted_iota(jnp.int32, (count, planes, lanes), 1).reshape(
            count * planes, lanes
        )

    def middle_layer(index, carry):
        lanes = pl.ds(pl.multiple_of(index * group, group), group)
        window = pl.ds(pl.multiple_of(index * group, group), group + 2 * edge)
        count = chunk_rows(two_ref.shape[0])
        plane = plane_index(count, group)
        for start in range(0, two_ref.shape[0], count):
            lhs = chained([one_ref[start + tap : start + tap + count, :, window] for tap in range(3)])
            value = jnp.dot(lhs, weight_middle_ref[...], preferred_element_type=jnp.float32)
            value = (
                value[:, group : 2 * group]
                + shifted(value[:, :group], plane, 1)
                + shifted(value[:, 2 * group :], plane, -1)
            )
            store(two_ref, start, count, lanes, value + bias_middle_ref[:, lanes], 1)
        return carry

    lax.fori_loop(0, groups, middle_layer, 0)

    count = chunk_rows(two_ref.shape[0])

    def last_layer(index, carry):
        start = index * count
        lhs = two_ref[pl.ds(start, count)].reshape(count * planes, two_ref.shape[2])
        value = jnp.dot(lhs, weight_last_ref[...], preferred_element_type=jnp.float32)
        taps_ref[pl.ds(start, count)] = value.reshape(count, planes, value.shape[1])
        return carry

    lax.fori_loop(0, two_ref.shape[0] // count, last_layer, 0)
    plane = plane_index(1, width)

    def last_sum(row):
        sums = []
        for plane_tap in range(3):
            running = None
            for row_tap in range(3):
                lanes = pl.ds((row_tap * 3 + plane_tap) * width, width)
                value = taps_ref[row + row_tap, :, lanes]
                running = value if running is None else running + value
            sums.append(running)
        value = sums[1] + shifted(sums[0], plane, 1) + shifted(sums[2], plane, -1)
        return prior_ref[row] + (value + bias_last_ref[...])

    if not turned_refs:
        for row in range(own_rows):
            out_ref[row] = last_sum(row)
        return

    turned_ref = turned_refs[0]
    for row in range(own_rows):
        turned_ref[pl.ds(row, width, stride=own_rows), :] = jnp.transpose(last_sum(row))
    blocks, _, x_count = out_ref.shape[:3]
    for block in range(blocks):
        for part in range(2):
            for inner in range(x_count):
                place = part * (width // 2) + block * x_count + inner
                out_ref[block, part, inner] = turned_ref[place * own_rows : (place + 1) * own_rows]


def banded(tiles, inner, outer, offset):
    shape = jnp.broadcast_shapes(tiles[0].shape, inner.shape, outer.shape)
    result = jnp.zeros(shape, jnp.bfloat16)
    for tap in range(3):
        result = jnp.where(inner - outer + offset == tap, tiles[tap], result)
    return result


def denoise(
    parts,
    features,
    prior_image,
    weight_first,
    bias_first,
    weight_middle,
    bias_middle,
    weight_last,
    bias_last,
):
    own_rows, planes, width = prior_image.shape
    turned = own_rows % 8 == 0
    out_shape = (parts, 2, width // (2 * parts), own_rows, planes) if turned else prior_image.shape
    readout = width // 2
    channels = weight_first.shape[3]
    span = readout * channels
    group = min(256, span)
    held = group // channels
    edge = 128
    reach = edge // channels
    window = group + 2 * edge

    def lane_place(count, inside):
        return jnp.arange(count * inside, dtype=jnp.int32) // inside

    tiles = jnp.transpose(weight_first, (2, 0, 1, 4, 3)).reshape(3, 18, 1, 1, channels)
    tiles = jnp.broadcast_to(tiles, (3, 18, 1, readout, channels)).reshape(3, 18, 1, span)
    first_table = banded(
        tiles,
        jnp.arange(readout, dtype=jnp.int32)[None, :, None],
        lane_place(readout, channels)[None, None, :],
        1,
    ).reshape(18 * readout, span)
    tiles = jnp.transpose(weight_middle, (2, 0, 4, 1, 3)).reshape(3, 3, 1, channels, 3, 1, channels)
    tiles = jnp.broadcast_to(tiles, (3, 3, 1, channels, 3, held, channels))
    tiles = tiles.reshape(3, 3, 1, channels, 3 * group)
    middle_table = banded(
        tiles,
        jnp.arange(window // channels, dtype=jnp.int32)[None, :, None, None] - reach,
        jnp.tile(lane_place(held, channels), 3)[None, None, None, :],
        1,
    ).reshape(3 * window, 3 * group)
    tiles = jnp.transpose(weight_last, (2, 4, 0, 1, 3)).reshape(3, 1, channels, 18, 1)
    tiles = jnp.broadcast_to(tiles, (3, 1, channels, 18, readout)).reshape(
        3, 1, channels, 18 * readout
    )
    last_table = banded(
        tiles,
        jnp.arange(readout, dtype=jnp.int32)[:, None, None],
        jnp.tile(jnp.arange(readout, dtype=jnp.int32), 18)[None, None, :],
        1,
    ).reshape(span, 18 * readout)

    rim = jnp.zeros_like(features[:, :1])
    features = jnp.concatenate(
        [
            jnp.concatenate([rim, features[:, :-1]], axis=1),
            features,
            jnp.concatenate([features[:, 1:], rim], axis=1),
        ],
        axis=2,
    )
    total = own_rows * lax.axis_size("slab") * lax.axis_size("coil")
    first = lax.axis_index(axes) * own_rows
    places = jnp.stack([first, jnp.asarray(total)]).astype(jnp.int32)
    vmem = pl.BlockSpec(memory_space=pltpu.VMEM)
    flops = 2 * own_rows * planes * (
        features.shape[2] * 3 * span * 3 // 2 + 9 * span * 512 * 5 // 4 + span * 18 * readout * 5 // 4
    )
    return pl.pallas_call(
        functools.partial(denoise_kernel, group),
        in_specs=[pl.BlockSpec(memory_space=pltpu.SMEM)] + [vmem] * 8,
        out_specs=vmem,
        out_shape=jax.ShapeDtypeStruct(out_shape, jnp.float32),
        scratch_shapes=[
            pltpu.VMEM((own_rows + 4, planes, span + 2 * edge), jnp.bfloat16),
            pltpu.VMEM((own_rows + 2, planes, span), jnp.bfloat16),
            pltpu.VMEM((own_rows + 2, planes, 18 * readout), jnp.float32),
        ]
        + [pltpu.VMEM((width * own_rows, planes), jnp.float32)] * turned,
        compiler_params=pltpu.CompilerParams(vmem_limit_bytes=40 * 1024 * 1024),
        cost_estimate=pl.CostEstimate(
            flops=int(flops), bytes_accessed=16 * 1024 * 1024, transcendentals=0
        ),
        name="denoise",
    )(
        places,
        features,
        prior_image,
        first_table,
        jnp.tile(bias_first, readout)[None, :],
        middle_table,
        jnp.tile(bias_middle, readout)[None, :],
        last_table,
        jnp.repeat(bias_last, readout)[None, :],
    )


def table_parts(table):
    high = table.astype(jnp.bfloat16)
    low = (table - high.astype(np.float64)).astype(jnp.bfloat16)
    return high, low


def dft_parts(length):
    positions = np.arange(length, dtype=np.int64)
    angles = (positions[:, None] * positions[None, :] % length) * (2.0 * math.pi / length)
    scale = 1.0 / math.sqrt(length)
    return np.cos(angles) * scale, np.sin(angles) * scale


def turn_block(length):
    cos_part, sin_part = dft_parts(length)
    return np.concatenate(
        [
            np.concatenate([cos_part, sin_part], axis=1),
            np.concatenate([-sin_part, cos_part], axis=1),
        ],
        axis=0,
    )


def dft_table(rows, planes):
    rows_high, rows_low = table_parts(turn_block(rows))
    planes_parts = np.concatenate(table_parts(turn_block(planes).T), axis=0)
    short = max(2 * rows - planes_parts.shape[0], 0)
    planes_parts = np.pad(planes_parts, ((0, short), (0, 0)))
    return np.concatenate([rows_high, rows_low, planes_parts], axis=1)


def half_tables(rows, planes):
    rows_parts = np.concatenate(table_parts(turn_block(rows // 2) * math.sqrt(0.5)), axis=1)
    planes_parts = np.concatenate(table_parts(turn_block(planes).T), axis=0)
    angles = np.arange(rows // 2) * (2.0 * math.pi / rows)
    turns = np.stack([np.cos(angles), np.sin(angles)])[:, :, None]
    turns = np.broadcast_to(turns, (2, rows // 2, planes)).astype(np.float32)
    return [rows_parts, planes_parts, turns]


def value_parts(value):
    high = value.astype(jnp.bfloat16)
    low = (value - high.astype(jnp.float32)).astype(jnp.bfloat16)
    return high, low


def tables_of(ref, rows, planes):
    high, low = ref[:, : 2 * rows], ref[:, 2 * rows : 4 * rows]
    row_table = jnp.concatenate([high, low, high], axis=1)
    high, low = ref[: 2 * planes, 4 * rows :], ref[2 * planes : 4 * planes, 4 * rows :]
    return row_table, jnp.concatenate([high, low, high], axis=0)


def along_planes(fields, table):
    rows, planes = fields[0][0].shape
    stacked = jnp.concatenate([jnp.concatenate(field, axis=1) for field in fields], axis=0)
    high, low = value_parts(stacked)
    moved = jnp.dot(
        jnp.concatenate([high, high, low], axis=1), table, preferred_element_type=jnp.float32
    )
    return [
        (
            moved[index * rows : (index + 1) * rows, :planes],
            moved[index * rows : (index + 1) * rows, planes:],
        )
        for index in range(len(fields))
    ]


def side_by_side(fields):
    return jnp.concatenate(
        [jnp.concatenate([field[part] for field in fields], axis=1) for part in range(2)], axis=0
    )


def along_rows(table, fields):
    rows, planes = fields[0][0].shape
    high, low = value_parts(side_by_side(fields))
    moved = jnp.dot(
        table, jnp.concatenate([high, high, low], axis=0), preferred_element_type=jnp.float32
    )
    return apart(moved, len(fields))


def apart(moved, count):
    rows = moved.shape[0] // 2
    planes = moved.shape[1] // count
    return [
        (
            moved[:rows, index * planes : (index + 1) * planes],
            moved[rows:, index * planes : (index + 1) * planes],
        )
        for index in range(count)
    ]


def plane_of(ref, part):
    value = ref[:, part, 0]
    return value.reshape(value.shape[0] * value.shape[1], value.shape[2])


def coil_plane(ref, coil):
    value = ref[:, coil, 0]
    return value.reshape(value.shape[0] * value.shape[1], value.shape[2])


def map_of(refs, coil):
    return [coil_plane(ref, coil).astype(jnp.float32) for ref in refs]


def image_sums(maps, fields):
    sums = None
    for (map_real, map_imag), (real, imag) in zip(maps, fields):
        terms = (map_real * real - map_imag * imag, -(map_real * imag + map_imag * real))
        sums = terms if sums is None else (sums[0] + terms[0], sums[1] + terms[1])
    return sums


def units_of(refs):
    count = refs[0].shape[1]
    held = 2 if count % 2 == 0 else 1
    return [tuple(range(first, first + held)) for first in range(0, count, held)]


def halved(fields, turns):
    evens, odds = [], []
    rows = fields[0][0].shape[0] // 2
    for real, imag in fields:
        evens.append((real[:rows] + real[rows:], imag[:rows] + imag[rows:]))
        real, imag = real[:rows] - real[rows:], imag[:rows] - imag[rows:]
        odds.append((real * turns[0] + imag * turns[1], imag * turns[0] - real * turns[1]))
    return evens, odds


def rejoined(evens, odds, turns):
    fields = []
    for (even_real, even_imag), (real, imag) in zip(evens, odds):
        real, imag = real * turns[0] + imag * turns[1], imag * turns[0] - real * turns[1]
        fields.append(
            (
                jnp.concatenate([even_real + real, even_real - real], axis=0),
                jnp.concatenate([even_imag + imag, even_imag - imag], axis=0),
            )
        )
    return fields


def masked(fields, mask):
    return [(real * mask, imag * -mask) for real, imag in fields]


def in_groups(values, size):
    return [values[first : first + size] for first in range(0, len(values), size)]


def normal_sums(maps_refs, real, imag, mask_ref, rows_ref, planes_ref, turns_ref):
    half = rows_ref.shape[1] // 2
    row_table = jnp.concatenate([rows_ref[:, :half], rows_ref[:, half:], rows_ref[:, :half]], axis=1)
    half = planes_ref.shape[0] // 2
    plane_table = jnp.concatenate([planes_ref[:half], planes_ref[half:], planes_ref[:half]], axis=0)
    turns = turns_ref[0], turns_ref[1]
    half = turns[0].shape[0]
    masks = mask_ref[:half], mask_ref[half:]
    coils = list(range(maps_refs[0].shape[1]))
    fields = []
    for group in in_groups(coils, 4):
        products = []
        for coil in group:
            map_real, map_imag = map_of(maps_refs, coil)
            products.append(
                (map_real * real - map_imag * imag, map_real * imag + map_imag * real)
            )
        fields += along_planes(products, plane_table)
    units = [halved(unit, turns) for unit in in_groups(fields, 2)]
    units = [[along_rows(row_table, part) for part in unit] for unit in units]
    units = [[masked(part, mask) for part, mask in zip(unit, masks)] for unit in units]
    units = [[along_rows(row_table, part) for part in unit] for unit in units]
    fields = sum((rejoined(*unit, turns) for unit in units), [])
    images = []
    for group in in_groups(fields, 4):
        images += along_planes(group, plane_table)
    total = None
    for group in in_groups(coils, 2):
        sums = image_sums(
            [map_of(maps_refs, coil) for coil in group], [images[coil] for coil in group]
        )
        total = sums if total is None else (total[0] + sums[0], total[1] + sums[1])
    return total


def accumulate(out_ref, values, places):
    shape = out_ref.shape[0], out_ref.shape[-2], out_ref.shape[-1]

    @pl.when(pl.program_id(1) == 0)
    def _():
        for value, place in zip(values, places):
            out_ref[(slice(None),) + place] = value.reshape(shape)

    @pl.when(pl.program_id(1) > 0)
    def _():
        for value, place in zip(values, places):
            out_ref[(slice(None),) + place] += value.reshape(shape)


def adjoint_kernel(
    spectra_real_ref, spectra_imag_ref, maps_real_ref, maps_imag_ref, mask_ref, table_ref, out_ref
):
    maps_refs = maps_real_ref, maps_imag_ref
    mask = mask_ref[...]
    rows, planes = mask.shape
    row_table, plane_table = tables_of(table_ref, rows, planes)
    units = units_of(maps_refs)
    images = []
    for unit in units:
        spectra = []
        for coil in unit:
            real, imag = (
                jnp.transpose(coil_plane(ref, coil).astype(jnp.float32))
                for ref in (spectra_real_ref, spectra_imag_ref)
            )
            spectra.append((real * mask, imag * -mask))
        spectrum = side_by_side(spectra).astype(jnp.bfloat16)
        moved = jnp.dot(
            row_table[:, : 4 * rows],
            jnp.concatenate([spectrum, spectrum], axis=0),
            preferred_element_type=jnp.float32,
        )
        images.append(apart(moved, len(unit)))
    images = [along_planes(image, plane_table) for image in images]
    total = None
    for unit, image in zip(units, images):
        sums = image_sums([map_of(maps_refs, coil) for coil in unit], image)
        total = sums if total is None else (total[0] + sums[0], total[1] + sums[1])
    accumulate(out_ref, total, ((0, 0), (1, 0)))


def product_kernel(maps_real_ref, maps_imag_ref, field_ref, *refs):
    constants, out_ref = refs[:-1], refs[-1]
    fields = [plane_of(field_ref, part) for part in range(2)]
    accumulate(
        out_ref,
        normal_sums((maps_real_ref, maps_imag_ref), *fields, *constants),
        ((0, 0), (1, 0)),
    )


def lane_sums(left, other):
    return jnp.sum(left[0] * other[0] + left[1] * other[1], axis=0, keepdims=True)


def twice_kernel(maps_real_ref, maps_imag_ref, adjoint_ref, denoised_ref, *refs):
    constants, out_ref = refs[:-1], refs[-1]
    maps_refs = maps_real_ref, maps_imag_ref
    x_index = pl.program_id(0)
    x_count = pl.num_programs(0)
    blocks, block_rows, planes = out_ref.shape[0], out_ref.shape[2], out_ref.shape[3]
    shape = blocks, block_rows, planes
    rights = [
        plane_of(adjoint_ref, part) + penalty * plane_of(denoised_ref, part) for part in range(2)
    ]
    fields = normal_sums(maps_refs, *rights, *constants)
    images = normal_sums(maps_refs, *fields, *constants)
    for part in range(2):
        out_ref[:, part * x_count + x_index] = images[part].reshape(shape)
        out_ref[:, (2 + part) * x_count + x_index] = fields[part].reshape(shape)
    totals = jnp.concatenate(
        [
            lane_sums(rights, rights),
            lane_sums(rights, fields),
            lane_sums(fields, fields),
            lane_sums(fields, images),
            jnp.zeros((block_rows - 4, planes), jnp.float32),
        ],
        axis=0,
    )[None]

    @pl.when(x_index == 0)
    def _():
        out_ref[:, 4 * x_count] = jnp.broadcast_to(totals, shape)

    @pl.when(x_index > 0)
    def _():
        out_ref[:, 4 * x_count] += totals


def held_coils(count):
    return max(size for size in (1, 2, 4, 8) if count % size == 0)


def whole(shape):
    return pl.BlockSpec(shape, lambda x, c: (0,) * len(shape))


def coils_spec(planes):
    values, first = planes
    slabs, coils, _, rows, lanes = values.shape
    return pl.BlockSpec(
        (slabs, held_coils(coils), 1, rows, lanes), lambda x, c: (0, c, first + x, 0, 0)
    )


def field_spec(shape):
    return pl.BlockSpec((shape[0], 2, 1) + shape[3:], lambda x, c: (0, 0, x, 0, 0))


def compute_params():
    return pltpu.CompilerParams(
        dimension_semantics=("arbitrary", "arbitrary"), vmem_limit_bytes=22 * 1024 * 1024
    )


def product_call(kernel, name, x_count, coil_planes, fields, extras, constants, outs, passes):
    coils = coil_planes[0][0].shape[1]
    mask = constants[0]
    rows, planes = mask.shape
    flops = 2 * 2 * rows * planes * (2 * rows + 2 * planes) * coils * x_count * passes
    values = [planes_of[0] for planes_of in coil_planes] + fields + extras + constants
    return pl.pallas_call(
        kernel,
        grid=(x_count, coils // held_coils(coils)),
        in_specs=[coils_spec(planes_of) for planes_of in coil_planes]
        + [field_spec(field.shape) for field in fields]
        + [whole(value.shape) for value in extras + constants],
        out_specs=[spec for spec, _ in outs],
        out_shape=[jax.ShapeDtypeStruct(shape, jnp.float32) for _, shape in outs],
        compiler_params=compute_params(),
        cost_estimate=pl.CostEstimate(
            flops=int(flops), bytes_accessed=8 * 1024 * 1024, transcendentals=0
        ),
        name=name,
    )(*values)


def adjoint_call(spectra, maps, constants, x_count, blocks):
    rows, planes = constants[0].shape
    shape = (blocks, 2, x_count, rows // blocks, planes)
    outs = [(field_spec(shape), shape)]
    return product_call(
        adjoint_kernel, "adjoint", x_count, spectra + maps, [], [], constants, outs, 3
    )[0]


def once_call(maps, field, constants):
    shape = field.shape
    outs = [(field_spec(shape), shape)]
    return product_call(
        product_kernel, "product", shape[2], maps, [field], [], constants, outs, 6
    )[0]


def twice_call(maps, adjoint, denoised, constants):
    blocks, _, x_count, block_rows, planes = adjoint.shape
    shape = (blocks, 4 * x_count + 1, block_rows, planes)
    outs = [(whole(shape), shape)]
    return product_call(
        twice_kernel, "products", x_count, maps, [adjoint, denoised], [], constants, outs, 12
    )[0]


def exchange(blocks, axis):
    return lax.all_to_all(blocks, axis, split_axis=0, concat_axis=0, tiled=True)


def x_first(cells, parts):
    rows, planes, width = cells.shape
    split = cells.reshape(rows, planes, 2, parts, width // (2 * parts))
    return jnp.transpose(split, (3, 2, 4, 0, 1))


def x_last(blocks):
    parts, _, x_count, rows, planes = blocks.shape
    return jnp.transpose(blocks, (3, 4, 1, 0, 2)).reshape(rows, planes, 2 * parts * x_count)


def factors(right_right, right_field, field_field, field_image):
    ratio = right_field / right_right
    alpha = right_right / (right_field + penalty * right_right)
    fresh = alpha * alpha * (field_field - ratio * right_field)
    weight = alpha * ratio + fresh / right_right
    mixed = weight * alpha
    curvature = (
        weight * weight * right_field - 2.0 * mixed * field_field + alpha * alpha * field_image
    ) + penalty * (
        weight * weight * right_right - 2.0 * mixed * right_field + alpha * alpha * field_field
    )
    second = fresh / curvature
    moved = alpha + second * weight
    bent = second * alpha
    return (moved, -bent), (alpha * ratio - penalty * second * weight, penalty * bent - moved, bent)


def finish_kernel(
    adjoint_ref, denoised_ref, moved_ref, solution_ref, residual_ref, rows_ref
):
    blocks, _, x_count, rows, planes = adjoint_ref.shape
    readout = blocks * x_count
    totals = jnp.sum(jnp.sum(moved_ref[:, 4 * x_count], axis=0), axis=1, keepdims=True)
    found = factors(*(totals[index : index + 1] for index in range(4)))
    for out_ref, scales in zip((solution_ref, residual_ref), found):
        scales = [jnp.broadcast_to(scale, (rows, planes))[None] for scale in scales]
        for part in range(2):
            for inner in range(x_count):
                right = adjoint_ref[:, part, inner] + penalty * denoised_ref[:, part, inner]
                value = (
                    scales[0] * right
                    + scales[1] * moved_ref[:, (2 + part) * x_count + inner]
                )
                if len(scales) > 2:
                    value = value + scales[2] * moved_ref[:, part * x_count + inner]
                for block in range(blocks):
                    place = part * readout + block * x_count + inner
                    rows_ref[place * rows : (place + 1) * rows] = value[block]
        for row in range(rows):
            out_ref[row] = jnp.transpose(rows_ref[pl.ds(row, 2 * readout, stride=rows), :])


def finish_call(adjoint, denoised, moved):
    blocks, _, x_count, rows, planes = adjoint.shape
    shape = (rows, planes, 2 * blocks * x_count)
    vmem = pl.BlockSpec(memory_space=pltpu.VMEM)
    return pl.pallas_call(
        finish_kernel,
        in_specs=[vmem] * 3,
        out_specs=[vmem] * 2,
        out_shape=[jax.ShapeDtypeStruct(shape, jnp.float32)] * 2,
        scratch_shapes=[pltpu.VMEM((2 * blocks * x_count * rows, planes), jnp.float32)],
        compiler_params=pltpu.CompilerParams(vmem_limit_bytes=12 * 1024 * 1024),
        cost_estimate=pl.CostEstimate(
            flops=8 * adjoint.size, bytes_accessed=24 * adjoint.size, transcendentals=0
        ),
        name="finish",
    )(adjoint, denoised, moved)


def body(
    prior_image,
    coil_maps,
    kspace,
    sampling,
    weight_first,
    bias_first,
    weight_middle,
    bias_middle,
    weight_last,
    bias_last,
):
    readout = prior_image.shape[2] // 2
    own_rows = prior_image.shape[0]
    planes = prior_image.shape[1]
    slabs = lax.axis_size("slab")
    coils = lax.axis_size("coil")
    devices = slabs * coils
    spread = readout % devices == 0 and own_rows % 8 == 0 and held_coils(coils) == coils
    parts = devices if spread else coils
    x_count = readout // parts
    mask = lax.all_gather(sampling.astype(jnp.bfloat16), "slab", axis=0, tiled=True)
    mask = jnp.transpose(mask).astype(jnp.float32)
    half_mask = jnp.concatenate([mask[::2], mask[1::2]], axis=0)
    features, mask, half_mask = lax.optimization_barrier(
        (with_halo(prior_image.astype(jnp.bfloat16), 3), mask, half_mask)
    )
    row_count = mask.shape[0]
    constants = [half_mask] + half_tables(row_count, planes)
    constants = [jnp.asarray(value) for value in constants]
    adjoint_constants = [mask, jnp.asarray(dft_table(row_count, planes))]

    def coils_to_x(values):
        blocks = x_first(values, parts)
        tail = (2 * x_count,) + blocks.shape[3:]
        if spread:
            blocks = exchange(blocks, axes).reshape((slabs, coils) + tail)
        else:
            blocks = exchange(blocks, "coil").reshape((slabs, coils // slabs) + tail)
            blocks = exchange(blocks, "slab")
        return [(blocks, 0), (blocks, x_count)]

    maps = coils_to_x(coil_maps[0])
    spectra = coils_to_x(kspace[0])
    blocks = denoise(
        parts,
        features,
        prior_image,
        weight_first,
        bias_first,
        weight_middle,
        bias_middle,
        weight_last,
        bias_last,
    )
    if blocks.ndim == 3:
        blocks = x_first(blocks, parts)
    if spread:
        adjoint = adjoint_call(spectra, maps, adjoint_constants, x_count, devices)
        payload, adjoint_back = lax.optimization_barrier(
            (
                twice_call(maps, adjoint, exchange(blocks, axes), constants),
                exchange(adjoint, axes),
            )
        )
        payload = exchange(payload, axes)
        return tuple(finish_call(adjoint_back, blocks, payload))

    tail = blocks.shape[1:3]

    def whole_rows(parts_in):
        moved = lax.all_gather(exchange(parts_in, "coil"), "slab", axis=0, tiled=True)
        return jnp.transpose(moved, (1, 2, 0, 3, 4)).reshape((1,) + tail + (-1, planes))

    def own_part(whole):
        rows = whole.shape[3] // slabs
        mine = lax.dynamic_slice_in_dim(whole, lax.axis_index("slab") * rows, rows, axis=3)
        split = jnp.transpose(mine.reshape(tail + (coils, own_rows, planes)), (2, 0, 1, 3, 4))
        return x_last(exchange(split, "coil"))

    adjoint = lax.psum(adjoint_call(spectra, maps, adjoint_constants, x_count, 1), "slab")
    right = adjoint + penalty * whole_rows(blocks)
    field = lax.psum(once_call(maps, right, constants), "slab")
    image = lax.psum(once_call(maps, field, constants), "slab")
    squares = lax.psum(
        jnp.stack(
            [
                jnp.sum(right * right),
                jnp.sum(right * field),
                jnp.sum(field * field),
                jnp.sum(field * image),
            ]
        ),
        "coil",
    )
    scales, others = factors(*(squares[index] for index in range(4)))
    right, field, image = own_part(right), own_part(field), own_part(image)
    return (
        scales[0] * right + scales[1] * field,
        others[0] * right + others[1] * field + others[2] * image,
    )


def solution(mesh):
    placed = (
        P(("slab", "coil"), None, None),
        P("coil", "slab", None, None),
        P("coil", "slab", None, None),
        P("slab", None),
        P(),
        P(),
        P(),
        P(),
        P(),
        P(),
    )
    return jax.shard_map(
        body,
        mesh=mesh,
        in_specs=placed,
        out_specs=(P(("slab", "coil"), None, None), P(("slab", "coil"), None, None)),
        check_vma=False,
    )
```

```python
import functools
import math

import jax
import jax.numpy as jnp
import numpy as np
from jax import lax
from jax.experimental import pallas as pl
from jax.experimental.pallas import tpu as pltpu
from jax.sharding import PartitionSpec as P

CG_ITERS = 2


penalty = 0.5
axes = ("slab", "coil")


def with_halo(cells, width):
    rows = cells.shape[0]
    count = lax.axis_size("slab") * lax.axis_size("coil")
    above, below = [], []
    for hop in range(1, -(-width // rows) + 1):
        taken = min(width - (hop - 1) * rows, rows)
        ends = count - hop
        tail = lax.slice_in_dim(cells, rows - taken, rows, axis=0)
        head = lax.slice_in_dim(cells, 0, taken, axis=0)
        above.insert(0, lax.ppermute(tail, axes, [(i, i + hop) for i in range(ends)]))
        below.append(lax.ppermute(head, axes, [(i + hop, i) for i in range(ends)]))
    return jnp.concatenate(above + [cells] + below, axis=0)


def chunk_rows(rows):
    return max(size for size in range(1, 13) if rows % size == 0)


def chained(lhs_pieces):
    rows = lhs_pieces[0].shape[0] * lhs_pieces[0].shape[1]
    lhs = jnp.concatenate(lhs_pieces, axis=2)
    return lhs.reshape(rows, lhs.shape[2])


def denoise_kernel(
    group,
    first_ref,
    features_ref,
    prior_ref,
    weight_first_ref,
    bias_first_ref,
    weight_middle_ref,
    bias_middle_ref,
    weight_last_ref,
    bias_last_ref,
    out_ref,
    one_ref,
    two_ref,
    taps_ref,
    *turned_refs,
):
    own_rows, planes, width = prior_ref.shape
    edge = (one_ref.shape[2] - two_ref.shape[2]) // 2
    groups = two_ref.shape[2] // group
    first = first_ref[0]
    total = first_ref[1]
    one_ref[:, :, :edge] = jnp.zeros(one_ref.shape[:2] + (edge,), one_ref.dtype)
    one_ref[:, :, edge + two_ref.shape[2] :] = jnp.zeros(
        one_ref.shape[:2] + (edge,), one_ref.dtype
    )

    def store(ref, start, count, lanes, value, reach):
        value = jnp.maximum(value, 0.0).reshape(count, planes, group)
        for row in range(count):
            place = first + (start + row - reach)
            kept = jnp.where((place >= 0) & (place < total), value[row], 0.0)
            ref[start + row, :, lanes] = kept.astype(ref.dtype)

    def first_layer(index, carry):
        lanes = pl.ds(pl.multiple_of(index * group, group), group)
        placed = pl.ds(pl.multiple_of(edge + index * group, 128), group)
        count = chunk_rows(one_ref.shape[0])
        for start in range(0, one_ref.shape[0], count):
            lhs = chained([features_ref[start + tap : start + tap + count] for tap in range(3)])
            value = jnp.dot(lhs, weight_first_ref[:, lanes], preferred_element_type=jnp.float32)
            store(one_ref, start, count, placed, value + bias_first_ref[:, lanes], 2)
        return carry

    lax.fori_loop(0, groups, first_layer, 0)

    def shifted(value, plane, step):
        rows = value.shape[0]
        if step > 0:
            return jnp.where(plane == 0, 0.0, pltpu.roll(value, 1, 0))
        return jnp.where(plane == planes - 1, 0.0, pltpu.roll(value, rows - 1, 0))

    def plane_index(count, lanes):
        return lax.broadcasted_iota(jnp.int32, (count, planes, lanes), 1).reshape(
            count * planes, lanes
        )

    def middle_layer(index, carry):
        lanes = pl.ds(pl.multiple_of(index * group, group), group)
        window = pl.ds(pl.multiple_of(index * group, group), group + 2 * edge)
        count = chunk_rows(two_ref.shape[0])
        plane = plane_index(count, group)
        for start in range(0, two_ref.shape[0], count):
            lhs = chained([one_ref[start + tap : start + tap + count, :, window] for tap in range(3)])
            value = jnp.dot(lhs, weight_middle_ref[...], preferred_element_type=jnp.float32)
            value = (
                value[:, group : 2 * group]
                + shifted(value[:, :group], plane, 1)
                + shifted(value[:, 2 * group :], plane, -1)
            )
            store(two_ref, start, count, lanes, value + bias_middle_ref[:, lanes], 1)
        return carry

    lax.fori_loop(0, groups, middle_layer, 0)

    count = chunk_rows(two_ref.shape[0])

    def last_layer(index, carry):
        start = index * count
        lhs = two_ref[pl.ds(start, count)].reshape(count * planes, two_ref.shape[2])
        value = jnp.dot(lhs, weight_last_ref[...], preferred_element_type=jnp.float32)
        taps_ref[pl.ds(start, count)] = value.reshape(count, planes, value.shape[1])
        return carry

    lax.fori_loop(0, two_ref.shape[0] // count, last_layer, 0)
    plane = plane_index(1, width)

    def last_sum(row):
        sums = []
        for plane_tap in range(3):
            running = None
            for row_tap in range(3):
                lanes = pl.ds((row_tap * 3 + plane_tap) * width, width)
                value = taps_ref[row + row_tap, :, lanes]
                running = value if running is None else running + value
            sums.append(running)
        value = sums[1] + shifted(sums[0], plane, 1) + shifted(sums[2], plane, -1)
        return prior_ref[row] + (value + bias_last_ref[...])

    if not turned_refs:
        for row in range(own_rows):
            out_ref[row] = last_sum(row)
        return

    turned_ref = turned_refs[0]
    for row in range(own_rows):
        turned_ref[pl.ds(row, width, stride=own_rows), :] = jnp.transpose(last_sum(row))
    blocks, _, x_count = out_ref.shape[:3]
    for block in range(blocks):
        for part in range(2):
            for inner in range(x_count):
                place = part * (width // 2) + block * x_count + inner
                out_ref[block, part, inner] = turned_ref[place * own_rows : (place + 1) * own_rows]


def banded(tiles, inner, outer, offset):
    shape = jnp.broadcast_shapes(tiles[0].shape, inner.shape, outer.shape)
    result = jnp.zeros(shape, jnp.bfloat16)
    for tap in range(3):
        result = jnp.where(inner - outer + offset == tap, tiles[tap], result)
    return result


def denoise(
    parts,
    features,
    prior_image,
    weight_first,
    bias_first,
    weight_middle,
    bias_middle,
    weight_last,
    bias_last,
):
    own_rows, planes, width = prior_image.shape
    turned = own_rows % 8 == 0
    out_shape = (parts, 2, width // (2 * parts), own_rows, planes) if turned else prior_image.shape
    readout = width // 2
    channels = weight_first.shape[3]
    span = readout * channels
    group = min(256, span)
    held = group // channels
    edge = 128
    reach = edge // channels
    window = group + 2 * edge

    def lane_place(count, inside):
        return jnp.arange(count * inside, dtype=jnp.int32) // inside

    tiles = jnp.transpose(weight_first, (2, 0, 1, 4, 3)).reshape(3, 18, 1, 1, channels)
    tiles = jnp.broadcast_to(tiles, (3, 18, 1, readout, channels)).reshape(3, 18, 1, span)
    first_table = banded(
        tiles,
        jnp.arange(readout, dtype=jnp.int32)[None, :, None],
        lane_place(readout, channels)[None, None, :],
        1,
    ).reshape(18 * readout, span)
    tiles = jnp.transpose(weight_middle, (2, 0, 4, 1, 3)).reshape(3, 3, 1, channels, 3, 1, channels)
    tiles = jnp.broadcast_to(tiles, (3, 3, 1, channels, 3, held, channels))
    tiles = tiles.reshape(3, 3, 1, channels, 3 * group)
    middle_table = banded(
        tiles,
        jnp.arange(window // channels, dtype=jnp.int32)[None, :, None, None] - reach,
        jnp.tile(lane_place(held, channels), 3)[None, None, None, :],
        1,
    ).reshape(3 * window, 3 * group)
    tiles = jnp.transpose(weight_last, (2, 4, 0, 1, 3)).reshape(3, 1, channels, 18, 1)
    tiles = jnp.broadcast_to(tiles, (3, 1, channels, 18, readout)).reshape(
        3, 1, channels, 18 * readout
    )
    last_table = banded(
        tiles,
        jnp.arange(readout, dtype=jnp.int32)[:, None, None],
        jnp.tile(jnp.arange(readout, dtype=jnp.int32), 18)[None, None, :],
        1,
    ).reshape(span, 18 * readout)

    rim = jnp.zeros_like(features[:, :1])
    features = jnp.concatenate(
        [
            jnp.concatenate([rim, features[:, :-1]], axis=1),
            features,
            jnp.concatenate([features[:, 1:], rim], axis=1),
        ],
        axis=2,
    )
    total = own_rows * lax.axis_size("slab") * lax.axis_size("coil")
    first = lax.axis_index(axes) * own_rows
    places = jnp.stack([first, jnp.asarray(total)]).astype(jnp.int32)
    vmem = pl.BlockSpec(memory_space=pltpu.VMEM)
    flops = 2 * own_rows * planes * (
        features.shape[2] * 3 * span * 3 // 2 + 9 * span * 512 * 5 // 4 + span * 18 * readout * 5 // 4
    )
    return pl.pallas_call(
        functools.partial(denoise_kernel, group),
        in_specs=[pl.BlockSpec(memory_space=pltpu.SMEM)] + [vmem] * 8,
        out_specs=vmem,
        out_shape=jax.ShapeDtypeStruct(out_shape, jnp.float32),
        scratch_shapes=[
            pltpu.VMEM((own_rows + 4, planes, span + 2 * edge), jnp.bfloat16),
            pltpu.VMEM((own_rows + 2, planes, span), jnp.bfloat16),
            pltpu.VMEM((own_rows + 2, planes, 18 * readout), jnp.float32),
        ]
        + [pltpu.VMEM((width * own_rows, planes), jnp.float32)] * turned,
        compiler_params=pltpu.CompilerParams(vmem_limit_bytes=40 * 1024 * 1024),
        cost_estimate=pl.CostEstimate(
            flops=int(flops), bytes_accessed=16 * 1024 * 1024, transcendentals=0
        ),
        name="denoise",
    )(
        places,
        features,
        prior_image,
        first_table,
        jnp.tile(bias_first, readout)[None, :],
        middle_table,
        jnp.tile(bias_middle, readout)[None, :],
        last_table,
        jnp.repeat(bias_last, readout)[None, :],
    )


def table_parts(table):
    high = table.astype(jnp.bfloat16)
    low = (table - high.astype(np.float64)).astype(jnp.bfloat16)
    return high, low


def dft_parts(length):
    positions = np.arange(length, dtype=np.int64)
    angles = (positions[:, None] * positions[None, :] % length) * (2.0 * math.pi / length)
    scale = 1.0 / math.sqrt(length)
    return np.cos(angles) * scale, np.sin(angles) * scale


def turn_block(length):
    cos_part, sin_part = dft_parts(length)
    return np.concatenate(
        [
            np.concatenate([cos_part, sin_part], axis=1),
            np.concatenate([-sin_part, cos_part], axis=1),
        ],
        axis=0,
    )


def dft_table(rows, planes):
    rows_high, rows_low = table_parts(turn_block(rows))
    planes_parts = np.concatenate(table_parts(turn_block(planes).T), axis=0)
    short = max(2 * rows - planes_parts.shape[0], 0)
    planes_parts = np.pad(planes_parts, ((0, short), (0, 0)))
    return np.concatenate([rows_high, rows_low, planes_parts], axis=1)


def half_tables(rows, planes):
    rows_parts = np.concatenate(table_parts(turn_block(rows // 2) * math.sqrt(0.5)), axis=1)
    planes_parts = np.concatenate(table_parts(turn_block(planes).T), axis=0)
    angles = np.arange(rows // 2) * (2.0 * math.pi / rows)
    turns = np.stack([np.cos(angles), np.sin(angles)])[:, :, None]
    turns = np.broadcast_to(turns, (2, rows // 2, planes)).astype(np.float32)
    return [rows_parts, planes_parts, turns]


def value_parts(value):
    high = value.astype(jnp.bfloat16)
    low = (value - high.astype(jnp.float32)).astype(jnp.bfloat16)
    return high, low


def tables_of(ref, rows, planes):
    high, low = ref[:, : 2 * rows], ref[:, 2 * rows : 4 * rows]
    row_table = jnp.concatenate([high, low, high], axis=1)
    high, low = ref[: 2 * planes, 4 * rows :], ref[2 * planes : 4 * planes, 4 * rows :]
    return row_table, jnp.concatenate([high, low, high], axis=0)


def along_planes(fields, table):
    rows, planes = fields[0][0].shape
    stacked = jnp.concatenate([jnp.concatenate(field, axis=1) for field in fields], axis=0)
    high, low = value_parts(stacked)
    moved = jnp.dot(
        jnp.concatenate([high, high, low], axis=1), table, preferred_element_type=jnp.float32
    )
    return [
        (
            moved[index * rows : (index + 1) * rows, :planes],
            moved[index * rows : (index + 1) * rows, planes:],
        )
        for index in range(len(fields))
    ]


def side_by_side(fields):
    return jnp.concatenate(
        [jnp.concatenate([field[part] for field in fields], axis=1) for part in range(2)], axis=0
    )


def along_rows(table, fields):
    rows, planes = fields[0][0].shape
    high, low = value_parts(side_by_side(fields))
    moved = jnp.dot(
        table, jnp.concatenate([high, high, low], axis=0), preferred_element_type=jnp.float32
    )
    return apart(moved, len(fields))


def apart(moved, count):
    rows = moved.shape[0] // 2
    planes = moved.shape[1] // count
    return [
        (
            moved[:rows, index * planes : (index + 1) * planes],
            moved[rows:, index * planes : (index + 1) * planes],
        )
        for index in range(count)
    ]


def plane_of(ref, part):
    value = ref[:, part, 0]
    return value.reshape(value.shape[0] * value.shape[1], value.shape[2])


def coil_plane(ref, coil):
    value = ref[:, coil, 0]
    return value.reshape(value.shape[0] * value.shape[1], value.shape[2])


def map_of(refs, coil):
    return [coil_plane(ref, coil).astype(jnp.float32) for ref in refs]


def image_sums(maps, fields):
    sums = None
    for (map_real, map_imag), (real, imag) in zip(maps, fields):
        terms = (map_real * real - map_imag * imag, -(map_real * imag + map_imag * real))
        sums = terms if sums is None else (sums[0] + terms[0], sums[1] + terms[1])
    return sums


def units_of(refs):
    count = refs[0].shape[1]
    held = 2 if count % 2 == 0 else 1
    return [tuple(range(first, first + held)) for first in range(0, count, held)]


def halved(fields, turns):
    evens, odds = [], []
    rows = fields[0][0].shape[0] // 2
    for real, imag in fields:
        evens.append((real[:rows] + real[rows:], imag[:rows] + imag[rows:]))
        real, imag = real[:rows] - real[rows:], imag[:rows] - imag[rows:]
        odds.append((real * turns[0] + imag * turns[1], imag * turns[0] - real * turns[1]))
    return evens, odds


def rejoined(evens, odds, turns):
    fields = []
    for (even_real, even_imag), (real, imag) in zip(evens, odds):
        real, imag = real * turns[0] + imag * turns[1], imag * turns[0] - real * turns[1]
        fields.append(
            (
                jnp.concatenate([even_real + real, even_real - real], axis=0),
                jnp.concatenate([even_imag + imag, even_imag - imag], axis=0),
            )
        )
    return fields


def masked(fields, mask):
    return [(real * mask, imag * -mask) for real, imag in fields]


def in_groups(values, size):
    return [values[first : first + size] for first in range(0, len(values), size)]


def normal_sums(maps_refs, real, imag, mask_ref, rows_ref, planes_ref, turns_ref):
    half = rows_ref.shape[1] // 2
    row_table = jnp.concatenate([rows_ref[:, :half], rows_ref[:, half:], rows_ref[:, :half]], axis=1)
    half = planes_ref.shape[0] // 2
    plane_table = jnp.concatenate([planes_ref[:half], planes_ref[half:], planes_ref[:half]], axis=0)
    turns = turns_ref[0], turns_ref[1]
    half = turns[0].shape[0]
    masks = tuple(mask_ref[pl.ds(odd, half, stride=2), :] for odd in range(2))
    coils = list(range(maps_refs[0].shape[1]))
    fields = []
    for group in in_groups(coils, 4):
        products = []
        for coil in group:
            map_real, map_imag = map_of(maps_refs, coil)
            products.append(
                (map_real * real - map_imag * imag, map_real * imag + map_imag * real)
            )
        fields += along_planes(products, plane_table)
    units = [halved(unit, turns) for unit in in_groups(fields, 2)]
    units = [[along_rows(row_table, part) for part in unit] for unit in units]
    units = [[masked(part, mask) for part, mask in zip(unit, masks)] for unit in units]
    units = [[along_rows(row_table, part) for part in unit] for unit in units]
    fields = sum((rejoined(*unit, turns) for unit in units), [])
    images = []
    for group in in_groups(fields, 4):
        images += along_planes(group, plane_table)
    total = None
    for group in in_groups(coils, 2):
        sums = image_sums(
            [map_of(maps_refs, coil) for coil in group], [images[coil] for coil in group]
        )
        total = sums if total is None else (total[0] + sums[0], total[1] + sums[1])
    return total


def accumulate(out_ref, values, places):
    shape = out_ref.shape[0], out_ref.shape[-2], out_ref.shape[-1]

    @pl.when(pl.program_id(1) == 0)
    def _():
        for value, place in zip(values, places):
            out_ref[(slice(None),) + place] = value.reshape(shape)

    @pl.when(pl.program_id(1) > 0)
    def _():
        for value, place in zip(values, places):
            out_ref[(slice(None),) + place] += value.reshape(shape)


def adjoint_kernel(
    spectra_real_ref, spectra_imag_ref, maps_real_ref, maps_imag_ref, mask_ref, table_ref, out_ref
):
    maps_refs = maps_real_ref, maps_imag_ref
    mask = mask_ref[...]
    rows, planes = mask.shape
    row_table, plane_table = tables_of(table_ref, rows, planes)
    units = units_of(maps_refs)
    images = []
    for unit in units:
        spectra = []
        for coil in unit:
            real, imag = (
                jnp.transpose(coil_plane(ref, coil).astype(jnp.float32))
                for ref in (spectra_real_ref, spectra_imag_ref)
            )
            spectra.append((real * mask, imag * -mask))
        spectrum = side_by_side(spectra).astype(jnp.bfloat16)
        moved = jnp.dot(
            row_table[:, : 4 * rows],
            jnp.concatenate([spectrum, spectrum], axis=0),
            preferred_element_type=jnp.float32,
        )
        images.append(apart(moved, len(unit)))
    images = [along_planes(image, plane_table) for image in images]
    total = None
    for unit, image in zip(units, images):
        sums = image_sums([map_of(maps_refs, coil) for coil in unit], image)
        total = sums if total is None else (total[0] + sums[0], total[1] + sums[1])
    accumulate(out_ref, total, ((0, 0), (1, 0)))


def product_kernel(maps_real_ref, maps_imag_ref, field_ref, *refs):
    constants, out_ref = refs[:-1], refs[-1]
    fields = [plane_of(field_ref, part) for part in range(2)]
    accumulate(
        out_ref,
        normal_sums((maps_real_ref, maps_imag_ref), *fields, *constants),
        ((0, 0), (1, 0)),
    )


def lane_sums(left, other):
    return jnp.sum(left[0] * other[0] + left[1] * other[1], axis=0, keepdims=True)


def twice_kernel(maps_real_ref, maps_imag_ref, adjoint_ref, denoised_ref, *refs):
    constants, out_ref = refs[:-1], refs[-1]
    maps_refs = maps_real_ref, maps_imag_ref
    x_index = pl.program_id(0)
    x_count = pl.num_programs(0)
    blocks, block_rows, planes = out_ref.shape[0], out_ref.shape[2], out_ref.shape[3]
    shape = blocks, block_rows, planes
    rights = [
        plane_of(adjoint_ref, part) + penalty * plane_of(denoised_ref, part) for part in range(2)
    ]
    fields = normal_sums(maps_refs, *rights, *constants)
    images = normal_sums(maps_refs, *fields, *constants)
    for part in range(2):
        out_ref[:, part * x_count + x_index] = images[part].reshape(shape)
        out_ref[:, (2 + part) * x_count + x_index] = fields[part].reshape(shape)
    totals = jnp.concatenate(
        [
            lane_sums(rights, rights),
            lane_sums(rights, fields),
            lane_sums(fields, fields),
            lane_sums(fields, images),
            jnp.zeros((block_rows - 4, planes), jnp.float32),
        ],
        axis=0,
    )[None]

    @pl.when(x_index == 0)
    def _():
        out_ref[:, 4 * x_count] = jnp.broadcast_to(totals, shape)

    @pl.when(x_index > 0)
    def _():
        out_ref[:, 4 * x_count] += totals


def held_coils(count):
    return max(size for size in (1, 2, 4, 8) if count % size == 0)


def whole(shape):
    return pl.BlockSpec(shape, lambda x, c: (0,) * len(shape))


def coils_spec(planes):
    values, first = planes
    slabs, coils, _, rows, lanes = values.shape
    return pl.BlockSpec(
        (slabs, held_coils(coils), 1, rows, lanes), lambda x, c: (0, c, first + x, 0, 0)
    )


def field_spec(shape):
    return pl.BlockSpec((shape[0], 2, 1) + shape[3:], lambda x, c: (0, 0, x, 0, 0))


def compute_params():
    return pltpu.CompilerParams(
        dimension_semantics=("arbitrary", "arbitrary"), vmem_limit_bytes=22 * 1024 * 1024
    )


def product_call(kernel, name, x_count, coil_planes, fields, extras, constants, outs, passes):
    coils = coil_planes[0][0].shape[1]
    mask = constants[0]
    rows, planes = mask.shape
    flops = 2 * 2 * rows * planes * (2 * rows + 2 * planes) * coils * x_count * passes
    values = [planes_of[0] for planes_of in coil_planes] + fields + extras + constants
    return pl.pallas_call(
        kernel,
        grid=(x_count, coils // held_coils(coils)),
        in_specs=[coils_spec(planes_of) for planes_of in coil_planes]
        + [field_spec(field.shape) for field in fields]
        + [whole(value.shape) for value in extras + constants],
        out_specs=[spec for spec, _ in outs],
        out_shape=[jax.ShapeDtypeStruct(shape, jnp.float32) for _, shape in outs],
        compiler_params=compute_params(),
        cost_estimate=pl.CostEstimate(
            flops=int(flops), bytes_accessed=8 * 1024 * 1024, transcendentals=0
        ),
        name=name,
    )(*values)


def adjoint_call(spectra, maps, constants, x_count, blocks):
    rows, planes = constants[0].shape
    shape = (blocks, 2, x_count, rows // blocks, planes)
    outs = [(field_spec(shape), shape)]
    return product_call(
        adjoint_kernel, "adjoint", x_count, spectra + maps, [], [], constants, outs, 3
    )[0]


def once_call(maps, field, constants):
    shape = field.shape
    outs = [(field_spec(shape), shape)]
    return product_call(
        product_kernel, "product", shape[2], maps, [field], [], constants, outs, 6
    )[0]


def twice_call(maps, adjoint, denoised, constants):
    blocks, _, x_count, block_rows, planes = adjoint.shape
    shape = (blocks, 4 * x_count + 1, block_rows, planes)
    outs = [(whole(shape), shape)]
    return product_call(
        twice_kernel, "products", x_count, maps, [adjoint, denoised], [], constants, outs, 12
    )[0]


def exchange(blocks, axis):
    return lax.all_to_all(blocks, axis, split_axis=0, concat_axis=0, tiled=True)


def x_first(cells, parts):
    rows, planes, width = cells.shape
    split = cells.reshape(rows, planes, 2, parts, width // (2 * parts))
    return jnp.transpose(split, (3, 2, 4, 0, 1))


def x_last(blocks):
    parts, _, x_count, rows, planes = blocks.shape
    return jnp.transpose(blocks, (3, 4, 1, 0, 2)).reshape(rows, planes, 2 * parts * x_count)


def factors(right_right, right_field, field_field, field_image):
    ratio = right_field / right_right
    alpha = right_right / (right_field + penalty * right_right)
    fresh = alpha * alpha * (field_field - ratio * right_field)
    weight = alpha * ratio + fresh / right_right
    mixed = weight * alpha
    curvature = (
        weight * weight * right_field - 2.0 * mixed * field_field + alpha * alpha * field_image
    ) + penalty * (
        weight * weight * right_right - 2.0 * mixed * right_field + alpha * alpha * field_field
    )
    second = fresh / curvature
    moved = alpha + second * weight
    bent = second * alpha
    return (moved, -bent), (alpha * ratio - penalty * second * weight, penalty * bent - moved, bent)


def finish_kernel(
    adjoint_ref, denoised_ref, moved_ref, solution_ref, residual_ref, rows_ref
):
    blocks, _, x_count, rows, planes = adjoint_ref.shape
    readout = blocks * x_count
    totals = jnp.sum(jnp.sum(moved_ref[:, 4 * x_count], axis=0), axis=1, keepdims=True)
    found = factors(*(totals[index : index + 1] for index in range(4)))
    for out_ref, scales in zip((solution_ref, residual_ref), found):
        scales = [jnp.broadcast_to(scale, (rows, planes))[None] for scale in scales]
        for part in range(2):
            for inner in range(x_count):
                right = adjoint_ref[:, part, inner] + penalty * denoised_ref[:, part, inner]
                value = (
                    scales[0] * right
                    + scales[1] * moved_ref[:, (2 + part) * x_count + inner]
                )
                if len(scales) > 2:
                    value = value + scales[2] * moved_ref[:, part * x_count + inner]
                for block in range(blocks):
                    place = part * readout + block * x_count + inner
                    rows_ref[place * rows : (place + 1) * rows] = value[block]
        for row in range(rows):
            out_ref[row] = jnp.transpose(rows_ref[pl.ds(row, 2 * readout, stride=rows), :])


def finish_call(adjoint, denoised, moved):
    blocks, _, x_count, rows, planes = adjoint.shape
    shape = (rows, planes, 2 * blocks * x_count)
    vmem = pl.BlockSpec(memory_space=pltpu.VMEM)
    return pl.pallas_call(
        finish_kernel,
        in_specs=[vmem] * 3,
        out_specs=[vmem] * 2,
        out_shape=[jax.ShapeDtypeStruct(shape, jnp.float32)] * 2,
        scratch_shapes=[pltpu.VMEM((2 * blocks * x_count * rows, planes), jnp.float32)],
        compiler_params=pltpu.CompilerParams(vmem_limit_bytes=32 * 1024 * 1024),
        cost_estimate=pl.CostEstimate(
            flops=8 * adjoint.size, bytes_accessed=24 * adjoint.size, transcendentals=0
        ),
        name="finish",
    )(adjoint, denoised, moved)


def body(
    prior_image,
    coil_maps,
    kspace,
    sampling,
    weight_first,
    bias_first,
    weight_middle,
    bias_middle,
    weight_last,
    bias_last,
):
    readout = prior_image.shape[2] // 2
    own_rows = prior_image.shape[0]
    planes = prior_image.shape[1]
    slabs = lax.axis_size("slab")
    coils = lax.axis_size("coil")
    devices = slabs * coils
    spread = readout % devices == 0 and own_rows % 8 == 0 and held_coils(coils) == coils
    parts = devices if spread else coils
    x_count = readout // parts
    mask = lax.all_gather(sampling.astype(jnp.bfloat16), "slab", axis=0, tiled=True)
    features, mask = lax.optimization_barrier(
        (with_halo(prior_image.astype(jnp.bfloat16), 3), mask)
    )
    mask = jnp.transpose(mask).astype(jnp.float32)
    row_count = mask.shape[0]
    constants = [mask] + half_tables(row_count, planes)
    constants = [jnp.asarray(value) for value in constants]
    adjoint_constants = [mask, jnp.asarray(dft_table(row_count, planes))]

    def coils_to_x(values):
        blocks = x_first(values, parts)
        tail = (2 * x_count,) + blocks.shape[3:]
        if spread:
            blocks = exchange(blocks, axes).reshape((slabs, coils) + tail)
        else:
            blocks = exchange(blocks, "coil").reshape((slabs, coils // slabs) + tail)
            blocks = exchange(blocks, "slab")
        return [(blocks, 0), (blocks, x_count)]

    maps = coils_to_x(coil_maps[0])
    spectra = coils_to_x(kspace[0])
    blocks = denoise(
        parts,
        features,
        prior_image,
        weight_first,
        bias_first,
        weight_middle,
        bias_middle,
        weight_last,
        bias_last,
    )
    if blocks.ndim == 3:
        blocks = x_first(blocks, parts)
    if spread:
        adjoint = adjoint_call(spectra, maps, adjoint_constants, x_count, devices)
        payload, adjoint_back = lax.optimization_barrier(
            (
                twice_call(maps, adjoint, exchange(blocks, axes), constants),
                exchange(adjoint, axes),
            )
        )
        payload = exchange(payload, axes)
        return tuple(finish_call(adjoint_back, blocks, payload))

    tail = blocks.shape[1:3]

    def whole_rows(parts_in):
        moved = lax.all_gather(exchange(parts_in, "coil"), "slab", axis=0, tiled=True)
        return jnp.transpose(moved, (1, 2, 0, 3, 4)).reshape((1,) + tail + (-1, planes))

    def own_part(whole):
        rows = whole.shape[3] // slabs
        mine = lax.dynamic_slice_in_dim(whole, lax.axis_index("slab") * rows, rows, axis=3)
        split = jnp.transpose(mine.reshape(tail + (coils, own_rows, planes)), (2, 0, 1, 3, 4))
        return x_last(exchange(split, "coil"))

    adjoint = lax.psum(adjoint_call(spectra, maps, adjoint_constants, x_count, 1), "slab")
    right = adjoint + penalty * whole_rows(blocks)
    field = lax.psum(once_call(maps, right, constants), "slab")
    image = lax.psum(once_call(maps, field, constants), "slab")
    squares = lax.psum(
        jnp.stack(
            [
                jnp.sum(right * right),
                jnp.sum(right * field),
                jnp.sum(field * field),
                jnp.sum(field * image),
            ]
        ),
        "coil",
    )
    scales, others = factors(*(squares[index] for index in range(4)))
    right, field, image = own_part(right), own_part(field), own_part(image)
    return (
        scales[0] * right + scales[1] * field,
        others[0] * right + others[1] * field + others[2] * image,
    )


def solution(mesh):
    placed = (
        P(("slab", "coil"), None, None),
        P("coil", "slab", None, None),
        P("coil", "slab", None, None),
        P("slab", None),
        P(),
        P(),
        P(),
        P(),
        P(),
        P(),
    )
    return jax.shard_map(
        body,
        mesh=mesh,
        in_specs=placed,
        out_specs=(P(("slab", "coil"), None, None), P(("slab", "coil"), None, None)),
        check_vma=False,
    )
```

```python
import functools
import math

import jax
import jax.numpy as jnp
import numpy as np
from jax import lax
from jax.experimental import pallas as pl
from jax.experimental.pallas import tpu as pltpu
from jax.sharding import PartitionSpec as P

CG_ITERS = 2


penalty = 0.5
axes = ("slab", "coil")


def with_halo(cells, width):
    rows = cells.shape[0]
    count = lax.axis_size("slab") * lax.axis_size("coil")
    above, below = [], []
    for hop in range(1, -(-width // rows) + 1):
        taken = min(width - (hop - 1) * rows, rows)
        ends = count - hop
        tail = lax.slice_in_dim(cells, rows - taken, rows, axis=0)
        head = lax.slice_in_dim(cells, 0, taken, axis=0)
        above.insert(0, lax.ppermute(tail, axes, [(i, i + hop) for i in range(ends)]))
        below.append(lax.ppermute(head, axes, [(i + hop, i) for i in range(ends)]))
    return jnp.concatenate(above + [cells] + below, axis=0)


def chunk_rows(rows):
    return max(size for size in range(1, 13) if rows % size == 0)


def chained(lhs_pieces):
    rows = lhs_pieces[0].shape[0] * lhs_pieces[0].shape[1]
    lhs = jnp.concatenate(lhs_pieces, axis=2)
    return lhs.reshape(rows, lhs.shape[2])


def denoise_kernel(
    group,
    first_ref,
    features_ref,
    prior_ref,
    weight_first_ref,
    bias_first_ref,
    weight_middle_ref,
    bias_middle_ref,
    weight_last_ref,
    bias_last_ref,
    out_ref,
    one_ref,
    two_ref,
    taps_ref,
    *turned_refs,
):
    own_rows, planes, width = prior_ref.shape
    edge = (one_ref.shape[2] - two_ref.shape[2]) // 2
    groups = two_ref.shape[2] // group
    first = first_ref[0]
    total = first_ref[1]
    one_ref[:, :, :edge] = jnp.zeros(one_ref.shape[:2] + (edge,), one_ref.dtype)
    one_ref[:, :, edge + two_ref.shape[2] :] = jnp.zeros(
        one_ref.shape[:2] + (edge,), one_ref.dtype
    )

    def store(ref, start, count, lanes, value, reach):
        value = jnp.maximum(value, 0.0).reshape(count, planes, group)
        for row in range(count):
            place = first + (start + row - reach)
            kept = jnp.where((place >= 0) & (place < total), value[row], 0.0)
            ref[start + row, :, lanes] = kept.astype(ref.dtype)

    def first_layer(index, carry):
        lanes = pl.ds(pl.multiple_of(index * group, group), group)
        placed = pl.ds(pl.multiple_of(edge + index * group, 128), group)
        count = chunk_rows(one_ref.shape[0])
        for start in range(0, one_ref.shape[0], count):
            lhs = chained([features_ref[start + tap : start + tap + count] for tap in range(3)])
            value = jnp.dot(lhs, weight_first_ref[:, lanes], preferred_element_type=jnp.float32)
            store(one_ref, start, count, placed, value + bias_first_ref[:, lanes], 2)
        return carry

    lax.fori_loop(0, groups, first_layer, 0)

    def shifted(value, plane, step):
        rows = value.shape[0]
        if step > 0:
            return jnp.where(plane == 0, 0.0, pltpu.roll(value, 1, 0))
        return jnp.where(plane == planes - 1, 0.0, pltpu.roll(value, rows - 1, 0))

    def plane_index(count, lanes):
        return lax.broadcasted_iota(jnp.int32, (count, planes, lanes), 1).reshape(
            count * planes, lanes
        )

    def middle_layer(index, carry):
        lanes = pl.ds(pl.multiple_of(index * group, group), group)
        window = pl.ds(pl.multiple_of(index * group, group), group + 2 * edge)
        count = chunk_rows(two_ref.shape[0])
        plane = plane_index(count, group)
        for start in range(0, two_ref.shape[0], count):
            lhs = chained([one_ref[start + tap : start + tap + count, :, window] for tap in range(3)])
            value = jnp.dot(lhs, weight_middle_ref[...], preferred_element_type=jnp.float32)
            value = (
                value[:, group : 2 * group]
                + shifted(value[:, :group], plane, 1)
                + shifted(value[:, 2 * group :], plane, -1)
            )
            store(two_ref, start, count, lanes, value + bias_middle_ref[:, lanes], 1)
        return carry

    lax.fori_loop(0, groups, middle_layer, 0)

    count = chunk_rows(two_ref.shape[0])

    def last_layer(index, carry):
        start = index * count
        lhs = two_ref[pl.ds(start, count)].reshape(count * planes, two_ref.shape[2])
        value = jnp.dot(lhs, weight_last_ref[...], preferred_element_type=jnp.float32)
        taps_ref[pl.ds(start, count)] = value.reshape(count, planes, value.shape[1])
        return carry

    lax.fori_loop(0, two_ref.shape[0] // count, last_layer, 0)
    plane = plane_index(1, width)

    def last_sum(row):
        sums = []
        for plane_tap in range(3):
            running = None
            for row_tap in range(3):
                lanes = pl.ds((row_tap * 3 + plane_tap) * width, width)
                value = taps_ref[row + row_tap, :, lanes]
                running = value if running is None else running + value
            sums.append(running)
        value = sums[1] + shifted(sums[0], plane, 1) + shifted(sums[2], plane, -1)
        return prior_ref[row] + (value + bias_last_ref[...])

    if not turned_refs:
        for row in range(own_rows):
            out_ref[row] = last_sum(row)
        return

    turned_ref = turned_refs[0]
    for row in range(own_rows):
        turned_ref[pl.ds(row, width, stride=own_rows), :] = jnp.transpose(last_sum(row))
    blocks, _, x_count = out_ref.shape[:3]
    for block in range(blocks):
        for part in range(2):
            for inner in range(x_count):
                place = part * (width // 2) + block * x_count + inner
                out_ref[block, part, inner] = turned_ref[place * own_rows : (place + 1) * own_rows]


def banded(tiles, inner, outer, offset):
    shape = jnp.broadcast_shapes(tiles[0].shape, inner.shape, outer.shape)
    result = jnp.zeros(shape, jnp.bfloat16)
    for tap in range(3):
        result = jnp.where(inner - outer + offset == tap, tiles[tap], result)
    return result


def denoise(
    parts,
    features,
    prior_image,
    weight_first,
    bias_first,
    weight_middle,
    bias_middle,
    weight_last,
    bias_last,
):
    own_rows, planes, width = prior_image.shape
    turned = own_rows % 8 == 0
    out_shape = (parts, 2, width // (2 * parts), own_rows, planes) if turned else prior_image.shape
    readout = width // 2
    channels = weight_first.shape[3]
    span = readout * channels
    group = min(256, span)
    held = group // channels
    edge = 128
    reach = edge // channels
    window = group + 2 * edge

    def lane_place(count, inside):
        return jnp.arange(count * inside, dtype=jnp.int32) // inside

    tiles = jnp.transpose(weight_first, (2, 0, 1, 4, 3)).reshape(3, 18, 1, 1, channels)
    tiles = jnp.broadcast_to(tiles, (3, 18, 1, readout, channels)).reshape(3, 18, 1, span)
    first_table = banded(
        tiles,
        jnp.arange(readout, dtype=jnp.int32)[None, :, None],
        lane_place(readout, channels)[None, None, :],
        1,
    ).reshape(18 * readout, span)
    tiles = jnp.transpose(weight_middle, (2, 0, 4, 1, 3)).reshape(3, 3, 1, channels, 3, 1, channels)
    tiles = jnp.broadcast_to(tiles, (3, 3, 1, channels, 3, held, channels))
    tiles = tiles.reshape(3, 3, 1, channels, 3 * group)
    middle_table = banded(
        tiles,
        jnp.arange(window // channels, dtype=jnp.int32)[None, :, None, None] - reach,
        jnp.tile(lane_place(held, channels), 3)[None, None, None, :],
        1,
    ).reshape(3 * window, 3 * group)
    tiles = jnp.transpose(weight_last, (2, 4, 0, 1, 3)).reshape(3, 1, channels, 18, 1)
    tiles = jnp.broadcast_to(tiles, (3, 1, channels, 18, readout)).reshape(
        3, 1, channels, 18 * readout
    )
    last_table = banded(
        tiles,
        jnp.arange(readout, dtype=jnp.int32)[:, None, None],
        jnp.tile(jnp.arange(readout, dtype=jnp.int32), 18)[None, None, :],
        1,
    ).reshape(span, 18 * readout)

    rim = jnp.zeros_like(features[:, :1])
    features = jnp.concatenate(
        [
            jnp.concatenate([rim, features[:, :-1]], axis=1),
            features,
            jnp.concatenate([features[:, 1:], rim], axis=1),
        ],
        axis=2,
    )
    total = own_rows * lax.axis_size("slab") * lax.axis_size("coil")
    first = lax.axis_index(axes) * own_rows
    places = jnp.stack([first, jnp.asarray(total)]).astype(jnp.int32)
    vmem = pl.BlockSpec(memory_space=pltpu.VMEM)
    flops = 2 * own_rows * planes * (
        features.shape[2] * 3 * span * 3 // 2 + 9 * span * 512 * 5 // 4 + span * 18 * readout * 5 // 4
    )
    return pl.pallas_call(
        functools.partial(denoise_kernel, group),
        in_specs=[pl.BlockSpec(memory_space=pltpu.SMEM)] + [vmem] * 8,
        out_specs=vmem,
        out_shape=jax.ShapeDtypeStruct(out_shape, jnp.float32),
        scratch_shapes=[
            pltpu.VMEM((own_rows + 4, planes, span + 2 * edge), jnp.bfloat16),
            pltpu.VMEM((own_rows + 2, planes, span), jnp.bfloat16),
            pltpu.VMEM((own_rows + 2, planes, 18 * readout), jnp.float32),
        ]
        + [pltpu.VMEM((width * own_rows, planes), jnp.float32)] * turned,
        compiler_params=pltpu.CompilerParams(vmem_limit_bytes=40 * 1024 * 1024),
        cost_estimate=pl.CostEstimate(
            flops=int(flops), bytes_accessed=16 * 1024 * 1024, transcendentals=0
        ),
        name="denoise",
    )(
        places,
        features,
        prior_image,
        first_table,
        jnp.tile(bias_first, readout)[None, :],
        middle_table,
        jnp.tile(bias_middle, readout)[None, :],
        last_table,
        jnp.repeat(bias_last, readout)[None, :],
    )


def table_parts(table):
    high = table.astype(jnp.bfloat16)
    low = (table - high.astype(np.float64)).astype(jnp.bfloat16)
    return high, low


def dft_parts(length):
    positions = np.arange(length, dtype=np.int64)
    angles = (positions[:, None] * positions[None, :] % length) * (2.0 * math.pi / length)
    scale = 1.0 / math.sqrt(length)
    return np.cos(angles) * scale, np.sin(angles) * scale


def turn_block(length):
    cos_part, sin_part = dft_parts(length)
    return np.concatenate(
        [
            np.concatenate([cos_part, sin_part], axis=1),
            np.concatenate([-sin_part, cos_part], axis=1),
        ],
        axis=0,
    )


def dft_table(rows, planes):
    rows_high, rows_low = table_parts(turn_block(rows))
    planes_parts = np.concatenate(table_parts(turn_block(planes).T), axis=0)
    short = max(2 * rows - planes_parts.shape[0], 0)
    planes_parts = np.pad(planes_parts, ((0, short), (0, 0)))
    return np.concatenate([rows_high, rows_low, planes_parts], axis=1)


def half_tables(rows, planes):
    rows_parts = np.concatenate(table_parts(turn_block(rows // 2) * math.sqrt(0.5)), axis=1)
    planes_parts = np.concatenate(table_parts(turn_block(planes).T), axis=0)
    angles = np.arange(rows // 2) * (2.0 * math.pi / rows)
    turns = np.stack([np.cos(angles), np.sin(angles)])[:, :, None]
    turns = np.broadcast_to(turns, (2, rows // 2, planes)).astype(np.float32)
    return [rows_parts, planes_parts, turns]


def value_parts(value):
    high = value.astype(jnp.bfloat16)
    low = (value - high.astype(jnp.float32)).astype(jnp.bfloat16)
    return high, low


def tables_of(ref, rows, planes):
    high, low = ref[:, : 2 * rows], ref[:, 2 * rows : 4 * rows]
    row_table = jnp.concatenate([high, low, high], axis=1)
    high, low = ref[: 2 * planes, 4 * rows :], ref[2 * planes : 4 * planes, 4 * rows :]
    return row_table, jnp.concatenate([high, low, high], axis=0)


def along_planes(fields, table):
    rows, planes = fields[0][0].shape
    stacked = jnp.concatenate([jnp.concatenate(field, axis=1) for field in fields], axis=0)
    high, low = value_parts(stacked)
    moved = jnp.dot(
        jnp.concatenate([high, high, low], axis=1), table, preferred_element_type=jnp.float32
    )
    return [
        (
            moved[index * rows : (index + 1) * rows, :planes],
            moved[index * rows : (index + 1) * rows, planes:],
        )
        for index in range(len(fields))
    ]


def side_by_side(fields):
    return jnp.concatenate(
        [jnp.concatenate([field[part] for field in fields], axis=1) for part in range(2)], axis=0
    )


def along_rows(table, fields):
    rows, planes = fields[0][0].shape
    high, low = value_parts(side_by_side(fields))
    moved = jnp.dot(
        table, jnp.concatenate([high, high, low], axis=0), preferred_element_type=jnp.float32
    )
    return apart(moved, len(fields))


def apart(moved, count):
    rows = moved.shape[0] // 2
    planes = moved.shape[1] // count
    return [
        (
            moved[:rows, index * planes : (index + 1) * planes],
            moved[rows:, index * planes : (index + 1) * planes],
        )
        for index in range(count)
    ]


def plane_of(ref, part):
    value = ref[:, part, 0]
    return value.reshape(value.shape[0] * value.shape[1], value.shape[2])


def coil_plane(ref, coil):
    value = ref[:, coil, 0]
    return value.reshape(value.shape[0] * value.shape[1], value.shape[2])


def map_of(refs, coil):
    return [coil_plane(ref, coil).astype(jnp.float32) for ref in refs]


def image_sums(maps, fields):
    sums = None
    for (map_real, map_imag), (real, imag) in zip(maps, fields):
        terms = (map_real * real - map_imag * imag, -(map_real * imag + map_imag * real))
        sums = terms if sums is None else (sums[0] + terms[0], sums[1] + terms[1])
    return sums


def units_of(refs):
    count = refs[0].shape[1]
    held = 2 if count % 2 == 0 else 1
    return [tuple(range(first, first + held)) for first in range(0, count, held)]


def halved(fields, turns):
    evens, odds = [], []
    rows = fields[0][0].shape[0] // 2
    for real, imag in fields:
        evens.append((real[:rows] + real[rows:], imag[:rows] + imag[rows:]))
        real, imag = real[:rows] - real[rows:], imag[:rows] - imag[rows:]
        odds.append((real * turns[0] + imag * turns[1], imag * turns[0] - real * turns[1]))
    return evens, odds


def rejoined(evens, odds, turns):
    fields = []
    for (even_real, even_imag), (real, imag) in zip(evens, odds):
        real, imag = real * turns[0] + imag * turns[1], imag * turns[0] - real * turns[1]
        fields.append(
            (
                jnp.concatenate([even_real + real, even_real - real], axis=0),
                jnp.concatenate([even_imag + imag, even_imag - imag], axis=0),
            )
        )
    return fields


def masked(fields, mask):
    return [(real * mask, imag * -mask) for real, imag in fields]


def in_groups(values, size):
    return [values[first : first + size] for first in range(0, len(values), size)]


def normal_sums(maps_refs, real, imag, mask_ref, rows_ref, planes_ref, turns_ref):
    half = rows_ref.shape[1] // 2
    row_table = jnp.concatenate([rows_ref[:, :half], rows_ref[:, half:], rows_ref[:, :half]], axis=1)
    half = planes_ref.shape[0] // 2
    plane_table = jnp.concatenate([planes_ref[:half], planes_ref[half:], planes_ref[:half]], axis=0)
    turns = turns_ref[0], turns_ref[1]
    half = turns[0].shape[0]
    masks = tuple(mask_ref[pl.ds(odd, half, stride=2), :] for odd in range(2))
    coils = list(range(maps_refs[0].shape[1]))
    fields = []
    for group in in_groups(coils, 4):
        products = []
        for coil in group:
            map_real, map_imag = map_of(maps_refs, coil)
            products.append(
                (map_real * real - map_imag * imag, map_real * imag + map_imag * real)
            )
        fields += along_planes(products, plane_table)
    units = [halved(unit, turns) for unit in in_groups(fields, 2)]
    units = [[along_rows(row_table, part) for part in unit] for unit in units]
    units = [[masked(part, mask) for part, mask in zip(unit, masks)] for unit in units]
    units = [[along_rows(row_table, part) for part in unit] for unit in units]
    fields = sum((rejoined(*unit, turns) for unit in units), [])
    images = []
    for group in in_groups(fields, 4):
        images += along_planes(group, plane_table)
    total = None
    for group in in_groups(coils, 2):
        sums = image_sums(
            [map_of(maps_refs, coil) for coil in group], [images[coil] for coil in group]
        )
        total = sums if total is None else (total[0] + sums[0], total[1] + sums[1])
    return total


def accumulate(out_ref, values, places):
    shape = out_ref.shape[0], out_ref.shape[-2], out_ref.shape[-1]

    @pl.when(pl.program_id(1) == 0)
    def _():
        for value, place in zip(values, places):
            out_ref[(slice(None),) + place] = value.reshape(shape)

    @pl.when(pl.program_id(1) > 0)
    def _():
        for value, place in zip(values, places):
            out_ref[(slice(None),) + place] += value.reshape(shape)


def adjoint_kernel(
    spectra_real_ref, spectra_imag_ref, maps_real_ref, maps_imag_ref, mask_ref, table_ref, out_ref
):
    maps_refs = maps_real_ref, maps_imag_ref
    mask = mask_ref[...]
    rows, planes = mask.shape
    row_table, plane_table = tables_of(table_ref, rows, planes)
    units = units_of(maps_refs)
    images = []
    for unit in units:
        spectra = []
        for coil in unit:
            real, imag = (
                jnp.transpose(coil_plane(ref, coil).astype(jnp.float32))
                for ref in (spectra_real_ref, spectra_imag_ref)
            )
            spectra.append((real * mask, imag * -mask))
        spectrum = side_by_side(spectra).astype(jnp.bfloat16)
        moved = jnp.dot(
            row_table[:, : 4 * rows],
            jnp.concatenate([spectrum, spectrum], axis=0),
            preferred_element_type=jnp.float32,
        )
        images.append(apart(moved, len(unit)))
    images = [along_planes(image, plane_table) for image in images]
    total = None
    for unit, image in zip(units, images):
        sums = image_sums([map_of(maps_refs, coil) for coil in unit], image)
        total = sums if total is None else (total[0] + sums[0], total[1] + sums[1])
    accumulate(out_ref, total, ((0, 0), (1, 0)))


def product_kernel(maps_real_ref, maps_imag_ref, field_ref, *refs):
    constants, out_ref = refs[:-1], refs[-1]
    fields = [plane_of(field_ref, part) for part in range(2)]
    accumulate(
        out_ref,
        normal_sums((maps_real_ref, maps_imag_ref), *fields, *constants),
        ((0, 0), (1, 0)),
    )


def lane_sums(left, other):
    return jnp.sum(left[0] * other[0] + left[1] * other[1], axis=0, keepdims=True)


def twice_kernel(maps_real_ref, maps_imag_ref, adjoint_ref, denoised_ref, *refs):
    constants, (out_ref, total_ref) = refs[:-2], refs[-2:]
    maps_refs = maps_real_ref, maps_imag_ref
    x_index = pl.program_id(0)
    x_count = pl.num_programs(0)
    blocks, block_rows, planes = out_ref.shape[0], out_ref.shape[2], out_ref.shape[3]
    shape = blocks, block_rows, planes
    rights = [
        plane_of(adjoint_ref, part) + penalty * plane_of(denoised_ref, part) for part in range(2)
    ]
    fields = normal_sums(maps_refs, *rights, *constants)
    images = normal_sums(maps_refs, *fields, *constants)
    for part in range(2):
        out_ref[:, part * x_count + x_index] = images[part].reshape(shape)
        out_ref[:, (2 + part) * x_count + x_index] = fields[part].reshape(shape)
    totals = jnp.concatenate(
        [
            lane_sums(rights, rights),
            lane_sums(rights, fields),
            lane_sums(fields, fields),
            lane_sums(fields, images),
            jnp.zeros((total_ref.shape[0] - 4, planes), jnp.float32),
        ],
        axis=0,
    )

    @pl.when(x_index == 0)
    def _():
        total_ref[...] = totals

    @pl.when(x_index > 0)
    def _():
        total_ref[...] += totals


def held_coils(count):
    return max(size for size in (1, 2, 4, 8) if count % size == 0)


def whole(shape):
    return pl.BlockSpec(shape, lambda x, c: (0,) * len(shape))


def coils_spec(planes):
    values, first = planes
    slabs, coils, _, rows, lanes = values.shape
    return pl.BlockSpec(
        (slabs, held_coils(coils), 1, rows, lanes), lambda x, c: (0, c, first + x, 0, 0)
    )


def field_spec(shape):
    return pl.BlockSpec((shape[0], 2, 1) + shape[3:], lambda x, c: (0, 0, x, 0, 0))


def compute_params():
    return pltpu.CompilerParams(
        dimension_semantics=("arbitrary", "arbitrary"), vmem_limit_bytes=22 * 1024 * 1024
    )


def product_call(kernel, name, x_count, coil_planes, fields, extras, constants, outs, passes):
    coils = coil_planes[0][0].shape[1]
    mask = constants[0]
    rows, planes = mask.shape
    flops = 2 * 2 * rows * planes * (2 * rows + 2 * planes) * coils * x_count * passes
    values = [planes_of[0] for planes_of in coil_planes] + fields + extras + constants
    return pl.pallas_call(
        kernel,
        grid=(x_count, coils // held_coils(coils)),
        in_specs=[coils_spec(planes_of) for planes_of in coil_planes]
        + [field_spec(field.shape) for field in fields]
        + [whole(value.shape) for value in extras + constants],
        out_specs=[spec for spec, _ in outs],
        out_shape=[jax.ShapeDtypeStruct(shape, jnp.float32) for _, shape in outs],
        compiler_params=compute_params(),
        cost_estimate=pl.CostEstimate(
            flops=int(flops), bytes_accessed=8 * 1024 * 1024, transcendentals=0
        ),
        name=name,
    )(*values)


def adjoint_call(spectra, maps, constants, x_count, blocks):
    rows, planes = constants[0].shape
    shape = (blocks, 2, x_count, rows // blocks, planes)
    outs = [(field_spec(shape), shape)]
    return product_call(
        adjoint_kernel, "adjoint", x_count, spectra + maps, [], [], constants, outs, 3
    )[0]


def once_call(maps, field, constants):
    shape = field.shape
    outs = [(field_spec(shape), shape)]
    return product_call(
        product_kernel, "product", shape[2], maps, [field], [], constants, outs, 6
    )[0]


def twice_call(maps, adjoint, denoised, constants):
    blocks, _, x_count, block_rows, planes = adjoint.shape
    shape = (blocks, 4 * x_count, block_rows, planes)
    outs = [(whole(shape), shape), (whole((8, planes)), (8, planes))]
    return product_call(
        twice_kernel, "products", x_count, maps, [adjoint, denoised], [], constants, outs, 12
    )


def exchange(blocks, axis):
    return lax.all_to_all(blocks, axis, split_axis=0, concat_axis=0, tiled=True)


def x_first(cells, parts):
    rows, planes, width = cells.shape
    split = cells.reshape(rows, planes, 2, parts, width // (2 * parts))
    return jnp.transpose(split, (3, 2, 4, 0, 1))


def x_last(blocks):
    parts, _, x_count, rows, planes = blocks.shape
    return jnp.transpose(blocks, (3, 4, 1, 0, 2)).reshape(rows, planes, 2 * parts * x_count)


def factors(right_right, right_field, field_field, field_image):
    ratio = right_field / right_right
    alpha = right_right / (right_field + penalty * right_right)
    fresh = alpha * alpha * (field_field - ratio * right_field)
    weight = alpha * ratio + fresh / right_right
    mixed = weight * alpha
    curvature = (
        weight * weight * right_field - 2.0 * mixed * field_field + alpha * alpha * field_image
    ) + penalty * (
        weight * weight * right_right - 2.0 * mixed * right_field + alpha * alpha * field_field
    )
    second = fresh / curvature
    moved = alpha + second * weight
    bent = second * alpha
    return (moved, -bent), (alpha * ratio - penalty * second * weight, penalty * bent - moved, bent)


def finish_kernel(
    adjoint_ref, denoised_ref, moved_ref, totals_ref, solution_ref, residual_ref, rows_ref
):
    blocks, _, x_count, rows, planes = adjoint_ref.shape
    readout = blocks * x_count
    totals = totals_ref[...].reshape(-1, 8, planes)
    totals = jnp.sum(jnp.sum(totals, axis=0), axis=1, keepdims=True)
    found = factors(*(totals[index : index + 1] for index in range(4)))
    for out_ref, scales in zip((solution_ref, residual_ref), found):
        scales = [jnp.broadcast_to(scale, (rows, planes))[None] for scale in scales]
        for part in range(2):
            for inner in range(x_count):
                right = adjoint_ref[:, part, inner] + penalty * denoised_ref[:, part, inner]
                value = (
                    scales[0] * right
                    + scales[1] * moved_ref[:, (2 + part) * x_count + inner]
                )
                if len(scales) > 2:
                    value = value + scales[2] * moved_ref[:, part * x_count + inner]
                for block in range(blocks):
                    place = part * readout + block * x_count + inner
                    rows_ref[place * rows : (place + 1) * rows] = value[block]
        for row in range(rows):
            out_ref[row] = jnp.transpose(rows_ref[pl.ds(row, 2 * readout, stride=rows), :])


def finish_call(adjoint, denoised, moved, totals):
    blocks, _, x_count, rows, planes = adjoint.shape
    shape = (rows, planes, 2 * blocks * x_count)
    vmem = pl.BlockSpec(memory_space=pltpu.VMEM)
    return pl.pallas_call(
        finish_kernel,
        in_specs=[vmem] * 4,
        out_specs=[vmem] * 2,
        out_shape=[jax.ShapeDtypeStruct(shape, jnp.float32)] * 2,
        scratch_shapes=[pltpu.VMEM((2 * blocks * x_count * rows, planes), jnp.float32)],
        compiler_params=pltpu.CompilerParams(vmem_limit_bytes=32 * 1024 * 1024),
        cost_estimate=pl.CostEstimate(
            flops=8 * adjoint.size, bytes_accessed=24 * adjoint.size, transcendentals=0
        ),
        name="finish",
    )(adjoint, denoised, moved, totals)


def body(
    prior_image,
    coil_maps,
    kspace,
    sampling,
    weight_first,
    bias_first,
    weight_middle,
    bias_middle,
    weight_last,
    bias_last,
):
    readout = prior_image.shape[2] // 2
    own_rows = prior_image.shape[0]
    planes = prior_image.shape[1]
    slabs = lax.axis_size("slab")
    coils = lax.axis_size("coil")
    devices = slabs * coils
    spread = readout % devices == 0 and own_rows % 8 == 0 and held_coils(coils) == coils
    parts = devices if spread else coils
    x_count = readout // parts
    mask = lax.all_gather(sampling.astype(jnp.bfloat16), "slab", axis=0, tiled=True)
    features, mask = lax.optimization_barrier(
        (with_halo(prior_image.astype(jnp.bfloat16), 3), mask)
    )
    mask = jnp.transpose(mask).astype(jnp.float32)
    row_count = mask.shape[0]
    constants = [mask] + half_tables(row_count, planes)
    constants = [jnp.asarray(value) for value in constants]
    adjoint_constants = [mask, jnp.asarray(dft_table(row_count, planes))]

    def coils_to_x(values):
        blocks = x_first(values, parts)
        tail = (2 * x_count,) + blocks.shape[3:]
        if spread:
            blocks = exchange(blocks, axes).reshape((slabs, coils) + tail)
        else:
            blocks = exchange(blocks, "coil").reshape((slabs, coils // slabs) + tail)
            blocks = exchange(blocks, "slab")
        return [(blocks, 0), (blocks, x_count)]

    maps = coils_to_x(coil_maps[0])
    spectra = coils_to_x(kspace[0])
    blocks = denoise(
        parts,
        features,
        prior_image,
        weight_first,
        bias_first,
        weight_middle,
        bias_middle,
        weight_last,
        bias_last,
    )
    if blocks.ndim == 3:
        blocks = x_first(blocks, parts)
    if spread:
        adjoint = adjoint_call(spectra, maps, adjoint_constants, x_count, devices)
        (payload, totals), adjoint_back = lax.optimization_barrier(
            (
                twice_call(maps, adjoint, exchange(blocks, axes), constants),
                exchange(adjoint, axes),
            )
        )
        moved = exchange(payload, axes)
        for axis in axes:
            totals = lax.all_gather(totals, axis, axis=0, tiled=True)
        return tuple(finish_call(adjoint_back, blocks, moved, totals))

    tail = blocks.shape[1:3]

    def whole_rows(parts_in):
        moved = lax.all_gather(exchange(parts_in, "coil"), "slab", axis=0, tiled=True)
        return jnp.transpose(moved, (1, 2, 0, 3, 4)).reshape((1,) + tail + (-1, planes))

    def own_part(whole):
        rows = whole.shape[3] // slabs
        mine = lax.dynamic_slice_in_dim(whole, lax.axis_index("slab") * rows, rows, axis=3)
        split = jnp.transpose(mine.reshape(tail + (coils, own_rows, planes)), (2, 0, 1, 3, 4))
        return x_last(exchange(split, "coil"))

    adjoint = lax.psum(adjoint_call(spectra, maps, adjoint_constants, x_count, 1), "slab")
    right = adjoint + penalty * whole_rows(blocks)
    field = lax.psum(once_call(maps, right, constants), "slab")
    image = lax.psum(once_call(maps, field, constants), "slab")
    squares = lax.psum(
        jnp.stack(
            [
                jnp.sum(right * right),
                jnp.sum(right * field),
                jnp.sum(field * field),
                jnp.sum(field * image),
            ]
        ),
        "coil",
    )
    scales, others = factors(*(squares[index] for index in range(4)))
    right, field, image = own_part(right), own_part(field), own_part(image)
    return (
        scales[0] * right + scales[1] * field,
        others[0] * right + others[1] * field + others[2] * image,
    )


def solution(mesh):
    placed = (
        P(("slab", "coil"), None, None),
        P("coil", "slab", None, None),
        P("coil", "slab", None, None),
        P("slab", None),
        P(),
        P(),
        P(),
        P(),
        P(),
        P(),
    )
    return jax.shard_map(
        body,
        mesh=mesh,
        in_specs=placed,
        out_specs=(P(("slab", "coil"), None, None), P(("slab", "coil"), None, None)),
        check_vma=False,
    )
```

```python
import functools
import math

import jax
import jax.numpy as jnp
import numpy as np
from jax import lax
from jax.experimental import pallas as pl
from jax.experimental.pallas import tpu as pltpu
from jax.sharding import PartitionSpec as P

CG_ITERS = 2


penalty = 0.5
axes = ("slab", "coil")


def with_halo(cells, width):
    rows = cells.shape[0]
    count = lax.axis_size("slab") * lax.axis_size("coil")
    above, below = [], []
    for hop in range(1, -(-width // rows) + 1):
        taken = min(width - (hop - 1) * rows, rows)
        ends = count - hop
        tail = lax.slice_in_dim(cells, rows - taken, rows, axis=0)
        head = lax.slice_in_dim(cells, 0, taken, axis=0)
        above.insert(0, lax.ppermute(tail, axes, [(i, i + hop) for i in range(ends)]))
        below.append(lax.ppermute(head, axes, [(i + hop, i) for i in range(ends)]))
    return jnp.concatenate(above + [cells] + below, axis=0)


def chunk_rows(rows):
    return max(size for size in range(1, 13) if rows % size == 0)


def chained(lhs_pieces):
    rows = lhs_pieces[0].shape[0] * lhs_pieces[0].shape[1]
    lhs = jnp.concatenate(lhs_pieces, axis=2)
    return lhs.reshape(rows, lhs.shape[2])


def denoise_kernel(
    group,
    first_ref,
    features_ref,
    prior_ref,
    weight_first_ref,
    bias_first_ref,
    weight_middle_ref,
    bias_middle_ref,
    weight_last_ref,
    bias_last_ref,
    out_ref,
    one_ref,
    two_ref,
    taps_ref,
    *turned_refs,
):
    own_rows, planes, width = prior_ref.shape
    edge = (one_ref.shape[2] - two_ref.shape[2]) // 2
    groups = two_ref.shape[2] // group
    first = first_ref[0]
    total = first_ref[1]
    one_ref[:, :, :edge] = jnp.zeros(one_ref.shape[:2] + (edge,), one_ref.dtype)
    one_ref[:, :, edge + two_ref.shape[2] :] = jnp.zeros(
        one_ref.shape[:2] + (edge,), one_ref.dtype
    )

    def store(ref, start, count, lanes, value, reach):
        value = jnp.maximum(value, 0.0).reshape(count, planes, group)
        for row in range(count):
            place = first + (start + row - reach)
            kept = jnp.where((place >= 0) & (place < total), value[row], 0.0)
            ref[start + row, :, lanes] = kept.astype(ref.dtype)

    def first_layer(index, carry):
        lanes = pl.ds(pl.multiple_of(index * group, group), group)
        placed = pl.ds(pl.multiple_of(edge + index * group, 128), group)
        count = chunk_rows(one_ref.shape[0])
        for start in range(0, one_ref.shape[0], count):
            lhs = chained([features_ref[start + tap : start + tap + count] for tap in range(3)])
            value = jnp.dot(lhs, weight_first_ref[:, lanes], preferred_element_type=jnp.float32)
            store(one_ref, start, count, placed, value + bias_first_ref[:, lanes], 2)
        return carry

    lax.fori_loop(0, groups, first_layer, 0)

    def shifted(value, plane, step):
        rows = value.shape[0]
        if step > 0:
            return jnp.where(plane == 0, 0.0, pltpu.roll(value, 1, 0))
        return jnp.where(plane == planes - 1, 0.0, pltpu.roll(value, rows - 1, 0))

    def plane_index(count, lanes):
        return lax.broadcasted_iota(jnp.int32, (count, planes, lanes), 1).reshape(
            count * planes, lanes
        )

    def middle_layer(index, carry):
        lanes = pl.ds(pl.multiple_of(index * group, group), group)
        window = pl.ds(pl.multiple_of(index * group, group), group + 2 * edge)
        count = chunk_rows(two_ref.shape[0])
        plane = plane_index(count, group)
        for start in range(0, two_ref.shape[0], count):
            lhs = chained([one_ref[start + tap : start + tap + count, :, window] for tap in range(3)])
            value = jnp.dot(lhs, weight_middle_ref[...], preferred_element_type=jnp.float32)
            value = (
                value[:, group : 2 * group]
                + shifted(value[:, :group], plane, 1)
                + shifted(value[:, 2 * group :], plane, -1)
            )
            store(two_ref, start, count, lanes, value + bias_middle_ref[:, lanes], 1)
        return carry

    lax.fori_loop(0, groups, middle_layer, 0)

    count = chunk_rows(two_ref.shape[0])

    def last_layer(index, carry):
        start = index * count
        lhs = two_ref[pl.ds(start, count)].reshape(count * planes, two_ref.shape[2])
        value = jnp.dot(lhs, weight_last_ref[...], preferred_element_type=jnp.float32)
        taps_ref[pl.ds(start, count)] = value.reshape(count, planes, value.shape[1])
        return carry

    lax.fori_loop(0, two_ref.shape[0] // count, last_layer, 0)
    plane = plane_index(1, width)

    def last_sum(row):
        sums = []
        for plane_tap in range(3):
            running = None
            for row_tap in range(3):
                lanes = pl.ds((row_tap * 3 + plane_tap) * width, width)
                value = taps_ref[row + row_tap, :, lanes]
                running = value if running is None else running + value
            sums.append(running)
        value = sums[1] + shifted(sums[0], plane, 1) + shifted(sums[2], plane, -1)
        return prior_ref[row] + (value + bias_last_ref[...])

    if not turned_refs:
        for row in range(own_rows):
            out_ref[row] = last_sum(row)
        return

    turned_ref = turned_refs[0]
    for row in range(own_rows):
        turned_ref[pl.ds(row, width, stride=own_rows), :] = jnp.transpose(last_sum(row))
    blocks, _, x_count = out_ref.shape[:3]
    for block in range(blocks):
        for part in range(2):
            for inner in range(x_count):
                place = part * (width // 2) + block * x_count + inner
                out_ref[block, part, inner] = turned_ref[place * own_rows : (place + 1) * own_rows]


def banded(tiles, inner, outer, offset):
    shape = jnp.broadcast_shapes(tiles[0].shape, inner.shape, outer.shape)
    result = jnp.zeros(shape, jnp.bfloat16)
    for tap in range(3):
        result = jnp.where(inner - outer + offset == tap, tiles[tap], result)
    return result


def denoise(
    parts,
    features,
    prior_image,
    weight_first,
    bias_first,
    weight_middle,
    bias_middle,
    weight_last,
    bias_last,
):
    own_rows, planes, width = prior_image.shape
    turned = own_rows % 8 == 0
    out_shape = (parts, 2, width // (2 * parts), own_rows, planes) if turned else prior_image.shape
    readout = width // 2
    channels = weight_first.shape[3]
    span = readout * channels
    group = min(256, span)
    held = group // channels
    edge = 128
    reach = edge // channels
    window = group + 2 * edge

    def lane_place(count, inside):
        return jnp.arange(count * inside, dtype=jnp.int32) // inside

    tiles = jnp.transpose(weight_first, (2, 0, 1, 4, 3)).reshape(3, 18, 1, 1, channels)
    tiles = jnp.broadcast_to(tiles, (3, 18, 1, readout, channels)).reshape(3, 18, 1, span)
    first_table = banded(
        tiles,
        jnp.arange(readout, dtype=jnp.int32)[None, :, None],
        lane_place(readout, channels)[None, None, :],
        1,
    ).reshape(18 * readout, span)
    tiles = jnp.transpose(weight_middle, (2, 0, 4, 1, 3)).reshape(3, 3, 1, channels, 3, 1, channels)
    tiles = jnp.broadcast_to(tiles, (3, 3, 1, channels, 3, held, channels))
    tiles = tiles.reshape(3, 3, 1, channels, 3 * group)
    middle_table = banded(
        tiles,
        jnp.arange(window // channels, dtype=jnp.int32)[None, :, None, None] - reach,
        jnp.tile(lane_place(held, channels), 3)[None, None, None, :],
        1,
    ).reshape(3 * window, 3 * group)
    tiles = jnp.transpose(weight_last, (2, 4, 0, 1, 3)).reshape(3, 1, channels, 18, 1)
    tiles = jnp.broadcast_to(tiles, (3, 1, channels, 18, readout)).reshape(
        3, 1, channels, 18 * readout
    )
    last_table = banded(
        tiles,
        jnp.arange(readout, dtype=jnp.int32)[:, None, None],
        jnp.tile(jnp.arange(readout, dtype=jnp.int32), 18)[None, None, :],
        1,
    ).reshape(span, 18 * readout)

    rim = jnp.zeros_like(features[:, :1])
    features = jnp.concatenate(
        [
            jnp.concatenate([rim, features[:, :-1]], axis=1),
            features,
            jnp.concatenate([features[:, 1:], rim], axis=1),
        ],
        axis=2,
    )
    total = own_rows * lax.axis_size("slab") * lax.axis_size("coil")
    first = lax.axis_index(axes) * own_rows
    places = jnp.stack([first, jnp.asarray(total)]).astype(jnp.int32)
    vmem = pl.BlockSpec(memory_space=pltpu.VMEM)
    flops = 2 * own_rows * planes * (
        features.shape[2] * 3 * span * 3 // 2 + 9 * span * 512 * 5 // 4 + span * 18 * readout * 5 // 4
    )
    return pl.pallas_call(
        functools.partial(denoise_kernel, group),
        in_specs=[pl.BlockSpec(memory_space=pltpu.SMEM)] + [vmem] * 8,
        out_specs=vmem,
        out_shape=jax.ShapeDtypeStruct(out_shape, jnp.float32),
        scratch_shapes=[
            pltpu.VMEM((own_rows + 4, planes, span + 2 * edge), jnp.bfloat16),
            pltpu.VMEM((own_rows + 2, planes, span), jnp.bfloat16),
            pltpu.VMEM((own_rows + 2, planes, 18 * readout), jnp.float32),
        ]
        + [pltpu.VMEM((width * own_rows, planes), jnp.float32)] * turned,
        compiler_params=pltpu.CompilerParams(vmem_limit_bytes=40 * 1024 * 1024),
        cost_estimate=pl.CostEstimate(
            flops=int(flops), bytes_accessed=16 * 1024 * 1024, transcendentals=0
        ),
        name="denoise",
    )(
        places,
        features,
        prior_image,
        first_table,
        jnp.tile(bias_first, readout)[None, :],
        middle_table,
        jnp.tile(bias_middle, readout)[None, :],
        last_table,
        jnp.repeat(bias_last, readout)[None, :],
    )


def table_parts(table):
    high = table.astype(jnp.bfloat16)
    low = (table - high.astype(np.float64)).astype(jnp.bfloat16)
    return high, low


def dft_parts(length):
    positions = np.arange(length, dtype=np.int64)
    angles = (positions[:, None] * positions[None, :] % length) * (2.0 * math.pi / length)
    scale = 1.0 / math.sqrt(length)
    return np.cos(angles) * scale, np.sin(angles) * scale


def turn_block(length):
    cos_part, sin_part = dft_parts(length)
    return np.concatenate(
        [
            np.concatenate([cos_part, sin_part], axis=1),
            np.concatenate([-sin_part, cos_part], axis=1),
        ],
        axis=0,
    )


def dft_table(rows, planes):
    rows_high, rows_low = table_parts(turn_block(rows))
    planes_parts = np.concatenate(table_parts(turn_block(planes).T), axis=0)
    short = max(2 * rows - planes_parts.shape[0], 0)
    planes_parts = np.pad(planes_parts, ((0, short), (0, 0)))
    return np.concatenate([rows_high, rows_low, planes_parts], axis=1)


def half_tables(rows, planes):
    rows_parts = np.concatenate(table_parts(turn_block(rows // 2) * math.sqrt(0.5)), axis=1)
    planes_parts = np.concatenate(table_parts(turn_block(planes).T), axis=0)
    angles = np.arange(rows // 2) * (2.0 * math.pi / rows)
    turns = np.stack([np.cos(angles), np.sin(angles)])[:, :, None]
    turns = np.broadcast_to(turns, (2, rows // 2, planes)).astype(np.float32)
    return [rows_parts, planes_parts, turns]


def value_parts(value):
    high = value.astype(jnp.bfloat16)
    low = (value - high.astype(jnp.float32)).astype(jnp.bfloat16)
    return high, low


def tables_of(ref, rows, planes):
    high, low = ref[:, : 2 * rows], ref[:, 2 * rows : 4 * rows]
    row_table = jnp.concatenate([high, low, high], axis=1)
    high, low = ref[: 2 * planes, 4 * rows :], ref[2 * planes : 4 * planes, 4 * rows :]
    return row_table, jnp.concatenate([high, low, high], axis=0)


def along_planes(fields, table):
    rows, planes = fields[0][0].shape
    stacked = jnp.concatenate([jnp.concatenate(field, axis=1) for field in fields], axis=0)
    high, low = value_parts(stacked)
    moved = jnp.dot(
        jnp.concatenate([high, high, low], axis=1), table, preferred_element_type=jnp.float32
    )
    return [
        (
            moved[index * rows : (index + 1) * rows, :planes],
            moved[index * rows : (index + 1) * rows, planes:],
        )
        for index in range(len(fields))
    ]


def side_by_side(fields):
    return jnp.concatenate(
        [jnp.concatenate([field[part] for field in fields], axis=1) for part in range(2)], axis=0
    )


def along_rows(table, fields):
    rows, planes = fields[0][0].shape
    high, low = value_parts(side_by_side(fields))
    moved = jnp.dot(
        table, jnp.concatenate([high, high, low], axis=0), preferred_element_type=jnp.float32
    )
    return apart(moved, len(fields))


def apart(moved, count):
    rows = moved.shape[0] // 2
    planes = moved.shape[1] // count
    return [
        (
            moved[:rows, index * planes : (index + 1) * planes],
            moved[rows:, index * planes : (index + 1) * planes],
        )
        for index in range(count)
    ]


def plane_of(ref, part):
    value = ref[:, part, 0]
    return value.reshape(value.shape[0] * value.shape[1], value.shape[2])


def coil_plane(ref, coil):
    value = ref[:, coil, 0]
    return value.reshape(value.shape[0] * value.shape[1], value.shape[2])


def map_of(refs, coil):
    return [coil_plane(ref, coil).astype(jnp.float32) for ref in refs]


def spectrum_plane(ref, coil, rows):
    value = ref[:, coil, 0]
    slabs, held, lanes = value.shape
    planes = held * lanes // rows
    pieces = [
        value[:, first : first + planes].reshape(slabs * planes, lanes)
        for first in range(0, held, planes)
    ]
    return jnp.concatenate(pieces, axis=1)


def image_sums(maps, fields):
    sums = None
    for (map_real, map_imag), (real, imag) in zip(maps, fields):
        terms = (map_real * real - map_imag * imag, -(map_real * imag + map_imag * real))
        sums = terms if sums is None else (sums[0] + terms[0], sums[1] + terms[1])
    return sums


def units_of(refs):
    count = refs[0].shape[1]
    held = 2 if count % 2 == 0 else 1
    return [tuple(range(first, first + held)) for first in range(0, count, held)]


def halved(fields, turns):
    evens, odds = [], []
    rows = fields[0][0].shape[0] // 2
    for real, imag in fields:
        evens.append((real[:rows] + real[rows:], imag[:rows] + imag[rows:]))
        real, imag = real[:rows] - real[rows:], imag[:rows] - imag[rows:]
        odds.append((real * turns[0] + imag * turns[1], imag * turns[0] - real * turns[1]))
    return evens, odds


def rejoined(evens, odds, turns):
    fields = []
    for (even_real, even_imag), (real, imag) in zip(evens, odds):
        real, imag = real * turns[0] + imag * turns[1], imag * turns[0] - real * turns[1]
        fields.append(
            (
                jnp.concatenate([even_real + real, even_real - real], axis=0),
                jnp.concatenate([even_imag + imag, even_imag - imag], axis=0),
            )
        )
    return fields


def masked(fields, mask):
    return [(real * mask, imag * -mask) for real, imag in fields]


def in_groups(values, size):
    return [values[first : first + size] for first in range(0, len(values), size)]


def normal_sums(maps_refs, real, imag, mask_ref, rows_ref, planes_ref, turns_ref):
    half = rows_ref.shape[1] // 2
    row_table = jnp.concatenate([rows_ref[:, :half], rows_ref[:, half:], rows_ref[:, :half]], axis=1)
    half = planes_ref.shape[0] // 2
    plane_table = jnp.concatenate([planes_ref[:half], planes_ref[half:], planes_ref[:half]], axis=0)
    turns = turns_ref[0], turns_ref[1]
    half = turns[0].shape[0]
    masks = tuple(mask_ref[pl.ds(odd, half, stride=2), :] for odd in range(2))
    coils = list(range(maps_refs[0].shape[1]))
    fields = []
    for group in in_groups(coils, 4):
        products = []
        for coil in group:
            map_real, map_imag = map_of(maps_refs, coil)
            products.append(
                (map_real * real - map_imag * imag, map_real * imag + map_imag * real)
            )
        fields += along_planes(products, plane_table)
    units = [halved(unit, turns) for unit in in_groups(fields, 2)]
    units = [[along_rows(row_table, part) for part in unit] for unit in units]
    units = [[masked(part, mask) for part, mask in zip(unit, masks)] for unit in units]
    units = [[along_rows(row_table, part) for part in unit] for unit in units]
    fields = sum((rejoined(*unit, turns) for unit in units), [])
    images = []
    for group in in_groups(fields, 4):
        images += along_planes(group, plane_table)
    total = None
    for group in in_groups(coils, 2):
        sums = image_sums(
            [map_of(maps_refs, coil) for coil in group], [images[coil] for coil in group]
        )
        total = sums if total is None else (total[0] + sums[0], total[1] + sums[1])
    return total


def accumulate(out_ref, values, places):
    shape = out_ref.shape[0], out_ref.shape[-2], out_ref.shape[-1]

    @pl.when(pl.program_id(1) == 0)
    def _():
        for value, place in zip(values, places):
            out_ref[(slice(None),) + place] = value.reshape(shape)

    @pl.when(pl.program_id(1) > 0)
    def _():
        for value, place in zip(values, places):
            out_ref[(slice(None),) + place] += value.reshape(shape)


def adjoint_kernel(
    spectra_real_ref, spectra_imag_ref, maps_real_ref, maps_imag_ref, mask_ref, table_ref, out_ref
):
    maps_refs = maps_real_ref, maps_imag_ref
    mask = mask_ref[...]
    rows, planes = mask.shape
    row_table, plane_table = tables_of(table_ref, rows, planes)
    units = units_of(maps_refs)
    images = []
    for unit in units:
        spectra = []
        for coil in unit:
            real, imag = (
                jnp.transpose(spectrum_plane(ref, coil, rows).astype(jnp.float32))
                for ref in (spectra_real_ref, spectra_imag_ref)
            )
            spectra.append((real * mask, imag * -mask))
        spectrum = side_by_side(spectra).astype(jnp.bfloat16)
        moved = jnp.dot(
            row_table[:, : 4 * rows],
            jnp.concatenate([spectrum, spectrum], axis=0),
            preferred_element_type=jnp.float32,
        )
        images.append(apart(moved, len(unit)))
    images = [along_planes(image, plane_table) for image in images]
    total = None
    for unit, image in zip(units, images):
        sums = image_sums([map_of(maps_refs, coil) for coil in unit], image)
        total = sums if total is None else (total[0] + sums[0], total[1] + sums[1])
    accumulate(out_ref, total, ((0, 0), (1, 0)))


def product_kernel(maps_real_ref, maps_imag_ref, field_ref, *refs):
    constants, out_ref = refs[:-1], refs[-1]
    fields = [plane_of(field_ref, part) for part in range(2)]
    accumulate(
        out_ref,
        normal_sums((maps_real_ref, maps_imag_ref), *fields, *constants),
        ((0, 0), (1, 0)),
    )


def lane_sums(left, other):
    return jnp.sum(left[0] * other[0] + left[1] * other[1], axis=0, keepdims=True)


def twice_kernel(maps_real_ref, maps_imag_ref, adjoint_ref, denoised_ref, *refs):
    constants, out_ref = refs[:-1], refs[-1]
    maps_refs = maps_real_ref, maps_imag_ref
    x_index = pl.program_id(0)
    x_count = pl.num_programs(0)
    blocks, block_rows, planes = out_ref.shape[0], out_ref.shape[2], out_ref.shape[3]
    shape = blocks, block_rows, planes
    rights = [
        plane_of(adjoint_ref, part) + penalty * plane_of(denoised_ref, part) for part in range(2)
    ]
    fields = normal_sums(maps_refs, *rights, *constants)
    images = normal_sums(maps_refs, *fields, *constants)
    for part in range(2):
        out_ref[:, part * x_count + x_index] = images[part].reshape(shape)
        out_ref[:, (2 + part) * x_count + x_index] = fields[part].reshape(shape)
    totals = jnp.concatenate(
        [
            lane_sums(rights, rights),
            lane_sums(rights, fields),
            lane_sums(fields, fields),
            lane_sums(fields, images),
            jnp.zeros((block_rows - 4, planes), jnp.float32),
        ],
        axis=0,
    )[None]

    @pl.when(x_index == 0)
    def _():
        out_ref[:, 4 * x_count] = jnp.broadcast_to(totals, shape)

    @pl.when(x_index > 0)
    def _():
        out_ref[:, 4 * x_count] += totals


def held_coils(count):
    return max(size for size in (1, 2, 4, 8) if count % size == 0)


def whole(shape):
    return pl.BlockSpec(shape, lambda x, c: (0,) * len(shape))


def coils_spec(planes):
    values, first = planes
    slabs, coils, _, rows, lanes = values.shape
    return pl.BlockSpec(
        (slabs, held_coils(coils), 1, rows, lanes), lambda x, c: (0, c, first + x, 0, 0)
    )


def field_spec(shape):
    return pl.BlockSpec((shape[0], 2, 1) + shape[3:], lambda x, c: (0, 0, x, 0, 0))


def compute_params():
    return pltpu.CompilerParams(
        dimension_semantics=("arbitrary", "arbitrary"), vmem_limit_bytes=22 * 1024 * 1024
    )


def product_call(kernel, name, x_count, coil_planes, fields, extras, constants, outs, passes):
    coils = coil_planes[0][0].shape[1]
    mask = constants[0]
    rows, planes = mask.shape
    flops = 2 * 2 * rows * planes * (2 * rows + 2 * planes) * coils * x_count * passes
    values = [planes_of[0] for planes_of in coil_planes] + fields + extras + constants
    return pl.pallas_call(
        kernel,
        grid=(x_count, coils // held_coils(coils)),
        in_specs=[coils_spec(planes_of) for planes_of in coil_planes]
        + [field_spec(field.shape) for field in fields]
        + [whole(value.shape) for value in extras + constants],
        out_specs=[spec for spec, _ in outs],
        out_shape=[jax.ShapeDtypeStruct(shape, jnp.float32) for _, shape in outs],
        compiler_params=compute_params(),
        cost_estimate=pl.CostEstimate(
            flops=int(flops), bytes_accessed=8 * 1024 * 1024, transcendentals=0
        ),
        name=name,
    )(*values)


def adjoint_call(spectra, maps, constants, x_count, blocks):
    rows, planes = constants[0].shape
    shape = (blocks, 2, x_count, rows // blocks, planes)
    outs = [(field_spec(shape), shape)]
    return product_call(
        adjoint_kernel, "adjoint", x_count, spectra + maps, [], [], constants, outs, 3
    )[0]


def once_call(maps, field, constants):
    shape = field.shape
    outs = [(field_spec(shape), shape)]
    return product_call(
        product_kernel, "product", shape[2], maps, [field], [], constants, outs, 6
    )[0]


def twice_call(maps, adjoint, denoised, constants):
    blocks, _, x_count, block_rows, planes = adjoint.shape
    shape = (blocks, 4 * x_count + 1, block_rows, planes)
    outs = [(whole(shape), shape)]
    return product_call(
        twice_kernel, "products", x_count, maps, [adjoint, denoised], [], constants, outs, 12
    )[0]


def pack_kernel(maps_ref, kspace_ref, prior_ref, order_ref, out_ref, features_ref, *rows_refs):
    rows, planes, width = maps_ref.shape[1:]
    parts, held = out_ref.shape[:2]
    held = held // 2
    for kind, (ref, rows_ref) in enumerate(zip((maps_ref, kspace_ref), rows_refs)):
        for row in range(0, rows, 2):
            moved = lax.dot_general(
                order_ref[...],
                ref[0, row : row + 2].reshape(2 * planes, width),
                (((1,), (1,)), ((), ())),
                preferred_element_type=jnp.float32,
            )
            for odd in range(2):
                lanes = slice(odd * planes, (odd + 1) * planes)
                rows_ref[pl.ds(row + odd, width, stride=rows), :] = moved[:, lanes]
        for part in range(parts):
            for inner in range(held):
                place = (part * held + inner) * rows
                out_ref[part, kind * held + inner] = rows_ref[place : place + rows].astype(
                    out_ref.dtype
                )
    features_ref[...] = prior_ref[...].astype(features_ref.dtype)


def pack_call(maps, kspace, prior, parts):
    _, slab_rows, planes, width = maps.shape
    slab_planes = kspace.shape[1]
    chunk = 16
    count = slab_rows // chunk
    inside = slab_planes // chunk
    held = width // parts
    lanes = np.arange(width).reshape(2, parts, held // 2).transpose(1, 0, 2).reshape(-1)
    order = (lanes[:, None] == np.arange(width)[None, :]).astype(jnp.bfloat16)
    shape = (parts, 2 * held, slab_rows, planes)
    return pl.pallas_call(
        pack_kernel,
        grid=(count,),
        in_specs=[
            pl.BlockSpec((1, chunk, planes, width), lambda g: (0, g, 0, 0)),
            pl.BlockSpec((1, chunk, planes, width), lambda g: (0, g % inside, g // inside, 0)),
            pl.BlockSpec(prior.shape, lambda g: (0, 0, 0)),
            pl.BlockSpec(order.shape, lambda g: (0, 0)),
        ],
        out_specs=[
            pl.BlockSpec((parts, 2 * held, chunk, planes), lambda g: (0, 0, g, 0)),
            pl.BlockSpec(prior.shape, lambda g: (0, 0, 0)),
        ],
        out_shape=[
            jax.ShapeDtypeStruct(shape, jnp.bfloat16),
            jax.ShapeDtypeStruct(prior.shape, jnp.bfloat16),
        ],
        scratch_shapes=[pltpu.VMEM((width * chunk, planes), jnp.float32)] * 2,
        compiler_params=pltpu.CompilerParams(vmem_limit_bytes=24 * 1024 * 1024),
        cost_estimate=pl.CostEstimate(
            flops=4 * maps.size * width, bytes_accessed=8 * maps.size, transcendentals=0
        ),
        name="pack",
    )(maps, kspace, prior, jnp.asarray(order))


def exchange(blocks, axis):
    return lax.all_to_all(blocks, axis, split_axis=0, concat_axis=0, tiled=True)


def x_first(cells, parts):
    rows, planes, width = cells.shape
    split = cells.reshape(rows, planes, 2, parts, width // (2 * parts))
    return jnp.transpose(split, (3, 2, 4, 0, 1))


def x_last(blocks):
    parts, _, x_count, rows, planes = blocks.shape
    return jnp.transpose(blocks, (3, 4, 1, 0, 2)).reshape(rows, planes, 2 * parts * x_count)


def factors(right_right, right_field, field_field, field_image):
    ratio = right_field / right_right
    alpha = right_right / (right_field + penalty * right_right)
    fresh = alpha * alpha * (field_field - ratio * right_field)
    weight = alpha * ratio + fresh / right_right
    mixed = weight * alpha
    curvature = (
        weight * weight * right_field - 2.0 * mixed * field_field + alpha * alpha * field_image
    ) + penalty * (
        weight * weight * right_right - 2.0 * mixed * right_field + alpha * alpha * field_field
    )
    second = fresh / curvature
    moved = alpha + second * weight
    bent = second * alpha
    return (moved, -bent), (alpha * ratio - penalty * second * weight, penalty * bent - moved, bent)


def finish_kernel(
    adjoint_ref, denoised_ref, moved_ref, solution_ref, residual_ref, rows_ref
):
    blocks, _, x_count, rows, planes = adjoint_ref.shape
    readout = blocks * x_count
    totals = jnp.sum(jnp.sum(moved_ref[:, 4 * x_count], axis=0), axis=1, keepdims=True)
    found = factors(*(totals[index : index + 1] for index in range(4)))
    for out_ref, scales in zip((solution_ref, residual_ref), found):
        scales = [jnp.broadcast_to(scale, (rows, planes))[None] for scale in scales]
        for part in range(2):
            for inner in range(x_count):
                right = adjoint_ref[:, part, inner] + penalty * denoised_ref[:, part, inner]
                value = (
                    scales[0] * right
                    + scales[1] * moved_ref[:, (2 + part) * x_count + inner]
                )
                if len(scales) > 2:
                    value = value + scales[2] * moved_ref[:, part * x_count + inner]
                for block in range(blocks):
                    place = part * readout + block * x_count + inner
                    rows_ref[place * rows : (place + 1) * rows] = value[block]
        for row in range(rows):
            out_ref[row] = jnp.transpose(rows_ref[pl.ds(row, 2 * readout, stride=rows), :])


def finish_call(adjoint, denoised, moved):
    blocks, _, x_count, rows, planes = adjoint.shape
    shape = (rows, planes, 2 * blocks * x_count)
    vmem = pl.BlockSpec(memory_space=pltpu.VMEM)
    return pl.pallas_call(
        finish_kernel,
        in_specs=[vmem] * 3,
        out_specs=[vmem] * 2,
        out_shape=[jax.ShapeDtypeStruct(shape, jnp.float32)] * 2,
        scratch_shapes=[pltpu.VMEM((2 * blocks * x_count * rows, planes), jnp.float32)],
        compiler_params=pltpu.CompilerParams(vmem_limit_bytes=32 * 1024 * 1024),
        cost_estimate=pl.CostEstimate(
            flops=8 * adjoint.size, bytes_accessed=24 * adjoint.size, transcendentals=0
        ),
        name="finish",
    )(adjoint, denoised, moved)


def body(
    prior_image,
    coil_maps,
    kspace,
    sampling,
    weight_first,
    bias_first,
    weight_middle,
    bias_middle,
    weight_last,
    bias_last,
):
    readout = prior_image.shape[2] // 2
    own_rows = prior_image.shape[0]
    planes = prior_image.shape[1]
    slabs = lax.axis_size("slab")
    coils = lax.axis_size("coil")
    devices = slabs * coils
    spread = readout % devices == 0 and own_rows % 8 == 0 and held_coils(coils) == coils
    spread = spread and coil_maps.shape[1] % 16 == 0
    spread = spread and kspace.shape[1] % 16 == 0 and kspace.shape[2] % planes == 0
    parts = devices if spread else coils
    x_count = readout // parts
    if spread:
        packed, features = pack_call(coil_maps, kspace, prior_image, parts)
    else:
        features = prior_image.astype(jnp.bfloat16)
    mask = lax.all_gather(sampling.astype(jnp.bfloat16), "slab", axis=0, tiled=True)
    features, mask = lax.optimization_barrier((with_halo(features, 3), mask))
    mask = jnp.transpose(mask).astype(jnp.float32)
    row_count = mask.shape[0]
    constants = [mask] + half_tables(row_count, planes)
    constants = [jnp.asarray(value) for value in constants]
    adjoint_constants = [mask, jnp.asarray(dft_table(row_count, planes))]

    def coils_to_x(values):
        blocks = x_first(values, parts)
        tail = (2 * x_count,) + blocks.shape[3:]
        blocks = exchange(blocks, "coil").reshape((slabs, coils // slabs) + tail)
        blocks = exchange(blocks, "slab")
        return [(blocks, 0), (blocks, x_count)]

    if spread:
        arrived = exchange(packed, axes)
        arrived = arrived.reshape((slabs, coils) + arrived.shape[1:])
        maps = [(arrived, 0), (arrived, x_count)]
        spectra = [(arrived, 2 * x_count), (arrived, 3 * x_count)]
    else:
        maps = coils_to_x(coil_maps[0])
        spectra = coils_to_x(kspace[0])

    blocks = denoise(
        parts,
        features,
        prior_image,
        weight_first,
        bias_first,
        weight_middle,
        bias_middle,
        weight_last,
        bias_last,
    )
    if blocks.ndim == 3:
        blocks = x_first(blocks, parts)
    if spread:
        adjoint = adjoint_call(spectra, maps, adjoint_constants, x_count, devices)
        payload, adjoint_back = lax.optimization_barrier(
            (
                twice_call(maps, adjoint, exchange(blocks, axes), constants),
                exchange(adjoint, axes),
            )
        )
        payload = exchange(payload, axes)
        return tuple(finish_call(adjoint_back, blocks, payload))

    tail = blocks.shape[1:3]

    def whole_rows(parts_in):
        moved = lax.all_gather(exchange(parts_in, "coil"), "slab", axis=0, tiled=True)
        return jnp.transpose(moved, (1, 2, 0, 3, 4)).reshape((1,) + tail + (-1, planes))

    def own_part(whole):
        rows = whole.shape[3] // slabs
        mine = lax.dynamic_slice_in_dim(whole, lax.axis_index("slab") * rows, rows, axis=3)
        split = jnp.transpose(mine.reshape(tail + (coils, own_rows, planes)), (2, 0, 1, 3, 4))
        return x_last(exchange(split, "coil"))

    adjoint = lax.psum(adjoint_call(spectra, maps, adjoint_constants, x_count, 1), "slab")
    right = adjoint + penalty * whole_rows(blocks)
    field = lax.psum(once_call(maps, right, constants), "slab")
    image = lax.psum(once_call(maps, field, constants), "slab")
    squares = lax.psum(
        jnp.stack(
            [
                jnp.sum(right * right),
                jnp.sum(right * field),
                jnp.sum(field * field),
                jnp.sum(field * image),
            ]
        ),
        "coil",
    )
    scales, others = factors(*(squares[index] for index in range(4)))
    right, field, image = own_part(right), own_part(field), own_part(image)
    return (
        scales[0] * right + scales[1] * field,
        others[0] * right + others[1] * field + others[2] * image,
    )


def solution(mesh):
    placed = (
        P(("slab", "coil"), None, None),
        P("coil", "slab", None, None),
        P("coil", "slab", None, None),
        P("slab", None),
        P(),
        P(),
        P(),
        P(),
        P(),
        P(),
    )
    return jax.shard_map(
        body,
        mesh=mesh,
        in_specs=placed,
        out_specs=(P(("slab", "coil"), None, None), P(("slab", "coil"), None, None)),
        check_vma=False,
    )
```

```python
import functools
import math

import jax
import jax.numpy as jnp
import numpy as np
from jax import lax
from jax.experimental import pallas as pl
from jax.experimental.pallas import tpu as pltpu
from jax.sharding import PartitionSpec as P

CG_ITERS = 2


penalty = 0.5
axes = ("slab", "coil")


def with_halo(cells, width):
    rows = cells.shape[0]
    count = lax.axis_size("slab") * lax.axis_size("coil")
    above, below = [], []
    for hop in range(1, -(-width // rows) + 1):
        taken = min(width - (hop - 1) * rows, rows)
        ends = count - hop
        tail = lax.slice_in_dim(cells, rows - taken, rows, axis=0)
        head = lax.slice_in_dim(cells, 0, taken, axis=0)
        above.insert(0, lax.ppermute(tail, axes, [(i, i + hop) for i in range(ends)]))
        below.append(lax.ppermute(head, axes, [(i + hop, i) for i in range(ends)]))
    return jnp.concatenate(above + [cells] + below, axis=0)


def chunk_rows(rows):
    return max(size for size in range(1, 13) if rows % size == 0)


def chained(lhs_pieces):
    rows = lhs_pieces[0].shape[0] * lhs_pieces[0].shape[1]
    lhs = jnp.concatenate(lhs_pieces, axis=2)
    return lhs.reshape(rows, lhs.shape[2])


def denoise_kernel(
    group,
    first_ref,
    features_ref,
    prior_ref,
    weight_first_ref,
    bias_first_ref,
    weight_middle_ref,
    bias_middle_ref,
    weight_last_ref,
    bias_last_ref,
    out_ref,
    one_ref,
    two_ref,
    taps_ref,
    *turned_refs,
):
    own_rows, planes, width = prior_ref.shape
    edge = (one_ref.shape[2] - two_ref.shape[2]) // 2
    groups = two_ref.shape[2] // group
    first = first_ref[0]
    total = first_ref[1]
    one_ref[:, :, :edge] = jnp.zeros(one_ref.shape[:2] + (edge,), one_ref.dtype)
    one_ref[:, :, edge + two_ref.shape[2] :] = jnp.zeros(
        one_ref.shape[:2] + (edge,), one_ref.dtype
    )

    def store(ref, start, count, lanes, value, reach):
        value = jnp.maximum(value, 0.0).reshape(count, planes, group)
        for row in range(count):
            place = first + (start + row - reach)
            kept = jnp.where((place >= 0) & (place < total), value[row], 0.0)
            ref[start + row, :, lanes] = kept.astype(ref.dtype)

    def first_layer(index, carry):
        lanes = pl.ds(pl.multiple_of(index * group, group), group)
        placed = pl.ds(pl.multiple_of(edge + index * group, 128), group)
        count = chunk_rows(one_ref.shape[0])
        for start in range(0, one_ref.shape[0], count):
            lhs = chained([features_ref[start + tap : start + tap + count] for tap in range(3)])
            value = jnp.dot(lhs, weight_first_ref[:, lanes], preferred_element_type=jnp.float32)
            store(one_ref, start, count, placed, value + bias_first_ref[:, lanes], 2)
        return carry

    lax.fori_loop(0, groups, first_layer, 0)

    def shifted(value, plane, step):
        rows = value.shape[0]
        if step > 0:
            return jnp.where(plane == 0, 0.0, pltpu.roll(value, 1, 0))
        return jnp.where(plane == planes - 1, 0.0, pltpu.roll(value, rows - 1, 0))

    def plane_index(count, lanes):
        return lax.broadcasted_iota(jnp.int32, (count, planes, lanes), 1).reshape(
            count * planes, lanes
        )

    def middle_layer(index, carry):
        lanes = pl.ds(pl.multiple_of(index * group, group), group)
        window = pl.ds(pl.multiple_of(index * group, group), group + 2 * edge)
        count = chunk_rows(two_ref.shape[0])
        plane = plane_index(count, group)
        for start in range(0, two_ref.shape[0], count):
            lhs = chained([one_ref[start + tap : start + tap + count, :, window] for tap in range(3)])
            value = jnp.dot(lhs, weight_middle_ref[...], preferred_element_type=jnp.float32)
            value = (
                value[:, group : 2 * group]
                + shifted(value[:, :group], plane, 1)
                + shifted(value[:, 2 * group :], plane, -1)
            )
            store(two_ref, start, count, lanes, value + bias_middle_ref[:, lanes], 1)
        return carry

    lax.fori_loop(0, groups, middle_layer, 0)

    count = chunk_rows(two_ref.shape[0])

    def last_layer(index, carry):
        start = index * count
        lhs = two_ref[pl.ds(start, count)].reshape(count * planes, two_ref.shape[2])
        value = jnp.dot(lhs, weight_last_ref[...], preferred_element_type=jnp.float32)
        taps_ref[pl.ds(start, count)] = value.reshape(count, planes, value.shape[1])
        return carry

    lax.fori_loop(0, two_ref.shape[0] // count, last_layer, 0)
    plane = plane_index(1, width)

    def last_sum(row):
        sums = []
        for plane_tap in range(3):
            running = None
            for row_tap in range(3):
                lanes = pl.ds((row_tap * 3 + plane_tap) * width, width)
                value = taps_ref[row + row_tap, :, lanes]
                running = value if running is None else running + value
            sums.append(running)
        value = sums[1] + shifted(sums[0], plane, 1) + shifted(sums[2], plane, -1)
        return prior_ref[row] + (value + bias_last_ref[...])

    if not turned_refs:
        for row in range(own_rows):
            out_ref[row] = last_sum(row)
        return

    turned_ref = turned_refs[0]
    for row in range(own_rows):
        turned_ref[pl.ds(row, width, stride=own_rows), :] = jnp.transpose(last_sum(row))
    blocks, _, x_count = out_ref.shape[:3]
    for block in range(blocks):
        for part in range(2):
            for inner in range(x_count):
                place = part * (width // 2) + block * x_count + inner
                out_ref[block, part, inner] = turned_ref[place * own_rows : (place + 1) * own_rows]


def banded(tiles, inner, outer, offset):
    shape = jnp.broadcast_shapes(tiles[0].shape, inner.shape, outer.shape)
    result = jnp.zeros(shape, jnp.bfloat16)
    for tap in range(3):
        result = jnp.where(inner - outer + offset == tap, tiles[tap], result)
    return result


def denoise(
    parts,
    features,
    prior_image,
    weight_first,
    bias_first,
    weight_middle,
    bias_middle,
    weight_last,
    bias_last,
):
    own_rows, planes, width = prior_image.shape
    turned = own_rows % 8 == 0
    out_shape = (parts, 2, width // (2 * parts), own_rows, planes) if turned else prior_image.shape
    readout = width // 2
    channels = weight_first.shape[3]
    span = readout * channels
    group = min(256, span)
    held = group // channels
    edge = 128
    reach = edge // channels
    window = group + 2 * edge

    def lane_place(count, inside):
        return jnp.arange(count * inside, dtype=jnp.int32) // inside

    tiles = jnp.transpose(weight_first, (2, 0, 1, 4, 3)).reshape(3, 18, 1, 1, channels)
    tiles = jnp.broadcast_to(tiles, (3, 18, 1, readout, channels)).reshape(3, 18, 1, span)
    first_table = banded(
        tiles,
        jnp.arange(readout, dtype=jnp.int32)[None, :, None],
        lane_place(readout, channels)[None, None, :],
        1,
    ).reshape(18 * readout, span)
    tiles = jnp.transpose(weight_middle, (2, 0, 4, 1, 3)).reshape(3, 3, 1, channels, 3, 1, channels)
    tiles = jnp.broadcast_to(tiles, (3, 3, 1, channels, 3, held, channels))
    tiles = tiles.reshape(3, 3, 1, channels, 3 * group)
    middle_table = banded(
        tiles,
        jnp.arange(window // channels, dtype=jnp.int32)[None, :, None, None] - reach,
        jnp.tile(lane_place(held, channels), 3)[None, None, None, :],
        1,
    ).reshape(3 * window, 3 * group)
    tiles = jnp.transpose(weight_last, (2, 4, 0, 1, 3)).reshape(3, 1, channels, 18, 1)
    tiles = jnp.broadcast_to(tiles, (3, 1, channels, 18, readout)).reshape(
        3, 1, channels, 18 * readout
    )
    last_table = banded(
        tiles,
        jnp.arange(readout, dtype=jnp.int32)[:, None, None],
        jnp.tile(jnp.arange(readout, dtype=jnp.int32), 18)[None, None, :],
        1,
    ).reshape(span, 18 * readout)

    rim = jnp.zeros_like(features[:, :1])
    features = jnp.concatenate(
        [
            jnp.concatenate([rim, features[:, :-1]], axis=1),
            features,
            jnp.concatenate([features[:, 1:], rim], axis=1),
        ],
        axis=2,
    )
    total = own_rows * lax.axis_size("slab") * lax.axis_size("coil")
    first = lax.axis_index(axes) * own_rows
    places = jnp.stack([first, jnp.asarray(total)]).astype(jnp.int32)
    vmem = pl.BlockSpec(memory_space=pltpu.VMEM)
    flops = 2 * own_rows * planes * (
        features.shape[2] * 3 * span * 3 // 2 + 9 * span * 512 * 5 // 4 + span * 18 * readout * 5 // 4
    )
    return pl.pallas_call(
        functools.partial(denoise_kernel, group),
        in_specs=[pl.BlockSpec(memory_space=pltpu.SMEM)] + [vmem] * 8,
        out_specs=vmem,
        out_shape=jax.ShapeDtypeStruct(out_shape, jnp.float32),
        scratch_shapes=[
            pltpu.VMEM((own_rows + 4, planes, span + 2 * edge), jnp.bfloat16),
            pltpu.VMEM((own_rows + 2, planes, span), jnp.bfloat16),
            pltpu.VMEM((own_rows + 2, planes, 18 * readout), jnp.float32),
        ]
        + [pltpu.VMEM((width * own_rows, planes), jnp.float32)] * turned,
        compiler_params=pltpu.CompilerParams(vmem_limit_bytes=40 * 1024 * 1024),
        cost_estimate=pl.CostEstimate(
            flops=int(flops), bytes_accessed=16 * 1024 * 1024, transcendentals=0
        ),
        name="denoise",
    )(
        places,
        features,
        prior_image,
        first_table,
        jnp.tile(bias_first, readout)[None, :],
        middle_table,
        jnp.tile(bias_middle, readout)[None, :],
        last_table,
        jnp.repeat(bias_last, readout)[None, :],
    )


def table_parts(table):
    high = table.astype(jnp.bfloat16)
    low = (table - high.astype(np.float64)).astype(jnp.bfloat16)
    return high, low


def dft_parts(length):
    positions = np.arange(length, dtype=np.int64)
    angles = (positions[:, None] * positions[None, :] % length) * (2.0 * math.pi / length)
    scale = 1.0 / math.sqrt(length)
    return np.cos(angles) * scale, np.sin(angles) * scale


def turn_block(length):
    cos_part, sin_part = dft_parts(length)
    return np.concatenate(
        [
            np.concatenate([cos_part, sin_part], axis=1),
            np.concatenate([-sin_part, cos_part], axis=1),
        ],
        axis=0,
    )


def dft_table(rows, planes):
    rows_high, rows_low = table_parts(turn_block(rows))
    planes_parts = np.concatenate(table_parts(turn_block(planes).T), axis=0)
    short = max(2 * rows - planes_parts.shape[0], 0)
    planes_parts = np.pad(planes_parts, ((0, short), (0, 0)))
    return np.concatenate([rows_high, rows_low, planes_parts], axis=1)


def half_tables(rows, planes):
    rows_parts = np.concatenate(table_parts(turn_block(rows // 2) * math.sqrt(0.5)), axis=1)
    planes_parts = np.concatenate(table_parts(turn_block(planes).T), axis=0)
    angles = np.arange(rows // 2) * (2.0 * math.pi / rows)
    turns = np.stack([np.cos(angles), np.sin(angles)])[:, :, None]
    turns = np.broadcast_to(turns, (2, rows // 2, planes)).astype(np.float32)
    return [rows_parts, planes_parts, turns]


def value_parts(value):
    high = value.astype(jnp.bfloat16)
    low = (value - high.astype(jnp.float32)).astype(jnp.bfloat16)
    return high, low


def tables_of(ref, rows, planes):
    high, low = ref[:, : 2 * rows], ref[:, 2 * rows : 4 * rows]
    row_table = jnp.concatenate([high, low, high], axis=1)
    high, low = ref[: 2 * planes, 4 * rows :], ref[2 * planes : 4 * planes, 4 * rows :]
    return row_table, jnp.concatenate([high, low, high], axis=0)


def along_planes(fields, table):
    rows, planes = fields[0][0].shape
    stacked = jnp.concatenate([jnp.concatenate(field, axis=1) for field in fields], axis=0)
    high, low = value_parts(stacked)
    moved = jnp.dot(
        jnp.concatenate([high, high, low], axis=1), table, preferred_element_type=jnp.float32
    )
    return [
        (
            moved[index * rows : (index + 1) * rows, :planes],
            moved[index * rows : (index + 1) * rows, planes:],
        )
        for index in range(len(fields))
    ]


def side_by_side(fields):
    return jnp.concatenate(
        [jnp.concatenate([field[part] for field in fields], axis=1) for part in range(2)], axis=0
    )


def along_rows(table, fields):
    rows, planes = fields[0][0].shape
    high, low = value_parts(side_by_side(fields))
    moved = jnp.dot(
        table, jnp.concatenate([high, high, low], axis=0), preferred_element_type=jnp.float32
    )
    return apart(moved, len(fields))


def apart(moved, count):
    rows = moved.shape[0] // 2
    planes = moved.shape[1] // count
    return [
        (
            moved[:rows, index * planes : (index + 1) * planes],
            moved[rows:, index * planes : (index + 1) * planes],
        )
        for index in range(count)
    ]


def plane_of(ref, part):
    value = ref[:, part, 0]
    return value.reshape(value.shape[0] * value.shape[1], value.shape[2])


def coil_plane(ref, coil):
    value = ref[:, coil, 0]
    return value.reshape(value.shape[0] * value.shape[1], value.shape[2])


def map_of(refs, coil):
    return [coil_plane(ref, coil).astype(jnp.float32) for ref in refs]


def image_sums(maps, fields):
    sums = None
    for (map_real, map_imag), (real, imag) in zip(maps, fields):
        terms = (map_real * real - map_imag * imag, -(map_real * imag + map_imag * real))
        sums = terms if sums is None else (sums[0] + terms[0], sums[1] + terms[1])
    return sums


def units_of(refs):
    count = refs[0].shape[1]
    held = 2 if count % 2 == 0 else 1
    return [tuple(range(first, first + held)) for first in range(0, count, held)]


def halved(fields, turns):
    evens, odds = [], []
    rows = fields[0][0].shape[0] // 2
    for real, imag in fields:
        evens.append((real[:rows] + real[rows:], imag[:rows] + imag[rows:]))
        real, imag = real[:rows] - real[rows:], imag[:rows] - imag[rows:]
        odds.append((real * turns[0] + imag * turns[1], imag * turns[0] - real * turns[1]))
    return evens, odds


def rejoined(evens, odds, turns):
    fields = []
    for (even_real, even_imag), (real, imag) in zip(evens, odds):
        real, imag = real * turns[0] + imag * turns[1], imag * turns[0] - real * turns[1]
        fields.append(
            (
                jnp.concatenate([even_real + real, even_real - real], axis=0),
                jnp.concatenate([even_imag + imag, even_imag - imag], axis=0),
            )
        )
    return fields


def masked(fields, mask):
    return [(real * mask, imag * -mask) for real, imag in fields]


def in_groups(values, size):
    return [values[first : first + size] for first in range(0, len(values), size)]


def normal_sums(maps_refs, real, imag, mask_ref, rows_ref, planes_ref, turns_ref):
    half = rows_ref.shape[1] // 2
    row_table = jnp.concatenate([rows_ref[:, :half], rows_ref[:, half:], rows_ref[:, :half]], axis=1)
    half = planes_ref.shape[0] // 2
    plane_table = jnp.concatenate([planes_ref[:half], planes_ref[half:], planes_ref[:half]], axis=0)
    turns = turns_ref[0], turns_ref[1]
    half = turns[0].shape[0]
    masks = tuple(mask_ref[pl.ds(odd, half, stride=2), :] for odd in range(2))
    coils = list(range(maps_refs[0].shape[1]))
    fields = []
    for group in in_groups(coils, 4):
        products = []
        for coil in group:
            map_real, map_imag = map_of(maps_refs, coil)
            products.append(
                (map_real * real - map_imag * imag, map_real * imag + map_imag * real)
            )
        fields += along_planes(products, plane_table)
    units = [halved(unit, turns) for unit in in_groups(fields, 2)]
    units = [[along_rows(row_table, part) for part in unit] for unit in units]
    units = [[masked(part, mask) for part, mask in zip(unit, masks)] for unit in units]
    units = [[along_rows(row_table, part) for part in unit] for unit in units]
    fields = sum((rejoined(*unit, turns) for unit in units), [])
    images = []
    for group in in_groups(fields, 4):
        images += along_planes(group, plane_table)
    total = None
    for group in in_groups(coils, 2):
        sums = image_sums(
            [map_of(maps_refs, coil) for coil in group], [images[coil] for coil in group]
        )
        total = sums if total is None else (total[0] + sums[0], total[1] + sums[1])
    return total


def accumulate(out_ref, values, places):
    shape = out_ref.shape[0], out_ref.shape[-2], out_ref.shape[-1]

    @pl.when(pl.program_id(1) == 0)
    def _():
        for value, place in zip(values, places):
            out_ref[(slice(None),) + place] = value.reshape(shape)

    @pl.when(pl.program_id(1) > 0)
    def _():
        for value, place in zip(values, places):
            out_ref[(slice(None),) + place] += value.reshape(shape)


def adjoint_kernel(
    spectra_real_ref, spectra_imag_ref, maps_real_ref, maps_imag_ref, mask_ref, table_ref, out_ref
):
    maps_refs = maps_real_ref, maps_imag_ref
    mask = mask_ref[...]
    rows, planes = mask.shape
    row_table, plane_table = tables_of(table_ref, rows, planes)
    units = units_of(maps_refs)
    images = []
    for unit in units:
        spectra = []
        for coil in unit:
            real, imag = (
                jnp.transpose(coil_plane(ref, coil).astype(jnp.float32))
                for ref in (spectra_real_ref, spectra_imag_ref)
            )
            spectra.append((real * mask, imag * -mask))
        spectrum = side_by_side(spectra).astype(jnp.bfloat16)
        moved = jnp.dot(
            row_table[:, : 4 * rows],
            jnp.concatenate([spectrum, spectrum], axis=0),
            preferred_element_type=jnp.float32,
        )
        images.append(apart(moved, len(unit)))
    images = [along_planes(image, plane_table) for image in images]
    total = None
    for unit, image in zip(units, images):
        sums = image_sums([map_of(maps_refs, coil) for coil in unit], image)
        total = sums if total is None else (total[0] + sums[0], total[1] + sums[1])
    accumulate(out_ref, total, ((0, 0), (1, 0)))


def product_kernel(maps_real_ref, maps_imag_ref, field_ref, *refs):
    constants, out_ref = refs[:-1], refs[-1]
    fields = [plane_of(field_ref, part) for part in range(2)]
    accumulate(
        out_ref,
        normal_sums((maps_real_ref, maps_imag_ref), *fields, *constants),
        ((0, 0), (1, 0)),
    )


def lane_sums(left, other):
    return jnp.sum(left[0] * other[0] + left[1] * other[1], axis=0, keepdims=True)


def twice_kernel(maps_real_ref, maps_imag_ref, adjoint_ref, denoised_ref, *refs):
    constants, out_ref = refs[:-1], refs[-1]
    maps_refs = maps_real_ref, maps_imag_ref
    x_index = pl.program_id(0)
    x_count = pl.num_programs(0)
    blocks, block_rows, planes = out_ref.shape[0], out_ref.shape[2], out_ref.shape[3]
    shape = blocks, block_rows, planes
    rights = [
        plane_of(adjoint_ref, part) + penalty * plane_of(denoised_ref, part) for part in range(2)
    ]
    fields = normal_sums(maps_refs, *rights, *constants)
    images = normal_sums(maps_refs, *fields, *constants)
    for part in range(2):
        out_ref[:, part * x_count + x_index] = images[part].reshape(shape)
        out_ref[:, (2 + part) * x_count + x_index] = fields[part].reshape(shape)
    totals = jnp.concatenate(
        [
            lane_sums(rights, rights),
            lane_sums(rights, fields),
            lane_sums(fields, fields),
            lane_sums(fields, images),
            jnp.zeros((block_rows - 4, planes), jnp.float32),
        ],
        axis=0,
    )[None]

    @pl.when(x_index == 0)
    def _():
        out_ref[:, 4 * x_count] = jnp.broadcast_to(totals, shape)

    @pl.when(x_index > 0)
    def _():
        out_ref[:, 4 * x_count] += totals


def held_coils(count):
    return max(size for size in (1, 2, 4, 8) if count % size == 0)


def whole(shape):
    return pl.BlockSpec(shape, lambda x, c: (0,) * len(shape))


def coils_spec(planes):
    values, first = planes
    slabs, coils, _, rows, lanes = values.shape
    return pl.BlockSpec(
        (slabs, held_coils(coils), 1, rows, lanes), lambda x, c: (0, c, first + x, 0, 0)
    )


def field_spec(shape):
    return pl.BlockSpec((shape[0], 2, 1) + shape[3:], lambda x, c: (0, 0, x, 0, 0))


def compute_params():
    return pltpu.CompilerParams(
        dimension_semantics=("arbitrary", "arbitrary"), vmem_limit_bytes=22 * 1024 * 1024
    )


def product_call(kernel, name, x_count, coil_planes, fields, extras, constants, outs, passes):
    coils = coil_planes[0][0].shape[1]
    mask = constants[0]
    rows, planes = mask.shape
    flops = 2 * 2 * rows * planes * (2 * rows + 2 * planes) * coils * x_count * passes
    values = [planes_of[0] for planes_of in coil_planes] + fields + extras + constants
    return pl.pallas_call(
        kernel,
        grid=(x_count, coils // held_coils(coils)),
        in_specs=[coils_spec(planes_of) for planes_of in coil_planes]
        + [field_spec(field.shape) for field in fields]
        + [whole(value.shape) for value in extras + constants],
        out_specs=[spec for spec, _ in outs],
        out_shape=[jax.ShapeDtypeStruct(shape, jnp.float32) for _, shape in outs],
        compiler_params=compute_params(),
        cost_estimate=pl.CostEstimate(
            flops=int(flops), bytes_accessed=8 * 1024 * 1024, transcendentals=0
        ),
        name=name,
    )(*values)


def adjoint_call(spectra, maps, constants, x_count, blocks):
    rows, planes = constants[0].shape
    shape = (blocks, 2, x_count, rows // blocks, planes)
    outs = [(field_spec(shape), shape)]
    return product_call(
        adjoint_kernel, "adjoint", x_count, spectra + maps, [], [], constants, outs, 3
    )[0]


def once_call(maps, field, constants):
    shape = field.shape
    outs = [(field_spec(shape), shape)]
    return product_call(
        product_kernel, "product", shape[2], maps, [field], [], constants, outs, 6
    )[0]


def twice_call(maps, adjoint, denoised, constants):
    blocks, _, x_count, block_rows, planes = adjoint.shape
    shape = (blocks, 4 * x_count + 1, block_rows, planes)
    outs = [(whole(shape), shape)]
    return product_call(
        twice_kernel, "products", x_count, maps, [adjoint, denoised], [], constants, outs, 12
    )[0]


def pack_kernel(maps_ref, prior_ref, order_ref, out_ref, features_ref, rows_ref):
    rows, planes, width = maps_ref.shape[1:]
    parts, held = out_ref.shape[:2]
    for row in range(0, rows, 2):
        moved = lax.dot_general(
            order_ref[...],
            maps_ref[0, row : row + 2].reshape(2 * planes, width),
            (((1,), (1,)), ((), ())),
            preferred_element_type=jnp.float32,
        )
        for odd in range(2):
            lanes = slice(odd * planes, (odd + 1) * planes)
            rows_ref[pl.ds(row + odd, width, stride=rows), :] = moved[:, lanes]
    for part in range(parts):
        for inner in range(held):
            place = (part * held + inner) * rows
            out_ref[part, inner] = rows_ref[place : place + rows].astype(out_ref.dtype)
    features_ref[...] = prior_ref[...].astype(features_ref.dtype)


def pack_call(maps, prior, parts):
    _, slab_rows, planes, width = maps.shape
    chunk = 16
    count = slab_rows // chunk
    own_rows = prior.shape[0] // count
    held = width // parts
    lanes = np.arange(width).reshape(2, parts, held // 2).transpose(1, 0, 2).reshape(-1)
    order = (lanes[:, None] == np.arange(width)[None, :]).astype(jnp.bfloat16)
    prior_spec = pl.BlockSpec((own_rows,) + prior.shape[1:], lambda g: (g, 0, 0))
    return pl.pallas_call(
        pack_kernel,
        grid=(count,),
        in_specs=[
            pl.BlockSpec((1, chunk, planes, width), lambda g: (0, g, 0, 0)),
            prior_spec,
            pl.BlockSpec(order.shape, lambda g: (0, 0)),
        ],
        out_specs=[
            pl.BlockSpec((parts, held, chunk, planes), lambda g: (0, 0, g, 0)),
            prior_spec,
        ],
        out_shape=[
            jax.ShapeDtypeStruct((parts, held, slab_rows, planes), jnp.bfloat16),
            jax.ShapeDtypeStruct(prior.shape, jnp.bfloat16),
        ],
        scratch_shapes=[pltpu.VMEM((width * chunk, planes), jnp.float32)],
        compiler_params=pltpu.CompilerParams(vmem_limit_bytes=60 * 1024 * 1024),
        cost_estimate=pl.CostEstimate(
            flops=2 * maps.size * width, bytes_accessed=5 * maps.size, transcendentals=0
        ),
        name="pack",
    )(maps, prior, jnp.asarray(order))


def exchange(blocks, axis):
    return lax.all_to_all(blocks, axis, split_axis=0, concat_axis=0, tiled=True)


def x_first(cells, parts):
    rows, planes, width = cells.shape
    split = cells.reshape(rows, planes, 2, parts, width // (2 * parts))
    return jnp.transpose(split, (3, 2, 4, 0, 1))


def x_last(blocks):
    parts, _, x_count, rows, planes = blocks.shape
    return jnp.transpose(blocks, (3, 4, 1, 0, 2)).reshape(rows, planes, 2 * parts * x_count)


def factors(right_right, right_field, field_field, field_image):
    ratio = right_field / right_right
    alpha = right_right / (right_field + penalty * right_right)
    fresh = alpha * alpha * (field_field - ratio * right_field)
    weight = alpha * ratio + fresh / right_right
    mixed = weight * alpha
    curvature = (
        weight * weight * right_field - 2.0 * mixed * field_field + alpha * alpha * field_image
    ) + penalty * (
        weight * weight * right_right - 2.0 * mixed * right_field + alpha * alpha * field_field
    )
    second = fresh / curvature
    moved = alpha + second * weight
    bent = second * alpha
    return (moved, -bent), (alpha * ratio - penalty * second * weight, penalty * bent - moved, bent)


def finish_kernel(
    adjoint_ref, denoised_ref, moved_ref, solution_ref, residual_ref, rows_ref
):
    blocks, _, x_count, rows, planes = adjoint_ref.shape
    readout = blocks * x_count
    totals = jnp.sum(jnp.sum(moved_ref[:, 4 * x_count], axis=0), axis=1, keepdims=True)
    found = factors(*(totals[index : index + 1] for index in range(4)))
    for out_ref, scales in zip((solution_ref, residual_ref), found):
        scales = [jnp.broadcast_to(scale, (rows, planes))[None] for scale in scales]
        for part in range(2):
            for inner in range(x_count):
                right = adjoint_ref[:, part, inner] + penalty * denoised_ref[:, part, inner]
                value = (
                    scales[0] * right
                    + scales[1] * moved_ref[:, (2 + part) * x_count + inner]
                )
                if len(scales) > 2:
                    value = value + scales[2] * moved_ref[:, part * x_count + inner]
                for block in range(blocks):
                    place = part * readout + block * x_count + inner
                    rows_ref[place * rows : (place + 1) * rows] = value[block]
        for row in range(rows):
            out_ref[row] = jnp.transpose(rows_ref[pl.ds(row, 2 * readout, stride=rows), :])


def finish_call(adjoint, denoised, moved):
    blocks, _, x_count, rows, planes = adjoint.shape
    shape = (rows, planes, 2 * blocks * x_count)
    vmem = pl.BlockSpec(memory_space=pltpu.VMEM)
    return pl.pallas_call(
        finish_kernel,
        in_specs=[vmem] * 3,
        out_specs=[vmem] * 2,
        out_shape=[jax.ShapeDtypeStruct(shape, jnp.float32)] * 2,
        scratch_shapes=[pltpu.VMEM((2 * blocks * x_count * rows, planes), jnp.float32)],
        compiler_params=pltpu.CompilerParams(vmem_limit_bytes=32 * 1024 * 1024),
        cost_estimate=pl.CostEstimate(
            flops=8 * adjoint.size, bytes_accessed=24 * adjoint.size, transcendentals=0
        ),
        name="finish",
    )(adjoint, denoised, moved)


def body(
    prior_image,
    coil_maps,
    kspace,
    sampling,
    weight_first,
    bias_first,
    weight_middle,
    bias_middle,
    weight_last,
    bias_last,
):
    readout = prior_image.shape[2] // 2
    own_rows = prior_image.shape[0]
    planes = prior_image.shape[1]
    slabs = lax.axis_size("slab")
    coils = lax.axis_size("coil")
    devices = slabs * coils
    spread = readout % devices == 0 and own_rows % 8 == 0 and held_coils(coils) == coils
    packs = spread and coil_maps.shape[1] % 16 == 0 and own_rows % (coil_maps.shape[1] // 16) == 0
    parts = devices if spread else coils
    x_count = readout // parts
    if packs:
        map_blocks, features = pack_call(coil_maps, prior_image, parts)
    else:
        map_blocks = x_first(coil_maps[0], parts)
        features = prior_image.astype(jnp.bfloat16)
    mask = lax.all_gather(sampling.astype(jnp.bfloat16), "slab", axis=0, tiled=True)
    features, mask = lax.optimization_barrier(
        (with_halo(features, 3), mask)
    )
    mask = jnp.transpose(mask).astype(jnp.float32)
    row_count = mask.shape[0]
    constants = [mask] + half_tables(row_count, planes)
    constants = [jnp.asarray(value) for value in constants]
    adjoint_constants = [mask, jnp.asarray(dft_table(row_count, planes))]

    def coils_to_x(blocks):
        tail = (2 * x_count,) + blocks.shape[-2:]
        if spread:
            blocks = exchange(blocks, axes).reshape((slabs, coils) + tail)
        else:
            blocks = exchange(blocks, "coil").reshape((slabs, coils // slabs) + tail)
            blocks = exchange(blocks, "slab")
        return [(blocks, 0), (blocks, x_count)]

    maps = coils_to_x(map_blocks)
    spectra = coils_to_x(x_first(kspace[0], parts))
    blocks = denoise(
        parts,
        features,
        prior_image,
        weight_first,
        bias_first,
        weight_middle,
        bias_middle,
        weight_last,
        bias_last,
    )
    if blocks.ndim == 3:
        blocks = x_first(blocks, parts)
    if spread:
        adjoint = adjoint_call(spectra, maps, adjoint_constants, x_count, devices)
        payload, adjoint_back = lax.optimization_barrier(
            (
                twice_call(maps, adjoint, exchange(blocks, axes), constants),
                exchange(adjoint, axes),
            )
        )
        payload = exchange(payload, axes)
        return tuple(finish_call(adjoint_back, blocks, payload))

    tail = blocks.shape[1:3]

    def whole_rows(parts_in):
        moved = lax.all_gather(exchange(parts_in, "coil"), "slab", axis=0, tiled=True)
        return jnp.transpose(moved, (1, 2, 0, 3, 4)).reshape((1,) + tail + (-1, planes))

    def own_part(whole):
        rows = whole.shape[3] // slabs
        mine = lax.dynamic_slice_in_dim(whole, lax.axis_index("slab") * rows, rows, axis=3)
        split = jnp.transpose(mine.reshape(tail + (coils, own_rows, planes)), (2, 0, 1, 3, 4))
        return x_last(exchange(split, "coil"))

    adjoint = lax.psum(adjoint_call(spectra, maps, adjoint_constants, x_count, 1), "slab")
    right = adjoint + penalty * whole_rows(blocks)
    field = lax.psum(once_call(maps, right, constants), "slab")
    image = lax.psum(once_call(maps, field, constants), "slab")
    squares = lax.psum(
        jnp.stack(
            [
                jnp.sum(right * right),
                jnp.sum(right * field),
                jnp.sum(field * field),
                jnp.sum(field * image),
            ]
        ),
        "coil",
    )
    scales, others = factors(*(squares[index] for index in range(4)))
    right, field, image = own_part(right), own_part(field), own_part(image)
    return (
        scales[0] * right + scales[1] * field,
        others[0] * right + others[1] * field + others[2] * image,
    )


def solution(mesh):
    placed = (
        P(("slab", "coil"), None, None),
        P("coil", "slab", None, None),
        P("coil", "slab", None, None),
        P("slab", None),
        P(),
        P(),
        P(),
        P(),
        P(),
        P(),
    )
    return jax.shard_map(
        body,
        mesh=mesh,
        in_specs=placed,
        out_specs=(P(("slab", "coil"), None, None), P(("slab", "coil"), None, None)),
        check_vma=False,
    )
```

```python
import functools
import math

import jax
import jax.numpy as jnp
import numpy as np
from jax import lax
from jax.experimental import pallas as pl
from jax.experimental.pallas import tpu as pltpu
from jax.sharding import PartitionSpec as P

CG_ITERS = 2


penalty = 0.5
axes = ("slab", "coil")


def with_halo(cells, width):
    rows = cells.shape[0]
    count = lax.axis_size("slab") * lax.axis_size("coil")
    above, below = [], []
    for hop in range(1, -(-width // rows) + 1):
        taken = min(width - (hop - 1) * rows, rows)
        ends = count - hop
        tail = lax.slice_in_dim(cells, rows - taken, rows, axis=0)
        head = lax.slice_in_dim(cells, 0, taken, axis=0)
        above.insert(0, lax.ppermute(tail, axes, [(i, i + hop) for i in range(ends)]))
        below.append(lax.ppermute(head, axes, [(i + hop, i) for i in range(ends)]))
    return jnp.concatenate(above + [cells] + below, axis=0)


def chunk_rows(rows):
    return max(size for size in range(1, 13) if rows % size == 0)


def chained(lhs_pieces):
    rows = lhs_pieces[0].shape[0] * lhs_pieces[0].shape[1]
    lhs = jnp.concatenate(lhs_pieces, axis=2)
    return lhs.reshape(rows, lhs.shape[2])


def denoise_kernel(
    group,
    first_ref,
    features_ref,
    prior_ref,
    weight_first_ref,
    bias_first_ref,
    weight_middle_ref,
    bias_middle_ref,
    weight_last_ref,
    bias_last_ref,
    out_ref,
    one_ref,
    two_ref,
    taps_ref,
    *turned_refs,
):
    own_rows, planes, width = prior_ref.shape
    edge = (one_ref.shape[2] - two_ref.shape[2]) // 2
    groups = two_ref.shape[2] // group
    first = first_ref[0]
    total = first_ref[1]
    one_ref[:, :, :edge] = jnp.zeros(one_ref.shape[:2] + (edge,), one_ref.dtype)
    one_ref[:, :, edge + two_ref.shape[2] :] = jnp.zeros(
        one_ref.shape[:2] + (edge,), one_ref.dtype
    )

    def store(ref, start, count, lanes, value, reach):
        value = jnp.maximum(value, 0.0).reshape(count, planes, group)
        for row in range(count):
            place = first + (start + row - reach)
            kept = jnp.where((place >= 0) & (place < total), value[row], 0.0)
            ref[start + row, :, lanes] = kept.astype(ref.dtype)

    def first_layer(index, carry):
        lanes = pl.ds(pl.multiple_of(index * group, group), group)
        placed = pl.ds(pl.multiple_of(edge + index * group, 128), group)
        count = chunk_rows(one_ref.shape[0])
        for start in range(0, one_ref.shape[0], count):
            lhs = chained([features_ref[start + tap : start + tap + count] for tap in range(3)])
            value = jnp.dot(lhs, weight_first_ref[:, lanes], preferred_element_type=jnp.float32)
            store(one_ref, start, count, placed, value + bias_first_ref[:, lanes], 2)
        return carry

    lax.fori_loop(0, groups, first_layer, 0)

    def shifted(value, plane, step):
        rows = value.shape[0]
        if step > 0:
            return jnp.where(plane == 0, 0.0, pltpu.roll(value, 1, 0))
        return jnp.where(plane == planes - 1, 0.0, pltpu.roll(value, rows - 1, 0))

    def plane_index(count, lanes):
        return lax.broadcasted_iota(jnp.int32, (count, planes, lanes), 1).reshape(
            count * planes, lanes
        )

    def middle_layer(index, carry):
        lanes = pl.ds(pl.multiple_of(index * group, group), group)
        window = pl.ds(pl.multiple_of(index * group, group), group + 2 * edge)
        count = chunk_rows(two_ref.shape[0])
        plane = plane_index(count, group)
        for start in range(0, two_ref.shape[0], count):
            lhs = chained([one_ref[start + tap : start + tap + count, :, window] for tap in range(3)])
            value = jnp.dot(lhs, weight_middle_ref[...], preferred_element_type=jnp.float32)
            value = (
                value[:, group : 2 * group]
                + shifted(value[:, :group], plane, 1)
                + shifted(value[:, 2 * group :], plane, -1)
            )
            store(two_ref, start, count, lanes, value + bias_middle_ref[:, lanes], 1)
        return carry

    lax.fori_loop(0, groups, middle_layer, 0)

    count = chunk_rows(two_ref.shape[0])

    def last_layer(index, carry):
        start = index * count
        lhs = two_ref[pl.ds(start, count)].reshape(count * planes, two_ref.shape[2])
        value = jnp.dot(lhs, weight_last_ref[...], preferred_element_type=jnp.float32)
        taps_ref[pl.ds(start, count)] = value.reshape(count, planes, value.shape[1])
        return carry

    lax.fori_loop(0, two_ref.shape[0] // count, last_layer, 0)
    plane = plane_index(1, width)

    def last_sum(row):
        sums = []
        for plane_tap in range(3):
            running = None
            for row_tap in range(3):
                lanes = pl.ds((row_tap * 3 + plane_tap) * width, width)
                value = taps_ref[row + row_tap, :, lanes]
                running = value if running is None else running + value
            sums.append(running)
        value = sums[1] + shifted(sums[0], plane, 1) + shifted(sums[2], plane, -1)
        return prior_ref[row] + (value + bias_last_ref[...])

    if not turned_refs:
        for row in range(own_rows):
            out_ref[row] = last_sum(row)
        return

    turned_ref = turned_refs[0]
    for row in range(own_rows):
        turned_ref[pl.ds(row, width, stride=own_rows), :] = jnp.transpose(last_sum(row))
    blocks, _, x_count = out_ref.shape[:3]
    for block in range(blocks):
        for part in range(2):
            for inner in range(x_count):
                place = part * (width // 2) + block * x_count + inner
                out_ref[block, part, inner] = turned_ref[place * own_rows : (place + 1) * own_rows]


def banded(tiles, inner, outer, offset):
    shape = jnp.broadcast_shapes(tiles[0].shape, inner.shape, outer.shape)
    result = jnp.zeros(shape, jnp.bfloat16)
    for tap in range(3):
        result = jnp.where(inner - outer + offset == tap, tiles[tap], result)
    return result


def denoise(
    parts,
    features,
    prior_image,
    weight_first,
    bias_first,
    weight_middle,
    bias_middle,
    weight_last,
    bias_last,
):
    own_rows, planes, width = prior_image.shape
    turned = own_rows % 8 == 0
    out_shape = (parts, 2, width // (2 * parts), own_rows, planes) if turned else prior_image.shape
    readout = width // 2
    channels = weight_first.shape[3]
    span = readout * channels
    group = min(256, span)
    held = group // channels
    edge = 128
    reach = edge // channels
    window = group + 2 * edge

    def lane_place(count, inside):
        return jnp.arange(count * inside, dtype=jnp.int32) // inside

    tiles = jnp.transpose(weight_first, (2, 0, 1, 4, 3)).reshape(3, 18, 1, 1, channels)
    tiles = jnp.broadcast_to(tiles, (3, 18, 1, readout, channels)).reshape(3, 18, 1, span)
    first_table = banded(
        tiles,
        jnp.arange(readout, dtype=jnp.int32)[None, :, None],
        lane_place(readout, channels)[None, None, :],
        1,
    ).reshape(18 * readout, span)
    tiles = jnp.transpose(weight_middle, (2, 0, 4, 1, 3)).reshape(3, 3, 1, channels, 3, 1, channels)
    tiles = jnp.broadcast_to(tiles, (3, 3, 1, channels, 3, held, channels))
    tiles = tiles.reshape(3, 3, 1, channels, 3 * group)
    middle_table = banded(
        tiles,
        jnp.arange(window // channels, dtype=jnp.int32)[None, :, None, None] - reach,
        jnp.tile(lane_place(held, channels), 3)[None, None, None, :],
        1,
    ).reshape(3 * window, 3 * group)
    tiles = jnp.transpose(weight_last, (2, 4, 0, 1, 3)).reshape(3, 1, channels, 18, 1)
    tiles = jnp.broadcast_to(tiles, (3, 1, channels, 18, readout)).reshape(
        3, 1, channels, 18 * readout
    )
    last_table = banded(
        tiles,
        jnp.arange(readout, dtype=jnp.int32)[:, None, None],
        jnp.tile(jnp.arange(readout, dtype=jnp.int32), 18)[None, None, :],
        1,
    ).reshape(span, 18 * readout)

    rim = jnp.zeros_like(features[:, :1])
    features = jnp.concatenate(
        [
            jnp.concatenate([rim, features[:, :-1]], axis=1),
            features,
            jnp.concatenate([features[:, 1:], rim], axis=1),
        ],
        axis=2,
    )
    total = own_rows * lax.axis_size("slab") * lax.axis_size("coil")
    first = lax.axis_index(axes) * own_rows
    places = jnp.stack([first, jnp.asarray(total)]).astype(jnp.int32)
    vmem = pl.BlockSpec(memory_space=pltpu.VMEM)
    flops = 2 * own_rows * planes * (
        features.shape[2] * 3 * span * 3 // 2 + 9 * span * 512 * 5 // 4 + span * 18 * readout * 5 // 4
    )
    return pl.pallas_call(
        functools.partial(denoise_kernel, group),
        in_specs=[pl.BlockSpec(memory_space=pltpu.SMEM)] + [vmem] * 8,
        out_specs=vmem,
        out_shape=jax.ShapeDtypeStruct(out_shape, jnp.float32),
        scratch_shapes=[
            pltpu.VMEM((own_rows + 4, planes, span + 2 * edge), jnp.bfloat16),
            pltpu.VMEM((own_rows + 2, planes, span), jnp.bfloat16),
            pltpu.VMEM((own_rows + 2, planes, 18 * readout), jnp.float32),
        ]
        + [pltpu.VMEM((width * own_rows, planes), jnp.float32)] * turned,
        compiler_params=pltpu.CompilerParams(vmem_limit_bytes=40 * 1024 * 1024),
        cost_estimate=pl.CostEstimate(
            flops=int(flops), bytes_accessed=16 * 1024 * 1024, transcendentals=0
        ),
        name="denoise",
    )(
        places,
        features,
        prior_image,
        first_table,
        jnp.tile(bias_first, readout)[None, :],
        middle_table,
        jnp.tile(bias_middle, readout)[None, :],
        last_table,
        jnp.repeat(bias_last, readout)[None, :],
    )


def table_parts(table):
    high = table.astype(jnp.bfloat16)
    low = (table - high.astype(np.float64)).astype(jnp.bfloat16)
    return high, low


def dft_parts(length):
    positions = np.arange(length, dtype=np.int64)
    angles = (positions[:, None] * positions[None, :] % length) * (2.0 * math.pi / length)
    scale = 1.0 / math.sqrt(length)
    return np.cos(angles) * scale, np.sin(angles) * scale


def turn_block(length):
    cos_part, sin_part = dft_parts(length)
    return np.concatenate(
        [
            np.concatenate([cos_part, sin_part], axis=1),
            np.concatenate([-sin_part, cos_part], axis=1),
        ],
        axis=0,
    )


def dft_table(rows, planes):
    rows_high, rows_low = table_parts(turn_block(rows))
    planes_parts = np.concatenate(table_parts(turn_block(planes).T), axis=0)
    short = max(2 * rows - planes_parts.shape[0], 0)
    planes_parts = np.pad(planes_parts, ((0, short), (0, 0)))
    return np.concatenate([rows_high, rows_low, planes_parts], axis=1)


def half_tables(rows, planes):
    rows_parts = np.concatenate(table_parts(turn_block(rows // 2) * math.sqrt(0.5)), axis=1)
    planes_parts = np.concatenate(table_parts(turn_block(planes).T), axis=0)
    angles = np.arange(rows // 2) * (2.0 * math.pi / rows)
    turns = np.stack([np.cos(angles), np.sin(angles)])[:, :, None]
    turns = np.broadcast_to(turns, (2, rows // 2, planes)).astype(np.float32)
    return [rows_parts, planes_parts, turns]


def value_parts(value):
    high = value.astype(jnp.bfloat16)
    low = (value - high.astype(jnp.float32)).astype(jnp.bfloat16)
    return high, low


def tables_of(ref, rows, planes):
    high, low = ref[:, : 2 * rows], ref[:, 2 * rows : 4 * rows]
    row_table = jnp.concatenate([high, low, high], axis=1)
    high, low = ref[: 2 * planes, 4 * rows :], ref[2 * planes : 4 * planes, 4 * rows :]
    return row_table, jnp.concatenate([high, low, high], axis=0)


def along_planes(fields, table):
    rows, planes = fields[0][0].shape
    stacked = jnp.concatenate([jnp.concatenate(field, axis=1) for field in fields], axis=0)
    high, low = value_parts(stacked)
    moved = jnp.dot(
        jnp.concatenate([high, high, low], axis=1), table, preferred_element_type=jnp.float32
    )
    return [
        (
            moved[index * rows : (index + 1) * rows, :planes],
            moved[index * rows : (index + 1) * rows, planes:],
        )
        for index in range(len(fields))
    ]


def side_by_side(fields):
    return jnp.concatenate(
        [jnp.concatenate([field[part] for field in fields], axis=1) for part in range(2)], axis=0
    )


def along_rows(table, fields):
    rows, planes = fields[0][0].shape
    high, low = value_parts(side_by_side(fields))
    moved = jnp.dot(
        table, jnp.concatenate([high, high, low], axis=0), preferred_element_type=jnp.float32
    )
    return apart(moved, len(fields))


def apart(moved, count):
    rows = moved.shape[0] // 2
    planes = moved.shape[1] // count
    return [
        (
            moved[:rows, index * planes : (index + 1) * planes],
            moved[rows:, index * planes : (index + 1) * planes],
        )
        for index in range(count)
    ]


def plane_of(ref, part):
    value = ref[:, part, 0]
    return value.reshape(value.shape[0] * value.shape[1], value.shape[2])


def coil_plane(ref, coil):
    value = ref[:, coil, 0]
    return value.reshape(value.shape[0] * value.shape[1], value.shape[2])


def map_of(refs, coil):
    return [coil_plane(ref, coil).astype(jnp.float32) for ref in refs]


def image_sums(maps, fields):
    sums = None
    for (map_real, map_imag), (real, imag) in zip(maps, fields):
        terms = (map_real * real - map_imag * imag, -(map_real * imag + map_imag * real))
        sums = terms if sums is None else (sums[0] + terms[0], sums[1] + terms[1])
    return sums


def units_of(refs):
    count = refs[0].shape[1]
    held = 2 if count % 2 == 0 else 1
    return [tuple(range(first, first + held)) for first in range(0, count, held)]


def halved(fields, turns):
    evens, odds = [], []
    rows = fields[0][0].shape[0] // 2
    for real, imag in fields:
        evens.append((real[:rows] + real[rows:], imag[:rows] + imag[rows:]))
        real, imag = real[:rows] - real[rows:], imag[:rows] - imag[rows:]
        odds.append((real * turns[0] + imag * turns[1], imag * turns[0] - real * turns[1]))
    return evens, odds


def rejoined(evens, odds, turns):
    fields = []
    for (even_real, even_imag), (real, imag) in zip(evens, odds):
        real, imag = real * turns[0] + imag * turns[1], imag * turns[0] - real * turns[1]
        fields.append(
            (
                jnp.concatenate([even_real + real, even_real - real], axis=0),
                jnp.concatenate([even_imag + imag, even_imag - imag], axis=0),
            )
        )
    return fields


def masked(fields, mask):
    return [(real * mask, imag * -mask) for real, imag in fields]


def in_groups(values, size):
    return [values[first : first + size] for first in range(0, len(values), size)]


def normal_sums(maps_refs, real, imag, mask_ref, rows_ref, planes_ref, turns_ref):
    half = rows_ref.shape[1] // 2
    row_table = jnp.concatenate([rows_ref[:, :half], rows_ref[:, half:], rows_ref[:, :half]], axis=1)
    half = planes_ref.shape[0] // 2
    plane_table = jnp.concatenate([planes_ref[:half], planes_ref[half:], planes_ref[:half]], axis=0)
    turns = turns_ref[0], turns_ref[1]
    half = turns[0].shape[0]
    masks = tuple(mask_ref[pl.ds(odd, half, stride=2), :] for odd in range(2))
    coils = list(range(maps_refs[0].shape[1]))
    fields = []
    for group in in_groups(coils, 4):
        products = []
        for coil in group:
            map_real, map_imag = map_of(maps_refs, coil)
            products.append(
                (map_real * real - map_imag * imag, map_real * imag + map_imag * real)
            )
        fields += along_planes(products, plane_table)
    units = [halved(unit, turns) for unit in in_groups(fields, 2)]
    units = [[along_rows(row_table, part) for part in unit] for unit in units]
    units = [[masked(part, mask) for part, mask in zip(unit, masks)] for unit in units]
    units = [[along_rows(row_table, part) for part in unit] for unit in units]
    fields = sum((rejoined(*unit, turns) for unit in units), [])
    images = []
    for group in in_groups(fields, 4):
        images += along_planes(group, plane_table)
    total = None
    for group in in_groups(coils, 2):
        sums = image_sums(
            [map_of(maps_refs, coil) for coil in group], [images[coil] for coil in group]
        )
        total = sums if total is None else (total[0] + sums[0], total[1] + sums[1])
    return total


def accumulate(out_ref, values, places):
    shape = out_ref.shape[0], out_ref.shape[-2], out_ref.shape[-1]

    @pl.when(pl.program_id(1) == 0)
    def _():
        for value, place in zip(values, places):
            out_ref[(slice(None),) + place] = value.reshape(shape)

    @pl.when(pl.program_id(1) > 0)
    def _():
        for value, place in zip(values, places):
            out_ref[(slice(None),) + place] += value.reshape(shape)


def adjoint_kernel(
    spectra_real_ref, spectra_imag_ref, maps_real_ref, maps_imag_ref, mask_ref, table_ref, out_ref
):
    maps_refs = maps_real_ref, maps_imag_ref
    mask = mask_ref[...]
    rows, planes = mask.shape
    row_table, plane_table = tables_of(table_ref, rows, planes)
    units = units_of(maps_refs)
    images = []
    for unit in units:
        spectra = []
        for coil in unit:
            real, imag = (
                jnp.transpose(coil_plane(ref, coil).astype(jnp.float32))
                for ref in (spectra_real_ref, spectra_imag_ref)
            )
            spectra.append((real * mask, imag * -mask))
        spectrum = side_by_side(spectra).astype(jnp.bfloat16)
        moved = jnp.dot(
            row_table[:, : 4 * rows],
            jnp.concatenate([spectrum, spectrum], axis=0),
            preferred_element_type=jnp.float32,
        )
        images.append(apart(moved, len(unit)))
    images = [along_planes(image, plane_table) for image in images]
    total = None
    for unit, image in zip(units, images):
        sums = image_sums([map_of(maps_refs, coil) for coil in unit], image)
        total = sums if total is None else (total[0] + sums[0], total[1] + sums[1])
    accumulate(out_ref, total, ((0, 0), (1, 0)))


def product_kernel(maps_real_ref, maps_imag_ref, field_ref, *refs):
    constants, out_ref = refs[:-1], refs[-1]
    fields = [plane_of(field_ref, part) for part in range(2)]
    accumulate(
        out_ref,
        normal_sums((maps_real_ref, maps_imag_ref), *fields, *constants),
        ((0, 0), (1, 0)),
    )


def lane_sums(left, other):
    return jnp.sum(left[0] * other[0] + left[1] * other[1], axis=0, keepdims=True)


def twice_kernel(maps_real_ref, maps_imag_ref, adjoint_ref, denoised_ref, *refs):
    constants, out_ref = refs[:-1], refs[-1]
    maps_refs = maps_real_ref, maps_imag_ref
    x_index = pl.program_id(0)
    x_count = pl.num_programs(0)
    blocks, block_rows, planes = out_ref.shape[0], out_ref.shape[2], out_ref.shape[3]
    shape = blocks, block_rows, planes
    rights = [
        plane_of(adjoint_ref, part) + penalty * plane_of(denoised_ref, part) for part in range(2)
    ]
    fields = normal_sums(maps_refs, *rights, *constants)
    images = normal_sums(maps_refs, *fields, *constants)
    for part in range(2):
        out_ref[:, part * x_count + x_index] = images[part].reshape(shape)
        out_ref[:, (2 + part) * x_count + x_index] = fields[part].reshape(shape)
    totals = jnp.concatenate(
        [
            lane_sums(rights, rights),
            lane_sums(rights, fields),
            lane_sums(fields, fields),
            lane_sums(fields, images),
            jnp.zeros((block_rows - 4, planes), jnp.float32),
        ],
        axis=0,
    )[None]

    @pl.when(x_index == 0)
    def _():
        out_ref[:, 4 * x_count] = jnp.broadcast_to(totals, shape)

    @pl.when(x_index > 0)
    def _():
        out_ref[:, 4 * x_count] += totals


def held_coils(count):
    return max(size for size in (1, 2, 4, 8) if count % size == 0)


def whole(shape):
    return pl.BlockSpec(shape, lambda x, c: (0,) * len(shape))


def coils_spec(planes):
    values, first = planes
    slabs, coils, _, rows, lanes = values.shape
    return pl.BlockSpec(
        (slabs, held_coils(coils), 1, rows, lanes), lambda x, c: (0, c, first + x, 0, 0)
    )


def field_spec(shape):
    return pl.BlockSpec((shape[0], 2, 1) + shape[3:], lambda x, c: (0, 0, x, 0, 0))


def compute_params():
    return pltpu.CompilerParams(
        dimension_semantics=("arbitrary", "arbitrary"), vmem_limit_bytes=22 * 1024 * 1024
    )


def product_call(kernel, name, x_count, coil_planes, fields, extras, constants, outs, passes):
    coils = coil_planes[0][0].shape[1]
    mask = constants[0]
    rows, planes = mask.shape
    flops = 2 * 2 * rows * planes * (2 * rows + 2 * planes) * coils * x_count * passes
    values = [planes_of[0] for planes_of in coil_planes] + fields + extras + constants
    return pl.pallas_call(
        kernel,
        grid=(x_count, coils // held_coils(coils)),
        in_specs=[coils_spec(planes_of) for planes_of in coil_planes]
        + [field_spec(field.shape) for field in fields]
        + [whole(value.shape) for value in extras + constants],
        out_specs=[spec for spec, _ in outs],
        out_shape=[jax.ShapeDtypeStruct(shape, jnp.float32) for _, shape in outs],
        compiler_params=compute_params(),
        cost_estimate=pl.CostEstimate(
            flops=int(flops), bytes_accessed=8 * 1024 * 1024, transcendentals=0
        ),
        name=name,
    )(*values)


def adjoint_call(spectra, maps, constants, x_count, blocks):
    rows, planes = constants[0].shape
    shape = (blocks, 2, x_count, rows // blocks, planes)
    outs = [(field_spec(shape), shape)]
    return product_call(
        adjoint_kernel, "adjoint", x_count, spectra + maps, [], [], constants, outs, 3
    )[0]


def once_call(maps, field, constants):
    shape = field.shape
    outs = [(field_spec(shape), shape)]
    return product_call(
        product_kernel, "product", shape[2], maps, [field], [], constants, outs, 6
    )[0]


def twice_call(maps, adjoint, denoised, constants):
    blocks, _, x_count, block_rows, planes = adjoint.shape
    shape = (blocks, 4 * x_count + 1, block_rows, planes)
    outs = [(whole(shape), shape)]
    return product_call(
        twice_kernel, "products", x_count, maps, [adjoint, denoised], [], constants, outs, 12
    )[0]


def pack_kernel(maps_ref, prior_ref, order_ref, out_ref, features_ref, rows_ref):
    rows, planes, width = maps_ref.shape[1:]
    parts, held = out_ref.shape[:2]
    chunk = pl.ds(pl.multiple_of(pl.program_id(0) * rows, rows), rows)
    for row in range(0, rows, 2):
        moved = lax.dot_general(
            order_ref[...],
            maps_ref[0, row : row + 2].reshape(2 * planes, width),
            (((1,), (1,)), ((), ())),
            preferred_element_type=jnp.float32,
        )
        for odd in range(2):
            lanes = slice(odd * planes, (odd + 1) * planes)
            rows_ref[pl.ds(row + odd, width, stride=rows), :] = moved[:, lanes]
    for part in range(parts):
        for inner in range(held):
            place = (part * held + inner) * rows
            out_ref[part, inner, chunk, :] = rows_ref[place : place + rows].astype(out_ref.dtype)
    features_ref[...] = prior_ref[...].astype(features_ref.dtype)


def pack_call(maps, prior, parts):
    _, slab_rows, planes, width = maps.shape
    chunk = 16
    count = slab_rows // chunk
    own_rows = prior.shape[0] // count
    held = width // parts
    lanes = np.arange(width).reshape(2, parts, held // 2).transpose(1, 0, 2).reshape(-1)
    order = (lanes[:, None] == np.arange(width)[None, :]).astype(jnp.bfloat16)
    prior_spec = pl.BlockSpec((own_rows,) + prior.shape[1:], lambda g: (g, 0, 0))
    return pl.pallas_call(
        pack_kernel,
        grid=(count,),
        in_specs=[
            pl.BlockSpec((1, chunk, planes, width), lambda g: (0, g, 0, 0)),
            prior_spec,
            pl.BlockSpec(order.shape, lambda g: (0, 0)),
        ],
        out_specs=[
            pl.BlockSpec((parts, held, slab_rows, planes), lambda g: (0, 0, 0, 0)),
            prior_spec,
        ],
        out_shape=[
            jax.ShapeDtypeStruct((parts, held, slab_rows, planes), jnp.bfloat16),
            jax.ShapeDtypeStruct(prior.shape, jnp.bfloat16),
        ],
        scratch_shapes=[pltpu.VMEM((width * chunk, planes), jnp.float32)],
        compiler_params=pltpu.CompilerParams(vmem_limit_bytes=60 * 1024 * 1024),
        cost_estimate=pl.CostEstimate(
            flops=2 * maps.size * width, bytes_accessed=5 * maps.size, transcendentals=0
        ),
        name="pack",
    )(maps, prior, jnp.asarray(order))


def exchange(blocks, axis):
    return lax.all_to_all(blocks, axis, split_axis=0, concat_axis=0, tiled=True)


def x_first(cells, parts):
    rows, planes, width = cells.shape
    split = cells.reshape(rows, planes, 2, parts, width // (2 * parts))
    return jnp.transpose(split, (3, 2, 4, 0, 1))


def x_last(blocks):
    parts, _, x_count, rows, planes = blocks.shape
    return jnp.transpose(blocks, (3, 4, 1, 0, 2)).reshape(rows, planes, 2 * parts * x_count)


def factors(right_right, right_field, field_field, field_image):
    ratio = right_field / right_right
    alpha = right_right / (right_field + penalty * right_right)
    fresh = alpha * alpha * (field_field - ratio * right_field)
    weight = alpha * ratio + fresh / right_right
    mixed = weight * alpha
    curvature = (
        weight * weight * right_field - 2.0 * mixed * field_field + alpha * alpha * field_image
    ) + penalty * (
        weight * weight * right_right - 2.0 * mixed * right_field + alpha * alpha * field_field
    )
    second = fresh / curvature
    moved = alpha + second * weight
    bent = second * alpha
    return (moved, -bent), (alpha * ratio - penalty * second * weight, penalty * bent - moved, bent)


def finish_kernel(
    adjoint_ref, denoised_ref, moved_ref, solution_ref, residual_ref, rows_ref
):
    blocks, _, x_count, rows, planes = adjoint_ref.shape
    readout = blocks * x_count
    totals = jnp.sum(jnp.sum(moved_ref[:, 4 * x_count], axis=0), axis=1, keepdims=True)
    found = factors(*(totals[index : index + 1] for index in range(4)))
    for out_ref, scales in zip((solution_ref, residual_ref), found):
        scales = [jnp.broadcast_to(scale, (rows, planes))[None] for scale in scales]
        for part in range(2):
            for inner in range(x_count):
                right = adjoint_ref[:, part, inner] + penalty * denoised_ref[:, part, inner]
                value = (
                    scales[0] * right
                    + scales[1] * moved_ref[:, (2 + part) * x_count + inner]
                )
                if len(scales) > 2:
                    value = value + scales[2] * moved_ref[:, part * x_count + inner]
                for block in range(blocks):
                    place = part * readout + block * x_count + inner
                    rows_ref[place * rows : (place + 1) * rows] = value[block]
        for row in range(rows):
            out_ref[row] = jnp.transpose(rows_ref[pl.ds(row, 2 * readout, stride=rows), :])


def finish_call(adjoint, denoised, moved):
    blocks, _, x_count, rows, planes = adjoint.shape
    shape = (rows, planes, 2 * blocks * x_count)
    vmem = pl.BlockSpec(memory_space=pltpu.VMEM)
    return pl.pallas_call(
        finish_kernel,
        in_specs=[vmem] * 3,
        out_specs=[vmem] * 2,
        out_shape=[jax.ShapeDtypeStruct(shape, jnp.float32)] * 2,
        scratch_shapes=[pltpu.VMEM((2 * blocks * x_count * rows, planes), jnp.float32)],
        compiler_params=pltpu.CompilerParams(vmem_limit_bytes=32 * 1024 * 1024),
        cost_estimate=pl.CostEstimate(
            flops=8 * adjoint.size, bytes_accessed=24 * adjoint.size, transcendentals=0
        ),
        name="finish",
    )(adjoint, denoised, moved)


def body(
    prior_image,
    coil_maps,
    kspace,
    sampling,
    weight_first,
    bias_first,
    weight_middle,
    bias_middle,
    weight_last,
    bias_last,
):
    readout = prior_image.shape[2] // 2
    own_rows = prior_image.shape[0]
    planes = prior_image.shape[1]
    slabs = lax.axis_size("slab")
    coils = lax.axis_size("coil")
    devices = slabs * coils
    spread = readout % devices == 0 and own_rows % 8 == 0 and held_coils(coils) == coils
    packs = spread and coil_maps.shape[1] % 16 == 0 and own_rows % (coil_maps.shape[1] // 16) == 0
    parts = devices if spread else coils
    x_count = readout // parts
    if packs:
        map_blocks, features = pack_call(coil_maps, prior_image, parts)
    else:
        map_blocks = x_first(coil_maps[0], parts)
        features = prior_image.astype(jnp.bfloat16)
    mask = lax.all_gather(sampling.astype(jnp.bfloat16), "slab", axis=0, tiled=True)
    features, mask = lax.optimization_barrier(
        (with_halo(features, 3), mask)
    )
    mask = jnp.transpose(mask).astype(jnp.float32)
    row_count = mask.shape[0]
    constants = [mask] + half_tables(row_count, planes)
    constants = [jnp.asarray(value) for value in constants]
    adjoint_constants = [mask, jnp.asarray(dft_table(row_count, planes))]

    def coils_to_x(blocks):
        tail = (2 * x_count,) + blocks.shape[-2:]
        if spread:
            blocks = exchange(blocks, axes).reshape((slabs, coils) + tail)
        else:
            blocks = exchange(blocks, "coil").reshape((slabs, coils // slabs) + tail)
            blocks = exchange(blocks, "slab")
        return [(blocks, 0), (blocks, x_count)]

    maps = coils_to_x(map_blocks)
    spectra = coils_to_x(x_first(kspace[0], parts))
    blocks = denoise(
        parts,
        features,
        prior_image,
        weight_first,
        bias_first,
        weight_middle,
        bias_middle,
        weight_last,
        bias_last,
    )
    if blocks.ndim == 3:
        blocks = x_first(blocks, parts)
    if spread:
        adjoint = adjoint_call(spectra, maps, adjoint_constants, x_count, devices)
        payload, adjoint_back = lax.optimization_barrier(
            (
                twice_call(maps, adjoint, exchange(blocks, axes), constants),
                exchange(adjoint, axes),
            )
        )
        payload = exchange(payload, axes)
        return tuple(finish_call(adjoint_back, blocks, payload))

    tail = blocks.shape[1:3]

    def whole_rows(parts_in):
        moved = lax.all_gather(exchange(parts_in, "coil"), "slab", axis=0, tiled=True)
        return jnp.transpose(moved, (1, 2, 0, 3, 4)).reshape((1,) + tail + (-1, planes))

    def own_part(whole):
        rows = whole.shape[3] // slabs
        mine = lax.dynamic_slice_in_dim(whole, lax.axis_index("slab") * rows, rows, axis=3)
        split = jnp.transpose(mine.reshape(tail + (coils, own_rows, planes)), (2, 0, 1, 3, 4))
        return x_last(exchange(split, "coil"))

    adjoint = lax.psum(adjoint_call(spectra, maps, adjoint_constants, x_count, 1), "slab")
    right = adjoint + penalty * whole_rows(blocks)
    field = lax.psum(once_call(maps, right, constants), "slab")
    image = lax.psum(once_call(maps, field, constants), "slab")
    squares = lax.psum(
        jnp.stack(
            [
                jnp.sum(right * right),
                jnp.sum(right * field),
                jnp.sum(field * field),
                jnp.sum(field * image),
            ]
        ),
        "coil",
    )
    scales, others = factors(*(squares[index] for index in range(4)))
    right, field, image = own_part(right), own_part(field), own_part(image)
    return (
        scales[0] * right + scales[1] * field,
        others[0] * right + others[1] * field + others[2] * image,
    )


def solution(mesh):
    placed = (
        P(("slab", "coil"), None, None),
        P("coil", "slab", None, None),
        P("coil", "slab", None, None),
        P("slab", None),
        P(),
        P(),
        P(),
        P(),
        P(),
        P(),
    )
    return jax.shard_map(
        body,
        mesh=mesh,
        in_specs=placed,
        out_specs=(P(("slab", "coil"), None, None), P(("slab", "coil"), None, None)),
        check_vma=False,
    )
```
